32 devices in a mesh: gx: 2 (over core), gy: 4 (over y, x), grp: 4 (over z).
Axes of the slice: x: 2, y: 2, z: 4, core: 2. Of those that a mesh axis runs over, the one named last changes fastest.
Arguments:
- field_in: bfloat16 [4, 16, 64, 1024], P('grp', 'gx', 'gy'), may hold values from -6 to 6
- first_weight: bfloat16 [3, 3, 3, 64, 64], replicated, may hold values from -0.15625 to 0.15625
- second_weight: bfloat16 [3, 3, 3, 64, 64], replicated, may hold values from -0.15625 to 0.15625
- cotangent: bfloat16 [4, 16, 64, 1024], P('grp', 'gx', 'gy'), may hold values from -6 to 6
Outputs:
- field_out: bfloat16 [4, 16, 64, 1024], P('grp', 'gx', 'gy')
- first_grad: float32 [3, 3, 3, 64, 64], replicated
- second_grad: float32 [3, 3, 3, 64, 64], replicated
The draws below stay inside these ranges and needn't reach their ends.
All inputs are finite; a program needn't handle non-finite values.
Results may differ from the reference program's by a relative error of at most 0.0095.
Values may be sent and summed in bfloat16 or wider, within the bound.
No kernel may reach another device: no remote copies, remote signals or barrier semaphores. Data moves between devices by JAX's collectives and lax.ppermute only.
A program may use at most 64 MiB of HBM per device.

```python
import math
import jax
import jax.numpy as jnp
from jax import lax

C = 64
NZ = 16
S = 4
NX = 16
NY = 64


def level_of(own_key, extent, cuts, smallest, high):
    level, own = 1.0, jax.random.fold_in(own_key, 6)
    for position, shards_of in cuts:
        heights = jnp.exp(jax.random.uniform(jax.random.fold_in(own, position), (shards_of,), jnp.float32, smallest / len(cuts), high / len(cuts)))
        level = level * jnp.repeat(heights, extent[position] // shards_of).reshape([-1 if axis == position else 1 for axis in range(len(extent))])
    return level


def gaussian(own_key, shape, deviation, most, shards=(), dtype=jnp.bfloat16):
    level = level_of(own_key, shape, shards, -0.22, 0.18) if shards else 1.0
    array = jax.random.normal(own_key, shape, jnp.float32) * deviation * level
    return jnp.minimum(jnp.maximum(array, -most), most).astype(dtype)


def setup_inputs(seed: int = 0) -> dict:
    streams_of = jax.random.split(jax.random.key(seed), 5)
    field_in = gaussian(streams_of[0], (S, NX, NY, NZ * C), 1.0, 6.0, ((0, 4), (1, 2), (2, 4)))
    first_weight = gaussian(streams_of[1], (3, 3, 3, C, C), (27 * C) ** -0.5, 0.15625)
    second_weight = gaussian(streams_of[2], (3, 3, 3, C, C), (27 * C) ** -0.5, 0.15625)
    cotangent = gaussian(streams_of[3], (S, NX, NY, NZ * C), 1.0, 6.0, ((0, 4), (1, 2), (2, 4)))
    return {"field_in": field_in, "first_weight": first_weight, "second_weight": second_weight, "cotangent": cotangent}


def conv_full(field, weight):
    return lax.conv_general_dilated(field, weight, (1, 1, 1), ((1, 1), (1, 1), (1, 1)), dimension_numbers=('NHWDC', 'HWDIO', 'NHWDC'), precision=lax.Precision.HIGHEST, preferred_element_type=jnp.float32)

def kernel_grad(field, grad_out):
    result = lax.conv_general_dilated(field, grad_out, (1, 1, 1), ((1, 1), (1, 1), (1, 1)), dimension_numbers=('CHWDN', 'IHWDO', 'NHWDC'), precision=lax.Precision.HIGHEST, preferred_element_type=jnp.float32)
    return jnp.transpose(result, (1, 2, 3, 0, 4))

def reference(field_in, first_weight, second_weight, cotangent):
    first_w = first_weight.astype(jnp.float32)
    second_w = second_weight.astype(jnp.float32)
    flipped = jnp.swapaxes(second_w[::-1, ::-1, ::-1], 3, 4)

    def one_sample(items):
        source, grad_out = items
        source = source.reshape(1, NX, NY, NZ, C).astype(jnp.float32)
        grad_out = grad_out.reshape(1, NX, NY, NZ, C).astype(jnp.float32)
        pre_first = conv_full(source, first_w)
        hidden = jax.nn.silu(pre_first).astype(jnp.bfloat16)
        hidden = lax.optimization_barrier(hidden).astype(jnp.float32)
        output = conv_full(hidden, second_w).astype(jnp.bfloat16)
        second_part = kernel_grad(hidden, grad_out)
        hidden_grad = conv_full(grad_out, flipped)
        sigma = jax.nn.sigmoid(pre_first)
        pre_grad = (hidden_grad * sigma * (1.0 + pre_first * (1.0 - sigma))).astype(jnp.bfloat16)
        pre_grad = lax.optimization_barrier(pre_grad).astype(jnp.float32)
        first_part = kernel_grad(source, pre_grad)
        return (output.reshape(NX, NY, NZ * C), first_part, second_part)
    outputs, first_parts, second_parts = lax.map(one_sample, (field_in, cotangent))
    factor = 1.0 / math.sqrt(S * NX * NY * NZ)
    return (outputs, lax.optimization_barrier(jnp.sum(first_parts, axis=0)) * factor, lax.optimization_barrier(jnp.sum(second_parts, axis=0)) * factor)
```

```python
import functools
import math

import jax
import jax.numpy as jnp
from jax import lax
from jax.experimental import pallas as pl
from jax.experimental.pallas import tpu as pltpu
from jax.sharding import PartitionSpec as P

C = 64
NZ = 16
BF16 = jnp.bfloat16
F32 = jnp.float32
TAPS = [(dx, dy) for dx in range(3) for dy in range(3)]
BLOCKS = 14


def swap(array):
    return lax.ppermute(array, "gx", [(0, 1), (1, 0)])


def shift(array, step):
    count = lax.axis_size("gy")
    return lax.ppermute(array, "gy", [(i, i + step) for i in range(count) if 0 <= i + step < count])


def dot(a, b):
    return jnp.dot(a, b, preferred_element_type=F32)


def dot_nt(a, b):
    return lax.dot_general(a, b, (((1,), (1,)), ((), ())), preferred_element_type=F32)


def band(taps):
    zero = jnp.zeros((C, C), BF16)
    left = jnp.concatenate(list(taps) + [zero], axis=0)
    right = jnp.concatenate([zero] + list(taps), axis=0)
    return jnp.concatenate([left, right], axis=1)


def band_flipped(taps):
    zero = jnp.zeros((C, C), BF16)
    back = list(taps)[::-1]
    upper = jnp.concatenate(back + [zero], axis=1)
    lower = jnp.concatenate([zero] + back, axis=1)
    return jnp.concatenate([upper, lower], axis=0)


def shifted_rows(scratch, target, width):
    rows = target.shape[2]
    target[0, :, :, pl.ds(width, scratch.shape[2])] = scratch[:, 7:7 + rows, :].astype(BF16)
    target[2, :, :, pl.ds(width, scratch.shape[2])] = scratch[:, 9:9 + rows, :].astype(BF16)


def weight_gradient(rows_t, taps_of, total):
    result = []
    for dx, dy in TAPS:
        full = dot(rows_t, taps_of(dx, dy)) * total
        result.append(full[0:C, 0:3 * C] + full[C:2 * C, C:4 * C])
    return result


def packed(pieces):
    blocks = [piece[:, 0:2 * C] for piece in pieces]
    for pair in range(0, 9, 2):
        second = pieces[pair + 1][:, 2 * C:3 * C] if pair + 1 < 9 else jnp.zeros((C, C), F32)
        blocks.append(jnp.concatenate([pieces[pair][:, 2 * C:3 * C], second], axis=1))
    return blocks


def layers(factor, gx_count, gy_count, field, cot, side, sent_head, sent_tail, from_prev, from_next, w1, w2,
           out, keep, send, fd, cd, hd, fs, cs, hs, es, eh, pf, w1b, w2b, wfb):
    nx, ny, width = field.shape
    pairs = NZ // 2
    lane = 2 * C
    gx = lax.axis_index("gx")
    gy = lax.axis_index("gy")
    low = (gx > 0).astype(F32)
    high = (gx < gx_count - 1).astype(F32)
    prev = (gy > 0).astype(F32)
    after = (gy < gy_count - 1).astype(F32)

    for t in range(9):
        w1b[t * 4 * C:(t + 1) * 4 * C, :] = band([w1[3 * t + z] for z in range(3)])
        w2b[t * 4 * C:(t + 1) * 4 * C, :] = band([w2[3 * t + z] for z in range(3)])
        wfb[:, t * 4 * C:(t + 1) * 4 * C] = band_flipped([w2[3 * (8 - t) + z] for z in range(3)])

    fs[2:2 + nx, 8:8 + ny, :] = field[...].astype(F32)
    fs[0:2, 8:8 + ny, :] = side[0:2].astype(F32) * low
    fs[2 + nx:4 + nx, 8:8 + ny, :] = side[0:2].astype(F32) * high
    cs[1:1 + nx, 8:8 + ny, :] = cot[...].astype(F32)
    cs[0:1, 8:8 + ny, :] = side[2:3].astype(F32) * low
    cs[1 + nx:2 + nx, 8:8 + ny, :] = side[2:3].astype(F32) * high

    rows_prev = from_prev[...].astype(F32) * prev
    rows_next = from_next[...].astype(F32) * after
    for x in range(nx + 4):
        fs[x, 7:8, :] = rows_prev[1, x:x + 1, :]
        fs[x, 8 + ny:9 + ny, :] = rows_next[0, x:x + 1, :]
    for x in range(nx + 2):
        cs[x, 7:8, :] = rows_prev[2, x + 1:x + 2, :]
        cs[x, 8 + ny:9 + ny, :] = rows_next[2, x + 1:x + 2, :]

    for copies in (fd, cd):
        copies[:, :, :, 0:lane] = jnp.zeros(copies.shape[:3] + (lane,), BF16)
        copies[:, :, :, lane + width:] = jnp.zeros(copies.shape[:3] + (lane,), BF16)
    for scratch, copies in ((fs, fd), (cs, cd)):
        shifted_rows(scratch, copies, lane)
        copies[1, :, :, lane:lane + width] = scratch[:, 8:8 + ny, :].astype(BF16)

    es[...] = jnp.zeros(es.shape, F32)
    for index, rows in enumerate((
        rows_prev[0], rows_prev[1], sent_head[0].astype(F32),
        sent_tail[1].astype(F32), rows_next[0], rows_next[1],
    )):
        es[index, 0:nx + 4, :] = rows
    eh[:, :, :, 0:lane] = jnp.zeros((9, 2, 16, lane), BF16)
    eh[:, :, :, lane + width:] = jnp.zeros((9, 2, 16, lane), BF16)
    for t, (dx, dy) in enumerate(TAPS):
        for end in range(2):
            eh[t, end, :, lane:lane + width] = es[3 * end + dy, dx:dx + 16, :].astype(BF16)

    depth = nx + 2
    main = depth * ny
    x_of = lax.broadcasted_iota(jnp.int32, (depth, ny, lane), 0)
    mask = jnp.where(x_of == 0, low, jnp.where(x_of == depth - 1, high, 1.0))
    end_of = lax.broadcasted_iota(jnp.int32, (2, 16, lane), 0)
    row_of = lax.broadcasted_iota(jnp.int32, (2, 16, lane), 1)
    end_mask = jnp.where(row_of == 0, low, jnp.where(row_of == depth - 1, high, 1.0)) * jnp.where(end_of == 0, prev, after)
    lane_of = lax.broadcasted_iota(jnp.int32, (1, 1, lane), 2)
    for p in range(pairs + 1):
        span = slice(lane * p, lane * (p + 2))
        here = slice(lane * p, lane * (p + 1))
        block = jnp.concatenate(
            [
                jnp.concatenate([fd[dy, dx:dx + depth, :, span].reshape(main, 2 * lane) for dx, dy in TAPS], axis=1),
                jnp.concatenate([eh[t, :, :, span].reshape(32, 2 * lane) for t in range(9)], axis=1),
            ],
            axis=0,
        )
        pre = dot(block, w1b[...])
        hidden = pre * jax.nn.sigmoid(pre)
        hidden_main = hidden[:main].reshape(depth, ny, lane) * mask
        hidden_ends = hidden[main:].reshape(2, 16, lane) * end_mask
        if p == 0:
            hidden_main = jnp.where(lane_of >= C, hidden_main, 0.0)
            hidden_ends = jnp.where(lane_of >= C, hidden_ends, 0.0)
        if p == pairs:
            hidden_main = jnp.where(lane_of < C, hidden_main, 0.0)
            hidden_ends = jnp.where(lane_of < C, hidden_ends, 0.0)
        pf[p] = pre[ny:ny + nx * ny]
        hs[:, 8:8 + ny, here] = hidden_main
        hd[1, :, :, here] = hidden_main.astype(BF16)
        for x in range(depth):
            hs[x, 7:8, here] = hidden_ends[0, x:x + 1, :]
            hs[x, 8 + ny:9 + ny, here] = hidden_ends[1, x:x + 1, :]
    shifted_rows(hs, hd, 0)

    cells = nx * ny

    def hidden_span(dx, dy, p):
        return hd[dy, dx:dx + nx, :, lane * p:lane * (p + 2)].reshape(cells, 2 * lane)

    def field_span(dx, dy, p):
        return fd[dy, dx + 1:dx + 1 + nx, :, lane * p:lane * (p + 2)].reshape(cells, 2 * lane)

    def cot_span(dx, dy, p):
        return cd[dy, dx:dx + nx, :, lane * p:lane * (p + 2)].reshape(cells, 2 * lane)

    cot_t = jnp.concatenate(
        [cot[:, :, lane * p:lane * (p + 1)].reshape(cells, lane).T for p in range(pairs)], axis=1)
    second = packed(weight_gradient(
        cot_t,
        lambda dx, dy: jnp.concatenate([hidden_span(dx, dy, p) for p in range(pairs)], axis=0),
        factor))

    grads_t = []
    for p in range(pairs + 1):
        grad = dot_nt(jnp.concatenate([cot_span(dx, dy, p) for dx, dy in TAPS], axis=1), wfb[...])
        pre = pf[p]
        sigma = jax.nn.sigmoid(pre)
        grad = grad * sigma * (1.0 + pre * (1.0 - sigma))
        if p == 0:
            grad = jnp.where(lane_of[0] >= C, grad, 0.0)
        if p == pairs:
            grad = jnp.where(lane_of[0] < C, grad, 0.0)
        grads_t.append(grad.astype(BF16).T)
    first = packed(weight_gradient(
        jnp.concatenate(grads_t, axis=1),
        lambda dx, dy: jnp.concatenate([field_span(dx, dy, p) for p in range(pairs + 1)], axis=0),
        factor))

    for index in range(BLOCKS):
        rows = slice(index * C, (index + 1) * C)
        keep[rows, :] = jnp.where(gx == 0, first[index], second[index])
        send[rows, :] = jnp.where(gx == 0, second[index], first[index]).astype(BF16)
    if keep.shape[0] > BLOCKS * C:
        rest = (keep.shape[0] - BLOCKS * C, lane)
        keep[BLOCKS * C:, :] = jnp.zeros(rest, F32)
        send[BLOCKS * C:, :] = jnp.zeros(rest, BF16)

    for p in range(pairs):
        block = jnp.concatenate([hidden_span(dx, dy, p) for dx, dy in TAPS], axis=1)
        out[:, :, lane * p:lane * (p + 1)] = dot(block, w2b[...]).astype(BF16).reshape(nx, ny, lane)


def unpack(mine, other, first, second):
    gx = lax.axis_index("gx")
    a = mine[...].astype(F32)
    b = other[...].astype(F32)
    for out, rows in ((first, jnp.where(gx == 0, a, b)), (second, jnp.where(gx == 0, b, a))):
        for t in range(9):
            turned = rows[t * C:(t + 1) * C].T
            out[3 * t] = turned[0:C]
            out[3 * t + 1] = turned[C:2 * C]
        for pair in range(5):
            turned = rows[(9 + pair) * C:(10 + pair) * C].T
            out[6 * pair + 2] = turned[0:C]
            if pair < 4:
                out[6 * pair + 5] = turned[C:2 * C]


def vmem(count):
    return [pl.BlockSpec(memory_space=pltpu.VMEM)] * count


def shards(field_in, first_weight, second_weight, cotangent):
    nx, ny, width = field_in.shape[1:]
    gx_count, gy_count, grp_count = (lax.axis_size(axis) for axis in ("gx", "gy", "grp"))
    total = field_in.shape[0] * nx * ny * NZ * gx_count * gy_count * grp_count
    factor = 1.0 / math.sqrt(total)
    ranks = gy_count * grp_count
    rows = -(-BLOCKS * C // (16 * ranks)) * 16 * ranks
    gx = lax.axis_index("gx")
    field = field_in[0]
    cot = cotangent[0]

    side = swap(jnp.concatenate(
        [
            jnp.where(gx == 0, field[nx - 2:nx], field[0:2]),
            jnp.where(gx == 0, cot[nx - 1:nx], cot[0:1]),
        ],
        axis=0,
    ))
    low = jnp.where(gx == 0, jnp.zeros_like(side), side)
    high = jnp.where(gx == 0, side, jnp.zeros_like(side))

    def edge(first_row, cot_row):
        fields = jnp.concatenate([a[:, first_row:first_row + 2] for a in (low[0:2], field, high[0:2])], axis=0)
        cots = jnp.concatenate([a[:, cot_row:cot_row + 1] for a in (low[2:3], cot, high[2:3])], axis=0)
        cots = jnp.pad(cots, ((1, 1), (0, 0), (0, 0)))
        return jnp.transpose(jnp.concatenate([fields, cots], axis=1), (1, 0, 2))

    head = edge(0, 0)
    tail = edge(ny - 2, ny - 1)
    from_prev = shift(tail, 1)
    from_next = shift(head, -1)

    lane = 2 * C
    wide = width + 2 * lane
    out, keep, send = pl.pallas_call(
        functools.partial(layers, factor, gx_count, gy_count),
        out_shape=[
            jax.ShapeDtypeStruct((nx, ny, width), BF16),
            jax.ShapeDtypeStruct((rows, lane), F32),
            jax.ShapeDtypeStruct((rows, lane), BF16),
        ],
        in_specs=vmem(9),
        out_specs=vmem(3),
        scratch_shapes=[
            pltpu.VMEM((3, nx + 4, ny, wide), BF16),
            pltpu.VMEM((3, nx + 2, ny, wide), BF16),
            pltpu.VMEM((3, nx + 2, ny, width + lane), BF16),
            pltpu.VMEM((nx + 4, ny + 16, width), F32),
            pltpu.VMEM((nx + 2, ny + 16, width), F32),
            pltpu.VMEM((nx + 2, ny + 16, width + lane), F32),
            pltpu.VMEM((6, 24, width), F32),
            pltpu.VMEM((9, 2, 16, wide), BF16),
            pltpu.VMEM((NZ // 2 + 1, nx * ny, lane), F32),
            pltpu.VMEM((9 * 4 * C, lane), BF16),
            pltpu.VMEM((9 * 4 * C, lane), BF16),
            pltpu.VMEM((lane, 9 * 4 * C), BF16),
        ],
        compiler_params=pltpu.CompilerParams(vmem_limit_bytes=56 * 1024 * 1024),
        name="layers",
    )(field, cot, side, head, tail, from_prev, from_next,
      first_weight.reshape(27, C, C), second_weight.reshape(27, C, C))

    both = (keep + swap(send).astype(F32)).astype(BF16).reshape(ranks, rows // ranks, lane)
    terms = lax.all_to_all(both, ("gy", "grp"), 0, 0)
    mine = jnp.sum(terms.astype(F32), axis=0).astype(BF16)
    mine = lax.all_to_all(jnp.broadcast_to(mine[None], terms.shape), ("gy", "grp"), 0, 0).reshape(rows, lane)
    other = swap(mine)
    first, second = pl.pallas_call(
        unpack,
        out_shape=[jax.ShapeDtypeStruct((27, C, C), F32)] * 2,
        in_specs=vmem(2),
        out_specs=vmem(2),
        name="unpack",
    )(mine, other)
    shape = (3, 3, 3, C, C)
    return out[None], first.reshape(shape), second.reshape(shape)


def solution(mesh):
    return jax.shard_map(
        shards,
        mesh=mesh,
        in_specs=(P("grp", "gx", "gy", None), P(), P(), P("grp", "gx", "gy", None)),
        out_specs=(P("grp", "gx", "gy", None), P(), P()),
        check_vma=False,
    )
```

```python
import functools
import math

import jax
import jax.numpy as jnp
from jax import lax
from jax.experimental import pallas as pl
from jax.experimental.pallas import tpu as pltpu
from jax.sharding import PartitionSpec as P

C = 64
NZ = 16
BF16 = jnp.bfloat16
F32 = jnp.float32
TAPS = [(dx, dy) for dx in range(3) for dy in range(3)]
BLOCKS = 14


def swap(array):
    return lax.ppermute(array, "gx", [(0, 1), (1, 0)])


def shift(array, step):
    count = lax.axis_size("gy")
    return lax.ppermute(array, "gy", [(i, i + step) for i in range(count) if 0 <= i + step < count])


def dot(a, b):
    return jnp.dot(a, b, preferred_element_type=F32)


def dot_nt(a, b):
    return lax.dot_general(a, b, (((1,), (1,)), ((), ())), preferred_element_type=F32)


def band(taps):
    zero = jnp.zeros((C, C), BF16)
    left = jnp.concatenate(list(taps) + [zero], axis=0)
    right = jnp.concatenate([zero] + list(taps), axis=0)
    return jnp.concatenate([left, right], axis=1)


def band_flipped(taps):
    zero = jnp.zeros((C, C), BF16)
    back = list(taps)[::-1]
    upper = jnp.concatenate(back + [zero], axis=1)
    lower = jnp.concatenate([zero] + back, axis=1)
    return jnp.concatenate([upper, lower], axis=0)


def shifted_rows(scratch, target, width):
    rows = target.shape[2]
    target[0, :, :, pl.ds(width, scratch.shape[2])] = scratch[:, 7:7 + rows, :].astype(BF16)
    target[2, :, :, pl.ds(width, scratch.shape[2])] = scratch[:, 9:9 + rows, :].astype(BF16)


def weight_gradient(rows_t, taps_of, total):
    result = []
    for dx, dy in TAPS:
        full = dot(rows_t, taps_of(dx, dy)) * total
        result.append(full[0:C, 0:3 * C] + full[C:2 * C, C:4 * C])
    return result


def packed(pieces):
    blocks = [piece[:, 0:2 * C] for piece in pieces]
    for pair in range(0, 9, 2):
        second = pieces[pair + 1][:, 2 * C:3 * C] if pair + 1 < 9 else jnp.zeros((C, C), F32)
        blocks.append(jnp.concatenate([pieces[pair][:, 2 * C:3 * C], second], axis=1))
    return blocks


def pack(field, cot, head, tail, side, rows):
    nx, ny, width = field.shape
    gx = lax.axis_index("gx")
    for x in range(nx):
        fields = field[x].astype(F32)
        cots = cot[x].astype(F32)
        for index, row in enumerate((fields[0:1], fields[1:2], cots[0:1], fields[ny - 2:ny - 1], fields[ny - 1:ny], cots[ny - 1:ny])):
            rows[index, x:x + 1, :] = row
    head[...] = rows[0:3].astype(BF16)
    tail[...] = rows[3:6].astype(BF16)

    @pl.when(gx == 0)
    def _():
        side[0:2] = field[nx - 2:nx]
        side[2:3] = cot[nx - 1:nx]

    @pl.when(gx != 0)
    def _():
        side[0:2] = field[0:2]
        side[2:3] = cot[0:1]


def prepare(w1, w2, cot, w1b, w2b, wfb, cot_t):
    cells = cot.shape[0] * cot.shape[1]
    lane = 2 * C
    for t in range(9):
        w1b[t * 4 * C:(t + 1) * 4 * C, :] = band([w1[3 * t + z] for z in range(3)])
        w2b[t * 4 * C:(t + 1) * 4 * C, :] = band([w2[3 * t + z] for z in range(3)])
        wfb[:, t * 4 * C:(t + 1) * 4 * C] = band_flipped([w2[3 * (8 - t) + z] for z in range(3)])
    for p in range(NZ // 2):
        cot_t[:, cells * p:cells * (p + 1)] = cot[:, :, lane * p:lane * (p + 1)].reshape(cells, lane).T


def layers(factor, gx_count, gy_count, field, cot, side, head, tail, from_prev, from_next, corner, w1b, wfb, cot_t,
           hd, keep, send, fd, cd, fs, cs, hs, es, ec, eh, pf):
    nx, ny, width = field.shape
    pairs = NZ // 2
    lane = 2 * C
    gx = lax.axis_index("gx")
    gy = lax.axis_index("gy")
    low = (gx > 0).astype(F32)
    high = (gx < gx_count - 1).astype(F32)
    prev = (gy > 0).astype(F32)
    after = (gy < gy_count - 1).astype(F32)

    fs[2:2 + nx, 8:8 + ny, :] = field[...].astype(F32)
    fs[0:2, 8:8 + ny, :] = side[0:2].astype(F32) * low
    fs[2 + nx:4 + nx, 8:8 + ny, :] = side[0:2].astype(F32) * high
    cs[1:1 + nx, 8:8 + ny, :] = cot[...].astype(F32)
    cs[0:1, 8:8 + ny, :] = side[2:3].astype(F32) * low
    cs[1 + nx:2 + nx, 8:8 + ny, :] = side[2:3].astype(F32) * high

    es[...] = jnp.zeros(es.shape, F32)
    ec[...] = jnp.zeros(ec.shape, F32)
    for end, own, there, scale in ((0, from_prev, 0, prev), (1, from_next, 3, after)):
        for target, index, source in ((es, 4 * end, 0), (es, 4 * end + 1, 1), (ec, end, 2)):
            other = corner[there + source].astype(F32) * scale
            target[index, 8:8 + nx, :] = own[source].astype(F32) * scale
            target[index, 6:8, :] = other[nx - 2:nx] * low
            target[index, 8 + nx:10 + nx, :] = other[0:2] * high
    es[2, 8:8 + nx, :] = head[0].astype(F32)
    es[3, 8:8 + nx, :] = tail[1].astype(F32)
    for x in (0, 1, nx + 2, nx + 3):
        es[2, 6 + x:7 + x, :] = fs[x, 8:9, :]
        es[3, 6 + x:7 + x, :] = fs[x, 7 + ny:8 + ny, :]

    for x in range(nx + 4):
        fs[x, 7:8, :] = es[1, 6 + x:7 + x, :]
        fs[x, 8 + ny:9 + ny, :] = es[4, 6 + x:7 + x, :]
    for x in range(nx + 2):
        cs[x, 7:8, :] = ec[0, 7 + x:8 + x, :]
        cs[x, 8 + ny:9 + ny, :] = ec[1, 7 + x:8 + x, :]

    for copies in (fd, cd):
        copies[:, :, :, 0:lane] = jnp.zeros(copies.shape[:3] + (lane,), BF16)
        copies[:, :, :, lane + width:] = jnp.zeros(copies.shape[:3] + (lane,), BF16)
    for scratch, copies in ((fs, fd), (cs, cd)):
        shifted_rows(scratch, copies, lane)
        copies[1, :, :, lane:lane + width] = scratch[:, 8:8 + ny, :].astype(BF16)

    eh[:, :, :, 0:lane] = jnp.zeros((9, 2, 16, lane), BF16)
    eh[:, :, :, lane + width:] = jnp.zeros((9, 2, 16, lane), BF16)
    for t, (dx, dy) in enumerate(TAPS):
        for end in range(2):
            eh[t, end, :, lane:lane + width] = es[3 * end + dy, 6 + dx:22 + dx, :].astype(BF16)

    depth = nx + 2
    main = depth * ny
    x_of = lax.broadcasted_iota(jnp.int32, (depth, ny, lane), 0)
    mask = jnp.where(x_of == 0, low, jnp.where(x_of == depth - 1, high, 1.0))
    end_of = lax.broadcasted_iota(jnp.int32, (2, 16, lane), 0)
    row_of = lax.broadcasted_iota(jnp.int32, (2, 16, lane), 1)
    end_mask = jnp.where(row_of == 0, low, jnp.where(row_of == depth - 1, high, 1.0)) * jnp.where(end_of == 0, prev, after)
    lane_of = lax.broadcasted_iota(jnp.int32, (1, 1, lane), 2)
    for p in range(pairs + 1):
        span = slice(lane * p, lane * (p + 2))
        here = slice(lane * p, lane * (p + 1))
        block = jnp.concatenate(
            [
                jnp.concatenate([fd[dy, dx:dx + depth, :, span].reshape(main, 2 * lane) for dx, dy in TAPS], axis=1),
                jnp.concatenate([eh[t, :, :, span].reshape(32, 2 * lane) for t in range(9)], axis=1),
            ],
            axis=0,
        )
        pre = dot(block, w1b[...])
        hidden = pre * jax.nn.sigmoid(pre)
        hidden_main = hidden[:main].reshape(depth, ny, lane) * mask
        hidden_ends = hidden[main:].reshape(2, 16, lane) * end_mask
        if p == 0:
            hidden_main = jnp.where(lane_of >= C, hidden_main, 0.0)
            hidden_ends = jnp.where(lane_of >= C, hidden_ends, 0.0)
        if p == pairs:
            hidden_main = jnp.where(lane_of < C, hidden_main, 0.0)
            hidden_ends = jnp.where(lane_of < C, hidden_ends, 0.0)
        pf[p] = pre[ny:ny + nx * ny]
        hs[:, 8:8 + ny, here] = hidden_main
        hd[1, :, :, here] = hidden_main.astype(BF16)
        for x in range(depth):
            hs[x, 7:8, here] = hidden_ends[0, x:x + 1, :]
            hs[x, 8 + ny:9 + ny, here] = hidden_ends[1, x:x + 1, :]
    shifted_rows(hs, hd, 0)

    cells = nx * ny

    def hidden_span(dx, dy, p):
        return hd[dy, dx:dx + nx, :, lane * p:lane * (p + 2)].reshape(cells, 2 * lane)

    def field_span(dx, dy, p):
        return fd[dy, dx + 1:dx + 1 + nx, :, lane * p:lane * (p + 2)].reshape(cells, 2 * lane)

    def cot_span(dx, dy, p):
        return cd[dy, dx:dx + nx, :, lane * p:lane * (p + 2)].reshape(cells, 2 * lane)

    second = packed(weight_gradient(
        cot_t[...],
        lambda dx, dy: jnp.concatenate([hidden_span(dx, dy, p) for p in range(pairs)], axis=0),
        factor))

    grads_t = []
    for p in range(pairs + 1):
        grad = dot_nt(jnp.concatenate([cot_span(dx, dy, p) for dx, dy in TAPS], axis=1), wfb[...])
        pre = pf[p]
        sigma = jax.nn.sigmoid(pre)
        grad = grad * sigma * (1.0 + pre * (1.0 - sigma))
        if p == 0:
            grad = jnp.where(lane_of[0] >= C, grad, 0.0)
        if p == pairs:
            grad = jnp.where(lane_of[0] < C, grad, 0.0)
        grads_t.append(grad.astype(BF16).T)
    first = packed(weight_gradient(
        jnp.concatenate(grads_t, axis=1),
        lambda dx, dy: jnp.concatenate([field_span(dx, dy, p) for p in range(pairs + 1)], axis=0),
        factor))

    for index in range(BLOCKS):
        rows = slice(index * C, (index + 1) * C)
        keep[rows, :] = jnp.where(gx == 0, first[index], second[index])
        send[rows, :] = jnp.where(gx == 0, second[index], first[index]).astype(BF16)
    if keep.shape[0] > BLOCKS * C:
        rest = (keep.shape[0] - BLOCKS * C, lane)
        keep[BLOCKS * C:, :] = jnp.zeros(rest, F32)
        send[BLOCKS * C:, :] = jnp.zeros(rest, BF16)


def output_conv(hd, w2b, out):
    nx, ny, _ = out.shape
    lane = 2 * C
    for p in range(NZ // 2):
        block = jnp.concatenate(
            [hd[dy, dx:dx + nx, :, lane * p:lane * (p + 2)].reshape(nx * ny, 2 * lane) for dx, dy in TAPS], axis=1)
        out[:, :, lane * p:lane * (p + 1)] = dot(block, w2b[...]).astype(BF16).reshape(nx, ny, lane)


def add_pair(keep, other, out):
    out[...] = (keep[...] + other[...].astype(F32)).astype(BF16)


def add_terms(terms, out):
    total = terms[0].astype(F32)
    for index in range(1, terms.shape[0]):
        total = total + terms[index].astype(F32)
    out[...] = total.astype(BF16)


def add_and_repeat(terms, out):
    total = terms[0].astype(F32)
    for index in range(1, terms.shape[0]):
        total = total + terms[index].astype(F32)
    total = total.astype(BF16)
    for index in range(out.shape[0]):
        out[index] = total


def unpack(mine, other, first, second):
    gx = lax.axis_index("gx")
    a = mine[...].astype(F32)
    b = other[...].astype(F32)
    for out, rows in ((first, jnp.where(gx == 0, a, b)), (second, jnp.where(gx == 0, b, a))):
        for t in range(9):
            turned = rows[t * C:(t + 1) * C].T
            out[3 * t] = turned[0:C]
            out[3 * t + 1] = turned[C:2 * C]
        for pair in range(5):
            turned = rows[(9 + pair) * C:(10 + pair) * C].T
            out[6 * pair + 2] = turned[0:C]
            if pair < 4:
                out[6 * pair + 5] = turned[C:2 * C]


def near(shape, dtype):
    return pltpu.VMEM(shape, dtype)


def call(body, name, inputs, outs, scratch=(), limit=16, flops=0):
    placed = [pltpu.with_memory_space_constraint(x, pltpu.VMEM) if held else x for x, held in inputs]
    size = sum(x.size * x.dtype.itemsize for x in placed)
    return pl.pallas_call(
        body,
        out_shape=list(outs),
        in_specs=[pl.BlockSpec(memory_space=pltpu.VMEM)] * len(placed),
        out_specs=[pl.BlockSpec(memory_space=pltpu.VMEM)] * len(outs),
        scratch_shapes=list(scratch),
        compiler_params=pltpu.CompilerParams(vmem_limit_bytes=limit * 1024 * 1024),
        cost_estimate=pl.CostEstimate(flops=flops, bytes_accessed=size, transcendentals=0),
        name=name,
    )(*placed)


def shards(field_in, first_weight, second_weight, cotangent):
    nx, ny, width = field_in.shape[1:]
    gx_count, gy_count, grp_count = (lax.axis_size(axis) for axis in ("gx", "gy", "grp"))
    total = field_in.shape[0] * nx * ny * NZ * gx_count * gy_count * grp_count
    factor = 1.0 / math.sqrt(total)
    ranks = gy_count * grp_count
    rows = -(-BLOCKS * C // (8 * ranks)) * 8 * ranks
    field = field_in[0]
    cot = cotangent[0]
    lane = 2 * C
    wide = width + 2 * lane
    pairs = NZ // 2
    cells = nx * ny

    head, tail, side = call(
        pack, "pack", [(field, False), (cot, False)],
        [near((3, nx, width), BF16), near((3, nx, width), BF16), near((3, ny, width), BF16)],
        [pltpu.VMEM((6, nx, width), F32)])
    from_next = shift(head, -1)
    from_prev = shift(tail, 1)
    side = swap(side)
    corner = swap(jnp.concatenate([from_prev, from_next], axis=0))

    w1b, w2b, wfb, cot_t = call(
        prepare, "prepare",
        [(first_weight.reshape(27, C, C), False), (second_weight.reshape(27, C, C), False), (cot, False)],
        [near((9 * 4 * C, lane), BF16), near((9 * 4 * C, lane), BF16), near((lane, 9 * 4 * C), BF16),
         near((lane, cells * pairs), BF16)])

    hd, keep, send = call(
        functools.partial(layers, factor, gx_count, gy_count), "layers",
        [(field, False), (cot, False)] + [(x, True) for x in (side, head, tail, from_prev, from_next, corner, w1b, wfb, cot_t)],
        [near((3, nx + 2, ny, width + lane), BF16), near((rows, lane), F32), near((rows, lane), BF16)],
        [
            pltpu.VMEM((3, nx + 4, ny, wide), BF16),
            pltpu.VMEM((3, nx + 2, ny, wide), BF16),
            pltpu.VMEM((nx + 4, ny + 16, width), F32),
            pltpu.VMEM((nx + 2, ny + 16, width), F32),
            pltpu.VMEM((nx + 2, ny + 16, width + lane), F32),
            pltpu.VMEM((6, 24, width), F32),
            pltpu.VMEM((2, 24, width), F32),
            pltpu.VMEM((9, 2, 16, wide), BF16),
            pltpu.VMEM((pairs + 1, cells, lane), F32),
        ],
        limit=32, flops=10 ** 10)

    other = swap(send)
    out, = call(
        output_conv, "output_conv", [(hd, True), (w2b, True)],
        [jax.ShapeDtypeStruct((nx, ny, width), BF16)], flops=2 * 10 ** 9)
    both, = call(add_pair, "add_pair", [(keep, True), (other, True)], [near((rows, lane), BF16)])
    terms = lax.all_to_all(both.reshape(gy_count, rows // gy_count, lane), "gy", 0, 0)
    part, = call(add_terms, "add_gy", [(terms, True)], [near(terms.shape[1:], BF16)])
    terms = lax.all_to_all(part.reshape(grp_count, rows // ranks, lane), "grp", 0, 0)
    spread, = call(add_and_repeat, "add_grp", [(terms, True)], [near(terms.shape, BF16)])
    part = lax.all_to_all(spread, "grp", 0, 0).reshape(1, rows // gy_count, lane)
    spread = jnp.broadcast_to(part, (gy_count,) + part.shape[1:])
    mine = lax.all_to_all(spread, "gy", 0, 0).reshape(rows, lane)
    other = swap(mine)
    first, second = call(
        unpack, "unpack", [(mine, True), (other, True)], [jax.ShapeDtypeStruct((27, C, C), F32)] * 2)
    shape = (3, 3, 3, C, C)
    return out[None], first.reshape(shape), second.reshape(shape)


def solution(mesh):
    return jax.shard_map(
        shards,
        mesh=mesh,
        in_specs=(P("grp", "gx", "gy", None), P(), P(), P("grp", "gx", "gy", None)),
        out_specs=(P("grp", "gx", "gy", None), P(), P()),
        check_vma=False,
    )
```

```python
import functools
import math

import jax
import jax.numpy as jnp
from jax import lax
from jax.experimental import pallas as pl
from jax.experimental.pallas import tpu as pltpu
from jax.sharding import PartitionSpec as P

C = 64
NZ = 16
BF16 = jnp.bfloat16
F32 = jnp.float32
TAPS = [(dx, dy) for dx in range(3) for dy in range(3)]
BLOCKS = 14


def swap(array):
    return lax.ppermute(array, "gx", [(0, 1), (1, 0)])


def dot(a, b):
    return jnp.dot(a, b, preferred_element_type=F32)


def dot_nt(a, b):
    return lax.dot_general(a, b, (((1,), (1,)), ((), ())), preferred_element_type=F32)


def band(taps):
    zero = jnp.zeros((C, C), BF16)
    left = jnp.concatenate(list(taps) + [zero], axis=0)
    right = jnp.concatenate([zero] + list(taps), axis=0)
    return jnp.concatenate([left, right], axis=1)


def band_flipped(taps):
    zero = jnp.zeros((C, C), BF16)
    back = list(taps)[::-1]
    upper = jnp.concatenate(back + [zero], axis=1)
    lower = jnp.concatenate([zero] + back, axis=1)
    return jnp.concatenate([upper, lower], axis=0)


def shifted_rows(scratch, target, width):
    rows = target.shape[2]
    target[0, :, :, pl.ds(width, scratch.shape[2])] = scratch[:, 7:7 + rows, :].astype(BF16)
    target[2, :, :, pl.ds(width, scratch.shape[2])] = scratch[:, 9:9 + rows, :].astype(BF16)


def weight_gradient(rows_t, taps_of, total):
    result = []
    for dx, dy in TAPS:
        full = dot(rows_t, taps_of(dx, dy)) * total
        result.append(full[0:C, 0:3 * C] + full[C:2 * C, C:4 * C])
    return result


def packed(pieces):
    blocks = [piece[:, 0:2 * C] for piece in pieces]
    for pair in range(0, 9, 2):
        second = pieces[pair + 1][:, 2 * C:3 * C] if pair + 1 < 9 else jnp.zeros((C, C), F32)
        blocks.append(jnp.concatenate([pieces[pair][:, 2 * C:3 * C], second], axis=1))
    return blocks


def pack(field_hbm, cot_hbm, field, cot, edge, given, rows, sems):
    copies = [
        pltpu.make_async_copy(source, target, sems.at[index])
        for index, (source, target) in enumerate(((field_hbm, field), (cot_hbm, cot)))
    ]
    for copy in copies:
        copy.start()
    for copy in copies:
        copy.wait()
    nx, ny, width = field.shape
    gx = lax.axis_index("gx")
    for x in range(nx):
        fields = field[x].astype(F32)
        cots = cot[x].astype(F32)
        for index, row in enumerate((fields[0:1], fields[1:2], cots[0:1], fields[ny - 2:ny - 1], fields[ny - 1:ny], cots[ny - 1:ny])):
            rows[index, x:x + 1, :] = row
    head = rows[0:3].astype(BF16)
    tail = rows[3:6].astype(BF16)

    @pl.when(gx == 0)
    def _():
        edge[...] = head
        given[:, ny:ny + nx] = tail
        given[0:2, 0:ny] = field[nx - 2:nx]
        given[2:3, 0:ny] = cot[nx - 1:nx]

    @pl.when(gx != 0)
    def _():
        edge[...] = tail
        given[:, ny:ny + nx] = head
        given[0:2, 0:ny] = field[0:2]
        given[2:3, 0:ny] = cot[0:1]


def join_edges(edge, taken, whole):
    nx = edge.shape[1]
    gx = lax.axis_index("gx")

    @pl.when(gx == 0)
    def _():
        whole[:, 0:nx] = edge[...]
        whole[:, nx:2 * nx] = taken[:, taken.shape[1] - nx:]

    @pl.when(gx != 0)
    def _():
        whole[:, 0:nx] = taken[:, taken.shape[1] - nx:]
        whole[:, nx:2 * nx] = edge[...]


def prepare(w1_hbm, w2_hbm, cot, w1b, w2b, wfb, cot_t, w1, w2, sems):
    copies = [
        pltpu.make_async_copy(source, target, sems.at[index])
        for index, (source, target) in enumerate(((w1_hbm, w1), (w2_hbm, w2)))
    ]
    for copy in copies:
        copy.start()
    cells = cot.shape[0] * cot.shape[1]
    lane = 2 * C
    for p in range(NZ // 2):
        cot_t[:, cells * p:cells * (p + 1)] = cot[:, :, lane * p:lane * (p + 1)].reshape(cells, lane).T
    for copy in copies:
        copy.wait()
    for t in range(9):
        w1b[t * 4 * C:(t + 1) * 4 * C, :] = band([w1[3 * t + z] for z in range(3)])
        w2b[t * 4 * C:(t + 1) * 4 * C, :] = band([w2[3 * t + z] for z in range(3)])
        wfb[:, t * 4 * C:(t + 1) * 4 * C] = band_flipped([w2[3 * (8 - t) + z] for z in range(3)])


def layers(factor, gx_count, gy_count, field, cot, side, near_rows, far_rows, w1b, wfb, cot_t,
           hd, keep, send, fd, cd, fs, cs, hs, es, ec, eh, pf):
    nx, ny, width = field.shape
    pairs = NZ // 2
    lane = 2 * C
    gx = lax.axis_index("gx")
    gy = lax.axis_index("gy")
    low = (gx > 0).astype(F32)
    high = (gx < gx_count - 1).astype(F32)
    prev = (gy > 0).astype(F32)
    after = (gy < gy_count - 1).astype(F32)

    fs[2:2 + nx, 8:8 + ny, :] = field[...].astype(F32)
    fs[0:2, 8:8 + ny, :] = side[0:2, 0:ny].astype(F32) * low
    fs[2 + nx:4 + nx, 8:8 + ny, :] = side[0:2, 0:ny].astype(F32) * high
    cs[1:1 + nx, 8:8 + ny, :] = cot[...].astype(F32)
    cs[0:1, 8:8 + ny, :] = side[2:3, 0:ny].astype(F32) * low
    cs[1 + nx:2 + nx, 8:8 + ny, :] = side[2:3, 0:ny].astype(F32) * high

    es[...] = jnp.zeros(es.shape, F32)
    ec[...] = jnp.zeros(ec.shape, F32)

    def place(first, last, from_row, to_row):
        span = slice(to_row, to_row + nx + 2)
        for target, index, source in (
            (es, 0, first[0]), (es, 1, first[1]), (ec, 0, first[2]),
            (es, 4, last[0]), (es, 5, last[1]), (ec, 1, last[2]),
        ):
            target[index, span, :] = source.astype(F32)[from_row:from_row + nx + 2]

    @pl.when(gx == 0)
    def _():
        place(near_rows, far_rows, 0, 8)

    @pl.when(gx != 0)
    def _():
        place(far_rows, near_rows, nx - 2, 6)

    for x in range(nx + 4):
        es[2, 6 + x:7 + x, :] = fs[x, 8:9, :]
        es[3, 6 + x:7 + x, :] = fs[x, 7 + ny:8 + ny, :]

    for x in range(nx + 4):
        fs[x, 7:8, :] = es[1, 6 + x:7 + x, :]
        fs[x, 8 + ny:9 + ny, :] = es[4, 6 + x:7 + x, :]
    for x in range(nx + 2):
        cs[x, 7:8, :] = ec[0, 7 + x:8 + x, :]
        cs[x, 8 + ny:9 + ny, :] = ec[1, 7 + x:8 + x, :]

    for copies in (fd, cd):
        copies[:, :, :, 0:lane] = jnp.zeros(copies.shape[:3] + (lane,), BF16)
        copies[:, :, :, lane + width:] = jnp.zeros(copies.shape[:3] + (lane,), BF16)
    for scratch, copies in ((fs, fd), (cs, cd)):
        shifted_rows(scratch, copies, lane)
        copies[1, :, :, lane:lane + width] = scratch[:, 8:8 + ny, :].astype(BF16)

    eh[:, :, :, 0:lane] = jnp.zeros((9, 2, 16, lane), BF16)
    eh[:, :, :, lane + width:] = jnp.zeros((9, 2, 16, lane), BF16)
    for t, (dx, dy) in enumerate(TAPS):
        for end in range(2):
            eh[t, end, :, lane:lane + width] = es[3 * end + dy, 6 + dx:22 + dx, :].astype(BF16)

    depth = nx + 2
    main = depth * ny
    x_of = lax.broadcasted_iota(jnp.int32, (depth, ny, lane), 0)
    mask = jnp.where(x_of == 0, low, jnp.where(x_of == depth - 1, high, 1.0))
    end_of = lax.broadcasted_iota(jnp.int32, (2, 16, lane), 0)
    row_of = lax.broadcasted_iota(jnp.int32, (2, 16, lane), 1)
    end_mask = jnp.where(row_of == 0, low, jnp.where(row_of == depth - 1, high, 1.0)) * jnp.where(end_of == 0, prev, after)
    lane_of = lax.broadcasted_iota(jnp.int32, (1, 1, lane), 2)
    for p in range(pairs + 1):
        span = slice(lane * p, lane * (p + 2))
        here = slice(lane * p, lane * (p + 1))
        block = jnp.concatenate(
            [
                jnp.concatenate([fd[dy, dx:dx + depth, :, span].reshape(main, 2 * lane) for dx, dy in TAPS], axis=1),
                jnp.concatenate([eh[t, :, :, span].reshape(32, 2 * lane) for t in range(9)], axis=1),
            ],
            axis=0,
        )
        pre = dot(block, w1b[...])
        hidden = pre * jax.nn.sigmoid(pre)
        hidden_main = hidden[:main].reshape(depth, ny, lane) * mask
        hidden_ends = hidden[main:].reshape(2, 16, lane) * end_mask
        if p == 0:
            hidden_main = jnp.where(lane_of >= C, hidden_main, 0.0)
            hidden_ends = jnp.where(lane_of >= C, hidden_ends, 0.0)
        if p == pairs:
            hidden_main = jnp.where(lane_of < C, hidden_main, 0.0)
            hidden_ends = jnp.where(lane_of < C, hidden_ends, 0.0)
        pf[p] = pre[ny:ny + nx * ny]
        hs[:, 8:8 + ny, here] = hidden_main
        hd[1, :, :, here] = hidden_main.astype(BF16)
        for x in range(depth):
            hs[x, 7:8, here] = hidden_ends[0, x:x + 1, :]
            hs[x, 8 + ny:9 + ny, here] = hidden_ends[1, x:x + 1, :]
    shifted_rows(hs, hd, 0)

    cells = nx * ny

    def hidden_span(dx, dy, p):
        return hd[dy, dx:dx + nx, :, lane * p:lane * (p + 2)].reshape(cells, 2 * lane)

    def field_span(dx, dy, p):
        return fd[dy, dx + 1:dx + 1 + nx, :, lane * p:lane * (p + 2)].reshape(cells, 2 * lane)

    def cot_span(dx, dy, p):
        return cd[dy, dx:dx + nx, :, lane * p:lane * (p + 2)].reshape(cells, 2 * lane)

    second = packed(weight_gradient(
        cot_t[...],
        lambda dx, dy: jnp.concatenate([hidden_span(dx, dy, p) for p in range(pairs)], axis=0),
        factor))

    grads_t = []
    for p in range(pairs + 1):
        grad = dot_nt(jnp.concatenate([cot_span(dx, dy, p) for dx, dy in TAPS], axis=1), wfb[...])
        pre = pf[p]
        sigma = jax.nn.sigmoid(pre)
        grad = grad * sigma * (1.0 + pre * (1.0 - sigma))
        if p == 0:
            grad = jnp.where(lane_of[0] >= C, grad, 0.0)
        if p == pairs:
            grad = jnp.where(lane_of[0] < C, grad, 0.0)
        grads_t.append(grad.astype(BF16).T)
    first = packed(weight_gradient(
        jnp.concatenate(grads_t, axis=1),
        lambda dx, dy: jnp.concatenate([field_span(dx, dy, p) for p in range(pairs + 1)], axis=0),
        factor))

    for index in range(BLOCKS):
        rows = slice(index * C, (index + 1) * C)
        keep[rows, :] = jnp.where(gx == 0, first[index], second[index])
        send[rows, :] = jnp.where(gx == 0, second[index], first[index]).astype(BF16)
    if keep.shape[0] > BLOCKS * C:
        rest = (keep.shape[0] - BLOCKS * C, lane)
        keep[BLOCKS * C:, :] = jnp.zeros(rest, F32)
        send[BLOCKS * C:, :] = jnp.zeros(rest, BF16)


def output_conv(hd, w2b, out):
    nx, ny, _ = out.shape
    lane = 2 * C
    for p in range(NZ // 2):
        block = jnp.concatenate(
            [hd[dy, dx:dx + nx, :, lane * p:lane * (p + 2)].reshape(nx * ny, 2 * lane) for dx, dy in TAPS], axis=1)
        out[:, :, lane * p:lane * (p + 1)] = dot(block, w2b[...]).astype(BF16).reshape(nx, ny, lane)


def add_pair(keep, other, out):
    out[...] = (keep[...] + other[...].astype(F32)).astype(BF16)


def add_terms(terms, out):
    total = terms[0].astype(F32)
    for index in range(1, terms.shape[0]):
        total = total + terms[index].astype(F32)
    out[...] = total.astype(BF16)


def unpack(mine, other, first, second):
    gx = lax.axis_index("gx")
    a = mine[...].astype(F32)
    b = other[...].astype(F32)
    for out, rows in ((first, jnp.where(gx == 0, a, b)), (second, jnp.where(gx == 0, b, a))):
        for t in range(9):
            turned = rows[t * C:(t + 1) * C].T
            out[3 * t] = turned[0:C]
            out[3 * t + 1] = turned[C:2 * C]
        for pair in range(5):
            turned = rows[(9 + pair) * C:(10 + pair) * C].T
            out[6 * pair + 2] = turned[0:C]
            if pair < 4:
                out[6 * pair + 5] = turned[C:2 * C]


def near(shape, dtype):
    return pltpu.VMEM(shape, dtype)


def call(body, name, inputs, outs, scratch=(), limit=16, flops=0):
    placed = [pltpu.with_memory_space_constraint(x, pltpu.VMEM if held else pltpu.HBM) for x, held in inputs]
    size = sum(x.size * x.dtype.itemsize for x, _ in inputs)
    return pl.pallas_call(
        body,
        out_shape=list(outs),
        in_specs=[pl.BlockSpec(memory_space=pltpu.VMEM if held else pl.ANY) for _, held in inputs],
        out_specs=[pl.BlockSpec(memory_space=pltpu.VMEM)] * len(outs),
        scratch_shapes=list(scratch),
        compiler_params=pltpu.CompilerParams(vmem_limit_bytes=limit * 1024 * 1024),
        cost_estimate=pl.CostEstimate(flops=flops, bytes_accessed=size, transcendentals=0),
        name=name,
    )(*placed)


def shards(field_in, first_weight, second_weight, cotangent):
    nx, ny, width = field_in.shape[1:]
    gx_count, gy_count, grp_count = (lax.axis_size(axis) for axis in ("gx", "gy", "grp"))
    total = field_in.shape[0] * nx * ny * NZ * gx_count * gy_count * grp_count
    factor = 1.0 / math.sqrt(total)
    rows = -(-BLOCKS * C // (8 * gy_count)) * 8 * gy_count
    lane = 2 * C
    wide = width + 2 * lane
    pairs = NZ // 2
    cells = nx * ny

    field, cot, edge, given = call(
        pack, "pack", [(field_in[0], False), (cotangent[0], False)],
        [near((nx, ny, width), BF16), near((nx, ny, width), BF16), near((3, nx, width), BF16), near((3, ny + nx, width), BF16)],
        [pltpu.VMEM((6, nx, width), F32), pltpu.SemaphoreType.DMA((2,))])
    side = swap(given)
    whole, = call(join_edges, "join_edges", [(edge, True), (side, True)], [near((3, 2 * nx, width), BF16)])
    ends = [(gy_count + j, j + 1) for j in range(gy_count - 1)]
    near_rows = lax.ppermute(whole, ("gx", "gy"), ends + [(b, a) for a, b in ends])
    w1b, w2b, wfb, cot_t = call(
        prepare, "prepare",
        [(first_weight.reshape(27, C, C), False), (second_weight.reshape(27, C, C), False), (cot, True)],
        [near((9 * 4 * C, lane), BF16), near((9 * 4 * C, lane), BF16), near((lane, 9 * 4 * C), BF16),
         near((lane, cells * pairs), BF16)],
        [pltpu.VMEM((27, C, C), BF16), pltpu.VMEM((27, C, C), BF16), pltpu.SemaphoreType.DMA((2,))])
    near_rows, w1b, w2b, wfb, cot_t = lax.optimization_barrier((near_rows, w1b, w2b, wfb, cot_t))
    far_rows = swap(near_rows)

    hd, keep, send = call(
        functools.partial(layers, factor, gx_count, gy_count), "layers",
        [(x, True) for x in (field, cot, side, near_rows, far_rows, w1b, wfb, cot_t)],
        [near((3, nx + 2, ny, width + lane), BF16), near((rows, lane), F32), near((rows, lane), BF16)],
        [
            pltpu.VMEM((3, nx + 4, ny, wide), BF16),
            pltpu.VMEM((3, nx + 2, ny, wide), BF16),
            pltpu.VMEM((nx + 4, ny + 16, width), F32),
            pltpu.VMEM((nx + 2, ny + 16, width), F32),
            pltpu.VMEM((nx + 2, ny + 16, width + lane), F32),
            pltpu.VMEM((6, 24, width), F32),
            pltpu.VMEM((2, 24, width), F32),
            pltpu.VMEM((9, 2, 16, wide), BF16),
            pltpu.VMEM((pairs + 1, cells, lane), F32),
        ],
        limit=32, flops=10 ** 10)

    other = swap(send)
    out, = call(
        output_conv, "output_conv", [(hd, True), (w2b, True)],
        [near((nx, ny, width), BF16)], flops=2 * 10 ** 9)
    other, out = lax.optimization_barrier((other, out))
    both, = call(add_pair, "add_pair", [(keep, True), (other, True)], [near((rows, lane), BF16)])
    terms = lax.all_to_all(both.reshape(gy_count, rows // gy_count, lane), "gy", 0, 0)
    part, = call(add_terms, "add_terms", [(terms, True)], [near(terms.shape[1:], BF16)])
    part = lax.psum(part, "grp")
    spread = jnp.broadcast_to(part[None], (gy_count,) + part.shape)
    mine = lax.all_to_all(spread, "gy", 0, 0).reshape(rows, lane)
    other = swap(mine)
    first, second = call(
        unpack, "unpack", [(mine, True), (other, True)], [jax.ShapeDtypeStruct((27, C, C), F32)] * 2)
    shape = (3, 3, 3, C, C)
    return out[None], first.reshape(shape), second.reshape(shape)


def solution(mesh):
    return jax.shard_map(
        shards,
        mesh=mesh,
        in_specs=(P("grp", "gx", "gy", None), P(), P(), P("grp", "gx", "gy", None)),
        out_specs=(P("grp", "gx", "gy", None), P(), P()),
        check_vma=False,
    )
```

```python
import functools
import math

import jax
import jax.numpy as jnp
from jax import lax
from jax.experimental import pallas as pl
from jax.experimental.pallas import tpu as pltpu
from jax.sharding import PartitionSpec as P

C = 64
NZ = 16
BF16 = jnp.bfloat16
F32 = jnp.float32
TAPS = [(dx, dy) for dx in range(3) for dy in range(3)]
BLOCKS = 14


def swap(array):
    return lax.ppermute(array, "gx", [(0, 1), (1, 0)])


def dot(a, b):
    return jnp.dot(a, b, preferred_element_type=F32)


def dot_nt(a, b):
    return lax.dot_general(a, b, (((1,), (1,)), ((), ())), preferred_element_type=F32)


def band(taps):
    zero = jnp.zeros((C, C), BF16)
    left = jnp.concatenate(list(taps) + [zero], axis=0)
    right = jnp.concatenate([zero] + list(taps), axis=0)
    return jnp.concatenate([left, right], axis=1)


def band_flipped(taps):
    zero = jnp.zeros((C, C), BF16)
    back = list(taps)[::-1]
    upper = jnp.concatenate(back + [zero], axis=1)
    lower = jnp.concatenate([zero] + back, axis=1)
    return jnp.concatenate([upper, lower], axis=0)


def shifted_rows(scratch, target, width):
    rows = target.shape[2]
    target[0, :, :, pl.ds(width, scratch.shape[2])] = scratch[:, 7:7 + rows, :].astype(BF16)
    target[2, :, :, pl.ds(width, scratch.shape[2])] = scratch[:, 9:9 + rows, :].astype(BF16)


def weight_gradient(rows_t, taps_of, total):
    result = []
    for dx, dy in TAPS:
        full = dot(rows_t, taps_of(dx, dy)) * total
        result.append(full[0:C, 0:3 * C] + full[C:2 * C, C:4 * C])
    return result


def packed(pieces):
    blocks = [piece[:, 0:2 * C] for piece in pieces]
    for pair in range(0, 9, 2):
        second = pieces[pair + 1][:, 2 * C:3 * C] if pair + 1 < 9 else jnp.zeros((C, C), F32)
        blocks.append(jnp.concatenate([pieces[pair][:, 2 * C:3 * C], second], axis=1))
    return blocks


def pack(field_hbm, cot_hbm, field, cot, edge, given, rows, sems):
    copies = [
        pltpu.make_async_copy(source, target, sems.at[index])
        for index, (source, target) in enumerate(((field_hbm, field), (cot_hbm, cot)))
    ]
    for copy in copies:
        copy.start()
    for copy in copies:
        copy.wait()
    nx, ny, width = field.shape
    gx = lax.axis_index("gx")
    for x in range(nx):
        fields = field[x].astype(F32)
        cots = cot[x].astype(F32)
        for index, row in enumerate((fields[0:1], fields[1:2], cots[0:1], fields[ny - 2:ny - 1], fields[ny - 1:ny], cots[ny - 1:ny])):
            rows[index, x:x + 1, :] = row
    head = rows[0:3].astype(BF16)
    tail = rows[3:6].astype(BF16)

    @pl.when(gx == 0)
    def _():
        edge[...] = head
        given[:, ny:ny + nx] = tail
        given[0:2, 0:ny] = field[nx - 2:nx]
        given[2:3, 0:ny] = cot[nx - 1:nx]

    @pl.when(gx != 0)
    def _():
        edge[...] = tail
        given[:, ny:ny + nx] = head
        given[0:2, 0:ny] = field[0:2]
        given[2:3, 0:ny] = cot[0:1]


def join_edges(edge, taken, whole):
    nx = edge.shape[1]
    gx = lax.axis_index("gx")

    @pl.when(gx == 0)
    def _():
        whole[:, 0:nx] = edge[...]
        whole[:, nx:2 * nx] = taken[:, taken.shape[1] - nx:]

    @pl.when(gx != 0)
    def _():
        whole[:, 0:nx] = taken[:, taken.shape[1] - nx:]
        whole[:, nx:2 * nx] = edge[...]


def prepare(w1_hbm, w2_hbm, cot, w1b, w2b, wfb, cot_t, w1, w2, sems):
    copies = [
        pltpu.make_async_copy(source, target, sems.at[index])
        for index, (source, target) in enumerate(((w1_hbm, w1), (w2_hbm, w2)))
    ]
    for copy in copies:
        copy.start()
    cells = cot.shape[0] * cot.shape[1]
    lane = 2 * C
    for p in range(NZ // 2):
        cot_t[:, cells * p:cells * (p + 1)] = cot[:, :, lane * p:lane * (p + 1)].reshape(cells, lane).T
    for copy in copies:
        copy.wait()
    for t in range(9):
        w1b[t * 4 * C:(t + 1) * 4 * C, :] = band([w1[3 * t + z] for z in range(3)])
        w2b[t * 4 * C:(t + 1) * 4 * C, :] = band([w2[3 * t + z] for z in range(3)])
        wfb[:, t * 4 * C:(t + 1) * 4 * C] = band_flipped([w2[3 * (8 - t) + z] for z in range(3)])


def layers(factor, gx_count, gy_count, field, cot, side, near_rows, far_rows, w1b, wfb, cot_t,
           hd, keep, send, fd, cd, fs, cs, hs, es, ec, eh, pf):
    nx, ny, width = field.shape
    pairs = NZ // 2
    lane = 2 * C
    gx = lax.axis_index("gx")
    gy = lax.axis_index("gy")
    low = (gx > 0).astype(F32)
    high = (gx < gx_count - 1).astype(F32)
    prev = (gy > 0).astype(F32)
    after = (gy < gy_count - 1).astype(F32)

    fs[2:2 + nx, 8:8 + ny, :] = field[...].astype(F32)
    fs[0:2, 8:8 + ny, :] = side[0:2, 0:ny].astype(F32) * low
    fs[2 + nx:4 + nx, 8:8 + ny, :] = side[0:2, 0:ny].astype(F32) * high
    cs[1:1 + nx, 8:8 + ny, :] = cot[...].astype(F32)
    cs[0:1, 8:8 + ny, :] = side[2:3, 0:ny].astype(F32) * low
    cs[1 + nx:2 + nx, 8:8 + ny, :] = side[2:3, 0:ny].astype(F32) * high

    es[...] = jnp.zeros(es.shape, F32)
    ec[...] = jnp.zeros(ec.shape, F32)

    def place(first, last, from_row, to_row):
        span = slice(to_row, to_row + nx + 2)
        for target, index, source in (
            (es, 0, first[0]), (es, 1, first[1]), (ec, 0, first[2]),
            (es, 4, last[0]), (es, 5, last[1]), (ec, 1, last[2]),
        ):
            target[index, span, :] = source.astype(F32)[from_row:from_row + nx + 2]

    @pl.when(gx == 0)
    def _():
        place(near_rows, far_rows, 0, 8)

    @pl.when(gx != 0)
    def _():
        place(far_rows, near_rows, nx - 2, 6)

    for x in range(nx + 4):
        es[2, 6 + x:7 + x, :] = fs[x, 8:9, :]
        es[3, 6 + x:7 + x, :] = fs[x, 7 + ny:8 + ny, :]

    for x in range(nx + 4):
        fs[x, 7:8, :] = es[1, 6 + x:7 + x, :]
        fs[x, 8 + ny:9 + ny, :] = es[4, 6 + x:7 + x, :]
    for x in range(nx + 2):
        cs[x, 7:8, :] = ec[0, 7 + x:8 + x, :]
        cs[x, 8 + ny:9 + ny, :] = ec[1, 7 + x:8 + x, :]

    for copies in (fd, cd):
        copies[:, :, :, 0:lane] = jnp.zeros(copies.shape[:3] + (lane,), BF16)
        copies[:, :, :, lane + width:] = jnp.zeros(copies.shape[:3] + (lane,), BF16)
    for scratch, copies in ((fs, fd), (cs, cd)):
        shifted_rows(scratch, copies, lane)
        copies[1, :, :, lane:lane + width] = scratch[:, 8:8 + ny, :].astype(BF16)

    eh[:, :, :, 0:lane] = jnp.zeros((9, 2, 16, lane), BF16)
    eh[:, :, :, lane + width:] = jnp.zeros((9, 2, 16, lane), BF16)
    for t, (dx, dy) in enumerate(TAPS):
        for end in range(2):
            eh[t, end, :, lane:lane + width] = es[3 * end + dy, 6 + dx:22 + dx, :].astype(BF16)

    depth = nx + 2
    main = depth * ny
    x_of = lax.broadcasted_iota(jnp.int32, (depth, ny, lane), 0)
    mask = jnp.where(x_of == 0, low, jnp.where(x_of == depth - 1, high, 1.0))
    end_of = lax.broadcasted_iota(jnp.int32, (2, 16, lane), 0)
    row_of = lax.broadcasted_iota(jnp.int32, (2, 16, lane), 1)
    end_mask = jnp.where(row_of == 0, low, jnp.where(row_of == depth - 1, high, 1.0)) * jnp.where(end_of == 0, prev, after)
    lane_of = lax.broadcasted_iota(jnp.int32, (1, 1, lane), 2)
    for p in range(pairs + 1):
        span = slice(lane * p, lane * (p + 2))
        here = slice(lane * p, lane * (p + 1))
        block = jnp.concatenate(
            [
                jnp.concatenate([fd[dy, dx:dx + depth, :, span].reshape(main, 2 * lane) for dx, dy in TAPS], axis=1),
                jnp.concatenate([eh[t, :, :, span].reshape(32, 2 * lane) for t in range(9)], axis=1),
            ],
            axis=0,
        )
        pre = dot(block, w1b[...])
        hidden = pre * jax.nn.sigmoid(pre)
        hidden_main = hidden[:main].reshape(depth, ny, lane) * mask
        hidden_ends = hidden[main:].reshape(2, 16, lane) * end_mask
        if p == 0:
            hidden_main = jnp.where(lane_of >= C, hidden_main, 0.0)
            hidden_ends = jnp.where(lane_of >= C, hidden_ends, 0.0)
        if p == pairs:
            hidden_main = jnp.where(lane_of < C, hidden_main, 0.0)
            hidden_ends = jnp.where(lane_of < C, hidden_ends, 0.0)
        pf[p] = pre[ny:ny + nx * ny]
        hs[:, 8:8 + ny, here] = hidden_main
        hd[1, :, :, here] = hidden_main.astype(BF16)
        for x in range(depth):
            hs[x, 7:8, here] = hidden_ends[0, x:x + 1, :]
            hs[x, 8 + ny:9 + ny, here] = hidden_ends[1, x:x + 1, :]
    shifted_rows(hs, hd, 0)

    cells = nx * ny

    def hidden_span(dx, dy, p):
        return hd[dy, dx:dx + nx, :, lane * p:lane * (p + 2)].reshape(cells, 2 * lane)

    def field_span(dx, dy, p):
        return fd[dy, dx + 1:dx + 1 + nx, :, lane * p:lane * (p + 2)].reshape(cells, 2 * lane)

    def cot_span(dx, dy, p):
        return cd[dy, dx:dx + nx, :, lane * p:lane * (p + 2)].reshape(cells, 2 * lane)

    second = packed(weight_gradient(
        cot_t[...],
        lambda dx, dy: jnp.concatenate([hidden_span(dx, dy, p) for p in range(pairs)], axis=0),
        factor))

    grads_t = []
    for p in range(pairs + 1):
        grad = dot_nt(jnp.concatenate([cot_span(dx, dy, p) for dx, dy in TAPS], axis=1), wfb[...])
        pre = pf[p]
        sigma = jax.nn.sigmoid(pre)
        grad = grad * sigma * (1.0 + pre * (1.0 - sigma))
        if p == 0:
            grad = jnp.where(lane_of[0] >= C, grad, 0.0)
        if p == pairs:
            grad = jnp.where(lane_of[0] < C, grad, 0.0)
        grads_t.append(grad.astype(BF16).T)
    first = packed(weight_gradient(
        jnp.concatenate(grads_t, axis=1),
        lambda dx, dy: jnp.concatenate([field_span(dx, dy, p) for p in range(pairs + 1)], axis=0),
        factor))

    for index in range(BLOCKS):
        rows = slice(index * C, (index + 1) * C)
        keep[rows, :] = jnp.where(gx == 0, first[index], second[index])
        send[rows, :] = jnp.where(gx == 0, second[index], first[index]).astype(BF16)
    if keep.shape[0] > BLOCKS * C:
        rest = (keep.shape[0] - BLOCKS * C, lane)
        keep[BLOCKS * C:, :] = jnp.zeros(rest, F32)
        send[BLOCKS * C:, :] = jnp.zeros(rest, BF16)


def output_conv(hd, w2b, out):
    nx, ny, _ = out.shape
    lane = 2 * C
    for p in range(NZ // 2):
        block = jnp.concatenate(
            [hd[dy, dx:dx + nx, :, lane * p:lane * (p + 2)].reshape(nx * ny, 2 * lane) for dx, dy in TAPS], axis=1)
        out[:, :, lane * p:lane * (p + 1)] = dot(block, w2b[...]).astype(BF16).reshape(nx, ny, lane)


def add_pair(keep, other, out):
    out[...] = (keep[...] + other[...].astype(F32)).astype(BF16)


def add_and_repeat(terms, out):
    total = terms[0].astype(F32)
    for index in range(1, terms.shape[0]):
        total = total + terms[index].astype(F32)
    total = total.astype(BF16)
    for index in range(out.shape[0]):
        out[index] = total


def unpack(mine, other, first, second):
    gx = lax.axis_index("gx")
    a = mine[...].astype(F32)
    b = other[...].astype(F32)
    for out, rows in ((first, jnp.where(gx == 0, a, b)), (second, jnp.where(gx == 0, b, a))):
        for t in range(9):
            turned = rows[t * C:(t + 1) * C].T
            out[3 * t] = turned[0:C]
            out[3 * t + 1] = turned[C:2 * C]
        for pair in range(5):
            turned = rows[(9 + pair) * C:(10 + pair) * C].T
            out[6 * pair + 2] = turned[0:C]
            if pair < 4:
                out[6 * pair + 5] = turned[C:2 * C]


def near(shape, dtype):
    return pltpu.VMEM(shape, dtype)


def call(body, name, inputs, outs, scratch=(), limit=16, flops=0):
    placed = [pltpu.with_memory_space_constraint(x, pltpu.VMEM if held else pltpu.HBM) for x, held in inputs]
    size = sum(x.size * x.dtype.itemsize for x, _ in inputs)
    return pl.pallas_call(
        body,
        out_shape=list(outs),
        in_specs=[pl.BlockSpec(memory_space=pltpu.VMEM if held else pl.ANY) for _, held in inputs],
        out_specs=[pl.BlockSpec(memory_space=pltpu.VMEM)] * len(outs),
        scratch_shapes=list(scratch),
        compiler_params=pltpu.CompilerParams(vmem_limit_bytes=limit * 1024 * 1024),
        cost_estimate=pl.CostEstimate(flops=flops, bytes_accessed=size, transcendentals=0),
        name=name,
    )(*placed)


def shards(field_in, first_weight, second_weight, cotangent):
    nx, ny, width = field_in.shape[1:]
    gx_count, gy_count, grp_count = (lax.axis_size(axis) for axis in ("gx", "gy", "grp"))
    total = field_in.shape[0] * nx * ny * NZ * gx_count * gy_count * grp_count
    factor = 1.0 / math.sqrt(total)
    ranks = gy_count * grp_count
    rows = -(-BLOCKS * C // (8 * ranks)) * 8 * ranks
    lane = 2 * C
    wide = width + 2 * lane
    pairs = NZ // 2
    cells = nx * ny

    field, cot, edge, given = call(
        pack, "pack", [(field_in[0], False), (cotangent[0], False)],
        [near((nx, ny, width), BF16), near((nx, ny, width), BF16), near((3, nx, width), BF16), near((3, ny + nx, width), BF16)],
        [pltpu.VMEM((6, nx, width), F32), pltpu.SemaphoreType.DMA((2,))])
    side = swap(given)
    whole, = call(join_edges, "join_edges", [(edge, True), (side, True)], [near((3, 2 * nx, width), BF16)])
    ends = [(gy_count + j, j + 1) for j in range(gy_count - 1)]
    near_rows = lax.ppermute(whole, ("gx", "gy"), ends + [(b, a) for a, b in ends])
    w1b, w2b, wfb, cot_t = call(
        prepare, "prepare",
        [(first_weight.reshape(27, C, C), False), (second_weight.reshape(27, C, C), False), (cot, True)],
        [near((9 * 4 * C, lane), BF16), near((9 * 4 * C, lane), BF16), near((lane, 9 * 4 * C), BF16),
         near((lane, cells * pairs), BF16)],
        [pltpu.VMEM((27, C, C), BF16), pltpu.VMEM((27, C, C), BF16), pltpu.SemaphoreType.DMA((2,))])
    near_rows, w1b, w2b, wfb, cot_t = lax.optimization_barrier((near_rows, w1b, w2b, wfb, cot_t))
    far_rows = swap(near_rows)

    hd, keep, send = call(
        functools.partial(layers, factor, gx_count, gy_count), "layers",
        [(x, True) for x in (field, cot, side, near_rows, far_rows, w1b, wfb, cot_t)],
        [near((3, nx + 2, ny, width + lane), BF16), near((rows, lane), F32), near((rows, lane), BF16)],
        [
            pltpu.VMEM((3, nx + 4, ny, wide), BF16),
            pltpu.VMEM((3, nx + 2, ny, wide), BF16),
            pltpu.VMEM((nx + 4, ny + 16, width), F32),
            pltpu.VMEM((nx + 2, ny + 16, width), F32),
            pltpu.VMEM((nx + 2, ny + 16, width + lane), F32),
            pltpu.VMEM((6, 24, width), F32),
            pltpu.VMEM((2, 24, width), F32),
            pltpu.VMEM((9, 2, 16, wide), BF16),
            pltpu.VMEM((pairs + 1, cells, lane), F32),
        ],
        limit=32, flops=10 ** 10)

    other = swap(send)
    out, = call(
        output_conv, "output_conv", [(hd, True), (w2b, True)],
        [near((nx, ny, width), BF16)], flops=2 * 10 ** 9)
    other, out = lax.optimization_barrier((other, out))
    both, = call(add_pair, "add_pair", [(keep, True), (other, True)], [near((rows, lane), BF16)])
    terms = lax.all_to_all(both.reshape(ranks, rows // ranks, lane), ("gy", "grp"), 0, 0)
    spread, = call(add_and_repeat, "add_and_repeat", [(terms, True)], [near(terms.shape, BF16)])
    mine = lax.all_to_all(spread, ("gy", "grp"), 0, 0).reshape(rows, lane)
    other = swap(mine)
    first, second = call(
        unpack, "unpack", [(mine, True), (other, True)], [jax.ShapeDtypeStruct((27, C, C), F32)] * 2)
    shape = (3, 3, 3, C, C)
    return out[None], first.reshape(shape), second.reshape(shape)


def solution(mesh):
    return jax.shard_map(
        shards,
        mesh=mesh,
        in_specs=(P("grp", "gx", "gy", None), P(), P(), P("grp", "gx", "gy", None)),
        out_specs=(P("grp", "gx", "gy", None), P(), P()),
        check_vma=False,
    )
```

```python
import functools
import math

import jax
import jax.numpy as jnp
from jax import lax
from jax.experimental import pallas as pl
from jax.experimental.pallas import tpu as pltpu
from jax.sharding import PartitionSpec as P

C = 64
NZ = 16
BF16 = jnp.bfloat16
F32 = jnp.float32
TAPS = [(dx, dy) for dy in range(3) for dx in range(3)]
BLOCKS = 14


def swap(array):
    return lax.ppermute(array, "gx", [(0, 1), (1, 0)])


def dot(a, b):
    return jnp.dot(a, b, preferred_element_type=F32)


def dot_nt(a, b):
    return lax.dot_general(a, b, (((1,), (1,)), ((), ())), preferred_element_type=F32)


def band(taps):
    zero = jnp.zeros((C, C), BF16)
    left = jnp.concatenate(list(taps) + [zero], axis=0)
    right = jnp.concatenate([zero] + list(taps), axis=0)
    return jnp.concatenate([left, right], axis=1)


def band_flipped(taps):
    zero = jnp.zeros((C, C), BF16)
    back = list(taps)[::-1]
    upper = jnp.concatenate(back + [zero], axis=1)
    lower = jnp.concatenate([zero] + back, axis=1)
    return jnp.concatenate([upper, lower], axis=0)


def weight_gradient(rows_t, taps_of, total):
    result = []
    for dx, dy in TAPS:
        full = dot(rows_t, taps_of(dx, dy)) * total
        result.append(full[0:C, 0:3 * C] + full[C:2 * C, C:4 * C])
    return result


def packed(pieces):
    blocks = [piece[:, 0:2 * C] for piece in pieces]
    for pair in range(0, 9, 2):
        second = pieces[pair + 1][:, 2 * C:3 * C] if pair + 1 < 9 else jnp.zeros((C, C), F32)
        blocks.append(jnp.concatenate([pieces[pair][:, 2 * C:3 * C], second], axis=1))
    return blocks


def pack(field_hbm, cot_hbm, field, cot, edge, given, rows, sems):
    copies = [
        pltpu.make_async_copy(source, target, sems.at[index])
        for index, (source, target) in enumerate(((field_hbm, field), (cot_hbm, cot)))
    ]
    for copy in copies:
        copy.start()
    for copy in copies:
        copy.wait()
    nx, ny, width = field.shape
    gx = lax.axis_index("gx")
    for x in range(nx):
        fields = field[x].astype(F32)
        cots = cot[x].astype(F32)
        for index, row in enumerate((fields[0:1], fields[1:2], cots[0:1], fields[ny - 2:ny - 1], fields[ny - 1:ny], cots[ny - 1:ny])):
            rows[index, x:x + 1, :] = row
    head = rows[0:3].astype(BF16)
    tail = rows[3:6].astype(BF16)

    @pl.when(gx == 0)
    def _():
        edge[...] = head
        given[:, ny:ny + nx] = tail
        given[0:2, 0:ny] = field[nx - 2:nx]
        given[2:3, 0:ny] = cot[nx - 1:nx]

    @pl.when(gx != 0)
    def _():
        edge[...] = tail
        given[:, ny:ny + nx] = head
        given[0:2, 0:ny] = field[0:2]
        given[2:3, 0:ny] = cot[0:1]


def join_edges(edge, taken, whole):
    nx = edge.shape[1]
    gx = lax.axis_index("gx")

    @pl.when(gx == 0)
    def _():
        whole[:, 0:nx] = edge[...]
        whole[:, nx:2 * nx] = taken[:, taken.shape[1] - nx:]

    @pl.when(gx != 0)
    def _():
        whole[:, 0:nx] = taken[:, taken.shape[1] - nx:]
        whole[:, nx:2 * nx] = edge[...]


def prepare(w1_hbm, w2_hbm, w1b, w2b, wfb, w1, w2, sems):
    copies = [
        pltpu.make_async_copy(source, target, sems.at[index])
        for index, (source, target) in enumerate(((w1_hbm, w1), (w2_hbm, w2)))
    ]
    for copy in copies:
        copy.start()
    for copy in copies:
        copy.wait()
    for t, (dx, dy) in enumerate(TAPS):
        rows = slice(t * 4 * C, (t + 1) * 4 * C)
        first = 9 * dx + 3 * dy
        w1b[rows, :] = band([w1[first + z] for z in range(3)])
        w2b[rows, :] = band([w2[first + z] for z in range(3)])
        wfb[:, rows] = band_flipped([w2[24 - first + z] for z in range(3)])


def extend(gx_count, target, own, side):
    gx = lax.axis_index("gx")
    nx, ny, _ = own.shape
    width = side.shape[0]
    target[width:width + nx, 8:8 + ny, :] = own[...].astype(F32)
    halo = side[:, 0:ny].astype(F32)
    target[0:width, 8:8 + ny, :] = halo * (gx > 0).astype(F32)
    target[width + nx:2 * width + nx, 8:8 + ny, :] = halo * (gx < gx_count - 1).astype(F32)


def blank_edges(copies, width):
    lane = 2 * C
    zero = jnp.zeros(copies.shape[:-1] + (lane,), BF16)
    copies[..., 0:lane] = zero
    copies[..., lane + width:] = zero


def fill_copies(scratch, copies):
    depth, _, width = scratch.shape
    ny = copies.shape[2]
    lane = 2 * C
    blank_edges(copies, width)
    zero = jnp.zeros((depth, 1, width), F32)
    scratch[:, 7:8, :] = zero
    scratch[:, 8 + ny:9 + ny, :] = zero
    for dy in range(3):
        copies[dy, :, :, lane:lane + width] = scratch[:, 7 + dy:7 + dy + ny, :].astype(BF16)


def interior_first(gx_count, field, cot, side, w1b, fs, middle, partial, cd, cot_t, fd, cs):
    nx, ny, width = field.shape
    lane = 2 * C
    cells = nx * ny
    depth = nx + 2
    extend(gx_count, fs, field, side.at[0:2])
    fill_copies(fs, fd)
    middle[...] = fd[1]
    for p in range(NZ // 2 + 1):
        span = slice(lane * p, lane * (p + 2))
        block = jnp.concatenate([fd[dy, dx:dx + depth, :, span].reshape(depth * ny, 2 * lane) for dx, dy in TAPS], axis=1)
        partial[:, :, lane * p:lane * (p + 1)] = dot(block, w1b[...]).reshape(depth, ny, lane)
    extend(gx_count, cs, cot, side.at[2:3])
    fill_copies(cs, cd)
    for p in range(NZ // 2):
        cot_t[:, cells * p:cells * (p + 1)] = cot[:, :, lane * p:lane * (p + 1)].reshape(cells, lane).T


def interior_grad(cd, wfb, partial):
    nx, ny, _ = partial.shape
    lane = 2 * C
    for p in range(NZ // 2 + 1):
        span = slice(lane * p, lane * (p + 2))
        block = jnp.concatenate([cd[dy, dx:dx + nx, :, span].reshape(nx * ny, 2 * lane) for dx, dy in TAPS], axis=1)
        partial[:, :, lane * p:lane * (p + 1)] = dot_nt(block, wfb[...]).reshape(nx, ny, lane)


def layers(factor, gx_count, gy_count, fs, middle, pre_part, grad_part, near_rows, far_rows, w1b, wfb, cot_t,
           hd, keep, send, fd, hs, es, ec, eh, eg, he, cr, pf, pg):
    nx = middle.shape[0] - 4
    ny = middle.shape[1]
    width = fs.shape[2]
    depth = nx + 2
    pairs = NZ // 2
    lane = 2 * C
    wide = width + lane
    cells = nx * ny
    gx = lax.axis_index("gx")
    gy = lax.axis_index("gy")
    low = (gx > 0).astype(F32)
    high = (gx < gx_count - 1).astype(F32)
    prev = (gy > 0).astype(F32)
    after = (gy < gy_count - 1).astype(F32)

    es[...] = jnp.zeros(es.shape, F32)
    ec[...] = jnp.zeros(ec.shape, F32)

    def place(first, last, from_row, to_row):
        span = slice(to_row, to_row + depth)
        for target, index, source in (
            (es, 0, first[0]), (es, 1, first[1]), (ec, 0, first[2]),
            (es, 4, last[0]), (es, 5, last[1]), (ec, 1, last[2]),
        ):
            target[index, span, :] = source.astype(F32)[from_row:from_row + depth]

    @pl.when(gx == 0)
    def _():
        place(near_rows, far_rows, 0, 8)

    @pl.when(gx != 0)
    def _():
        place(far_rows, near_rows, nx - 2, 6)

    for x in range(nx + 4):
        es[2, 6 + x:7 + x, :] = fs[x, 8:9, :]
        es[3, 6 + x:7 + x, :] = fs[x, 7 + ny:8 + ny, :]

    blank_edges(eh, width)
    blank_edges(eg, width)
    for t, (dx, dy) in enumerate(TAPS):
        for end in range(2):
            eh[t, end, :, lane:lane + width] = es[3 * end + dy, 6 + dx:22 + dx, :].astype(BF16)
    for dx in range(3):
        for end in range(2):
            eg[dx, end, :, lane:lane + width] = ec[end, 7 + dx:23 + dx, :].astype(BF16)

    def spans(pick):
        return jnp.concatenate([pick(slice(lane * p, lane * (p + 2))) for p in range(pairs + 1)], axis=0)

    def lanes(rows, count):
        return [rows[count * p:count * (p + 1)] for p in range(pairs + 1)]

    ends = lanes(dot(spans(lambda span: jnp.concatenate(
        [eh[t, :, :, span].reshape(32, 2 * lane) for t in range(9)], axis=1)), w1b[...]), 32)
    taps = (slice(0, 12 * C), slice(24 * C, 36 * C))
    for end in range(2):
        term = lanes(dot(spans(lambda span: jnp.concatenate(
            [eh[3 + dx, end, :, span] for dx in range(3)], axis=1)), w1b[taps[end], :]), 16)
        term_grad = lanes(dot_nt(spans(lambda span: jnp.concatenate(
            [eg[dx, end, :, span] for dx in range(3)], axis=1)), wfb[:, taps[end]]), 16)
        for p in range(pairs + 1):
            cr[end, :, lane * p:lane * (p + 1)] = term[p]
            cr[2 + end, :, lane * p:lane * (p + 1)] = term_grad[p]

    lane_of = lax.broadcasted_iota(jnp.int32, (1, wide), 1)
    inside = ((lane_of >= C) & (lane_of < wide - C)).astype(F32)
    row_of = lax.broadcasted_iota(jnp.int32, (ny, wide), 0)
    is_first = row_of == 0
    is_last = row_of == ny - 1
    end_row = lax.broadcasted_iota(jnp.int32, (16, lane), 0)
    end_x = jnp.where(end_row == 0, low, jnp.where(end_row == depth - 1, high, 1.0))
    for p in range(pairs + 1):
        here = slice(lane * p, lane * (p + 1))
        value = ends[p]
        value = value * jax.nn.sigmoid(value)
        he[0, :, here] = value[0:16] * end_x * prev * inside[:, here]
        he[1, :, here] = value[16:32] * end_x * after * inside[:, here]
    for x in range(depth):
        pre = pre_part[x]
        pre = pre + jnp.where(is_first, cr[0, x:x + 1, :], 0.0) + jnp.where(is_last, cr[1, x:x + 1, :], 0.0)
        sigma = jax.nn.sigmoid(pre)
        if 0 < x < depth - 1:
            grad = grad_part[x - 1]
            grad = grad + jnp.where(is_first, cr[2, x - 1:x, :], 0.0) + jnp.where(is_last, cr[3, x - 1:x, :], 0.0)
            pg[x - 1] = (grad * sigma * (1.0 + pre * (1.0 - sigma)) * inside).astype(BF16)
        hidden = pre * sigma * inside
        if x == 0:
            hidden = hidden * low
        if x == depth - 1:
            hidden = hidden * high
        hs[x, 8:8 + ny, :] = hidden
        hd[1, x] = hidden.astype(BF16)
        hd[0, x] = jnp.where(is_first, he[0, x:x + 1, :], hs[x, 7:7 + ny, :]).astype(BF16)
        hd[2, x] = jnp.where(is_last, he[1, x:x + 1, :], hs[x, 9:9 + ny, :]).astype(BF16)

    def hidden_span(dx, dy, p):
        return hd[dy, dx:dx + nx, :, lane * p:lane * (p + 2)].reshape(cells, 2 * lane)

    second = packed(weight_gradient(
        cot_t[...],
        lambda dx, dy: jnp.concatenate([hidden_span(dx, dy, p) for p in range(pairs)], axis=0),
        factor))

    blank_edges(fd, width)
    first_row = is_first[:, 0:width]
    last_row = is_last[:, 0:width]
    for x in range(depth):
        fd[0, x, :, lane:lane + width] = jnp.where(first_row, es[1, 7 + x:8 + x, :], fs[x + 1, 7:7 + ny, :]).astype(BF16)
        fd[1, x, :, lane:lane + width] = jnp.where(last_row, es[4, 7 + x:8 + x, :], fs[x + 1, 9:9 + ny, :]).astype(BF16)

    def field_span(dx, dy, p):
        span = slice(lane * p, lane * (p + 2))
        if dy == 1:
            return middle[dx + 1:dx + 1 + nx, :, span].reshape(cells, 2 * lane)
        return fd[dy // 2, dx:dx + nx, :, span].reshape(cells, 2 * lane)

    grad_t = jnp.concatenate(
        [pg[:, :, lane * p:lane * (p + 1)].reshape(cells, lane).T for p in range(pairs + 1)], axis=1)
    first = packed(weight_gradient(
        grad_t,
        lambda dx, dy: jnp.concatenate([field_span(dx, dy, p) for p in range(pairs + 1)], axis=0),
        factor))

    for index in range(BLOCKS):
        rows = slice(index * C, (index + 1) * C)
        keep[rows, :] = jnp.where(gx == 0, first[index], second[index])
        send[rows, :] = jnp.where(gx == 0, second[index], first[index]).astype(BF16)
    if keep.shape[0] > BLOCKS * C:
        rest = (keep.shape[0] - BLOCKS * C, lane)
        keep[BLOCKS * C:, :] = jnp.zeros(rest, F32)
        send[BLOCKS * C:, :] = jnp.zeros(rest, BF16)


def output_conv(hd, w2b, out):
    nx, ny, _ = out.shape
    lane = 2 * C
    for p in range(NZ // 2):
        block = jnp.concatenate(
            [hd[dy, dx:dx + nx, :, lane * p:lane * (p + 2)].reshape(nx * ny, 2 * lane) for dx, dy in TAPS], axis=1)
        out[:, :, lane * p:lane * (p + 1)] = dot(block, w2b[...]).astype(BF16).reshape(nx, ny, lane)


def add_pair(keep, other, out):
    out[...] = (keep[...] + other[...].astype(F32)).astype(BF16)


def add_and_repeat(terms, out):
    total = terms[0].astype(F32)
    for index in range(1, terms.shape[0]):
        total = total + terms[index].astype(F32)
    total = total.astype(BF16)
    for index in range(out.shape[0]):
        out[index] = total


def unpack(mine, other, first, second):
    gx = lax.axis_index("gx")
    a = mine[...].astype(F32)
    b = other[...].astype(F32)
    for out, rows in ((first, jnp.where(gx == 0, a, b)), (second, jnp.where(gx == 0, b, a))):
        for t, (dx, dy) in enumerate(TAPS):
            turned = rows[t * C:(t + 1) * C].T
            out[9 * dx + 3 * dy] = turned[0:C]
            out[9 * dx + 3 * dy + 1] = turned[C:2 * C]
        for pair in range(5):
            turned = rows[(9 + pair) * C:(10 + pair) * C].T
            for half in range(2 if pair < 4 else 1):
                dx, dy = TAPS[2 * pair + half]
                out[9 * dx + 3 * dy + 2] = turned[half * C:(half + 1) * C]


def near(shape, dtype):
    return pltpu.VMEM(shape, dtype)


def call(body, name, inputs, outs, scratch=(), limit=16, flops=0):
    placed = [pltpu.with_memory_space_constraint(x, pltpu.VMEM if held else pltpu.HBM) for x, held in inputs]
    size = sum(x.size * x.dtype.itemsize for x, _ in inputs)
    return pl.pallas_call(
        body,
        out_shape=list(outs),
        in_specs=[pl.BlockSpec(memory_space=pltpu.VMEM if held else pl.ANY) for _, held in inputs],
        out_specs=[pl.BlockSpec(memory_space=pltpu.VMEM)] * len(outs),
        scratch_shapes=list(scratch),
        compiler_params=pltpu.CompilerParams(vmem_limit_bytes=limit * 1024 * 1024),
        cost_estimate=pl.CostEstimate(flops=flops, bytes_accessed=size, transcendentals=0),
        name=name,
    )(*placed)


def shards(field_in, first_weight, second_weight, cotangent):
    nx, ny, width = field_in.shape[1:]
    gx_count, gy_count, grp_count = (lax.axis_size(axis) for axis in ("gx", "gy", "grp"))
    total = field_in.shape[0] * nx * ny * NZ * gx_count * gy_count * grp_count
    factor = 1.0 / math.sqrt(total)
    ranks = gy_count * grp_count
    rows = -(-BLOCKS * C // (8 * ranks)) * 8 * ranks
    lane = 2 * C
    wide = width + 2 * lane
    pairs = NZ // 2
    cells = nx * ny

    field, cot, edge, given = call(
        pack, "pack", [(field_in[0], False), (cotangent[0], False)],
        [near((nx, ny, width), BF16), near((nx, ny, width), BF16), near((3, nx, width), BF16), near((3, ny + nx, width), BF16)],
        [pltpu.VMEM((6, nx, width), F32), pltpu.SemaphoreType.DMA((2,))])
    side = swap(given)
    w1b, w2b, wfb = call(
        prepare, "prepare",
        [(first_weight.reshape(27, C, C), False), (second_weight.reshape(27, C, C), False)],
        [near((9 * 4 * C, lane), BF16), near((9 * 4 * C, lane), BF16), near((lane, 9 * 4 * C), BF16)],
        [pltpu.VMEM((27, C, C), BF16), pltpu.VMEM((27, C, C), BF16), pltpu.SemaphoreType.DMA((2,))])
    side, w1b, w2b, wfb = lax.optimization_barrier((side, w1b, w2b, wfb))
    whole, = call(join_edges, "join_edges", [(edge, True), (side, True)], [near((3, 2 * nx, width), BF16)])
    ends = [(gy_count + j, j + 1) for j in range(gy_count - 1)]
    near_rows = lax.ppermute(whole, ("gx", "gy"), ends + [(b, a) for a, b in ends])
    fs, middle, pre_part, cd, cot_t = call(
        functools.partial(interior_first, gx_count), "interior_first",
        [(x, True) for x in (field, cot, side, w1b)],
        [
            near((nx + 4, ny + 16, width), F32),
            near((nx + 4, ny, wide), BF16),
            near((nx + 2, ny, width + lane), F32),
            near((3, nx + 2, ny, wide), BF16),
            near((lane, cells * pairs), BF16),
        ],
        [pltpu.VMEM((3, nx + 4, ny, wide), BF16), pltpu.VMEM((nx + 2, ny + 16, width), F32)],
        flops=4 * 10 ** 9)
    near_rows, fs, middle, pre_part, cd, cot_t = lax.optimization_barrier((near_rows, fs, middle, pre_part, cd, cot_t))
    far_rows = swap(near_rows)
    grad_part, = call(
        interior_grad, "interior_grad", [(cd, True), (wfb, True)], [near((nx, ny, width + lane), F32)], flops=3 * 10 ** 9)
    far_rows, grad_part = lax.optimization_barrier((far_rows, grad_part))

    hd, keep, send = call(
        functools.partial(layers, factor, gx_count, gy_count), "layers",
        [(x, True) for x in (fs, middle, pre_part, grad_part, near_rows, far_rows, w1b, wfb, cot_t)],
        [near((3, nx + 2, ny, width + lane), BF16), near((rows, lane), F32), near((rows, lane), BF16)],
        [
            pltpu.VMEM((2, nx + 2, ny, wide), BF16),
            pltpu.VMEM((nx + 2, ny + 16, width + lane), F32),
            pltpu.VMEM((6, 24, width), F32),
            pltpu.VMEM((2, 32, width), F32),
            pltpu.VMEM((9, 2, 16, wide), BF16),
            pltpu.VMEM((3, 2, 16, wide), BF16),
            pltpu.VMEM((2, 16, width + lane), F32),
            pltpu.VMEM((4, 16, width + lane), F32),
            pltpu.VMEM((nx, ny, width + lane), F32),
            pltpu.VMEM((nx, ny, width + lane), BF16),
        ],
        limit=32, flops=10 ** 10)

    other = swap(send)
    out, = call(
        output_conv, "output_conv", [(hd, True), (w2b, True)],
        [near((nx, ny, width), BF16)], flops=2 * 10 ** 9)
    other, out = lax.optimization_barrier((other, out))
    both, = call(add_pair, "add_pair", [(keep, True), (other, True)], [near((rows, lane), BF16)])
    terms = lax.all_to_all(both.reshape(ranks, rows // ranks, lane), ("gy", "grp"), 0, 0)
    spread, = call(add_and_repeat, "add_and_repeat", [(terms, True)], [near(terms.shape, BF16)])
    mine = lax.all_to_all(spread, ("gy", "grp"), 0, 0).reshape(rows, lane)
    other = swap(mine)
    first, second = call(
        unpack, "unpack", [(mine, True), (other, True)], [jax.ShapeDtypeStruct((27, C, C), F32)] * 2)
    shape = (3, 3, 3, C, C)
    return out[None], first.reshape(shape), second.reshape(shape)


def solution(mesh):
    return jax.shard_map(
        shards,
        mesh=mesh,
        in_specs=(P("grp", "gx", "gy", None), P(), P(), P("grp", "gx", "gy", None)),
        out_specs=(P("grp", "gx", "gy", None), P(), P()),
        check_vma=False,
    )
```

```python
import functools
import math

import jax
import jax.numpy as jnp
from jax import lax
from jax.experimental import pallas as pl
from jax.experimental.pallas import tpu as pltpu
from jax.sharding import PartitionSpec as P

C = 64
NZ = 16
BF16 = jnp.bfloat16
F32 = jnp.float32
TAPS = [(dx, dy) for dy in range(3) for dx in range(3)]
BLOCKS = 14


def swap(array):
    return lax.ppermute(array, "gx", [(0, 1), (1, 0)])


def dot(a, b):
    return jnp.dot(a, b, preferred_element_type=F32)


def dot_nt(a, b):
    return lax.dot_general(a, b, (((1,), (1,)), ((), ())), preferred_element_type=F32)


def band(taps):
    zero = jnp.zeros((C, C), BF16)
    left = jnp.concatenate(list(taps) + [zero], axis=0)
    right = jnp.concatenate([zero] + list(taps), axis=0)
    return jnp.concatenate([left, right], axis=1)


def band_flipped(taps):
    zero = jnp.zeros((C, C), BF16)
    back = list(taps)[::-1]
    upper = jnp.concatenate(back + [zero], axis=1)
    lower = jnp.concatenate([zero] + back, axis=1)
    return jnp.concatenate([upper, lower], axis=0)


def weight_gradient(products, factor):
    result = []
    for full in products:
        for dx in range(3):
            part = full[2 * C * dx:2 * C * (dx + 1)] * factor
            result.append(part[0:C, 0:3 * C] + part[C:2 * C, C:4 * C])
    return result


def turn_rows(source, x):
    lane = 2 * C
    return jnp.concatenate([source[x, :, lane * p:lane * (p + 1)] for p in range(NZ // 2)], axis=0).T


def stack_shifts(target, source):
    lane = 2 * C
    nx = source.shape[0]
    cells = source.shape[1] * NZ // 2
    target[...] = jnp.zeros(target.shape, BF16)
    for x in range(nx):
        turned = turn_rows(source, x)
        for dx in range(3):
            target[lane * dx:lane * (dx + 1), cells * (x + dx):cells * (x + dx + 1)] = turned


def packed(pieces):
    blocks = [piece[:, 0:2 * C] for piece in pieces]
    for pair in range(0, 9, 2):
        second = pieces[pair + 1][:, 2 * C:3 * C] if pair + 1 < 9 else jnp.zeros((C, C), F32)
        blocks.append(jnp.concatenate([pieces[pair][:, 2 * C:3 * C], second], axis=1))
    return blocks


def pack(field_hbm, cot_hbm, field, cot, edge, given, rows, sems):
    copies = [
        pltpu.make_async_copy(source, target, sems.at[index])
        for index, (source, target) in enumerate(((field_hbm, field), (cot_hbm, cot)))
    ]
    for copy in copies:
        copy.start()
    for copy in copies:
        copy.wait()
    nx, ny, width = field.shape
    gx = lax.axis_index("gx")
    for x in range(nx):
        fields = field[x].astype(F32)
        cots = cot[x].astype(F32)
        for index, row in enumerate((fields[0:1], fields[1:2], cots[0:1], fields[ny - 2:ny - 1], fields[ny - 1:ny], cots[ny - 1:ny])):
            rows[index, x:x + 1, :] = row
    head = rows[0:3].astype(BF16)
    tail = rows[3:6].astype(BF16)

    @pl.when(gx == 0)
    def _():
        edge[...] = head
        given[:, ny:ny + nx] = tail
        given[0:2, 0:ny] = field[nx - 2:nx]
        given[2:3, 0:ny] = cot[nx - 1:nx]

    @pl.when(gx != 0)
    def _():
        edge[...] = tail
        given[:, ny:ny + nx] = head
        given[0:2, 0:ny] = field[0:2]
        given[2:3, 0:ny] = cot[0:1]


def join_edges(edge, taken, whole):
    nx = edge.shape[1]
    gx = lax.axis_index("gx")

    @pl.when(gx == 0)
    def _():
        whole[:, 0:nx] = edge[...]
        whole[:, nx:2 * nx] = taken[:, taken.shape[1] - nx:]

    @pl.when(gx != 0)
    def _():
        whole[:, 0:nx] = taken[:, taken.shape[1] - nx:]
        whole[:, nx:2 * nx] = edge[...]


def load_weights(w1_hbm, w2_hbm, w1, w2, sems):
    copies = [
        pltpu.make_async_copy(source, target, sems.at[index])
        for index, (source, target) in enumerate(((w1_hbm, w1), (w2_hbm, w2)))
    ]
    for copy in copies:
        copy.start()
    for copy in copies:
        copy.wait()


def make_bands(w1, w2, w1b, w2b, wfb):
    for t, (dx, dy) in enumerate(TAPS):
        rows = slice(t * 4 * C, (t + 1) * 4 * C)
        first = 9 * dx + 3 * dy
        w1b[rows, :] = band([w1[first + z] for z in range(3)])
        w2b[rows, :] = band([w2[first + z] for z in range(3)])
        wfb[:, rows] = band_flipped([w2[24 - first + z] for z in range(3)])


def extend(gx_count, target, own, side):
    gx = lax.axis_index("gx")
    nx, ny, _ = own.shape
    width = side.shape[0]
    target[width:width + nx, 8:8 + ny, :] = own[...].astype(F32)
    halo = side[:, 0:ny].astype(F32)
    target[0:width, 8:8 + ny, :] = halo * (gx > 0).astype(F32)
    target[width + nx:2 * width + nx, 8:8 + ny, :] = halo * (gx < gx_count - 1).astype(F32)


def blank_edges(copies, width):
    lane = 2 * C
    zero = jnp.zeros(copies.shape[:-1] + (lane,), BF16)
    copies[..., 0:lane] = zero
    copies[..., lane + width:] = zero


def fill_copies(scratch, copies):
    depth, _, width = scratch.shape
    ny = copies.shape[2]
    lane = 2 * C
    blank_edges(copies, width)
    zero = jnp.zeros((depth, 1, width), F32)
    scratch[:, 7:8, :] = zero
    scratch[:, 8 + ny:9 + ny, :] = zero
    for dy in range(3):
        copies[dy, :, :, lane:lane + width] = scratch[:, 7 + dy:7 + dy + ny, :].astype(BF16)


def interior_first(gx_count, field, cot, side, w1, w2, fs, middle, partial, cd, cot_t, w1b, w2b, wfb, fd, cs):
    nx, ny, width = field.shape
    lane = 2 * C
    depth = nx + 2
    make_bands(w1, w2, w1b, w2b, wfb)
    extend(gx_count, fs, field, side.at[0:2])
    fill_copies(fs, fd)
    middle[...] = fd[1]
    for p in range(NZ // 2 + 1):
        span = slice(lane * p, lane * (p + 2))
        block = jnp.concatenate([fd[dy, dx:dx + depth, :, span].reshape(depth * ny, 2 * lane) for dx, dy in TAPS], axis=1)
        partial[:, :, lane * p:lane * (p + 1)] = dot(block, w1b[...]).reshape(depth, ny, lane)
    extend(gx_count, cs, cot, side.at[2:3])
    fill_copies(cs, cd)
    stack_shifts(cot_t, cot)


def interior_grad(cd, wfb, partial):
    nx, ny, _ = partial.shape
    lane = 2 * C
    for p in range(NZ // 2 + 1):
        span = slice(lane * p, lane * (p + 2))
        block = jnp.concatenate([cd[dy, dx:dx + nx, :, span].reshape(nx * ny, 2 * lane) for dx, dy in TAPS], axis=1)
        partial[:, :, lane * p:lane * (p + 1)] = dot_nt(block, wfb[...]).reshape(nx, ny, lane)


def layers(factor, gx_count, gy_count, fs, middle, pre_part, grad_part, near_rows, far_rows, w1b, wfb, cot_t,
           hd, keep, send, fd, hs, es, ec, eh, eg, he, cr, pg, pt):
    nx = middle.shape[0] - 4
    ny = middle.shape[1]
    width = fs.shape[2]
    depth = nx + 2
    pairs = NZ // 2
    lane = 2 * C
    wide = width + lane
    cells = nx * ny
    gx = lax.axis_index("gx")
    gy = lax.axis_index("gy")
    low = (gx > 0).astype(F32)
    high = (gx < gx_count - 1).astype(F32)
    prev = (gy > 0).astype(F32)
    after = (gy < gy_count - 1).astype(F32)

    es[...] = jnp.zeros(es.shape, F32)
    ec[...] = jnp.zeros(ec.shape, F32)

    def place(first, last, from_row, to_row):
        span = slice(to_row, to_row + depth)
        for target, index, source in (
            (es, 0, first[0]), (es, 1, first[1]), (ec, 0, first[2]),
            (es, 4, last[0]), (es, 5, last[1]), (ec, 1, last[2]),
        ):
            target[index, span, :] = source.astype(F32)[from_row:from_row + depth]

    @pl.when(gx == 0)
    def _():
        place(near_rows, far_rows, 0, 8)

    @pl.when(gx != 0)
    def _():
        place(far_rows, near_rows, nx - 2, 6)

    for x in range(nx + 4):
        es[2, 6 + x:7 + x, :] = fs[x, 8:9, :]
        es[3, 6 + x:7 + x, :] = fs[x, 7 + ny:8 + ny, :]

    blank_edges(eh, width)
    blank_edges(eg, width)
    for t, (dx, dy) in enumerate(TAPS):
        for end in range(2):
            eh[t, end, :, lane:lane + width] = es[3 * end + dy, 6 + dx:22 + dx, :].astype(BF16)
    for dx in range(3):
        for end in range(2):
            eg[dx, end, :, lane:lane + width] = ec[end, 7 + dx:23 + dx, :].astype(BF16)

    def spans(pick):
        return jnp.concatenate([pick(slice(lane * p, lane * (p + 2))) for p in range(pairs + 1)], axis=0)

    def lanes(rows, count):
        return [rows[count * p:count * (p + 1)] for p in range(pairs + 1)]

    ends = lanes(dot(spans(lambda span: jnp.concatenate(
        [eh[t, :, :, span].reshape(32, 2 * lane) for t in range(9)], axis=1)), w1b[...]), 32)
    taps = (slice(0, 12 * C), slice(24 * C, 36 * C))
    for end in range(2):
        term = lanes(dot(spans(lambda span: jnp.concatenate(
            [eh[3 + dx, end, :, span] for dx in range(3)], axis=1)), w1b[taps[end], :]), 16)
        term_grad = lanes(dot_nt(spans(lambda span: jnp.concatenate(
            [eg[dx, end, :, span] for dx in range(3)], axis=1)), wfb[:, taps[end]]), 16)
        for p in range(pairs + 1):
            cr[end, :, lane * p:lane * (p + 1)] = term[p]
            cr[2 + end, :, lane * p:lane * (p + 1)] = term_grad[p]

    lane_of = lax.broadcasted_iota(jnp.int32, (1, wide), 1)
    inside = ((lane_of >= C) & (lane_of < wide - C)).astype(F32)
    row_of = lax.broadcasted_iota(jnp.int32, (ny, wide), 0)
    is_first = row_of == 0
    is_last = row_of == ny - 1
    end_row = lax.broadcasted_iota(jnp.int32, (16, lane), 0)
    end_x = jnp.where(end_row == 0, low, jnp.where(end_row == depth - 1, high, 1.0))
    for p in range(pairs + 1):
        here = slice(lane * p, lane * (p + 1))
        value = ends[p]
        value = value * jax.nn.sigmoid(value)
        he[0, :, here] = value[0:16] * end_x * prev * inside[:, here]
        he[1, :, here] = value[16:32] * end_x * after * inside[:, here]
    for x in range(depth):
        pre = pre_part[x]
        pre = pre + jnp.where(is_first, cr[0, x:x + 1, :], 0.0) + jnp.where(is_last, cr[1, x:x + 1, :], 0.0)
        sigma = jax.nn.sigmoid(pre)
        if 0 < x < depth - 1:
            grad = grad_part[x - 1]
            grad = grad + jnp.where(is_first, cr[2, x - 1:x, :], 0.0) + jnp.where(is_last, cr[3, x - 1:x, :], 0.0)
            pg[x - 1] = (grad * sigma * (1.0 + pre * (1.0 - sigma)) * inside).astype(BF16)
        hidden = pre * sigma * inside
        if x == 0:
            hidden = hidden * low
        if x == depth - 1:
            hidden = hidden * high
        hs[x, 8:8 + ny, :] = hidden
        hd[1, x] = hidden.astype(BF16)
        hd[0, x] = jnp.where(is_first, he[0, x:x + 1, :], hs[x, 7:7 + ny, :]).astype(BF16)
        hd[2, x] = jnp.where(is_last, he[1, x:x + 1, :], hs[x, 9:9 + ny, :]).astype(BF16)

    def by_rows(pick, count):
        return jnp.concatenate(
            [pick(x, slice(lane * p, lane * (p + 2))) for x in range(depth) for p in range(count)], axis=0)

    second = packed(weight_gradient(
        [dot(cot_t[...], by_rows(lambda x, span: hd[dy, x, :, span], pairs)) for dy in range(3)], factor))

    blank_edges(fd, width)
    first_row = is_first[:, 0:width]
    last_row = is_last[:, 0:width]
    for x in range(depth):
        fd[0, x, :, lane:lane + width] = jnp.where(first_row, es[1, 7 + x:8 + x, :], fs[x + 1, 7:7 + ny, :]).astype(BF16)
        fd[1, x, :, lane:lane + width] = jnp.where(last_row, es[4, 7 + x:8 + x, :], fs[x + 1, 9:9 + ny, :]).astype(BF16)

    def field_row(dy, x, span):
        return middle[x + 1, :, span] if dy == 1 else fd[dy // 2, x, :, span]

    stack_shifts(pt, pg)
    last = pg[:, :, lane * pairs:].reshape(cells, lane)
    extra = 2 * lane - cells
    last_t = jnp.concatenate(
        [
            jnp.concatenate([jnp.zeros((ny * dx, lane), BF16)] * (dx > 0) + [last, jnp.zeros((extra - ny * dx, lane), BF16)], axis=0).T
            for dx in range(3)
        ],
        axis=0,
    )
    span = slice(lane * pairs, lane * (pairs + 2))
    pad = jnp.zeros((2 * lane - depth * ny, 2 * lane), BF16)
    first = packed(weight_gradient(
        [
            dot(pt[...], by_rows(lambda x, span: field_row(dy, x, span), pairs))
            + dot(last_t, jnp.concatenate([field_row(dy, x, span) for x in range(depth)] + [pad], axis=0))
            for dy in range(3)
        ],
        factor))

    for index in range(BLOCKS):
        rows = slice(index * C, (index + 1) * C)
        keep[rows, :] = jnp.where(gx == 0, first[index], second[index])
        send[rows, :] = jnp.where(gx == 0, second[index], first[index]).astype(BF16)
    if keep.shape[0] > BLOCKS * C:
        rest = (keep.shape[0] - BLOCKS * C, lane)
        keep[BLOCKS * C:, :] = jnp.zeros(rest, F32)
        send[BLOCKS * C:, :] = jnp.zeros(rest, BF16)


def output_conv(hd, w2b, out):
    nx, ny, _ = out.shape
    lane = 2 * C
    for p in range(NZ // 2):
        block = jnp.concatenate(
            [hd[dy, dx:dx + nx, :, lane * p:lane * (p + 2)].reshape(nx * ny, 2 * lane) for dx, dy in TAPS], axis=1)
        out[:, :, lane * p:lane * (p + 1)] = dot(block, w2b[...]).astype(BF16).reshape(nx, ny, lane)


def add_pair(keep, other, out):
    out[...] = (keep[...] + other[...].astype(F32)).astype(BF16)


def add_and_repeat(terms, out):
    total = terms[0].astype(F32)
    for index in range(1, terms.shape[0]):
        total = total + terms[index].astype(F32)
    total = total.astype(BF16)
    for index in range(out.shape[0]):
        out[index] = total


def unpack(mine, other, first, second, held, sems):
    gx = lax.axis_index("gx")
    copies = []
    for which, out in enumerate((first, second)):
        def block(index):
            rows = slice(index * C, (index + 1) * C)
            a = mine[rows, :].astype(F32)
            b = other[rows, :].astype(F32)
            return (jnp.where(gx == 0, a, b) if which == 0 else jnp.where(gx == 0, b, a)).T

        for t, (dx, dy) in enumerate(TAPS):
            turned = block(t)
            if t % 2 == 0:
                rest = block(9 + t // 2)
            place = 9 * dx + 3 * dy
            held[which, place] = turned[0:C]
            held[which, place + 1] = turned[C:2 * C]
            held[which, place + 2] = rest[C * (t % 2):C * (t % 2 + 1)]
            copy = pltpu.make_async_copy(held.at[which, place:place + 3], out.at[place:place + 3], sems.at[which, t])
            copy.start()
            copies.append(copy)
    for copy in copies:
        copy.wait()


def near(shape, dtype):
    return pltpu.VMEM(shape, dtype)


def call(body, name, inputs, outs, scratch=(), limit=16, flops=0, far=False):
    placed = [pltpu.with_memory_space_constraint(x, pltpu.VMEM if held else pltpu.HBM) for x, held in inputs]
    size = sum(x.size * x.dtype.itemsize for x, _ in inputs)
    return pl.pallas_call(
        body,
        out_shape=list(outs),
        in_specs=[pl.BlockSpec(memory_space=pltpu.VMEM if held else pl.ANY) for _, held in inputs],
        out_specs=[pl.BlockSpec(memory_space=pl.ANY if far else pltpu.VMEM)] * len(outs),
        scratch_shapes=list(scratch),
        compiler_params=pltpu.CompilerParams(vmem_limit_bytes=limit * 1024 * 1024),
        cost_estimate=pl.CostEstimate(flops=flops, bytes_accessed=size, transcendentals=0),
        name=name,
    )(*placed)


def shards(field_in, first_weight, second_weight, cotangent):
    nx, ny, width = field_in.shape[1:]
    gx_count, gy_count, grp_count = (lax.axis_size(axis) for axis in ("gx", "gy", "grp"))
    total = field_in.shape[0] * nx * ny * NZ * gx_count * gy_count * grp_count
    factor = 1.0 / math.sqrt(total)
    ranks = gy_count * grp_count
    rows = -(-BLOCKS * C // (8 * ranks)) * 8 * ranks
    lane = 2 * C
    wide = width + 2 * lane
    pairs = NZ // 2

    field, cot, edge, given = call(
        pack, "pack", [(field_in[0], False), (cotangent[0], False)],
        [near((nx, ny, width), BF16), near((nx, ny, width), BF16), near((3, nx, width), BF16), near((3, ny + nx, width), BF16)],
        [pltpu.VMEM((6, nx, width), F32), pltpu.SemaphoreType.DMA((2,))])
    side = swap(given)
    w1, w2 = call(
        load_weights, "load_weights",
        [(first_weight.reshape(27, C, C), False), (second_weight.reshape(27, C, C), False)],
        [near((27, C, C), BF16)] * 2, [pltpu.SemaphoreType.DMA((2,))])
    side, w1, w2 = lax.optimization_barrier((side, w1, w2))
    whole, = call(join_edges, "join_edges", [(edge, True), (side, True)], [near((3, 2 * nx, width), BF16)])
    ends = [(gy_count + j, j + 1) for j in range(gy_count - 1)]
    near_rows = lax.ppermute(whole, ("gx", "gy"), ends + [(b, a) for a, b in ends])
    fs, middle, pre_part, cd, cot_t, w1b, w2b, wfb = call(
        functools.partial(interior_first, gx_count), "interior_first",
        [(x, True) for x in (field, cot, side, w1, w2)],
        [
            near((nx + 4, ny + 16, width), F32),
            near((nx + 4, ny, wide), BF16),
            near((nx + 2, ny, width + lane), F32),
            near((3, nx + 2, ny, wide), BF16),
            near((3 * lane, (nx + 2) * ny * pairs), BF16),
            near((9 * 4 * C, lane), BF16),
            near((9 * 4 * C, lane), BF16),
            near((lane, 9 * 4 * C), BF16),
        ],
        [pltpu.VMEM((3, nx + 4, ny, wide), BF16), pltpu.VMEM((nx + 2, ny + 16, width), F32)],
        flops=4 * 10 ** 9)
    near_rows, pre_part, wfb = lax.optimization_barrier((near_rows, pre_part, wfb))
    far_rows = swap(near_rows)
    grad_part, = call(
        interior_grad, "interior_grad", [(cd, True), (wfb, True)], [near((nx, ny, width + lane), F32)], flops=3 * 10 ** 9)
    far_rows, grad_part = lax.optimization_barrier((far_rows, grad_part))

    hd, keep, send = call(
        functools.partial(layers, factor, gx_count, gy_count), "layers",
        [(x, True) for x in (fs, middle, pre_part, grad_part, near_rows, far_rows, w1b, wfb, cot_t)],
        [near((3, nx + 2, ny, width + lane), BF16), near((rows, lane), F32), near((rows, lane), BF16)],
        [
            pltpu.VMEM((2, nx + 2, ny, wide), BF16),
            pltpu.VMEM((nx + 2, ny + 16, width + lane), F32),
            pltpu.VMEM((6, 24, width), F32),
            pltpu.VMEM((2, 32, width), F32),
            pltpu.VMEM((9, 2, 16, wide), BF16),
            pltpu.VMEM((3, 2, 16, wide), BF16),
            pltpu.VMEM((2, 16, width + lane), F32),
            pltpu.VMEM((4, 16, width + lane), F32),
            pltpu.VMEM((nx, ny, width + lane), BF16),
            pltpu.VMEM((3 * lane, (nx + 2) * ny * pairs), BF16),
        ],
        limit=32, flops=10 ** 10)

    other = swap(send)
    out, = call(
        output_conv, "output_conv", [(hd, True), (w2b, True)],
        [near((nx, ny, width), BF16)], flops=2 * 10 ** 9)
    other, out = lax.optimization_barrier((other, out))
    both, = call(add_pair, "add_pair", [(keep, True), (other, True)], [near((rows, lane), BF16)])
    terms = lax.all_to_all(both.reshape(ranks, rows // ranks, lane), ("gy", "grp"), 0, 0)
    spread, = call(add_and_repeat, "add_and_repeat", [(terms, True)], [near(terms.shape, BF16)])
    mine = lax.all_to_all(spread, ("gy", "grp"), 0, 0).reshape(rows, lane)
    other = swap(mine)
    first, second = call(
        unpack, "unpack", [(mine, True), (other, True)], [pltpu.HBM((27, C, C), F32)] * 2,
        [pltpu.VMEM((2, 27, C, C), F32), pltpu.SemaphoreType.DMA((2, 9))], far=True)
    shape = (3, 3, 3, C, C)
    return out[None], first.reshape(shape), second.reshape(shape)


def solution(mesh):
    return jax.shard_map(
        shards,
        mesh=mesh,
        in_specs=(P("grp", "gx", "gy", None), P(), P(), P("grp", "gx", "gy", None)),
        out_specs=(P("grp", "gx", "gy", None), P(), P()),
        check_vma=False,
    )
```

```python
import functools
import math

import jax
import jax.numpy as jnp
from jax import lax
from jax.experimental import pallas as pl
from jax.experimental.pallas import tpu as pltpu
from jax.sharding import PartitionSpec as P

C = 64
NZ = 16
BF16 = jnp.bfloat16
F32 = jnp.float32
TAPS = [(dx, dy) for dy in range(3) for dx in range(3)]
BLOCKS = 14
EARLY = 3


def swap(array):
    return lax.ppermute(array, "gx", [(0, 1), (1, 0)])


def dot(a, b):
    return jnp.dot(a, b, preferred_element_type=F32)


def dot_nt(a, b):
    return lax.dot_general(a, b, (((1,), (1,)), ((), ())), preferred_element_type=F32)


def band(taps):
    zero = jnp.zeros((C, C), BF16)
    left = jnp.concatenate(list(taps) + [zero], axis=0)
    right = jnp.concatenate([zero] + list(taps), axis=0)
    return jnp.concatenate([left, right], axis=1)


def band_flipped(taps):
    zero = jnp.zeros((C, C), BF16)
    back = list(taps)[::-1]
    upper = jnp.concatenate(back + [zero], axis=1)
    lower = jnp.concatenate([zero] + back, axis=1)
    return jnp.concatenate([upper, lower], axis=0)


def weight_gradient(rows_t, taps_of, total):
    result = []
    for dx, dy in TAPS:
        full = dot(rows_t, taps_of(dx, dy)) * total
        result.append(full[0:C, 0:3 * C] + full[C:2 * C, C:4 * C])
    return result


def packed(pieces):
    blocks = [piece[:, 0:2 * C] for piece in pieces]
    for pair in range(0, 9, 2):
        second = pieces[pair + 1][:, 2 * C:3 * C] if pair + 1 < 9 else jnp.zeros((C, C), F32)
        blocks.append(jnp.concatenate([pieces[pair][:, 2 * C:3 * C], second], axis=1))
    return blocks


def pack(field_hbm, cot_hbm, field, cot, edge, given, rows, sems):
    copies = [
        pltpu.make_async_copy(source, target, sems.at[index])
        for index, (source, target) in enumerate(((field_hbm, field), (cot_hbm, cot)))
    ]
    for copy in copies:
        copy.start()
    for copy in copies:
        copy.wait()
    nx, ny, width = field.shape
    gx = lax.axis_index("gx")
    for x in range(nx):
        fields = field[x].astype(F32)
        cots = cot[x].astype(F32)
        for index, row in enumerate((fields[0:1], fields[1:2], cots[0:1], fields[ny - 2:ny - 1], fields[ny - 1:ny], cots[ny - 1:ny])):
            rows[index, x:x + 1, :] = row
    head = rows[0:3].astype(BF16)
    tail = rows[3:6].astype(BF16)

    @pl.when(gx == 0)
    def _():
        edge[...] = head
        given[:, ny:ny + nx] = tail
        given[0:2, 0:ny] = field[nx - 2:nx]
        given[2:3, 0:ny] = cot[nx - 1:nx]

    @pl.when(gx != 0)
    def _():
        edge[...] = tail
        given[:, ny:ny + nx] = head
        given[0:2, 0:ny] = field[0:2]
        given[2:3, 0:ny] = cot[0:1]


def join_edges(edge, taken, whole):
    nx = edge.shape[1]
    gx = lax.axis_index("gx")

    @pl.when(gx == 0)
    def _():
        whole[:, 0:nx] = edge[...]
        whole[:, nx:2 * nx] = taken[:, taken.shape[1] - nx:]

    @pl.when(gx != 0)
    def _():
        whole[:, 0:nx] = taken[:, taken.shape[1] - nx:]
        whole[:, nx:2 * nx] = edge[...]


def load_weights(w1_hbm, w2_hbm, w1, w2, sems):
    copies = [
        pltpu.make_async_copy(source, target, sems.at[index])
        for index, (source, target) in enumerate(((w1_hbm, w1), (w2_hbm, w2)))
    ]
    for copy in copies:
        copy.start()
    for copy in copies:
        copy.wait()


def make_bands(w1, w2, w1b, w2b, wfb):
    for t, (dx, dy) in enumerate(TAPS):
        rows = slice(t * 4 * C, (t + 1) * 4 * C)
        first = 9 * dx + 3 * dy
        w1b[rows, :] = band([w1[first + z] for z in range(3)])
        w2b[rows, :] = band([w2[first + z] for z in range(3)])
        wfb[:, rows] = band_flipped([w2[24 - first + z] for z in range(3)])


def extend(gx_count, target, own, side):
    gx = lax.axis_index("gx")
    nx, ny, _ = own.shape
    width = side.shape[0]
    target[width:width + nx, 8:8 + ny, :] = own[...].astype(F32)
    halo = side[:, 0:ny].astype(F32)
    target[0:width, 8:8 + ny, :] = halo * (gx > 0).astype(F32)
    target[width + nx:2 * width + nx, 8:8 + ny, :] = halo * (gx < gx_count - 1).astype(F32)


def blank_edges(copies, width):
    lane = 2 * C
    zero = jnp.zeros(copies.shape[:-1] + (lane,), BF16)
    copies[..., 0:lane] = zero
    copies[..., lane + width:] = zero


def fill_copies(scratch, copies):
    depth, _, width = scratch.shape
    ny = copies.shape[2]
    lane = 2 * C
    blank_edges(copies, width)
    zero = jnp.zeros((depth, 1, width), F32)
    scratch[:, 7:8, :] = zero
    scratch[:, 8 + ny:9 + ny, :] = zero
    for dy in range(3):
        copies[dy, :, :, lane:lane + width] = scratch[:, 7 + dy:7 + dy + ny, :].astype(BF16)


def interior_first(gx_count, field, cot, side, w1, w2, fs, middle, partial, cd, cot_t, w1b, w2b, wfb, grad_part, fd, cs):
    nx, ny, width = field.shape
    lane = 2 * C
    depth = nx + 2
    make_bands(w1, w2, w1b, w2b, wfb)
    extend(gx_count, fs, field, side.at[0:2])
    fill_copies(fs, fd)
    middle[...] = fd[1]
    for p in range(NZ // 2 + 1):
        span = slice(lane * p, lane * (p + 2))
        block = jnp.concatenate([fd[dy, dx:dx + depth, :, span].reshape(depth * ny, 2 * lane) for dx, dy in TAPS], axis=1)
        partial[:, :, lane * p:lane * (p + 1)] = dot(block, w1b[...]).reshape(depth, ny, lane)
    extend(gx_count, cs, cot, side.at[2:3])
    fill_copies(cs, cd)
    cells = nx * ny
    for p in range(NZ // 2):
        cot_t[:, cells * p:cells * (p + 1)] = cot[:, :, lane * p:lane * (p + 1)].reshape(cells, lane).T
    interior_grad(range(EARLY), cd, wfb, grad_part)


def interior_grad(pairs, cd, wfb, partial):
    nx, ny, _ = partial.shape
    lane = 2 * C
    for p in pairs:
        span = slice(lane * p, lane * (p + 2))
        block = jnp.concatenate([cd[dy, dx:dx + nx, :, span].reshape(nx * ny, 2 * lane) for dx, dy in TAPS], axis=1)
        here = lane * (p - pairs[0])
        partial[:, :, here:here + lane] = dot_nt(block, wfb[...]).reshape(nx, ny, lane)


def layers(factor, gx_count, gy_count, fs, middle, pre_part, grad_early, grad_late, near_rows, far_rows, w1b, wfb, cot_t,
           hd, keep, send, fd, hs, es, ec, eh, eg, he, cr, pg):
    nx = middle.shape[0] - 4
    ny = middle.shape[1]
    width = fs.shape[2]
    depth = nx + 2
    pairs = NZ // 2
    lane = 2 * C
    wide = width + lane
    cells = nx * ny
    gx = lax.axis_index("gx")
    gy = lax.axis_index("gy")
    low = (gx > 0).astype(F32)
    high = (gx < gx_count - 1).astype(F32)
    prev = (gy > 0).astype(F32)
    after = (gy < gy_count - 1).astype(F32)

    es[...] = jnp.zeros(es.shape, F32)
    ec[...] = jnp.zeros(ec.shape, F32)

    def place(first, last, from_row, to_row):
        span = slice(to_row, to_row + depth)
        for target, index, source in (
            (es, 0, first[0]), (es, 1, first[1]), (ec, 0, first[2]),
            (es, 4, last[0]), (es, 5, last[1]), (ec, 1, last[2]),
        ):
            target[index, span, :] = source.astype(F32)[from_row:from_row + depth]

    @pl.when(gx == 0)
    def _():
        place(near_rows, far_rows, 0, 8)

    @pl.when(gx != 0)
    def _():
        place(far_rows, near_rows, nx - 2, 6)

    for x in range(nx + 4):
        es[2, 6 + x:7 + x, :] = fs[x, 8:9, :]
        es[3, 6 + x:7 + x, :] = fs[x, 7 + ny:8 + ny, :]

    blank_edges(eh, width)
    blank_edges(eg, width)
    for t, (dx, dy) in enumerate(TAPS):
        for end in range(2):
            eh[t, end, :, lane:lane + width] = es[3 * end + dy, 6 + dx:22 + dx, :].astype(BF16)
    for dx in range(3):
        for end in range(2):
            eg[dx, end, :, lane:lane + width] = ec[end, 7 + dx:23 + dx, :].astype(BF16)

    def spans(pick):
        return jnp.concatenate([pick(slice(lane * p, lane * (p + 2))) for p in range(pairs + 1)], axis=0)

    def lanes(rows, count):
        return [rows[count * p:count * (p + 1)] for p in range(pairs + 1)]

    ends = lanes(dot(spans(lambda span: jnp.concatenate(
        [eh[t, :, :, span].reshape(32, 2 * lane) for t in range(9)], axis=1)), w1b[...]), 32)
    taps = (slice(0, 12 * C), slice(24 * C, 36 * C))
    for end in range(2):
        term = lanes(dot(spans(lambda span: jnp.concatenate(
            [eh[3 + dx, end, :, span] for dx in range(3)], axis=1)), w1b[taps[end], :]), 16)
        term_grad = lanes(dot_nt(spans(lambda span: jnp.concatenate(
            [eg[dx, end, :, span] for dx in range(3)], axis=1)), wfb[:, taps[end]]), 16)
        for p in range(pairs + 1):
            cr[end, :, lane * p:lane * (p + 1)] = term[p]
            cr[2 + end, :, lane * p:lane * (p + 1)] = term_grad[p]

    lane_of = lax.broadcasted_iota(jnp.int32, (1, wide), 1)
    inside = ((lane_of >= C) & (lane_of < wide - C)).astype(F32)
    row_of = lax.broadcasted_iota(jnp.int32, (ny, wide), 0)
    is_first = row_of == 0
    is_last = row_of == ny - 1
    end_row = lax.broadcasted_iota(jnp.int32, (16, lane), 0)
    end_x = jnp.where(end_row == 0, low, jnp.where(end_row == depth - 1, high, 1.0))
    for p in range(pairs + 1):
        here = slice(lane * p, lane * (p + 1))
        value = ends[p]
        value = value * jax.nn.sigmoid(value)
        he[0, :, here] = value[0:16] * end_x * prev * inside[:, here]
        he[1, :, here] = value[16:32] * end_x * after * inside[:, here]
    for x in range(depth):
        pre = pre_part[x]
        pre = pre + jnp.where(is_first, cr[0, x:x + 1, :], 0.0) + jnp.where(is_last, cr[1, x:x + 1, :], 0.0)
        sigma = jax.nn.sigmoid(pre)
        if 0 < x < depth - 1:
            grad = jnp.concatenate([grad_early[x - 1], grad_late[x - 1]], axis=1)
            grad = grad + jnp.where(is_first, cr[2, x - 1:x, :], 0.0) + jnp.where(is_last, cr[3, x - 1:x, :], 0.0)
            pg[x - 1] = (grad * sigma * (1.0 + pre * (1.0 - sigma)) * inside).astype(BF16)
        hidden = pre * sigma * inside
        if x == 0:
            hidden = hidden * low
        if x == depth - 1:
            hidden = hidden * high
        hs[x, 8:8 + ny, :] = hidden
        hd[1, x] = hidden.astype(BF16)
        hd[0, x] = jnp.where(is_first, he[0, x:x + 1, :], hs[x, 7:7 + ny, :]).astype(BF16)
        hd[2, x] = jnp.where(is_last, he[1, x:x + 1, :], hs[x, 9:9 + ny, :]).astype(BF16)

    def hidden_span(dx, dy, p):
        return hd[dy, dx:dx + nx, :, lane * p:lane * (p + 2)].reshape(cells, 2 * lane)

    second = packed(weight_gradient(
        cot_t[...],
        lambda dx, dy: jnp.concatenate([hidden_span(dx, dy, p) for p in range(pairs)], axis=0),
        factor))

    blank_edges(fd, width)
    first_row = is_first[:, 0:width]
    last_row = is_last[:, 0:width]
    for x in range(depth):
        fd[0, x, :, lane:lane + width] = jnp.where(first_row, es[1, 7 + x:8 + x, :], fs[x + 1, 7:7 + ny, :]).astype(BF16)
        fd[1, x, :, lane:lane + width] = jnp.where(last_row, es[4, 7 + x:8 + x, :], fs[x + 1, 9:9 + ny, :]).astype(BF16)

    def field_span(dx, dy, p):
        span = slice(lane * p, lane * (p + 2))
        if dy == 1:
            return middle[dx + 1:dx + 1 + nx, :, span].reshape(cells, 2 * lane)
        return fd[dy // 2, dx:dx + nx, :, span].reshape(cells, 2 * lane)

    grad_t = jnp.concatenate(
        [pg[:, :, lane * p:lane * (p + 1)].reshape(cells, lane).T for p in range(pairs + 1)], axis=1)
    first = packed(weight_gradient(
        grad_t,
        lambda dx, dy: jnp.concatenate([field_span(dx, dy, p) for p in range(pairs + 1)], axis=0),
        factor))

    for index in range(BLOCKS):
        rows = slice(index * C, (index + 1) * C)
        keep[rows, :] = jnp.where(gx == 0, first[index], second[index])
        send[rows, :] = jnp.where(gx == 0, second[index], first[index]).astype(BF16)
    if keep.shape[0] > BLOCKS * C:
        rest = (keep.shape[0] - BLOCKS * C, lane)
        keep[BLOCKS * C:, :] = jnp.zeros(rest, F32)
        send[BLOCKS * C:, :] = jnp.zeros(rest, BF16)


def output_conv(hd, w2b, out):
    nx, ny, _ = out.shape
    lane = 2 * C
    for p in range(NZ // 2):
        block = jnp.concatenate(
            [hd[dy, dx:dx + nx, :, lane * p:lane * (p + 2)].reshape(nx * ny, 2 * lane) for dx, dy in TAPS], axis=1)
        out[:, :, lane * p:lane * (p + 1)] = dot(block, w2b[...]).astype(BF16).reshape(nx, ny, lane)


def add_pair(keep, other, out):
    out[...] = (keep[...] + other[...].astype(F32)).astype(BF16)


def add_and_repeat(terms, out):
    total = terms[0].astype(F32)
    for index in range(1, terms.shape[0]):
        total = total + terms[index].astype(F32)
    total = total.astype(BF16)
    for index in range(out.shape[0]):
        out[index] = total


def unpack(mine, other, first, second):
    gx = lax.axis_index("gx")
    a = mine[...].astype(F32)
    b = other[...].astype(F32)
    for out, rows in ((first, jnp.where(gx == 0, a, b)), (second, jnp.where(gx == 0, b, a))):
        for t, (dx, dy) in enumerate(TAPS):
            turned = rows[t * C:(t + 1) * C].T
            out[9 * dx + 3 * dy] = turned[0:C]
            out[9 * dx + 3 * dy + 1] = turned[C:2 * C]
        for pair in range(5):
            turned = rows[(9 + pair) * C:(10 + pair) * C].T
            for half in range(2 if pair < 4 else 1):
                dx, dy = TAPS[2 * pair + half]
                out[9 * dx + 3 * dy + 2] = turned[half * C:(half + 1) * C]


def near(shape, dtype):
    return pltpu.VMEM(shape, dtype)


def call(body, name, inputs, outs, scratch=(), limit=16, flops=0):
    placed = [pltpu.with_memory_space_constraint(x, pltpu.VMEM if held else pltpu.HBM) for x, held in inputs]
    size = sum(x.size * x.dtype.itemsize for x, _ in inputs)
    return pl.pallas_call(
        body,
        out_shape=list(outs),
        in_specs=[pl.BlockSpec(memory_space=pltpu.VMEM if held else pl.ANY) for _, held in inputs],
        out_specs=[pl.BlockSpec(memory_space=pltpu.VMEM)] * len(outs),
        scratch_shapes=list(scratch),
        compiler_params=pltpu.CompilerParams(vmem_limit_bytes=limit * 1024 * 1024),
        cost_estimate=pl.CostEstimate(flops=flops, bytes_accessed=size, transcendentals=0),
        name=name,
    )(*placed)


def shards(field_in, first_weight, second_weight, cotangent):
    nx, ny, width = field_in.shape[1:]
    gx_count, gy_count, grp_count = (lax.axis_size(axis) for axis in ("gx", "gy", "grp"))
    total = field_in.shape[0] * nx * ny * NZ * gx_count * gy_count * grp_count
    factor = 1.0 / math.sqrt(total)
    ranks = gy_count * grp_count
    rows = -(-BLOCKS * C // (8 * ranks)) * 8 * ranks
    lane = 2 * C
    wide = width + 2 * lane
    pairs = NZ // 2

    field, cot, edge, given = call(
        pack, "pack", [(field_in[0], False), (cotangent[0], False)],
        [near((nx, ny, width), BF16), near((nx, ny, width), BF16), near((3, nx, width), BF16), near((3, ny + nx, width), BF16)],
        [pltpu.VMEM((6, nx, width), F32), pltpu.SemaphoreType.DMA((2,))])
    side = swap(given)
    w1, w2 = call(
        load_weights, "load_weights",
        [(first_weight.reshape(27, C, C), False), (second_weight.reshape(27, C, C), False)],
        [near((27, C, C), BF16)] * 2, [pltpu.SemaphoreType.DMA((2,))])
    side, w1, w2 = lax.optimization_barrier((side, w1, w2))
    whole, = call(join_edges, "join_edges", [(edge, True), (side, True)], [near((3, 2 * nx, width), BF16)])
    ends = [(gy_count + j, j + 1) for j in range(gy_count - 1)]
    near_rows = lax.ppermute(whole, ("gx", "gy"), ends + [(b, a) for a, b in ends])
    fs, middle, pre_part, cd, cot_t, w1b, w2b, wfb, grad_early = call(
        functools.partial(interior_first, gx_count), "interior_first",
        [(x, True) for x in (field, cot, side, w1, w2)],
        [
            near((nx + 4, ny + 16, width), F32),
            near((nx + 4, ny, wide), BF16),
            near((nx + 2, ny, width + lane), F32),
            near((3, nx + 2, ny, wide), BF16),
            near((lane, nx * ny * pairs), BF16),
            near((9 * 4 * C, lane), BF16),
            near((9 * 4 * C, lane), BF16),
            near((lane, 9 * 4 * C), BF16),
            near((nx, ny, EARLY * lane), F32),
        ],
        [pltpu.VMEM((3, nx + 4, ny, wide), BF16), pltpu.VMEM((nx + 2, ny + 16, width), F32)],
        flops=4 * 10 ** 9)
    near_rows, pre_part, wfb = lax.optimization_barrier((near_rows, pre_part, wfb))
    far_rows = swap(near_rows)
    grad_late, = call(
        functools.partial(interior_grad, range(EARLY, pairs + 1)), "interior_grad", [(cd, True), (wfb, True)],
        [near((nx, ny, (pairs + 1 - EARLY) * lane), F32)], flops=3 * 10 ** 9)
    far_rows, grad_late = lax.optimization_barrier((far_rows, grad_late))

    hd, keep, send = call(
        functools.partial(layers, factor, gx_count, gy_count), "layers",
        [(x, True) for x in (fs, middle, pre_part, grad_early, grad_late, near_rows, far_rows, w1b, wfb, cot_t)],
        [near((3, nx + 2, ny, width + lane), BF16), near((rows, lane), F32), near((rows, lane), BF16)],
        [
            pltpu.VMEM((2, nx + 2, ny, wide), BF16),
            pltpu.VMEM((nx + 2, ny + 16, width + lane), F32),
            pltpu.VMEM((6, 24, width), F32),
            pltpu.VMEM((2, 32, width), F32),
            pltpu.VMEM((9, 2, 16, wide), BF16),
            pltpu.VMEM((3, 2, 16, wide), BF16),
            pltpu.VMEM((2, 16, width + lane), F32),
            pltpu.VMEM((4, 16, width + lane), F32),
            pltpu.VMEM((nx, ny, width + lane), BF16),
        ],
        limit=32, flops=10 ** 10)

    other = swap(send)
    out, = call(
        output_conv, "output_conv", [(hd, True), (w2b, True)],
        [near((nx, ny, width), BF16)], flops=2 * 10 ** 9)
    other, out = lax.optimization_barrier((other, out))
    both, = call(add_pair, "add_pair", [(keep, True), (other, True)], [near((rows, lane), BF16)])
    terms = lax.all_to_all(both.reshape(ranks, rows // ranks, lane), ("gy", "grp"), 0, 0)
    spread, = call(add_and_repeat, "add_and_repeat", [(terms, True)], [near(terms.shape, BF16)])
    mine = lax.all_to_all(spread, ("gy", "grp"), 0, 0).reshape(rows, lane)
    other = swap(mine)
    first, second = call(
        unpack, "unpack", [(mine, True), (other, True)], [jax.ShapeDtypeStruct((27, C, C), F32)] * 2)
    shape = (3, 3, 3, C, C)
    return out[None], first.reshape(shape), second.reshape(shape)


def solution(mesh):
    return jax.shard_map(
        shards,
        mesh=mesh,
        in_specs=(P("grp", "gx", "gy", None), P(), P(), P("grp", "gx", "gy", None)),
        out_specs=(P("grp", "gx", "gy", None), P(), P()),
        check_vma=False,
    )
```

```python
import functools
import math

import jax
import jax.numpy as jnp
from jax import lax
from jax.experimental import pallas as pl
from jax.experimental.pallas import tpu as pltpu
from jax.sharding import PartitionSpec as P

C = 64
NZ = 16
BF16 = jnp.bfloat16
F32 = jnp.float32
TAPS = [(dx, dy) for dy in range(3) for dx in range(3)]
BLOCKS = 14
EARLY = 3


def swap(array):
    return lax.ppermute(array, "gx", [(0, 1), (1, 0)])


def dot(a, b):
    return jnp.dot(a, b, preferred_element_type=F32)


def dot_nt(a, b):
    return lax.dot_general(a, b, (((1,), (1,)), ((), ())), preferred_element_type=F32)


def band(taps):
    zero = jnp.zeros((C, C), BF16)
    left = jnp.concatenate(list(taps) + [zero], axis=0)
    right = jnp.concatenate([zero] + list(taps), axis=0)
    return jnp.concatenate([left, right], axis=1)


def band_flipped(taps):
    zero = jnp.zeros((C, C), BF16)
    back = list(taps)[::-1]
    upper = jnp.concatenate(back + [zero], axis=1)
    lower = jnp.concatenate([zero] + back, axis=1)
    return jnp.concatenate([upper, lower], axis=0)


def weight_gradient(rows_t, taps_of, total):
    result = []
    for dx, dy in TAPS:
        full = dot(rows_t, taps_of(dx, dy)) * total
        result.append(full[0:C, 0:3 * C] + full[C:2 * C, C:4 * C])
    return result


def packed(pieces):
    blocks = [piece[:, 0:2 * C] for piece in pieces]
    for pair in range(0, 9, 2):
        second = pieces[pair + 1][:, 2 * C:3 * C] if pair + 1 < 9 else jnp.zeros((C, C), F32)
        blocks.append(jnp.concatenate([pieces[pair][:, 2 * C:3 * C], second], axis=1))
    return blocks


def pack(field_hbm, cot_hbm, field, cot, edge, given, rows, sems):
    copies = [
        pltpu.make_async_copy(source, target, sems.at[index])
        for index, (source, target) in enumerate(((field_hbm, field), (cot_hbm, cot)))
    ]
    for copy in copies:
        copy.start()
    for copy in copies:
        copy.wait()
    nx, ny, width = field.shape
    gx = lax.axis_index("gx")
    for x in range(nx):
        fields = field[x].astype(F32)
        cots = cot[x].astype(F32)
        for index, row in enumerate((fields[0:1], fields[1:2], cots[0:1], fields[ny - 2:ny - 1], fields[ny - 1:ny], cots[ny - 1:ny])):
            rows[index, x:x + 1, :] = row
    head = rows[0:3].astype(BF16)
    tail = rows[3:6].astype(BF16)

    @pl.when(gx == 0)
    def _():
        edge[...] = head
        given[:, ny:ny + nx] = tail
        given[0:2, 0:ny] = field[nx - 2:nx]
        given[2:3, 0:ny] = cot[nx - 1:nx]

    @pl.when(gx != 0)
    def _():
        edge[...] = tail
        given[:, ny:ny + nx] = head
        given[0:2, 0:ny] = field[0:2]
        given[2:3, 0:ny] = cot[0:1]


def join_edges(edge, taken, whole):
    nx = edge.shape[1]
    gx = lax.axis_index("gx")

    @pl.when(gx == 0)
    def _():
        whole[:, 0:nx] = edge[...]
        whole[:, nx:2 * nx] = taken[:, taken.shape[1] - nx:]

    @pl.when(gx != 0)
    def _():
        whole[:, 0:nx] = taken[:, taken.shape[1] - nx:]
        whole[:, nx:2 * nx] = edge[...]


def load_weights(w1_hbm, w2_hbm, w1, w2, sems):
    copies = [
        pltpu.make_async_copy(source, target, sems.at[index])
        for index, (source, target) in enumerate(((w1_hbm, w1), (w2_hbm, w2)))
    ]
    for copy in copies:
        copy.start()
    for copy in copies:
        copy.wait()


def make_bands(w1, w2, w1b, w2b, wfb):
    for t, (dx, dy) in enumerate(TAPS):
        rows = slice(t * 4 * C, (t + 1) * 4 * C)
        first = 9 * dx + 3 * dy
        w1b[rows, :] = band([w1[first + z] for z in range(3)])
        w2b[rows, :] = band([w2[first + z] for z in range(3)])
        wfb[:, rows] = band_flipped([w2[24 - first + z] for z in range(3)])


def extend(gx_count, target, own, side):
    gx = lax.axis_index("gx")
    nx, ny, _ = own.shape
    width = side.shape[0]
    target[width:width + nx, 8:8 + ny, :] = own[...].astype(F32)
    halo = side[:, 0:ny].astype(F32)
    target[0:width, 8:8 + ny, :] = halo * (gx > 0).astype(F32)
    target[width + nx:2 * width + nx, 8:8 + ny, :] = halo * (gx < gx_count - 1).astype(F32)


def blank_edges(copies, width):
    lane = 2 * C
    zero = jnp.zeros(copies.shape[:-1] + (lane,), BF16)
    copies[..., 0:lane] = zero
    copies[..., lane + width:] = zero


def fill_copies(scratch, copies):
    depth, _, width = scratch.shape
    ny = copies.shape[2]
    lane = 2 * C
    blank_edges(copies, width)
    zero = jnp.zeros((depth, 1, width), F32)
    scratch[:, 7:8, :] = zero
    scratch[:, 8 + ny:9 + ny, :] = zero
    for dy in range(3):
        copies[dy, :, :, lane:lane + width] = scratch[:, 7 + dy:7 + dy + ny, :].astype(BF16)


def interior_first(gx_count, field, cot, side, w1, w2, fs, middle, partial, cd, cot_t, w1b, w2b, wfb, grad_part, fd, cs):
    nx, ny, width = field.shape
    lane = 2 * C
    depth = nx + 2
    make_bands(w1, w2, w1b, w2b, wfb)
    extend(gx_count, fs, field, side.at[0:2])
    fill_copies(fs, fd)
    middle[...] = fd[1]
    for p in range(NZ // 2 + 1):
        span = slice(lane * p, lane * (p + 2))
        block = jnp.concatenate([fd[dy, dx:dx + depth, :, span].reshape(depth * ny, 2 * lane) for dx, dy in TAPS], axis=1)
        partial[:, :, lane * p:lane * (p + 1)] = dot(block, w1b[...]).reshape(depth, ny, lane)
    extend(gx_count, cs, cot, side.at[2:3])
    fill_copies(cs, cd)
    cells = nx * ny
    for p in range(NZ // 2):
        cot_t[:, cells * p:cells * (p + 1)] = cot[:, :, lane * p:lane * (p + 1)].reshape(cells, lane).T
    interior_grad(range(EARLY), cd, wfb, grad_part)


def interior_grad(pairs, cd, wfb, partial):
    nx, ny, _ = partial.shape
    lane = 2 * C
    for p in pairs:
        span = slice(lane * p, lane * (p + 2))
        block = jnp.concatenate([cd[dy, dx:dx + nx, :, span].reshape(nx * ny, 2 * lane) for dx, dy in TAPS], axis=1)
        here = lane * (p - pairs[0])
        partial[:, :, here:here + lane] = dot_nt(block, wfb[...]).reshape(nx, ny, lane)


def layers(factor, gx_count, gy_count, fs, middle, pre_part, grad_early, grad_late, near_rows, far_rows, w1b, wfb, cot_t,
           hd, pg, fd, send, hs, es, ec, eh, eg, he, cr):
    nx = middle.shape[0] - 4
    ny = middle.shape[1]
    width = fs.shape[2]
    depth = nx + 2
    pairs = NZ // 2
    lane = 2 * C
    wide = width + lane
    cells = nx * ny
    gx = lax.axis_index("gx")
    gy = lax.axis_index("gy")
    low = (gx > 0).astype(F32)
    high = (gx < gx_count - 1).astype(F32)
    prev = (gy > 0).astype(F32)
    after = (gy < gy_count - 1).astype(F32)

    es[...] = jnp.zeros(es.shape, F32)
    ec[...] = jnp.zeros(ec.shape, F32)

    def place(first, last, from_row, to_row):
        span = slice(to_row, to_row + depth)
        for target, index, source in (
            (es, 0, first[0]), (es, 1, first[1]), (ec, 0, first[2]),
            (es, 4, last[0]), (es, 5, last[1]), (ec, 1, last[2]),
        ):
            target[index, span, :] = source.astype(F32)[from_row:from_row + depth]

    @pl.when(gx == 0)
    def _():
        place(near_rows, far_rows, 0, 8)

    @pl.when(gx != 0)
    def _():
        place(far_rows, near_rows, nx - 2, 6)

    for x in range(nx + 4):
        es[2, 6 + x:7 + x, :] = fs[x, 8:9, :]
        es[3, 6 + x:7 + x, :] = fs[x, 7 + ny:8 + ny, :]

    blank_edges(eh, width)
    blank_edges(eg, width)
    for t, (dx, dy) in enumerate(TAPS):
        for end in range(2):
            eh[t, end, :, lane:lane + width] = es[3 * end + dy, 6 + dx:22 + dx, :].astype(BF16)
    for dx in range(3):
        for end in range(2):
            eg[dx, end, :, lane:lane + width] = ec[end, 7 + dx:23 + dx, :].astype(BF16)

    def spans(pick):
        return jnp.concatenate([pick(slice(lane * p, lane * (p + 2))) for p in range(pairs + 1)], axis=0)

    def lanes(rows, count):
        return [rows[count * p:count * (p + 1)] for p in range(pairs + 1)]

    ends = lanes(dot(spans(lambda span: jnp.concatenate(
        [eh[t, :, :, span].reshape(32, 2 * lane) for t in range(9)], axis=1)), w1b[...]), 32)
    taps = (slice(0, 12 * C), slice(24 * C, 36 * C))
    for end in range(2):
        term = lanes(dot(spans(lambda span: jnp.concatenate(
            [eh[3 + dx, end, :, span] for dx in range(3)], axis=1)), w1b[taps[end], :]), 16)
        term_grad = lanes(dot_nt(spans(lambda span: jnp.concatenate(
            [eg[dx, end, :, span] for dx in range(3)], axis=1)), wfb[:, taps[end]]), 16)
        for p in range(pairs + 1):
            cr[end, :, lane * p:lane * (p + 1)] = term[p]
            cr[2 + end, :, lane * p:lane * (p + 1)] = term_grad[p]

    lane_of = lax.broadcasted_iota(jnp.int32, (1, wide), 1)
    inside = ((lane_of >= C) & (lane_of < wide - C)).astype(F32)
    row_of = lax.broadcasted_iota(jnp.int32, (ny, wide), 0)
    is_first = row_of == 0
    is_last = row_of == ny - 1
    end_row = lax.broadcasted_iota(jnp.int32, (16, lane), 0)
    end_x = jnp.where(end_row == 0, low, jnp.where(end_row == depth - 1, high, 1.0))
    for p in range(pairs + 1):
        here = slice(lane * p, lane * (p + 1))
        value = ends[p]
        value = value * jax.nn.sigmoid(value)
        he[0, :, here] = value[0:16] * end_x * prev * inside[:, here]
        he[1, :, here] = value[16:32] * end_x * after * inside[:, here]
    for x in range(depth):
        pre = pre_part[x]
        pre = pre + jnp.where(is_first, cr[0, x:x + 1, :], 0.0) + jnp.where(is_last, cr[1, x:x + 1, :], 0.0)
        sigma = jax.nn.sigmoid(pre)
        if 0 < x < depth - 1:
            grad = jnp.concatenate([grad_early[x - 1], grad_late[x - 1]], axis=1)
            grad = grad + jnp.where(is_first, cr[2, x - 1:x, :], 0.0) + jnp.where(is_last, cr[3, x - 1:x, :], 0.0)
            pg[x - 1] = (grad * sigma * (1.0 + pre * (1.0 - sigma)) * inside).astype(BF16)
        hidden = pre * sigma * inside
        if x == 0:
            hidden = hidden * low
        if x == depth - 1:
            hidden = hidden * high
        hs[x, 8:8 + ny, :] = hidden
        hd[1, x] = hidden.astype(BF16)
        hd[0, x] = jnp.where(is_first, he[0, x:x + 1, :], hs[x, 7:7 + ny, :]).astype(BF16)
        hd[2, x] = jnp.where(is_last, he[1, x:x + 1, :], hs[x, 9:9 + ny, :]).astype(BF16)

    blank_edges(fd, width)
    first_row = is_first[:, 0:width]
    last_row = is_last[:, 0:width]
    for x in range(depth):
        fd[0, x, :, lane:lane + width] = jnp.where(first_row, es[1, 7 + x:8 + x, :], fs[x + 1, 7:7 + ny, :]).astype(BF16)
        fd[1, x, :, lane:lane + width] = jnp.where(last_row, es[4, 7 + x:8 + x, :], fs[x + 1, 9:9 + ny, :]).astype(BF16)

    @pl.when(gx == 0)
    def _():
        store_blocks(send, second_gradient(factor, hd, cot_t))

    @pl.when(gx != 0)
    def _():
        store_blocks(send, first_gradient(factor, middle, fd, pg))


def second_gradient(factor, hd, cot_t):
    nx, ny = hd.shape[1] - 2, hd.shape[2]
    lane = 2 * C

    def hidden_span(dx, dy, p):
        return hd[dy, dx:dx + nx, :, lane * p:lane * (p + 2)].reshape(nx * ny, 2 * lane)

    return packed(weight_gradient(
        cot_t[...],
        lambda dx, dy: jnp.concatenate([hidden_span(dx, dy, p) for p in range(NZ // 2)], axis=0),
        factor))


def first_gradient(factor, middle, fd, pg):
    nx, ny, _ = pg.shape
    cells = nx * ny
    pairs = NZ // 2
    lane = 2 * C

    def field_span(dx, dy, p):
        span = slice(lane * p, lane * (p + 2))
        if dy == 1:
            return middle[dx + 1:dx + 1 + nx, :, span].reshape(cells, 2 * lane)
        return fd[dy // 2, dx:dx + nx, :, span].reshape(cells, 2 * lane)

    grad_t = jnp.concatenate(
        [pg[:, :, lane * p:lane * (p + 1)].reshape(cells, lane).T for p in range(pairs + 1)], axis=1)
    return packed(weight_gradient(
        grad_t,
        lambda dx, dy: jnp.concatenate([field_span(dx, dy, p) for p in range(pairs + 1)], axis=0),
        factor))


def store_blocks(target, blocks):
    for index, block in enumerate(blocks):
        target[index * C:(index + 1) * C, :] = block.astype(target.dtype)
    if target.shape[0] > BLOCKS * C:
        target[BLOCKS * C:, :] = jnp.zeros((target.shape[0] - BLOCKS * C, 2 * C), target.dtype)


def keep_sums(factor, hd, pg, fd, middle, cot_t, w2b, keep, out):
    gx = lax.axis_index("gx")

    @pl.when(gx == 0)
    def _():
        store_blocks(keep, first_gradient(factor, middle, fd, pg))

    @pl.when(gx != 0)
    def _():
        store_blocks(keep, second_gradient(factor, hd, cot_t))

    conv_pairs(range(0, NZ // 4), hd, w2b, out)


def conv_pairs(pairs, hd, w2b, out):
    nx, ny, _ = out.shape
    lane = 2 * C
    for p in pairs:
        block = jnp.concatenate(
            [hd[dy, dx:dx + nx, :, lane * p:lane * (p + 2)].reshape(nx * ny, 2 * lane) for dx, dy in TAPS], axis=1)
        here = lane * (p - pairs[0])
        out[:, :, here:here + lane] = dot(block, w2b[...]).astype(BF16).reshape(nx, ny, lane)


def finish_conv(hd, w2b, half, out, rest, sems):
    done = half.shape[2]
    step = done // 2
    copies = [pltpu.make_async_copy(half, out.at[:, :, 0:done], sems.at[0])]
    copies[0].start()
    for part in range(2):
        piece = rest.at[part]
        first = NZ // 4 + part * NZ // 8
        conv_pairs(range(first, first + NZ // 8), hd, w2b, piece)
        start = done + part * step
        copies.append(pltpu.make_async_copy(piece, out.at[:, :, start:start + step], sems.at[1 + part]))
        copies[-1].start()
    for copy in copies:
        copy.wait()


def add_pair(keep, other, out):
    out[...] = (keep[...] + other[...].astype(F32)).astype(BF16)


def add_and_repeat(terms, out):
    total = terms[0].astype(F32)
    for index in range(1, terms.shape[0]):
        total = total + terms[index].astype(F32)
    total = total.astype(BF16)
    for index in range(out.shape[0]):
        out[index] = total


def unpack(mine, other, first, second):
    gx = lax.axis_index("gx")
    a = mine[...].astype(F32)
    b = other[...].astype(F32)
    for out, rows in ((first, jnp.where(gx == 0, a, b)), (second, jnp.where(gx == 0, b, a))):
        for t, (dx, dy) in enumerate(TAPS):
            turned = rows[t * C:(t + 1) * C].T
            out[9 * dx + 3 * dy] = turned[0:C]
            out[9 * dx + 3 * dy + 1] = turned[C:2 * C]
        for pair in range(5):
            turned = rows[(9 + pair) * C:(10 + pair) * C].T
            for half in range(2 if pair < 4 else 1):
                dx, dy = TAPS[2 * pair + half]
                out[9 * dx + 3 * dy + 2] = turned[half * C:(half + 1) * C]


def near(shape, dtype):
    return pltpu.VMEM(shape, dtype)


def call(body, name, inputs, outs, scratch=(), limit=16, flops=0, far=False):
    placed = [pltpu.with_memory_space_constraint(x, pltpu.VMEM if held else pltpu.HBM) for x, held in inputs]
    size = sum(x.size * x.dtype.itemsize for x, _ in inputs)
    return pl.pallas_call(
        body,
        out_shape=list(outs),
        in_specs=[pl.BlockSpec(memory_space=pltpu.VMEM if held else pl.ANY) for _, held in inputs],
        out_specs=[pl.BlockSpec(memory_space=pl.ANY if far else pltpu.VMEM)] * len(outs),
        scratch_shapes=list(scratch),
        compiler_params=pltpu.CompilerParams(vmem_limit_bytes=limit * 1024 * 1024),
        cost_estimate=pl.CostEstimate(flops=flops, bytes_accessed=size, transcendentals=0),
        name=name,
    )(*placed)


def shards(field_in, first_weight, second_weight, cotangent):
    nx, ny, width = field_in.shape[1:]
    gx_count, gy_count, grp_count = (lax.axis_size(axis) for axis in ("gx", "gy", "grp"))
    total = field_in.shape[0] * nx * ny * NZ * gx_count * gy_count * grp_count
    factor = 1.0 / math.sqrt(total)
    ranks = gy_count * grp_count
    rows = -(-BLOCKS * C // (8 * ranks)) * 8 * ranks
    lane = 2 * C
    wide = width + 2 * lane
    pairs = NZ // 2

    field, cot, edge, given = call(
        pack, "pack", [(field_in[0], False), (cotangent[0], False)],
        [near((nx, ny, width), BF16), near((nx, ny, width), BF16), near((3, nx, width), BF16), near((3, ny + nx, width), BF16)],
        [pltpu.VMEM((6, nx, width), F32), pltpu.SemaphoreType.DMA((2,))])
    side = swap(given)
    w1, w2 = call(
        load_weights, "load_weights",
        [(first_weight.reshape(27, C, C), False), (second_weight.reshape(27, C, C), False)],
        [near((27, C, C), BF16)] * 2, [pltpu.SemaphoreType.DMA((2,))])
    side, w1, w2 = lax.optimization_barrier((side, w1, w2))
    whole, = call(join_edges, "join_edges", [(edge, True), (side, True)], [near((3, 2 * nx, width), BF16)])
    ends = [(gy_count + j, j + 1) for j in range(gy_count - 1)]
    near_rows = lax.ppermute(whole, ("gx", "gy"), ends + [(b, a) for a, b in ends])
    fs, middle, pre_part, cd, cot_t, w1b, w2b, wfb, grad_early = call(
        functools.partial(interior_first, gx_count), "interior_first",
        [(x, True) for x in (field, cot, side, w1, w2)],
        [
            near((nx + 4, ny + 16, width), F32),
            near((nx + 4, ny, wide), BF16),
            near((nx + 2, ny, width + lane), F32),
            near((3, nx + 2, ny, wide), BF16),
            near((lane, nx * ny * pairs), BF16),
            near((9 * 4 * C, lane), BF16),
            near((9 * 4 * C, lane), BF16),
            near((lane, 9 * 4 * C), BF16),
            near((nx, ny, EARLY * lane), F32),
        ],
        [pltpu.VMEM((3, nx + 4, ny, wide), BF16), pltpu.VMEM((nx + 2, ny + 16, width), F32)],
        flops=4 * 10 ** 9)
    near_rows, pre_part, wfb = lax.optimization_barrier((near_rows, pre_part, wfb))
    far_rows = swap(near_rows)
    grad_late, = call(
        functools.partial(interior_grad, range(EARLY, pairs + 1)), "interior_grad", [(cd, True), (wfb, True)],
        [near((nx, ny, (pairs + 1 - EARLY) * lane), F32)], flops=3 * 10 ** 9)
    far_rows, grad_late = lax.optimization_barrier((far_rows, grad_late))

    hd, pg, fd, send = call(
        functools.partial(layers, factor, gx_count, gy_count), "layers",
        [(x, True) for x in (fs, middle, pre_part, grad_early, grad_late, near_rows, far_rows, w1b, wfb, cot_t)],
        [
            near((3, nx + 2, ny, width + lane), BF16),
            near((nx, ny, width + lane), BF16),
            near((2, nx + 2, ny, wide), BF16),
            near((rows, lane), BF16),
        ],
        [
            pltpu.VMEM((nx + 2, ny + 16, width + lane), F32),
            pltpu.VMEM((6, 24, width), F32),
            pltpu.VMEM((2, 32, width), F32),
            pltpu.VMEM((9, 2, 16, wide), BF16),
            pltpu.VMEM((3, 2, 16, wide), BF16),
            pltpu.VMEM((2, 16, width + lane), F32),
            pltpu.VMEM((4, 16, width + lane), F32),
        ],
        limit=32, flops=10 ** 10)

    other = swap(send)
    keep, half = call(
        functools.partial(keep_sums, factor), "keep_sums",
        [(x, True) for x in (hd, pg, fd, middle, cot_t, w2b)],
        [near((rows, lane), F32), near((nx, ny, width // 2), BF16)], flops=5 * 10 ** 9)
    other, keep, half = lax.optimization_barrier((other, keep, half))
    both, = call(add_pair, "add_pair", [(keep, True), (other, True)], [near((rows, lane), BF16)])
    terms = lax.all_to_all(both.reshape(ranks, rows // ranks, lane), ("gy", "grp"), 0, 0)
    spread, = call(add_and_repeat, "add_and_repeat", [(terms, True)], [near(terms.shape, BF16)])
    mine = lax.all_to_all(spread, ("gy", "grp"), 0, 0).reshape(rows, lane)
    mine, hd, w2b, half = lax.optimization_barrier((mine, hd, w2b, half))
    other = swap(mine)
    out, = call(
        finish_conv, "finish_conv", [(hd, True), (w2b, True), (half, True)],
        [pltpu.HBM((nx, ny, width), BF16)],
        [pltpu.VMEM((2, nx, ny, width // 4), BF16), pltpu.SemaphoreType.DMA((3,))], flops=2 * 10 ** 9, far=True)
    other, out = lax.optimization_barrier((other, out))
    first, second = call(
        unpack, "unpack", [(mine, True), (other, True)], [jax.ShapeDtypeStruct((27, C, C), F32)] * 2)
    shape = (3, 3, 3, C, C)
    return out[None], first.reshape(shape), second.reshape(shape)


def solution(mesh):
    return jax.shard_map(
        shards,
        mesh=mesh,
        in_specs=(P("grp", "gx", "gy", None), P(), P(), P("grp", "gx", "gy", None)),
        out_specs=(P("grp", "gx", "gy", None), P(), P()),
        check_vma=False,
    )
```

```python
import functools
import math

import jax
import jax.numpy as jnp
from jax import lax
from jax.experimental import pallas as pl
from jax.experimental.pallas import tpu as pltpu
from jax.sharding import PartitionSpec as P

C = 64
NZ = 16
BF16 = jnp.bfloat16
F32 = jnp.float32
TAPS = [(dx, dy) for dy in range(3) for dx in range(3)]
BLOCKS = 14


def swap(array):
    return lax.ppermute(array, "gx", [(0, 1), (1, 0)])


def dot(a, b):
    return jnp.dot(a, b, preferred_element_type=F32)


def dot_nt(a, b):
    return lax.dot_general(a, b, (((1,), (1,)), ((), ())), preferred_element_type=F32)


def band(taps):
    zero = jnp.zeros((C, C), BF16)
    left = jnp.concatenate(list(taps) + [zero], axis=0)
    right = jnp.concatenate([zero] + list(taps), axis=0)
    return jnp.concatenate([left, right], axis=1)


def band_flipped(taps):
    zero = jnp.zeros((C, C), BF16)
    back = list(taps)[::-1]
    upper = jnp.concatenate(back + [zero], axis=1)
    lower = jnp.concatenate([zero] + back, axis=1)
    return jnp.concatenate([upper, lower], axis=0)


def packed(pieces):
    blocks = [piece[:, 0:2 * C] for piece in pieces]
    for pair in range(0, 9, 2):
        second = pieces[pair + 1][:, 2 * C:3 * C] if pair + 1 < 9 else jnp.zeros((C, C), F32)
        blocks.append(jnp.concatenate([pieces[pair][:, 2 * C:3 * C], second], axis=1))
    return blocks


def pack_edges(field_hbm, cot_hbm, field, cot, edge, given, rows, sems):
    copies = [
        pltpu.make_async_copy(source, target, sems.at[index])
        for index, (source, target) in enumerate(((field_hbm, field), (cot_hbm, cot)))
    ]
    for copy in copies:
        copy.start()
    for copy in copies:
        copy.wait()
    nx, ny, _ = field.shape
    gx = lax.axis_index("gx")
    for x in range(nx):
        fields = field[x].astype(F32)
        cots = cot[x].astype(F32)
        for index, row in enumerate((fields[0:1], fields[1:2], cots[0:1], fields[ny - 2:ny - 1], fields[ny - 1:ny], cots[ny - 1:ny])):
            rows[index, x:x + 1, :] = row
    head = rows[0:3].astype(BF16)
    tail = rows[3:6].astype(BF16)
    edge[...] = jnp.where(gx == 0, head, tail)
    given[...] = jnp.where(gx == 0, tail, head)


def join_edges(edge, taken, whole):
    nx = edge.shape[1]
    gx = lax.axis_index("gx")

    @pl.when(gx == 0)
    def _():
        whole[:, 0:nx] = edge[...]
        whole[:, nx:2 * nx] = taken[...]

    @pl.when(gx != 0)
    def _():
        whole[:, 0:nx] = taken[...]
        whole[:, nx:2 * nx] = edge[...]


def put_rows(scratch, start, rows):
    lane = 2 * C
    for tile in range(scratch.shape[0]):
        scratch[tile, start:start + rows.shape[0], :] = rows[:, lane * tile:lane * (tile + 1)]


def take_rows(scratch, start, count, stride):
    return jnp.concatenate(
        [scratch[tile, pl.ds(start, count, stride=stride), :] for tile in range(scratch.shape[0])], axis=1).astype(BF16)


def turn_rows(source, scratch):
    nx, ny, _ = source.shape
    for x in range(nx):
        put_rows(scratch, x * ny, source[x].astype(F32))
    return [take_rows(scratch, y, nx, ny) for y in range(ny)]


def pack_halves(field, cot, w1_hbm, w2_hbm, own, bulk, w1, w2, turned_f, turned_c, scratch, sems):
    copies = [
        pltpu.make_async_copy(source, target, sems.at[index])
        for index, (source, target) in enumerate(((w1_hbm, w1), (w2_hbm, w2)))
    ]
    for copy in copies:
        copy.start()
    ny = field.shape[1]
    half = ny // 2
    for source, target in ((field, turned_f), (cot, turned_c)):
        for y, rows in enumerate(turn_rows(source, scratch)):
            target[y] = rows
    low_f, high_f = turned_f.at[0:half + 2], turned_f.at[half - 2:ny]
    low_c, high_c = turned_c.at[0:half + 1], turned_c.at[half - 1:ny]
    gx = lax.axis_index("gx")

    def place(mine_f, mine_c, given_f, given_c):
        own[0:half + 2] = mine_f[...]
        own[half + 2:] = mine_c[...]
        bulk[0:half + 2] = given_f[...]
        bulk[half + 2:] = given_c[...]

    @pl.when(gx == 0)
    def _():
        place(low_f, low_c, high_f, high_c)

    @pl.when(gx != 0)
    def _():
        place(high_f, high_c, low_f, low_c)

    for copy in copies:
        copy.wait()


def make_bands(w1, w2, w1b, w2b, wfb):
    for t, (dx, dy) in enumerate(TAPS):
        rows = slice(t * 4 * C, (t + 1) * 4 * C)
        first = 9 * dx + 3 * dy
        w1b[rows, :] = band([w1[first + z] for z in range(3)])
        w2b[rows, :] = band([w2[first + z] for z in range(3)])
        wfb[:, rows] = band_flipped([w2[24 - first + z] for z in range(3)])


def blank_edges(copies):
    lane = 2 * C
    zero = jnp.zeros(copies.shape[:-1] + (lane,), BF16)
    copies[..., 0:lane] = zero
    copies[..., copies.shape[-1] - lane:] = zero


def blank_rows(scratch):
    zero = jnp.zeros((scratch.shape[0], 1, scratch.shape[2]), F32)
    scratch[:, 7:8, :] = zero
    scratch[:, scratch.shape[1] - 8:scratch.shape[1] - 7, :] = zero


def shift_rows(scratch, copies, start, first_lane):
    count, rows, width = scratch.shape
    for dx in range(3):
        copies[dx, pl.ds(start, count), :, first_lane:first_lane + width] = scratch[:, 7 + dx:rows - 9 + dx, :].astype(BF16)


def inside_lanes(p):
    lane_of = lax.broadcasted_iota(jnp.int32, (1, 2 * C), 1)
    if p == 0:
        return (lane_of >= C).astype(F32)
    if p == NZ // 2:
        return (lane_of < C).astype(F32)
    return 1.0


def windows(copies, first, count, p):
    lane = 2 * C
    rows = copies.shape[2]
    return jnp.concatenate(
        [
            copies[dx, pl.ds(first + dy, count), :, lane * p:lane * (p + 2)].reshape(count * rows, 2 * lane)
            for dx, dy in TAPS
        ],
        axis=1,
    )


def pre_gradient(grad, pre, p):
    sigma = jax.nn.sigmoid(pre)
    return grad * sigma * (1.0 + pre * (1.0 - sigma)) * inside_lanes(p)


def interior(own, got, w1, w2, fd, cd, hd, pg, acc1, acc2, w1b, w2b, wfb, fs, cs, hs, pre):
    gx = lax.axis_index("gx")
    nx = own.shape[1]
    across = 2 * nx
    count = pg.shape[0]
    cells = count * across
    lane = 2 * C
    pairs = NZ // 2
    make_bands(w1, w2, w1b, w2b, wfb)

    def place(left, right):
        for scratch, start, size in ((fs, 0, count + 2), (cs, count + 2, count + 1)):
            scratch[:, 8:8 + nx, :] = left[start:start + size].astype(F32)
            scratch[:, 8 + nx:8 + across, :] = right[start:start + size].astype(F32)

    @pl.when(gx == 0)
    def _():
        place(own, got)

    @pl.when(gx != 0)
    def _():
        place(got, own)

    for scratch in (fs, cs, hs):
        blank_rows(scratch)
    blank_edges(fd)
    blank_edges(cd)
    shift_rows(fs, fd, 2 - 2 * gx, lane)
    shift_rows(cs, cd, 1 - gx, lane)
    for p in range(pairs + 1):
        here = slice(lane * p, lane * (p + 1))
        value = dot(windows(fd, 2 - 2 * gx, count, p), w1b[...])
        pre[:, :, here] = value.reshape(count, across, lane)
        hidden = value * jax.nn.sigmoid(value) * inside_lanes(p)
        hs[:, 8:8 + across, here] = hidden.reshape(count, across, lane)
    hd[:, pl.ds(8 * gx, 2)] = jnp.zeros((3, 2) + hd.shape[2:], BF16)
    shift_rows(hs, hd, 2 - 2 * gx, 0)
    for p in range(pairs + 1):
        here = slice(lane * p, lane * (p + 1))
        grad = dot_nt(windows(cd, 1 - gx, count - 1, p), wfb[...])
        grad = pre_gradient(grad, pre[pl.ds(gx, count - 1), :, here].reshape((count - 1) * across, lane), p)
        pg[pl.ds(1 - gx, count - 1), :, here] = grad.astype(BF16).reshape(count - 1, across, lane)
    pg[pl.ds((count - 1) * gx, 1)] = jnp.zeros((1,) + pg.shape[1:], BF16)

    cot_t = jnp.concatenate(
        [cd[1, 1:1 + count, :, lane * (p + 1):lane * (p + 2)].reshape(cells, lane).T for p in range(pairs)], axis=1)
    grad_t = jnp.concatenate(
        [pg[:, :, lane * p:lane * (p + 1)].reshape(cells, lane).T for p in range(pairs + 1)], axis=1)
    for t, (dx, dy) in enumerate(TAPS):
        acc2[t] = dot(cot_t, jnp.concatenate(
            [hd[dx, dy:dy + count, :, lane * p:lane * (p + 2)].reshape(cells, 2 * lane) for p in range(pairs)], axis=0))
        acc1[t] = dot(grad_t, jnp.concatenate(
            [fd[dx, 1 + dy:1 + dy + count, :, lane * p:lane * (p + 2)].reshape(cells, 2 * lane) for p in range(pairs + 1)], axis=0))


def folded(total, factor):
    total = total * factor
    return total[0:C, 0:3 * C] + total[C:2 * C, C:4 * C]


def second_sums(factor, side, hd, cd, acc2):
    lane = 2 * C
    pairs = NZ // 2
    last = hd.shape[1] - 3
    late = ((0, 1), (0,), ()) if side == 0 else ((), (last,), (last - 1, last))
    pieces = []
    for t, (dx, dy) in enumerate(TAPS):
        total = acc2[t]
        if late[dy]:
            cots = jnp.concatenate(
                [cd[1, 1 + y, :, lane * (p + 1):lane * (p + 2)] for y in late[dy] for p in range(pairs)], axis=0)
            rows = jnp.concatenate(
                [hd[dx, y + dy, :, lane * p:lane * (p + 2)] for y in late[dy] for p in range(pairs)], axis=0)
            total = total + dot(cots.T, rows)
        pieces.append(folded(total, factor))
    return packed(pieces)


def first_sums(factor, side, fd, pg, acc1):
    lane = 2 * C
    pairs = NZ // 2
    count, across, _ = pg.shape
    y = 0 if side == 0 else count - 1
    extra = 2 * lane - (pairs + 1) * across
    grad_t = jnp.concatenate(
        [pg[y, :, lane * p:lane * (p + 1)] for p in range(pairs + 1)] + [jnp.zeros((extra, lane), BF16)], axis=0).T
    pad = jnp.zeros((extra, 2 * lane), BF16)
    return packed([
        folded(acc1[t] + dot(grad_t, jnp.concatenate(
            [fd[dx, y + dy + 1, :, lane * p:lane * (p + 2)] for p in range(pairs + 1)] + [pad], axis=0)), factor)
        for t, (dx, dy) in enumerate(TAPS)
    ])


def store_blocks(target, blocks):
    for index, block in enumerate(blocks):
        target[index * C:(index + 1) * C, :] = block.astype(target.dtype)
    if target.shape[0] > BLOCKS * C:
        target[BLOCKS * C:, :] = jnp.zeros((target.shape[0] - BLOCKS * C, 2 * C), target.dtype)


def late_rows(factor, gy_count, fd_in, cd_in, hd_in, pg_in, rows, acc1, acc2, w1b, wfb, fd, cd, hd, pg, send, rs, hs):
    gx = lax.axis_index("gx")
    gy = lax.axis_index("gy")
    count, across, _ = pg.shape
    lane = 2 * C
    pairs = NZ // 2
    rs[:, 8:8 + across, :] = rows[...].astype(F32)
    blank_rows(rs)
    blank_rows(hs)
    shift_rows(rs.at[0:2], fd, (count + 2) * gx, lane)
    shift_rows(rs.at[2:3], cd, (count + 1) * gx, lane)
    value = dot(jnp.concatenate([windows(fd, count * gx, 2, p) for p in range(pairs + 1)], axis=0), w1b[...])
    grad = dot_nt(jnp.concatenate([windows(cd, (count - 1) * gx, 1, p) for p in range(pairs + 1)], axis=0), wfb[...])
    before = jnp.where((gx == 0) & (gy == 0), 0.0, 1.0)
    beyond = jnp.where((gx != 0) & (gy == gy_count - 1), 0.0, 1.0)
    for p in range(pairs + 1):
        here = slice(lane * p, lane * (p + 1))
        early = value[2 * across * p:2 * across * p + across]
        later = value[2 * across * p + across:2 * across * (p + 1)]
        hs[0, 8:8 + across, here] = early * jax.nn.sigmoid(early) * inside_lanes(p) * before
        hs[1, 8:8 + across, here] = later * jax.nn.sigmoid(later) * inside_lanes(p) * beyond
        mine = pre_gradient(grad[across * p:across * (p + 1)], jnp.where(gx == 0, later, early), p)
        pg[pl.ds((count - 1) * gx, 1), :, here] = mine.astype(BF16)[None]
    shift_rows(hs, hd, count * gx, 0)

    @pl.when(gx == 0)
    def _():
        store_blocks(send, second_sums(factor, 0, hd, cd, acc2))

    @pl.when(gx != 0)
    def _():
        store_blocks(send, first_sums(factor, 1, fd, pg, acc1))


def keep_sums(factor, fd, cd, hd, pg, acc1, acc2, w2b, keep, mine, given):
    gx = lax.axis_index("gx")
    count, across, _ = pg.shape
    lane = 2 * C
    half = across // 2

    @pl.when(gx == 0)
    def _():
        store_blocks(keep, first_sums(factor, 0, fd, pg, acc1))

    @pl.when(gx != 0)
    def _():
        store_blocks(keep, second_sums(factor, 1, hd, cd, acc2))

    for p in range(NZ // 2):
        here = slice(lane * p, lane * (p + 1))
        value = dot(windows(hd, 0, count, p), w2b[...]).reshape(count, across, lane)
        left, right = value[:, 0:half], value[:, half:across]
        mine[:, :, here] = jnp.where(gx == 0, left, right).astype(BF16)
        given[:, :, here] = jnp.where(gx == 0, right, left).astype(BF16)


def finish_output(mine, other, out, turned, scratch, sems):
    count, nx, width = mine.shape
    gx = lax.axis_index("gx")
    for y in range(count):
        a = mine[y].astype(F32)
        b = other[y].astype(F32)
        put_rows(scratch, y * nx, jnp.where(gx == 0, a, b))
        put_rows(scratch, (count + y) * nx, jnp.where(gx == 0, b, a))
    copies = []
    for x in range(nx):
        turned[x] = take_rows(scratch, x, 2 * count, nx)
        if x % 2:
            copies.append(pltpu.make_async_copy(turned.at[x - 1:x + 1], out.at[x - 1:x + 1], sems.at[x // 2]))
            copies[-1].start()
    for copy in copies:
        copy.wait()


def add_pair(keep, other, out):
    out[...] = (keep[...] + other[...].astype(F32)).astype(BF16)


def add_and_repeat(terms, out):
    total = terms[0].astype(F32)
    for index in range(1, terms.shape[0]):
        total = total + terms[index].astype(F32)
    total = total.astype(BF16)
    for index in range(out.shape[0]):
        out[index] = total


def unpack(mine, other, first, second):
    gx = lax.axis_index("gx")
    a = mine[...].astype(F32)
    b = other[...].astype(F32)
    for out, rows in ((first, jnp.where(gx == 0, a, b)), (second, jnp.where(gx == 0, b, a))):
        for t, (dx, dy) in enumerate(TAPS):
            turned = rows[t * C:(t + 1) * C].T
            out[9 * dx + 3 * dy] = turned[0:C]
            out[9 * dx + 3 * dy + 1] = turned[C:2 * C]
        for pair in range(5):
            turned = rows[(9 + pair) * C:(10 + pair) * C].T
            for half in range(2 if pair < 4 else 1):
                dx, dy = TAPS[2 * pair + half]
                out[9 * dx + 3 * dy + 2] = turned[half * C:(half + 1) * C]


def near(shape, dtype):
    return pltpu.VMEM(shape, dtype)


def call(body, name, inputs, outs, scratch=(), limit=16, flops=0, far=False, aliases=None):
    placed = [pltpu.with_memory_space_constraint(x, pltpu.VMEM if held else pltpu.HBM) for x, held in inputs]
    size = sum(x.size * x.dtype.itemsize for x, _ in inputs)
    return pl.pallas_call(
        body,
        out_shape=list(outs),
        in_specs=[pl.BlockSpec(memory_space=pltpu.VMEM if held else pl.ANY) for _, held in inputs],
        out_specs=[pl.BlockSpec(memory_space=pl.ANY if far else pltpu.VMEM)] * len(outs),
        scratch_shapes=list(scratch),
        input_output_aliases=aliases or {},
        compiler_params=pltpu.CompilerParams(vmem_limit_bytes=limit * 1024 * 1024),
        cost_estimate=pl.CostEstimate(flops=flops, bytes_accessed=size, transcendentals=0),
        name=name,
    )(*placed)


def shards(field_in, first_weight, second_weight, cotangent):
    nx, ny, width = field_in.shape[1:]
    gx_count, gy_count, grp_count = (lax.axis_size(axis) for axis in ("gx", "gy", "grp"))
    total = field_in.shape[0] * nx * ny * NZ * gx_count * gy_count * grp_count
    factor = 1.0 / math.sqrt(total)
    ranks = gy_count * grp_count
    rows = -(-BLOCKS * C // (8 * ranks)) * 8 * ranks
    lane = 2 * C
    wide = width + 2 * lane
    count = ny // 2
    across = 2 * nx
    size = 2 * count + 3

    field, cot, edge, given = call(
        pack_edges, "pack_edges", [(field_in[0], False), (cotangent[0], False)],
        [near((nx, ny, width), BF16), near((nx, ny, width), BF16), near((3, nx, width), BF16), near((3, nx, width), BF16)],
        [pltpu.VMEM((6, nx, width), F32), pltpu.SemaphoreType.DMA((2,))])
    taken = swap(given)
    own, bulk, w1, w2 = call(
        pack_halves, "pack_halves",
        [(field, True), (cot, True), (first_weight.reshape(27, C, C), False), (second_weight.reshape(27, C, C), False)],
        [near((size, nx, width), BF16), near((size, nx, width), BF16), near((27, C, C), BF16), near((27, C, C), BF16)],
        [
            pltpu.VMEM((ny, nx, width), BF16),
            pltpu.VMEM((ny, nx, width), BF16),
            pltpu.VMEM((width // lane, nx * ny, lane), F32),
            pltpu.SemaphoreType.DMA((2,)),
        ])
    bulk, taken, w1, w2 = lax.optimization_barrier((bulk, taken, w1, w2))
    got = swap(bulk)
    whole, = call(join_edges, "join_edges", [(edge, True), (taken, True)], [near((3, across, width), BF16)])
    ends = [(gy_count + j, j + 1) for j in range(gy_count - 1)]
    late = lax.ppermute(whole, ("gx", "gy"), ends + [(b, a) for a, b in ends])
    held = [
        near((3, count + 4, across, wide), BF16),
        near((3, count + 2, across, wide), BF16),
        near((3, count + 2, across, width + lane), BF16),
        near((count, across, width + lane), BF16),
    ]
    fd, cd, hd, pg, acc1, acc2, w1b, w2b, wfb = call(
        interior, "interior",
        [(x, True) for x in (own, got, w1, w2)],
        held + [
            near((9, lane, 2 * lane), F32),
            near((9, lane, 2 * lane), F32),
            near((9 * 4 * C, lane), BF16),
            near((9 * 4 * C, lane), BF16),
            near((lane, 9 * 4 * C), BF16),
        ],
        [
            pltpu.VMEM((count + 2, across + 16, width), F32),
            pltpu.VMEM((count + 1, across + 16, width), F32),
            pltpu.VMEM((count, across + 16, width + lane), F32),
            pltpu.VMEM((count, across, width + lane), F32),
        ],
        limit=32, flops=4 * 10 ** 9)
    fd, cd, hd, pg, send = call(
        functools.partial(late_rows, factor, gy_count), "late_rows",
        [(x, True) for x in (fd, cd, hd, pg, late, acc1, acc2, w1b, wfb)],
        held + [near((rows, lane), BF16)],
        [pltpu.VMEM((3, across + 16, width), F32), pltpu.VMEM((2, across + 16, width + lane), F32)],
        limit=32, flops=10 ** 9, aliases={0: 0, 1: 1, 2: 2, 3: 3})

    other = swap(send)
    keep, mine, given = call(
        functools.partial(keep_sums, factor), "keep_sums",
        [(x, True) for x in (fd, cd, hd, pg, acc1, acc2, w2b)],
        [near((rows, lane), F32), near((count, nx, width), BF16), near((count, nx, width), BF16)], flops=4 * 10 ** 9)
    other, keep = lax.optimization_barrier((other, keep))
    both, = call(add_pair, "add_pair", [(keep, True), (other, True)], [near((rows, lane), BF16)])
    given_out = swap(given)
    terms = lax.all_to_all(both.reshape(ranks, rows // ranks, lane), ("gy", "grp"), 0, 0)
    spread, = call(add_and_repeat, "add_and_repeat", [(terms, True)], [near(terms.shape, BF16)])
    sums = lax.all_to_all(spread, ("gy", "grp"), 0, 0).reshape(rows, lane)
    sums, mine, given_out = lax.optimization_barrier((sums, mine, given_out))
    other = swap(sums)
    out, = call(
        finish_output, "finish_output", [(mine, True), (given_out, True)],
        [pltpu.HBM((nx, ny, width), BF16)],
        [pltpu.VMEM((nx, ny, width), BF16), pltpu.VMEM((width // lane, nx * ny, lane), F32), pltpu.SemaphoreType.DMA((nx // 2,))], far=True)
    other, out = lax.optimization_barrier((other, out))
    first, second = call(
        unpack, "unpack", [(sums, True), (other, True)], [jax.ShapeDtypeStruct((27, C, C), F32)] * 2)
    shape = (3, 3, 3, C, C)
    return out[None], first.reshape(shape), second.reshape(shape)


def solution(mesh):
    return jax.shard_map(
        shards,
        mesh=mesh,
        in_specs=(P("grp", "gx", "gy", None), P(), P(), P("grp", "gx", "gy", None)),
        out_specs=(P("grp", "gx", "gy", None), P(), P()),
        check_vma=False,
    )
```

```python
import functools
import math

import jax
import jax.numpy as jnp
from jax import lax
from jax.experimental import pallas as pl
from jax.experimental.pallas import tpu as pltpu
from jax.sharding import PartitionSpec as P

C = 64
NZ = 16
BF16 = jnp.bfloat16
F32 = jnp.float32
TAPS = [(dx, dy) for dy in range(3) for dx in range(3)]
BLOCKS = 14


def swap(array):
    return lax.ppermute(array, "gx", [(0, 1), (1, 0)])


def dot(a, b):
    return jnp.dot(a, b, preferred_element_type=F32)


def dot_nt(a, b):
    return lax.dot_general(a, b, (((1,), (1,)), ((), ())), preferred_element_type=F32)


def band(taps):
    zero = jnp.zeros((C, C), BF16)
    left = jnp.concatenate(list(taps) + [zero], axis=0)
    right = jnp.concatenate([zero] + list(taps), axis=0)
    return jnp.concatenate([left, right], axis=1)


def band_flipped(taps):
    zero = jnp.zeros((C, C), BF16)
    back = list(taps)[::-1]
    upper = jnp.concatenate(back + [zero], axis=1)
    lower = jnp.concatenate([zero] + back, axis=1)
    return jnp.concatenate([upper, lower], axis=0)


def packed(pieces):
    blocks = [piece[:, 0:2 * C] for piece in pieces]
    for pair in range(0, 9, 2):
        second = pieces[pair + 1][:, 2 * C:3 * C] if pair + 1 < 9 else jnp.zeros((C, C), F32)
        blocks.append(jnp.concatenate([pieces[pair][:, 2 * C:3 * C], second], axis=1))
    return blocks


def pack_edges(field_hbm, cot_hbm, w1_hbm, w2_hbm, field, cot, edge, given, w1, w2, rows, sems):
    copies = [
        pltpu.make_async_copy(source, target, sems.at[index])
        for index, (source, target) in enumerate(((field_hbm, field), (cot_hbm, cot), (w1_hbm, w1), (w2_hbm, w2)))
    ]
    for copy in copies:
        copy.start()
    for copy in copies[:2]:
        copy.wait()
    nx, ny, _ = field.shape
    gx = lax.axis_index("gx")
    for x in range(nx):
        fields = field[x].astype(F32)
        cots = cot[x].astype(F32)
        for index, row in enumerate((fields[0:1], fields[1:2], cots[0:1], fields[ny - 2:ny - 1], fields[ny - 1:ny], cots[ny - 1:ny])):
            rows[index, x:x + 1, :] = row
    head = rows[0:3].astype(BF16)
    tail = rows[3:6].astype(BF16)
    edge[...] = jnp.where(gx == 0, head, tail)
    given[...] = jnp.where(gx == 0, tail, head)
    for copy in copies[2:]:
        copy.wait()


def join_edges(edge, taken, whole):
    nx = edge.shape[1]
    gx = lax.axis_index("gx")

    @pl.when(gx == 0)
    def _():
        whole[:, 0:nx] = edge[...]
        whole[:, nx:2 * nx] = taken[...]

    @pl.when(gx != 0)
    def _():
        whole[:, 0:nx] = taken[...]
        whole[:, nx:2 * nx] = edge[...]


def put_rows(scratch, start, rows):
    lane = 2 * C
    for tile in range(scratch.shape[0]):
        scratch[tile, start:start + rows.shape[0], :] = rows[:, lane * tile:lane * (tile + 1)]


def take_rows(scratch, start, count, stride):
    return jnp.concatenate(
        [scratch[tile, pl.ds(start, count, stride=stride), :] for tile in range(scratch.shape[0])], axis=1).astype(BF16)


def turn_rows(source, scratch):
    nx, ny, _ = source.shape
    for x in range(nx):
        put_rows(scratch, x * ny, source[x].astype(F32))
    return [take_rows(scratch, y, nx, ny) for y in range(ny)]


def pack_halves(field, cot, w1, w2, own, bulk, w1b, w2b, wfb, turned_f, turned_c, scratch):
    ny = field.shape[1]
    half = ny // 2
    for source, target in ((field, turned_f), (cot, turned_c)):
        for y, rows in enumerate(turn_rows(source, scratch)):
            target[y] = rows
    low_f, high_f = turned_f.at[0:half + 2], turned_f.at[half - 2:ny]
    low_c, high_c = turned_c.at[0:half + 1], turned_c.at[half - 1:ny]
    gx = lax.axis_index("gx")

    def place(mine_f, mine_c, given_f, given_c):
        own[0:half + 2] = mine_f[...]
        own[half + 2:] = mine_c[...]
        bulk[0:half + 2] = given_f[...]
        bulk[half + 2:] = given_c[...]

    @pl.when(gx == 0)
    def _():
        place(low_f, low_c, high_f, high_c)

    @pl.when(gx != 0)
    def _():
        place(high_f, high_c, low_f, low_c)

    make_bands(w1, w2, w1b, w2b, wfb)


def make_bands(w1, w2, w1b, w2b, wfb):
    for t, (dx, dy) in enumerate(TAPS):
        rows = slice(t * 4 * C, (t + 1) * 4 * C)
        first = 9 * dx + 3 * dy
        w1b[rows, :] = band([w1[first + z] for z in range(3)])
        w2b[rows, :] = band([w2[first + z] for z in range(3)])
        wfb[:, rows] = band_flipped([w2[24 - first + z] for z in range(3)])


def blank_edges(copies):
    lane = 2 * C
    zero = jnp.zeros(copies.shape[:-1] + (lane,), BF16)
    copies[..., 0:lane] = zero
    copies[..., copies.shape[-1] - lane:] = zero


def blank_rows(scratch):
    zero = jnp.zeros((scratch.shape[0], 1, scratch.shape[2]), F32)
    scratch[:, 7:8, :] = zero
    scratch[:, scratch.shape[1] - 8:scratch.shape[1] - 7, :] = zero


def shift_rows(scratch, copies, start, first_lane):
    count, rows, width = scratch.shape
    for dx in range(3):
        copies[dx, pl.ds(start, count), :, first_lane:first_lane + width] = scratch[:, 7 + dx:rows - 9 + dx, :].astype(BF16)


def inside_lanes(p):
    lane_of = lax.broadcasted_iota(jnp.int32, (1, 2 * C), 1)
    if p == 0:
        return (lane_of >= C).astype(F32)
    if p == NZ // 2:
        return (lane_of < C).astype(F32)
    return 1.0


def windows(copies, first, count, p):
    lane = 2 * C
    rows = copies.shape[2]
    return jnp.concatenate(
        [
            copies[dx, pl.ds(first + dy, count), :, lane * p:lane * (p + 2)].reshape(count * rows, 2 * lane)
            for dx, dy in TAPS
        ],
        axis=1,
    )


def pre_gradient(grad, pre, p):
    sigma = jax.nn.sigmoid(pre)
    return grad * sigma * (1.0 + pre * (1.0 - sigma)) * inside_lanes(p)


def interior(own, got, w1b, wfb, fd, cd, hd, pg, acc, fs, cs, hs, pre):
    gx = lax.axis_index("gx")
    nx = own.shape[1]
    across = 2 * nx
    count = pg.shape[0]
    cells = count * across
    lane = 2 * C
    pairs = NZ // 2

    def place(left, right):
        for scratch, start, size in ((fs, 0, count + 2), (cs, count + 2, count + 1)):
            scratch[:, 8:8 + nx, :] = left[start:start + size].astype(F32)
            scratch[:, 8 + nx:8 + across, :] = right[start:start + size].astype(F32)

    @pl.when(gx == 0)
    def _():
        place(own, got)

    @pl.when(gx != 0)
    def _():
        place(got, own)

    for scratch in (fs, cs, hs):
        blank_rows(scratch)
    blank_edges(fd)
    blank_edges(cd)
    shift_rows(fs, fd, 2 - 2 * gx, lane)
    shift_rows(cs, cd, 1 - gx, lane)
    for p in range(pairs + 1):
        here = slice(lane * p, lane * (p + 1))
        value = dot(windows(fd, 2 - 2 * gx, count, p), w1b[...])
        pre[:, :, here] = value.reshape(count, across, lane)
        hidden = value * jax.nn.sigmoid(value) * inside_lanes(p)
        hs[:, 8:8 + across, here] = hidden.reshape(count, across, lane)
    hd[:, pl.ds(8 * gx, 2)] = jnp.zeros((3, 2) + hd.shape[2:], BF16)
    shift_rows(hs, hd, 2 - 2 * gx, 0)
    for p in range(pairs + 1):
        here = slice(lane * p, lane * (p + 1))
        grad = dot_nt(windows(cd, 1 - gx, count - 1, p), wfb[...])
        grad = pre_gradient(grad, pre[pl.ds(gx, count - 1), :, here].reshape((count - 1) * across, lane), p)
        pg[pl.ds(1 - gx, count - 1), :, here] = grad.astype(BF16).reshape(count - 1, across, lane)
    pg[pl.ds((count - 1) * gx, 1)] = jnp.zeros((1,) + pg.shape[1:], BF16)

    @pl.when(gx == 0)
    def _():
        for t, total in enumerate(second_products(hd, cd)):
            acc[t] = total

    @pl.when(gx != 0)
    def _():
        for t, total in enumerate(first_products(fd, pg)):
            acc[t] = total


def second_products(hd, cd):
    lane = 2 * C
    pairs = NZ // 2
    count, across = hd.shape[1] - 2, hd.shape[2]
    cells = count * across
    cot_t = jnp.concatenate(
        [cd[1, 1:1 + count, :, lane * (p + 1):lane * (p + 2)].reshape(cells, lane).T for p in range(pairs)], axis=1)
    return [
        dot(cot_t, jnp.concatenate(
            [hd[dx, dy:dy + count, :, lane * p:lane * (p + 2)].reshape(cells, 2 * lane) for p in range(pairs)], axis=0))
        for dx, dy in TAPS
    ]


def first_products(fd, pg):
    lane = 2 * C
    pairs = NZ // 2
    count, across, _ = pg.shape
    cells = count * across
    grad_t = jnp.concatenate(
        [pg[:, :, lane * p:lane * (p + 1)].reshape(cells, lane).T for p in range(pairs + 1)], axis=1)
    return [
        dot(grad_t, jnp.concatenate(
            [fd[dx, 1 + dy:1 + dy + count, :, lane * p:lane * (p + 2)].reshape(cells, 2 * lane) for p in range(pairs + 1)], axis=0))
        for dx, dy in TAPS
    ]


def folded(total, factor):
    total = total * factor
    return total[0:C, 0:3 * C] + total[C:2 * C, C:4 * C]


def second_late(hd, cd):
    lane = 2 * C
    pairs = NZ // 2
    late = ((0, 1), (0,), ())
    products = []
    for dx, dy in TAPS:
        if late[dy]:
            cots = jnp.concatenate(
                [cd[1, 1 + y, :, lane * (p + 1):lane * (p + 2)] for y in late[dy] for p in range(pairs)], axis=0)
            rows = jnp.concatenate(
                [hd[dx, y + dy, :, lane * p:lane * (p + 2)] for y in late[dy] for p in range(pairs)], axis=0)
            products.append(dot(cots.T, rows))
        else:
            products.append(0.0)
    return products


def first_late(fd, pg):
    lane = 2 * C
    pairs = NZ // 2
    count, across, _ = pg.shape
    y = count - 1
    extra = 2 * lane - (pairs + 1) * across
    grad_t = jnp.concatenate(
        [pg[y, :, lane * p:lane * (p + 1)] for p in range(pairs + 1)] + [jnp.zeros((extra, lane), BF16)], axis=0).T
    pad = jnp.zeros((extra, 2 * lane), BF16)
    return [
        dot(grad_t, jnp.concatenate(
            [fd[dx, y + dy + 1, :, lane * p:lane * (p + 2)] for p in range(pairs + 1)] + [pad], axis=0))
        for dx, dy in TAPS
    ]


def sums_of(factor, products):
    return packed([folded(product, factor) for product in products])


def store_blocks(target, blocks):
    for index, block in enumerate(blocks):
        target[index * C:(index + 1) * C, :] = block.astype(target.dtype)
    if target.shape[0] > BLOCKS * C:
        target[BLOCKS * C:, :] = jnp.zeros((target.shape[0] - BLOCKS * C, 2 * C), target.dtype)


def late_rows(factor, gy_count, fd_in, cd_in, hd_in, pg_in, rows, acc, w1b, wfb, fd, cd, hd, pg, send, rs, hs):
    gx = lax.axis_index("gx")
    gy = lax.axis_index("gy")
    count, across, _ = pg.shape
    lane = 2 * C
    pairs = NZ // 2
    rs[:, 8:8 + across, :] = rows[...].astype(F32)
    blank_rows(rs)
    blank_rows(hs)
    shift_rows(rs.at[0:2], fd, (count + 2) * gx, lane)
    shift_rows(rs.at[2:3], cd, (count + 1) * gx, lane)
    value = dot(jnp.concatenate([windows(fd, count * gx, 2, p) for p in range(pairs + 1)], axis=0), w1b[...])
    grad = dot_nt(jnp.concatenate([windows(cd, (count - 1) * gx, 1, p) for p in range(pairs + 1)], axis=0), wfb[...])
    before = jnp.where((gx == 0) & (gy == 0), 0.0, 1.0)
    beyond = jnp.where((gx != 0) & (gy == gy_count - 1), 0.0, 1.0)
    for p in range(pairs + 1):
        here = slice(lane * p, lane * (p + 1))
        early = value[2 * across * p:2 * across * p + across]
        later = value[2 * across * p + across:2 * across * (p + 1)]
        hs[0, 8:8 + across, here] = early * jax.nn.sigmoid(early) * inside_lanes(p) * before
        hs[1, 8:8 + across, here] = later * jax.nn.sigmoid(later) * inside_lanes(p) * beyond
        mine = pre_gradient(grad[across * p:across * (p + 1)], jnp.where(gx == 0, later, early), p)
        pg[pl.ds((count - 1) * gx, 1), :, here] = mine.astype(BF16)[None]
    shift_rows(hs, hd, count * gx, 0)

    @pl.when(gx == 0)
    def _():
        store_blocks(send, sums_of(factor, [acc[t] + late for t, late in enumerate(second_late(hd, cd))]))

    @pl.when(gx != 0)
    def _():
        store_blocks(send, sums_of(factor, [acc[t] + late for t, late in enumerate(first_late(fd, pg))]))


def keep_sums(factor, fd, cd, hd, pg, keep):
    gx = lax.axis_index("gx")

    @pl.when(gx == 0)
    def _():
        store_blocks(keep, sums_of(factor, first_products(fd, pg)))

    @pl.when(gx != 0)
    def _():
        store_blocks(keep, sums_of(factor, second_products(hd, cd)))


def output_conv(hd, w2b, mine, given):
    gx = lax.axis_index("gx")
    count, half, _ = mine.shape
    lane = 2 * C
    for p in range(NZ // 2):
        here = slice(lane * p, lane * (p + 1))
        value = dot(windows(hd, 0, count, p), w2b[...]).reshape(count, 2 * half, lane)
        left, right = value[:, 0:half], value[:, half:]
        mine[:, :, here] = jnp.where(gx == 0, left, right).astype(BF16)
        given[:, :, here] = jnp.where(gx == 0, right, left).astype(BF16)


def finish_output(mine, other, out, turned, scratch, sems):
    count, nx, width = mine.shape
    gx = lax.axis_index("gx")
    for y in range(count):
        a = mine[y].astype(F32)
        b = other[y].astype(F32)
        put_rows(scratch, y * nx, jnp.where(gx == 0, a, b))
        put_rows(scratch, (count + y) * nx, jnp.where(gx == 0, b, a))
    copies = []
    for x in range(nx):
        turned[x] = take_rows(scratch, x, 2 * count, nx)
        if x % 2:
            copies.append(pltpu.make_async_copy(turned.at[x - 1:x + 1], out.at[x - 1:x + 1], sems.at[x // 2]))
            copies[-1].start()
    for copy in copies:
        copy.wait()


def add_pair(keep, other, out):
    out[...] = (keep[...] + other[...].astype(F32)).astype(BF16)


def add_and_repeat(terms, out):
    total = terms[0].astype(F32)
    for index in range(1, terms.shape[0]):
        total = total + terms[index].astype(F32)
    total = total.astype(BF16)
    for index in range(out.shape[0]):
        out[index] = total


def unpack(rows, held):
    for t, (dx, dy) in enumerate(TAPS):
        turned = rows[t * C:(t + 1) * C, :].astype(F32).T
        held[9 * dx + 3 * dy] = turned[0:C]
        held[9 * dx + 3 * dy + 1] = turned[C:2 * C]
    for pair in range(5):
        turned = rows[(9 + pair) * C:(10 + pair) * C, :].astype(F32).T
        for half in range(2 if pair < 4 else 1):
            dx, dy = TAPS[2 * pair + half]
            held[9 * dx + 3 * dy + 2] = turned[half * C:(half + 1) * C]


def write_either(is_first, held, first, second, sem):
    for chosen, target in ((is_first, first), (jnp.logical_not(is_first), second)):
        @pl.when(chosen)
        def _():
            copy = pltpu.make_async_copy(held, target, sem.at[0])
            copy.start()
            copy.wait()


def unpack_own(rows, first, second, held, sem):
    unpack(rows, held)
    write_either(lax.axis_index("gx") == 0, held, first, second, sem)


def unpack_other(rows, first_in, second_in, first, second, held, sem):
    unpack(rows, held)
    write_either(lax.axis_index("gx") != 0, held, first, second, sem)


def near(shape, dtype):
    return pltpu.VMEM(shape, dtype)


def call(body, name, inputs, outs, scratch=(), limit=16, flops=0, far=False, aliases=None):
    placed = [pltpu.with_memory_space_constraint(x, pltpu.VMEM if held else pltpu.HBM) for x, held in inputs]
    size = sum(x.size * x.dtype.itemsize for x, _ in inputs)
    return pl.pallas_call(
        body,
        out_shape=list(outs),
        in_specs=[pl.BlockSpec(memory_space=pltpu.VMEM if held else pl.ANY) for _, held in inputs],
        out_specs=[pl.BlockSpec(memory_space=pl.ANY if far else pltpu.VMEM)] * len(outs),
        scratch_shapes=list(scratch),
        input_output_aliases=aliases or {},
        compiler_params=pltpu.CompilerParams(vmem_limit_bytes=limit * 1024 * 1024),
        cost_estimate=pl.CostEstimate(flops=flops, bytes_accessed=size, transcendentals=0),
        name=name,
    )(*placed)


def shards(field_in, first_weight, second_weight, cotangent):
    nx, ny, width = field_in.shape[1:]
    gx_count, gy_count, grp_count = (lax.axis_size(axis) for axis in ("gx", "gy", "grp"))
    total = field_in.shape[0] * nx * ny * NZ * gx_count * gy_count * grp_count
    factor = 1.0 / math.sqrt(total)
    ranks = gy_count * grp_count
    rows = -(-BLOCKS * C // (8 * ranks)) * 8 * ranks
    lane = 2 * C
    wide = width + 2 * lane
    count = ny // 2
    across = 2 * nx
    size = 2 * count + 3

    field, cot, edge, given, w1, w2 = call(
        pack_edges, "pack_edges",
        [(x, False) for x in (field_in[0], cotangent[0], first_weight.reshape(27, C, C), second_weight.reshape(27, C, C))],
        [
            near((nx, ny, width), BF16),
            near((nx, ny, width), BF16),
            near((3, nx, width), BF16),
            near((3, nx, width), BF16),
            near((27, C, C), BF16),
            near((27, C, C), BF16),
        ],
        [pltpu.VMEM((6, nx, width), F32), pltpu.SemaphoreType.DMA((4,))])
    taken = swap(given)
    own, bulk, w1b, w2b, wfb = call(
        pack_halves, "pack_halves", [(x, True) for x in (field, cot, w1, w2)],
        [
            near((size, nx, width), BF16),
            near((size, nx, width), BF16),
            near((9 * 4 * C, lane), BF16),
            near((9 * 4 * C, lane), BF16),
            near((lane, 9 * 4 * C), BF16),
        ],
        [
            pltpu.VMEM((ny, nx, width), BF16),
            pltpu.VMEM((ny, nx, width), BF16),
            pltpu.VMEM((width // lane, nx * ny, lane), F32),
        ], flops=10 ** 9)
    bulk, taken, wfb = lax.optimization_barrier((bulk, taken, wfb))
    got = swap(bulk)
    whole, = call(join_edges, "join_edges", [(edge, True), (taken, True)], [near((3, across, width), BF16)])
    ends = [(gy_count + j, j + 1) for j in range(gy_count - 1)]
    late = lax.ppermute(whole, ("gx", "gy"), ends + [(b, a) for a, b in ends])
    held = [
        near((3, count + 4, across, wide), BF16),
        near((3, count + 2, across, wide), BF16),
        near((3, count + 2, across, width + lane), BF16),
        near((count, across, width + lane), BF16),
    ]
    fd, cd, hd, pg, acc = call(
        interior, "interior",
        [(x, True) for x in (own, got, w1b, wfb)],
        held + [near((9, lane, 2 * lane), F32)],
        [
            pltpu.VMEM((count + 2, across + 16, width), F32),
            pltpu.VMEM((count + 1, across + 16, width), F32),
            pltpu.VMEM((count, across + 16, width + lane), F32),
            pltpu.VMEM((count, across, width + lane), F32),
        ],
        limit=32, flops=4 * 10 ** 9)
    fd, cd, hd, pg, send = call(
        functools.partial(late_rows, factor, gy_count), "late_rows",
        [(x, True) for x in (fd, cd, hd, pg, late, acc, w1b, wfb)],
        held + [near((rows, lane), BF16)],
        [pltpu.VMEM((3, across + 16, width), F32), pltpu.VMEM((2, across + 16, width + lane), F32)],
        limit=32, flops=10 ** 9, aliases={0: 0, 1: 1, 2: 2, 3: 3})

    other = swap(send)
    keep, = call(
        functools.partial(keep_sums, factor), "keep_sums",
        [(x, True) for x in (fd, cd, hd, pg)], [near((rows, lane), F32)], flops=2 * 10 ** 9)
    other, keep = lax.optimization_barrier((other, keep))
    both, = call(add_pair, "add_pair", [(keep, True), (other, True)], [near((rows, lane), BF16)])
    terms = lax.all_to_all(both.reshape(ranks, rows // ranks, lane), ("gy", "grp"), 0, 0)
    spread, = call(add_and_repeat, "add_and_repeat", [(terms, True)], [near(terms.shape, BF16)])
    spread, hd, w2b = lax.optimization_barrier((spread, hd, w2b))
    sums = lax.all_to_all(spread, ("gy", "grp"), 0, 0).reshape(rows, lane)
    mine, given = call(
        output_conv, "output_conv", [(hd, True), (w2b, True)],
        [near((count, nx, width), BF16), near((count, nx, width), BF16)], flops=2 * 10 ** 9)
    given = swap(given)
    out, = call(
        finish_output, "finish_output", [(mine, True), (given, True)],
        [pltpu.HBM((nx, ny, width), BF16)],
        [pltpu.VMEM((nx, ny, width), BF16), pltpu.VMEM((width // lane, nx * ny, lane), F32), pltpu.SemaphoreType.DMA((nx // 2,))], far=True)
    sums, out = lax.optimization_barrier((sums, out))
    other = swap(sums)
    outs = [pltpu.HBM((27, C, C), F32)] * 2
    scratch = [pltpu.VMEM((27, C, C), F32), pltpu.SemaphoreType.DMA((1,))]
    first, second = call(unpack_own, "unpack_own", [(sums, True)], outs, scratch, far=True)
    other, first, second = lax.optimization_barrier((other, first, second))
    first, second = call(
        unpack_other, "unpack_other", [(other, True), (first, False), (second, False)], outs, scratch, far=True,
        aliases={1: 0, 2: 1})
    shape = (3, 3, 3, C, C)
    return out[None], first.reshape(shape), second.reshape(shape)


def solution(mesh):
    return jax.shard_map(
        shards,
        mesh=mesh,
        in_specs=(P("grp", "gx", "gy", None), P(), P(), P("grp", "gx", "gy", None)),
        out_specs=(P("grp", "gx", "gy", None), P(), P()),
        check_vma=False,
    )
```

```python
import functools
import math

import jax
import jax.numpy as jnp
from jax import lax
from jax.experimental import pallas as pl
from jax.experimental.pallas import tpu as pltpu
from jax.sharding import PartitionSpec as P

C = 64
NZ = 16
BF16 = jnp.bfloat16
F32 = jnp.float32
TAPS = [(dx, dy) for dy in range(3) for dx in range(3)]
BLOCKS = 14


def swap(array):
    return lax.ppermute(array, "gx", [(0, 1), (1, 0)])


def dot(a, b):
    return jnp.dot(a, b, preferred_element_type=F32)


def dot_nt(a, b):
    return lax.dot_general(a, b, (((1,), (1,)), ((), ())), preferred_element_type=F32)


def band(taps):
    zero = jnp.zeros((C, C), BF16)
    left = jnp.concatenate(list(taps) + [zero], axis=0)
    right = jnp.concatenate([zero] + list(taps), axis=0)
    return jnp.concatenate([left, right], axis=1)


def band_flipped(taps):
    zero = jnp.zeros((C, C), BF16)
    back = list(taps)[::-1]
    upper = jnp.concatenate(back + [zero], axis=1)
    lower = jnp.concatenate([zero] + back, axis=1)
    return jnp.concatenate([upper, lower], axis=0)


def packed(pieces):
    blocks = [piece[:, 0:2 * C] for piece in pieces]
    for pair in range(0, 9, 2):
        second = pieces[pair + 1][:, 2 * C:3 * C] if pair + 1 < 9 else jnp.zeros((C, C), F32)
        blocks.append(jnp.concatenate([pieces[pair][:, 2 * C:3 * C], second], axis=1))
    return blocks


def pack_edges(field_hbm, cot_hbm, w1_hbm, w2_hbm, field, cot, edge, given, w1, w2, rows, sems):
    copies = [
        pltpu.make_async_copy(source, target, sems.at[index])
        for index, (source, target) in enumerate(((field_hbm, field), (cot_hbm, cot), (w1_hbm, w1), (w2_hbm, w2)))
    ]
    for copy in copies:
        copy.start()
    for copy in copies[:2]:
        copy.wait()
    nx, ny, _ = field.shape
    gx = lax.axis_index("gx")
    for x in range(nx):
        fields = field[x].astype(F32)
        cots = cot[x].astype(F32)
        for index, row in enumerate((fields[0:1], fields[1:2], cots[0:1], fields[ny - 2:ny - 1], fields[ny - 1:ny], cots[ny - 1:ny])):
            rows[index, x:x + 1, :] = row
    head = rows[0:3].astype(BF16)
    tail = rows[3:6].astype(BF16)
    edge[...] = jnp.where(gx == 0, head, tail)
    given[...] = jnp.where(gx == 0, tail, head)
    for copy in copies[2:]:
        copy.wait()


def join_edges(edge, taken, whole):
    nx = edge.shape[1]
    gx = lax.axis_index("gx")

    @pl.when(gx == 0)
    def _():
        whole[:, 0:nx] = edge[...]
        whole[:, nx:2 * nx] = taken[...]

    @pl.when(gx != 0)
    def _():
        whole[:, 0:nx] = taken[...]
        whole[:, nx:2 * nx] = edge[...]


def put_rows(scratch, start, rows):
    lane = 2 * C
    for tile in range(scratch.shape[0]):
        scratch[tile, start:start + rows.shape[0], :] = rows[:, lane * tile:lane * (tile + 1)]


def take_rows(scratch, start, count, stride):
    return jnp.concatenate(
        [scratch[tile, pl.ds(start, count, stride=stride), :] for tile in range(scratch.shape[0])], axis=1).astype(BF16)


def pack_halves(field, cot, w1, w2, own, bulk, w1b, wfb, turned_f, turned_c):
    nx, ny, _ = field.shape
    half = ny // 2
    for source, target in ((field, turned_f), (cot, turned_c)):
        for x in range(nx):
            put_rows(target, x * ny, source[x].astype(F32))
    gx = lax.axis_index("gx")

    def place(target, first_f, first_c):
        for y in range(half + 2):
            target[y] = take_rows(turned_f, first_f + y, nx, ny)
        for y in range(half + 1):
            target[half + 2 + y] = take_rows(turned_c, first_c + y, nx, ny)

    @pl.when(gx == 0)
    def _():
        place(own, 0, 0)
        place(bulk, half - 2, half - 1)

    @pl.when(gx != 0)
    def _():
        place(own, half - 2, half - 1)
        place(bulk, 0, 0)

    make_bands(w1, w2, w1b, wfb)


def make_bands(w1, w2, w1b, wfb):
    for t, (dx, dy) in enumerate(TAPS):
        rows = slice(t * 4 * C, (t + 1) * 4 * C)
        first = 9 * dx + 3 * dy
        w1b[rows, :] = band([w1[first + z] for z in range(3)])
        wfb[:, rows] = band_flipped([w2[24 - first + z] for z in range(3)])


def blank_edges(copies):
    lane = 2 * C
    zero = jnp.zeros(copies.shape[:-1] + (lane,), BF16)
    copies[..., 0:lane] = zero
    copies[..., copies.shape[-1] - lane:] = zero


def blank_rows(scratch):
    zero = jnp.zeros((scratch.shape[0], 1, scratch.shape[2]), F32)
    scratch[:, 7:8, :] = zero
    scratch[:, scratch.shape[1] - 8:scratch.shape[1] - 7, :] = zero


def shift_rows(scratch, copies, start, first_lane, taps=(0, 1, 2)):
    count, rows, width = scratch.shape
    for dx in taps:
        copies[dx, pl.ds(start, count), :, first_lane:first_lane + width] = scratch[:, 7 + dx:rows - 9 + dx, :].astype(BF16)


def inside_lanes(p):
    lane_of = lax.broadcasted_iota(jnp.int32, (1, 2 * C), 1)
    if p == 0:
        return (lane_of >= C).astype(F32)
    if p == NZ // 2:
        return (lane_of < C).astype(F32)
    return 1.0


def windows(copies, first, count, p):
    lane = 2 * C
    rows = copies.shape[2]
    return jnp.concatenate(
        [
            copies[dx, pl.ds(first + dy, count), :, lane * p:lane * (p + 2)].reshape(count * rows, 2 * lane)
            for dx, dy in TAPS
        ],
        axis=1,
    )


def pre_gradient(grad, pre, p):
    sigma = jax.nn.sigmoid(pre)
    return grad * sigma * (1.0 + pre * (1.0 - sigma)) * inside_lanes(p)


def interior(own, got, w1b, wfb, fd, cd, hd, pg, acc, fs, cs, hs, pre):
    gx = lax.axis_index("gx")
    nx, width = own.shape[1:]
    across = 2 * nx
    count = pg.shape[0]
    cells = count * across
    lane = 2 * C
    pairs = NZ // 2

    def place(left, right):
        for scratch, copies, offset, start, size in ((fs, fd, 2 - 2 * gx, 0, count + 2), (cs, cd, 1 - gx, count + 2, count + 1)):
            for source, row in ((left, 0), (right, nx)):
                rows = source[start:start + size]
                scratch[:, 8 + row:8 + row + nx, :] = rows.astype(F32)
                copies[1, pl.ds(offset, size), row:row + nx, lane:lane + width] = rows

    @pl.when(gx == 0)
    def _():
        place(own, got)

    @pl.when(gx != 0)
    def _():
        place(got, own)

    for scratch in (fs, cs, hs):
        blank_rows(scratch)
    blank_edges(fd)
    blank_edges(cd)
    shift_rows(fs, fd, 2 - 2 * gx, lane, (0, 2))
    shift_rows(cs, cd, 1 - gx, lane, (0, 2))
    for p in range(pairs + 1):
        here = slice(lane * p, lane * (p + 1))
        value = dot(windows(fd, 2 - 2 * gx, count, p), w1b[...])
        pre[:, :, here] = value.reshape(count, across, lane)
        hidden = value * jax.nn.sigmoid(value) * inside_lanes(p)
        hidden = hidden.reshape(count, across, lane)
        hs[:, 8:8 + across, here] = hidden
        hd[1, pl.ds(2 - 2 * gx, count), :, here] = hidden.astype(BF16)
    hd[:, pl.ds(count * gx, 2)] = jnp.zeros((3, 2) + hd.shape[2:], BF16)
    shift_rows(hs, hd, 2 - 2 * gx, 0, (0, 2))
    for p in range(pairs + 1):
        here = slice(lane * p, lane * (p + 1))
        grad = dot_nt(windows(cd, 1 - gx, count - 1, p), wfb[...])
        grad = pre_gradient(grad, pre[pl.ds(gx, count - 1), :, here].reshape((count - 1) * across, lane), p)
        pg[pl.ds(1 - gx, count - 1), :, here] = grad.astype(BF16).reshape(count - 1, across, lane)
    pg[pl.ds((count - 1) * gx, 1)] = jnp.zeros((1,) + pg.shape[1:], BF16)

    @pl.when(gx == 0)
    def _():
        for t, total in enumerate(second_products(hd, cd)):
            acc[t] = total

    @pl.when(gx != 0)
    def _():
        for t, total in enumerate(first_products(fd, pg)):
            acc[t] = total


def second_products(hd, cd):
    lane = 2 * C
    pairs = NZ // 2
    count, across = hd.shape[1] - 2, hd.shape[2]
    cells = count * across
    cot_t = jnp.concatenate(
        [cd[1, 1:1 + count, :, lane * (p + 1):lane * (p + 2)].reshape(cells, lane).T for p in range(pairs)], axis=1)
    return [
        dot(cot_t, jnp.concatenate(
            [hd[dx, dy:dy + count, :, lane * p:lane * (p + 2)].reshape(cells, 2 * lane) for p in range(pairs)], axis=0))
        for dx, dy in TAPS
    ]


def first_products(fd, pg):
    lane = 2 * C
    pairs = NZ // 2
    count, across, _ = pg.shape
    cells = count * across
    grad_t = jnp.concatenate(
        [pg[:, :, lane * p:lane * (p + 1)].reshape(cells, lane).T for p in range(pairs + 1)], axis=1)
    return [
        dot(grad_t, jnp.concatenate(
            [fd[dx, 1 + dy:1 + dy + count, :, lane * p:lane * (p + 2)].reshape(cells, 2 * lane) for p in range(pairs + 1)], axis=0))
        for dx, dy in TAPS
    ]


def folded(total):
    return total[0:C, 0:3 * C] + total[C:2 * C, C:4 * C]


def second_late(hd, cd):
    lane = 2 * C
    pairs = NZ // 2
    late = ((0, 1), (0,), ())
    products = []
    for dx, dy in TAPS:
        if late[dy]:
            cots = jnp.concatenate(
                [cd[1, 1 + y, :, lane * (p + 1):lane * (p + 2)] for y in late[dy] for p in range(pairs)], axis=0)
            rows = jnp.concatenate(
                [hd[dx, y + dy, :, lane * p:lane * (p + 2)] for y in late[dy] for p in range(pairs)], axis=0)
            products.append(dot(cots.T, rows))
        else:
            products.append(0.0)
    return products


def first_late(fd, pg):
    lane = 2 * C
    pairs = NZ // 2
    count, across, _ = pg.shape
    y = count - 1
    extra = 2 * lane - (pairs + 1) * across
    grad_t = jnp.concatenate(
        [pg[y, :, lane * p:lane * (p + 1)] for p in range(pairs + 1)] + [jnp.zeros((extra, lane), BF16)], axis=0).T
    pad = jnp.zeros((extra, 2 * lane), BF16)
    return [
        dot(grad_t, jnp.concatenate(
            [fd[dx, y + dy + 1, :, lane * p:lane * (p + 2)] for p in range(pairs + 1)] + [pad], axis=0))
        for dx, dy in TAPS
    ]


def sums_of(products):
    return packed([folded(product) for product in products])


def store_blocks(target, blocks):
    for index, block in enumerate(blocks):
        target[index * C:(index + 1) * C, :] = block.astype(target.dtype)
    if target.shape[0] > BLOCKS * C:
        target[BLOCKS * C:, :] = jnp.zeros((target.shape[0] - BLOCKS * C, 2 * C), target.dtype)


def late_rows(gy_count, fd_in, cd_in, hd_in, pg_in, rows, acc, w1b, wfb, fd, cd, hd, pg, send, rs, hs):
    gx = lax.axis_index("gx")
    gy = lax.axis_index("gy")
    count, across, _ = pg.shape
    lane = 2 * C
    pairs = NZ // 2
    rs[:, 8:8 + across, :] = rows[...].astype(F32)
    blank_rows(rs)
    blank_rows(hs)
    shift_rows(rs.at[0:2], fd, (count + 2) * gx, lane)
    shift_rows(rs.at[2:3], cd, (count + 1) * gx, lane)
    value = dot(jnp.concatenate([windows(fd, count * gx, 2, p) for p in range(pairs + 1)], axis=0), w1b[...])
    grad = dot_nt(jnp.concatenate([windows(cd, (count - 1) * gx, 1, p) for p in range(pairs + 1)], axis=0), wfb[...])
    before = jnp.where((gx == 0) & (gy == 0), 0.0, 1.0)
    beyond = jnp.where((gx != 0) & (gy == gy_count - 1), 0.0, 1.0)
    for p in range(pairs + 1):
        here = slice(lane * p, lane * (p + 1))
        early = value[2 * across * p:2 * across * p + across]
        later = value[2 * across * p + across:2 * across * (p + 1)]
        hs[0, 8:8 + across, here] = early * jax.nn.sigmoid(early) * inside_lanes(p) * before
        hs[1, 8:8 + across, here] = later * jax.nn.sigmoid(later) * inside_lanes(p) * beyond
        mine = pre_gradient(grad[across * p:across * (p + 1)], jnp.where(gx == 0, later, early), p)
        pg[pl.ds((count - 1) * gx, 1), :, here] = mine.astype(BF16)[None]
    shift_rows(hs, hd, count * gx, 0)

    @pl.when(gx == 0)
    def _():
        store_blocks(send, sums_of([acc[t] + late for t, late in enumerate(second_late(hd, cd))]))

    @pl.when(gx != 0)
    def _():
        store_blocks(send, sums_of([acc[t] + late for t, late in enumerate(first_late(fd, pg))]))


def keep_sums(fd, cd, hd, pg, keep):
    gx = lax.axis_index("gx")

    @pl.when(gx == 0)
    def _():
        store_blocks(keep, sums_of(first_products(fd, pg)))

    @pl.when(gx != 0)
    def _():
        store_blocks(keep, sums_of(second_products(hd, cd)))


def output_conv(hd, w2, mine, given, w2b):
    for t, (dx, dy) in enumerate(TAPS):
        w2b[t * 4 * C:(t + 1) * 4 * C, :] = band([w2[9 * dx + 3 * dy + z] for z in range(3)])
    gx = lax.axis_index("gx")
    count, half, _ = mine.shape
    lane = 2 * C
    for p in range(NZ // 2):
        here = slice(lane * p, lane * (p + 1))
        value = dot(windows(hd, 0, count, p), w2b[...]).reshape(count, 2 * half, lane)
        left, right = value[:, 0:half], value[:, half:]
        mine[:, :, here] = jnp.where(gx == 0, left, right).astype(BF16)
        given[:, :, here] = jnp.where(gx == 0, right, left).astype(BF16)


def finish_output(mine, other, out, turned, scratch, sems):
    count, nx, width = mine.shape
    gx = lax.axis_index("gx")
    for y in range(count):
        a = mine[y].astype(F32)
        b = other[y].astype(F32)
        put_rows(scratch, y * nx, jnp.where(gx == 0, a, b))
        put_rows(scratch, (count + y) * nx, jnp.where(gx == 0, b, a))
    copies = []
    for x in range(nx):
        turned[x] = take_rows(scratch, x, 2 * count, nx)
        if x % 2:
            copies.append(pltpu.make_async_copy(turned.at[x - 1:x + 1], out.at[x - 1:x + 1], sems.at[x // 2]))
            copies[-1].start()
    for copy in copies:
        copy.wait()


def add_pair(keep, other, out):
    out[...] = (keep[...] + other[...].astype(F32)).astype(BF16)


def add_and_repeat(terms, out, held, sems):
    total = terms[0].astype(F32)
    for index in range(1, terms.shape[0]):
        total = total + terms[index].astype(F32)
    held[...] = total.astype(BF16)
    copies = [pltpu.make_async_copy(held, out.at[index], sems.at[index]) for index in range(terms.shape[0])]
    for copy in copies:
        copy.start()
    for copy in copies:
        copy.wait()


def unpack(factor, rows, held):
    for t, (dx, dy) in enumerate(TAPS):
        turned = rows[t * C:(t + 1) * C, :].astype(F32).T * factor
        held[9 * dx + 3 * dy] = turned[0:C]
        held[9 * dx + 3 * dy + 1] = turned[C:2 * C]
    for pair in range(5):
        turned = rows[(9 + pair) * C:(10 + pair) * C, :].astype(F32).T * factor
        for half in range(2 if pair < 4 else 1):
            dx, dy = TAPS[2 * pair + half]
            held[9 * dx + 3 * dy + 2] = turned[half * C:(half + 1) * C]


def write_either(is_first, held, first, second, sem):
    for chosen, target in ((is_first, first), (jnp.logical_not(is_first), second)):
        @pl.when(chosen)
        def _():
            copy = pltpu.make_async_copy(held, target, sem.at[0])
            copy.start()
            copy.wait()


def unpack_own(factor, rows, first, second, held, sem):
    unpack(factor, rows, held)
    write_either(lax.axis_index("gx") == 0, held, first, second, sem)


def unpack_other(factor, rows, first_in, second_in, first, second, held, sem):
    unpack(factor, rows, held)
    write_either(lax.axis_index("gx") != 0, held, first, second, sem)


def near(shape, dtype):
    return pltpu.VMEM(shape, dtype)


def call(body, name, inputs, outs, scratch=(), limit=16, flops=0, far=False, aliases=None):
    placed = [pltpu.with_memory_space_constraint(x, pltpu.VMEM if held else pltpu.HBM) for x, held in inputs]
    size = sum(x.size * x.dtype.itemsize for x, _ in inputs)
    return pl.pallas_call(
        body,
        out_shape=list(outs),
        in_specs=[pl.BlockSpec(memory_space=pltpu.VMEM if held else pl.ANY) for _, held in inputs],
        out_specs=[pl.BlockSpec(memory_space=pl.ANY if far else pltpu.VMEM)] * len(outs),
        scratch_shapes=list(scratch),
        input_output_aliases=aliases or {},
        compiler_params=pltpu.CompilerParams(vmem_limit_bytes=limit * 1024 * 1024),
        cost_estimate=pl.CostEstimate(flops=flops, bytes_accessed=size, transcendentals=0),
        name=name,
    )(*placed)


def shards(field_in, first_weight, second_weight, cotangent):
    nx, ny, width = field_in.shape[1:]
    gx_count, gy_count, grp_count = (lax.axis_size(axis) for axis in ("gx", "gy", "grp"))
    total = field_in.shape[0] * nx * ny * NZ * gx_count * gy_count * grp_count
    factor = 1.0 / math.sqrt(total)
    ranks = gy_count * grp_count
    rows = -(-BLOCKS * C // (8 * ranks)) * 8 * ranks
    lane = 2 * C
    wide = width + 2 * lane
    count = ny // 2
    across = 2 * nx
    size = 2 * count + 3

    field, cot, edge, given, w1, w2 = call(
        pack_edges, "pack_edges",
        [(x, False) for x in (field_in[0], cotangent[0], first_weight.reshape(27, C, C), second_weight.reshape(27, C, C))],
        [
            near((nx, ny, width), BF16),
            near((nx, ny, width), BF16),
            near((3, nx, width), BF16),
            near((3, nx, width), BF16),
            near((27, C, C), BF16),
            near((27, C, C), BF16),
        ],
        [pltpu.VMEM((6, nx, width), F32), pltpu.SemaphoreType.DMA((4,))])
    taken = swap(given)
    own, bulk, w1b, wfb = call(
        pack_halves, "pack_halves", [(x, True) for x in (field, cot, w1, w2)],
        [
            near((size, nx, width), BF16),
            near((size, nx, width), BF16),
            near((9 * 4 * C, lane), BF16),
            near((lane, 9 * 4 * C), BF16),
        ],
        [pltpu.VMEM((width // lane, nx * ny, lane), F32)] * 2, flops=10 ** 9)
    bulk, taken, wfb = lax.optimization_barrier((bulk, taken, wfb))
    got = swap(bulk)
    whole, = call(join_edges, "join_edges", [(edge, True), (taken, True)], [near((3, across, width), BF16)])
    ends = [(gy_count + j, j + 1) for j in range(gy_count - 1)]
    late = lax.ppermute(whole, ("gx", "gy"), ends + [(b, a) for a, b in ends])
    held = [
        near((3, count + 4, across, wide), BF16),
        near((3, count + 2, across, wide), BF16),
        near((3, count + 2, across, width + lane), BF16),
        near((count, across, width + lane), BF16),
    ]
    fd, cd, hd, pg, acc = call(
        interior, "interior",
        [(x, True) for x in (own, got, w1b, wfb)],
        held + [near((9, lane, 2 * lane), F32)],
        [
            pltpu.VMEM((count + 2, across + 16, width), F32),
            pltpu.VMEM((count + 1, across + 16, width), F32),
            pltpu.VMEM((count, across + 16, width + lane), F32),
            pltpu.VMEM((count, across, width + lane), F32),
        ],
        limit=32, flops=4 * 10 ** 9)
    fd, cd, hd, pg, send = call(
        functools.partial(late_rows, gy_count), "late_rows",
        [(x, True) for x in (fd, cd, hd, pg, late, acc, w1b, wfb)],
        held + [near((rows, lane), BF16)],
        [pltpu.VMEM((3, across + 16, width), F32), pltpu.VMEM((2, across + 16, width + lane), F32)],
        limit=32, flops=10 ** 9, aliases={0: 0, 1: 1, 2: 2, 3: 3})

    other = swap(send)
    keep, = call(
        keep_sums, "keep_sums",
        [(x, True) for x in (fd, cd, hd, pg)], [near((rows, lane), F32)], flops=2 * 10 ** 9)
    other, keep = lax.optimization_barrier((other, keep))
    both, = call(add_pair, "add_pair", [(keep, True), (other, True)], [near((rows, lane), BF16)])
    terms = lax.all_to_all(both.reshape(ranks, rows // ranks, lane), ("gy", "grp"), 0, 0)
    spread, = call(
        add_and_repeat, "add_and_repeat", [(terms, True)], [pltpu.HBM(terms.shape, BF16)],
        [pltpu.VMEM(terms.shape[1:], BF16), pltpu.SemaphoreType.DMA((ranks,))], far=True)
    spread, hd, w2 = lax.optimization_barrier((spread, hd, w2))
    sums = lax.all_to_all(spread, ("gy", "grp"), 0, 0).reshape(rows, lane)
    mine, given = call(
        output_conv, "output_conv", [(hd, True), (w2, True)],
        [near((count, nx, width), BF16), near((count, nx, width), BF16)],
        [pltpu.VMEM((9 * 4 * C, lane), BF16)], flops=2 * 10 ** 9)
    given = swap(given)
    out, = call(
        finish_output, "finish_output", [(mine, True), (given, True)],
        [pltpu.HBM((nx, ny, width), BF16)],
        [pltpu.VMEM((nx, ny, width), BF16), pltpu.VMEM((width // lane, nx * ny, lane), F32), pltpu.SemaphoreType.DMA((nx // 2,))], far=True)
    sums, out = lax.optimization_barrier((sums, out))
    other = swap(sums)
    outs = [pltpu.HBM((27, C, C), F32)] * 2
    scratch = [pltpu.VMEM((27, C, C), F32), pltpu.SemaphoreType.DMA((1,))]
    first, second = call(functools.partial(unpack_own, factor), "unpack_own", [(sums, True)], outs, scratch, far=True)
    other, first, second = lax.optimization_barrier((other, first, second))
    first, second = call(
        functools.partial(unpack_other, factor), "unpack_other", [(other, True), (first, False), (second, False)], outs, scratch, far=True,
        aliases={1: 0, 2: 1})
    shape = (3, 3, 3, C, C)
    return out[None], first.reshape(shape), second.reshape(shape)


def solution(mesh):
    return jax.shard_map(
        shards,
        mesh=mesh,
        in_specs=(P("grp", "gx", "gy", None), P(), P(), P("grp", "gx", "gy", None)),
        out_specs=(P("grp", "gx", "gy", None), P(), P()),
        check_vma=False,
    )
```

```python
import functools
import math

import jax
import jax.numpy as jnp
from jax import lax
from jax.experimental import pallas as pl
from jax.experimental.pallas import tpu as pltpu
from jax.sharding import PartitionSpec as P

C = 64
NZ = 16
BF16 = jnp.bfloat16
F32 = jnp.float32
TAPS = [(dx, dy) for dy in range(3) for dx in range(3)]
BLOCKS = 14


def swap(array):
    return lax.ppermute(array, "gx", [(0, 1), (1, 0)])


def dot(a, b):
    return jnp.dot(a, b, preferred_element_type=F32)


def dot_nt(a, b):
    return lax.dot_general(a, b, (((1,), (1,)), ((), ())), preferred_element_type=F32)


def band(taps):
    zero = jnp.zeros((C, C), BF16)
    left = jnp.concatenate(list(taps) + [zero], axis=0)
    right = jnp.concatenate([zero] + list(taps), axis=0)
    return jnp.concatenate([left, right], axis=1)


def band_flipped(taps):
    zero = jnp.zeros((C, C), BF16)
    back = list(taps)[::-1]
    upper = jnp.concatenate(back + [zero], axis=1)
    lower = jnp.concatenate([zero] + back, axis=1)
    return jnp.concatenate([upper, lower], axis=0)


def packed(pieces):
    blocks = [piece[:, 0:2 * C] for piece in pieces]
    for pair in range(0, 9, 2):
        second = pieces[pair + 1][:, 2 * C:3 * C] if pair + 1 < 9 else jnp.zeros((C, C), F32)
        blocks.append(jnp.concatenate([pieces[pair][:, 2 * C:3 * C], second], axis=1))
    return blocks


def pack_edges(field_hbm, cot_hbm, w1_hbm, w2_hbm, field, cot, edge, given, w1, w2, rows, sems):
    copies = [
        pltpu.make_async_copy(source, target, sems.at[index])
        for index, (source, target) in enumerate(((field_hbm, field), (cot_hbm, cot), (w1_hbm, w1), (w2_hbm, w2)))
    ]
    for copy in copies:
        copy.start()
    for copy in copies[:2]:
        copy.wait()
    nx, ny, _ = field.shape
    gx = lax.axis_index("gx")
    for x in range(nx):
        fields = field[x].astype(F32)
        cots = cot[x].astype(F32)
        for index, row in enumerate((fields[0:1], fields[1:2], cots[0:1], fields[ny - 2:ny - 1], fields[ny - 1:ny], cots[ny - 1:ny])):
            rows[index, x:x + 1, :] = row
    head = rows[0:3].astype(BF16)
    tail = rows[3:6].astype(BF16)
    edge[...] = jnp.where(gx == 0, head, tail)
    given[...] = jnp.where(gx == 0, tail, head)
    for copy in copies[2:]:
        copy.wait()


def join_edges(edge, taken, whole):
    nx = edge.shape[1]
    gx = lax.axis_index("gx")

    @pl.when(gx == 0)
    def _():
        whole[:, 0:nx] = edge[...]
        whole[:, nx:2 * nx] = taken[...]

    @pl.when(gx != 0)
    def _():
        whole[:, 0:nx] = taken[...]
        whole[:, nx:2 * nx] = edge[...]


def put_rows(scratch, start, rows):
    lane = 2 * C
    for tile in range(scratch.shape[0]):
        scratch[tile, start:start + rows.shape[0], :] = rows[:, lane * tile:lane * (tile + 1)]


def take_rows(scratch, start, count, stride):
    return jnp.concatenate(
        [scratch[tile, pl.ds(start, count, stride=stride), :] for tile in range(scratch.shape[0])], axis=1).astype(BF16)


def pack_halves(field, cot, w1, w2, own, bulk, w1b, wfb, turned_f, turned_c):
    nx, ny, _ = field.shape
    half = ny // 2
    for source, target in ((field, turned_f), (cot, turned_c)):
        for x in range(nx):
            put_rows(target, x * ny, source[x].astype(F32))
    gx = lax.axis_index("gx")

    def place(target, first_f, first_c):
        for y in range(half + 2):
            target[y] = take_rows(turned_f, first_f + y, nx, ny)
        for y in range(half + 1):
            target[half + 2 + y] = take_rows(turned_c, first_c + y, nx, ny)

    @pl.when(gx == 0)
    def _():
        place(own, 0, 0)
        place(bulk, half - 2, half - 1)

    @pl.when(gx != 0)
    def _():
        place(own, half - 2, half - 1)
        place(bulk, 0, 0)

    make_bands(w1, w2, w1b, wfb)


def make_bands(w1, w2, w1b, wfb):
    for t, (dx, dy) in enumerate(TAPS):
        rows = slice(t * 4 * C, (t + 1) * 4 * C)
        first = 9 * dx + 3 * dy
        w1b[rows, :] = band([w1[first + z] for z in range(3)])
        wfb[:, rows] = band_flipped([w2[24 - first + z] for z in range(3)])


def blank_edges(copies):
    lane = 2 * C
    zero = jnp.zeros(copies.shape[:-1] + (lane,), BF16)
    copies[..., 0:lane] = zero
    copies[..., copies.shape[-1] - lane:] = zero


def blank_rows(scratch):
    zero = jnp.zeros((scratch.shape[0], 1, scratch.shape[2]), F32)
    scratch[:, 7:8, :] = zero
    scratch[:, scratch.shape[1] - 8:scratch.shape[1] - 7, :] = zero


def shift_rows(scratch, copies, start, first_lane, taps=(0, 1, 2)):
    count, rows, width = scratch.shape
    for dx in taps:
        copies[dx, pl.ds(start, count), :, first_lane:first_lane + width] = scratch[:, 7 + dx:rows - 9 + dx, :].astype(BF16)


def inside_lanes(p):
    lane_of = lax.broadcasted_iota(jnp.int32, (1, 2 * C), 1)
    if p == 0:
        return (lane_of >= C).astype(F32)
    if p == NZ // 2:
        return (lane_of < C).astype(F32)
    return 1.0


def windows(copies, first, count, p):
    lane = 2 * C
    rows = copies.shape[2]
    return jnp.concatenate(
        [
            copies[dx, pl.ds(first + dy, count), :, lane * p:lane * (p + 2)].reshape(count * rows, 2 * lane)
            for dx, dy in TAPS
        ],
        axis=1,
    )


def pre_gradient(grad, pre, p):
    sigma = jax.nn.sigmoid(pre)
    return grad * sigma * (1.0 + pre * (1.0 - sigma)) * inside_lanes(p)


def interior(own, got, w1b, wfb, fd, cd, hd, pg, hs, acc, fs, cs, pre):
    gx = lax.axis_index("gx")
    nx, width = own.shape[1:]
    across = 2 * nx
    count = pg.shape[0]
    cells = count * across
    lane = 2 * C
    pairs = NZ // 2

    def place(left, right):
        for scratch, copies, offset, start, size in ((fs, fd, 2 - 2 * gx, 0, count + 2), (cs, cd, 1 - gx, count + 2, count + 1)):
            for source, row in ((left, 0), (right, nx)):
                rows = source[start:start + size]
                scratch[:, 8 + row:8 + row + nx, :] = rows.astype(F32)
                copies[1, pl.ds(offset, size), row:row + nx, lane:lane + width] = rows

    @pl.when(gx == 0)
    def _():
        place(own, got)

    @pl.when(gx != 0)
    def _():
        place(got, own)

    for scratch in (fs, cs, hs):
        blank_rows(scratch)
    blank_edges(fd)
    blank_edges(cd)
    shift_rows(fs, fd, 2 - 2 * gx, lane, (0, 2))
    shift_rows(cs, cd, 1 - gx, lane, (0, 2))
    for group in range(0, pairs + 1, 3):
        value = dot(jnp.concatenate([windows(fd, 2 - 2 * gx, count, p) for p in range(group, group + 3)], axis=0), w1b[...])
        for p in range(group, group + 3):
            here = slice(lane * p, lane * (p + 1))
            part = value[cells * (p - group):cells * (p - group + 1)]
            pre[:, :, here] = part.reshape(count, across, lane)
            hidden = (part * jax.nn.sigmoid(part) * inside_lanes(p)).reshape(count, across, lane)
            hs[pl.ds(2 - 2 * gx, count), 8:8 + across, here] = hidden
            hd[1, pl.ds(2 - 2 * gx, count), :, here] = hidden.astype(BF16)
    cells = cells - across
    for group in range(0, pairs + 1, 3):
        value = dot_nt(jnp.concatenate([windows(cd, 1 - gx, count - 1, p) for p in range(group, group + 3)], axis=0), wfb[...])
        for p in range(group, group + 3):
            here = slice(lane * p, lane * (p + 1))
            part = value[cells * (p - group):cells * (p - group + 1)]
            grad = pre_gradient(part, pre[pl.ds(gx, count - 1), :, here].reshape(cells, lane), p)
            pg[pl.ds(1 - gx, count - 1), :, here] = grad.astype(BF16).reshape(count - 1, across, lane)
    pg[pl.ds((count - 1) * gx, 1)] = jnp.zeros((1,) + pg.shape[1:], BF16)

    @pl.when(gx == 0)
    def _():
        hd[:, 0:2] = jnp.zeros((3, 2) + hd.shape[2:], BF16)
        shift_rows(hs.at[2:2 + count], hd, 2, 0, (0, 2))
        for t, total in enumerate(second_products(hd, cd)):
            acc[t] = total

    @pl.when(gx != 0)
    def _():
        for t, total in enumerate(first_products(fd, pg)):
            acc[t] = total


def second_products(hd, cd):
    lane = 2 * C
    pairs = NZ // 2
    count, across = hd.shape[1] - 2, hd.shape[2]
    cells = count * across
    cot_t = jnp.concatenate(
        [cd[1, 1:1 + count, :, lane * (p + 1):lane * (p + 2)].reshape(cells, lane).T for p in range(pairs)], axis=1)
    return [
        dot(cot_t, jnp.concatenate(
            [hd[dx, dy:dy + count, :, lane * p:lane * (p + 2)].reshape(cells, 2 * lane) for p in range(pairs)], axis=0))
        for dx, dy in TAPS
    ]


def first_products(fd, pg):
    lane = 2 * C
    pairs = NZ // 2
    count, across, _ = pg.shape
    cells = count * across
    grad_t = jnp.concatenate(
        [pg[:, :, lane * p:lane * (p + 1)].reshape(cells, lane).T for p in range(pairs + 1)], axis=1)
    return [
        dot(grad_t, jnp.concatenate(
            [fd[dx, 1 + dy:1 + dy + count, :, lane * p:lane * (p + 2)].reshape(cells, 2 * lane) for p in range(pairs + 1)], axis=0))
        for dx, dy in TAPS
    ]


def folded(total):
    return total[0:C, 0:3 * C] + total[C:2 * C, C:4 * C]


def second_late(hd, cd):
    lane = 2 * C
    pairs = NZ // 2
    late = ((0, 1), (0,), ())
    products = []
    for dx, dy in TAPS:
        if late[dy]:
            cots = jnp.concatenate(
                [cd[1, 1 + y, :, lane * (p + 1):lane * (p + 2)] for y in late[dy] for p in range(pairs)], axis=0)
            rows = jnp.concatenate(
                [hd[dx, y + dy, :, lane * p:lane * (p + 2)] for y in late[dy] for p in range(pairs)], axis=0)
            products.append(dot(cots.T, rows))
        else:
            products.append(0.0)
    return products


def first_late(fd, pg):
    lane = 2 * C
    pairs = NZ // 2
    count, across, _ = pg.shape
    y = count - 1
    extra = 2 * lane - (pairs + 1) * across
    grad_t = jnp.concatenate(
        [pg[y, :, lane * p:lane * (p + 1)] for p in range(pairs + 1)] + [jnp.zeros((extra, lane), BF16)], axis=0).T
    pad = jnp.zeros((extra, 2 * lane), BF16)
    return [
        dot(grad_t, jnp.concatenate(
            [fd[dx, y + dy + 1, :, lane * p:lane * (p + 2)] for p in range(pairs + 1)] + [pad], axis=0))
        for dx, dy in TAPS
    ]


def sums_of(products):
    return packed([folded(product) for product in products])


def store_blocks(target, blocks):
    for index, block in enumerate(blocks):
        target[index * C:(index + 1) * C, :] = block.astype(target.dtype)
    if target.shape[0] > BLOCKS * C:
        target[BLOCKS * C:, :] = jnp.zeros((target.shape[0] - BLOCKS * C, 2 * C), target.dtype)


def late_rows(gy_count, fd_in, cd_in, hd_in, pg_in, hs_in, rows, acc, w1b, wfb, fd, cd, hd, pg, hs, send, rs):
    gx = lax.axis_index("gx")
    gy = lax.axis_index("gy")
    count, across, _ = pg.shape
    lane = 2 * C
    pairs = NZ // 2
    rs[:, 8:8 + across, :] = rows[...].astype(F32)
    blank_rows(rs)
    shift_rows(rs.at[0:2], fd, (count + 2) * gx, lane)
    shift_rows(rs.at[2:3], cd, (count + 1) * gx, lane)
    value = dot(jnp.concatenate([windows(fd, count * gx, 2, p) for p in range(pairs + 1)], axis=0), w1b[...])
    grad = dot_nt(jnp.concatenate([windows(cd, (count - 1) * gx, 1, p) for p in range(pairs + 1)], axis=0), wfb[...])
    before = jnp.where((gx == 0) & (gy == 0), 0.0, 1.0)
    beyond = jnp.where((gx != 0) & (gy == gy_count - 1), 0.0, 1.0)
    for p in range(pairs + 1):
        here = slice(lane * p, lane * (p + 1))
        early = value[2 * across * p:2 * across * p + across]
        later = value[2 * across * p + across:2 * across * (p + 1)]
        both = jnp.stack([
            early * jax.nn.sigmoid(early) * inside_lanes(p) * before,
            later * jax.nn.sigmoid(later) * inside_lanes(p) * beyond,
        ])
        hs[pl.ds(count * gx, 2), 8:8 + across, here] = both
        hd[1, pl.ds(count * gx, 2), :, here] = both.astype(BF16)
        mine = pre_gradient(grad[across * p:across * (p + 1)], jnp.where(gx == 0, later, early), p)
        pg[pl.ds((count - 1) * gx, 1), :, here] = mine.astype(BF16)[None]

    @pl.when(gx == 0)
    def _():
        shift_rows(hs.at[0:2], hd, 0, 0, (0, 2))
        store_blocks(send, sums_of([acc[t] + late for t, late in enumerate(second_late(hd, cd))]))

    @pl.when(gx != 0)
    def _():
        store_blocks(send, sums_of([acc[t] + late for t, late in enumerate(first_late(fd, pg))]))


def keep_sums(fd, cd, hd_in, pg, hs, hd, keep):
    gx = lax.axis_index("gx")

    @pl.when(gx == 0)
    def _():
        store_blocks(keep, sums_of(first_products(fd, pg)))

    @pl.when(gx != 0)
    def _():
        shift_rows(hs, hd, 0, 0, (0, 2))
        store_blocks(keep, sums_of(second_products(hd, cd)))


def output_conv(hd, w2, mine, given, w2b):
    for t, (dx, dy) in enumerate(TAPS):
        w2b[t * 4 * C:(t + 1) * 4 * C, :] = band([w2[9 * dx + 3 * dy + z] for z in range(3)])
    gx = lax.axis_index("gx")
    count, half, _ = mine.shape
    lane = 2 * C
    for p in range(NZ // 2):
        here = slice(lane * p, lane * (p + 1))
        value = dot(windows(hd, 0, count, p), w2b[...]).reshape(count, 2 * half, lane)
        left, right = value[:, 0:half], value[:, half:]
        mine[:, :, here] = jnp.where(gx == 0, left, right).astype(BF16)
        given[:, :, here] = jnp.where(gx == 0, right, left).astype(BF16)


def finish_output(mine, other, out, turned, scratch, sems):
    count, nx, width = mine.shape
    gx = lax.axis_index("gx")
    for y in range(count):
        a = mine[y].astype(F32)
        b = other[y].astype(F32)
        put_rows(scratch, y * nx, jnp.where(gx == 0, a, b))
        put_rows(scratch, (count + y) * nx, jnp.where(gx == 0, b, a))
    copies = []
    for x in range(nx):
        turned[x] = take_rows(scratch, x, 2 * count, nx)
        if x % 2:
            copies.append(pltpu.make_async_copy(turned.at[x - 1:x + 1], out.at[x - 1:x + 1], sems.at[x // 2]))
            copies[-1].start()
    for copy in copies:
        copy.wait()


def add_pair(keep, other, out):
    out[...] = (keep[...] + other[...].astype(F32)).astype(BF16)


def add_and_repeat(terms, out):
    total = terms[0].astype(F32)
    for index in range(1, terms.shape[0]):
        total = total + terms[index].astype(F32)
    total = total.astype(BF16)
    for index in range(out.shape[0]):
        out[index] = total


def unpack(factor, rows, held):
    for t, (dx, dy) in enumerate(TAPS):
        turned = rows[t * C:(t + 1) * C, :].astype(F32).T * factor
        held[9 * dx + 3 * dy] = turned[0:C]
        held[9 * dx + 3 * dy + 1] = turned[C:2 * C]
    for pair in range(5):
        turned = rows[(9 + pair) * C:(10 + pair) * C, :].astype(F32).T * factor
        for half in range(2 if pair < 4 else 1):
            dx, dy = TAPS[2 * pair + half]
            held[9 * dx + 3 * dy + 2] = turned[half * C:(half + 1) * C]


def write_either(is_first, held, first, second, sem):
    for chosen, target in ((is_first, first), (jnp.logical_not(is_first), second)):
        @pl.when(chosen)
        def _():
            copy = pltpu.make_async_copy(held, target, sem.at[0])
            copy.start()
            copy.wait()


def unpack_own(factor, rows, first, second, held, sem):
    unpack(factor, rows, held)
    write_either(lax.axis_index("gx") == 0, held, first, second, sem)


def unpack_other(factor, rows, first_in, second_in, first, second, held, sem):
    unpack(factor, rows, held)
    write_either(lax.axis_index("gx") != 0, held, first, second, sem)


def near(shape, dtype):
    return pltpu.VMEM(shape, dtype)


def call(body, name, inputs, outs, scratch=(), limit=16, flops=0, far=False, aliases=None):
    placed = [pltpu.with_memory_space_constraint(x, pltpu.VMEM if held else pltpu.HBM) for x, held in inputs]
    size = sum(x.size * x.dtype.itemsize for x, _ in inputs)
    return pl.pallas_call(
        body,
        out_shape=list(outs),
        in_specs=[pl.BlockSpec(memory_space=pltpu.VMEM if held else pl.ANY) for _, held in inputs],
        out_specs=[pl.BlockSpec(memory_space=pl.ANY if far else pltpu.VMEM)] * len(outs),
        scratch_shapes=list(scratch),
        input_output_aliases=aliases or {},
        compiler_params=pltpu.CompilerParams(vmem_limit_bytes=limit * 1024 * 1024),
        cost_estimate=pl.CostEstimate(flops=flops, bytes_accessed=size, transcendentals=0),
        name=name,
    )(*placed)


def shards(field_in, first_weight, second_weight, cotangent):
    nx, ny, width = field_in.shape[1:]
    gx_count, gy_count, grp_count = (lax.axis_size(axis) for axis in ("gx", "gy", "grp"))
    total = field_in.shape[0] * nx * ny * NZ * gx_count * gy_count * grp_count
    factor = 1.0 / math.sqrt(total)
    ranks = gy_count * grp_count
    rows = -(-BLOCKS * C // (8 * ranks)) * 8 * ranks
    lane = 2 * C
    wide = width + 2 * lane
    count = ny // 2
    across = 2 * nx
    size = 2 * count + 3

    field, cot, edge, given, w1, w2 = call(
        pack_edges, "pack_edges",
        [(x, False) for x in (field_in[0], cotangent[0], first_weight.reshape(27, C, C), second_weight.reshape(27, C, C))],
        [
            near((nx, ny, width), BF16),
            near((nx, ny, width), BF16),
            near((3, nx, width), BF16),
            near((3, nx, width), BF16),
            near((27, C, C), BF16),
            near((27, C, C), BF16),
        ],
        [pltpu.VMEM((6, nx, width), F32), pltpu.SemaphoreType.DMA((4,))])
    taken = swap(given)
    own, bulk, w1b, wfb = call(
        pack_halves, "pack_halves", [(x, True) for x in (field, cot, w1, w2)],
        [
            near((size, nx, width), BF16),
            near((size, nx, width), BF16),
            near((9 * 4 * C, lane), BF16),
            near((lane, 9 * 4 * C), BF16),
        ],
        [pltpu.VMEM((width // lane, nx * ny, lane), F32)] * 2, flops=10 ** 9)
    bulk, taken, wfb = lax.optimization_barrier((bulk, taken, wfb))
    got = swap(bulk)
    whole, = call(join_edges, "join_edges", [(edge, True), (taken, True)], [near((3, across, width), BF16)])
    ends = [(gy_count + j, j + 1) for j in range(gy_count - 1)]
    late = lax.ppermute(whole, ("gx", "gy"), ends + [(b, a) for a, b in ends])
    held = [
        near((3, count + 4, across, wide), BF16),
        near((3, count + 2, across, wide), BF16),
        near((3, count + 2, across, width + lane), BF16),
        near((count, across, width + lane), BF16),
        near((count + 2, across + 16, width + lane), F32),
    ]
    fd, cd, hd, pg, hs, acc = call(
        interior, "interior",
        [(x, True) for x in (own, got, w1b, wfb)],
        held + [near((9, lane, 2 * lane), F32)],
        [
            pltpu.VMEM((count + 2, across + 16, width), F32),
            pltpu.VMEM((count + 1, across + 16, width), F32),
            pltpu.VMEM((count, across, width + lane), F32),
        ],
        limit=32, flops=4 * 10 ** 9)
    fd, cd, hd, pg, hs, send = call(
        functools.partial(late_rows, gy_count), "late_rows",
        [(x, True) for x in (fd, cd, hd, pg, hs, late, acc, w1b, wfb)],
        held + [near((rows, lane), BF16)],
        [pltpu.VMEM((3, across + 16, width), F32)],
        limit=32, flops=10 ** 9, aliases={0: 0, 1: 1, 2: 2, 3: 3, 4: 4})

    other = swap(send)
    hd, keep = call(
        keep_sums, "keep_sums",
        [(x, True) for x in (fd, cd, hd, pg, hs)], [held[2], near((rows, lane), F32)], flops=2 * 10 ** 9, aliases={2: 0})
    other, keep = lax.optimization_barrier((other, keep))
    both, = call(add_pair, "add_pair", [(keep, True), (other, True)], [near((rows, lane), BF16)])
    terms = lax.all_to_all(both.reshape(ranks, rows // ranks, lane), ("gy", "grp"), 0, 0)
    spread, = call(add_and_repeat, "add_and_repeat", [(terms, True)], [near(terms.shape, BF16)])
    spread, hd, w2 = lax.optimization_barrier((spread, hd, w2))
    sums = lax.all_to_all(spread, ("gy", "grp"), 0, 0).reshape(rows, lane)
    mine, given = call(
        output_conv, "output_conv", [(hd, True), (w2, True)],
        [near((count, nx, width), BF16), near((count, nx, width), BF16)],
        [pltpu.VMEM((9 * 4 * C, lane), BF16)], flops=2 * 10 ** 9)
    given = swap(given)
    out, = call(
        finish_output, "finish_output", [(mine, True), (given, True)],
        [pltpu.HBM((nx, ny, width), BF16)],
        [pltpu.VMEM((nx, ny, width), BF16), pltpu.VMEM((width // lane, nx * ny, lane), F32), pltpu.SemaphoreType.DMA((nx // 2,))], far=True)
    sums, out = lax.optimization_barrier((sums, out))
    other = swap(sums)
    outs = [pltpu.HBM((27, C, C), F32)] * 2
    scratch = [pltpu.VMEM((27, C, C), F32), pltpu.SemaphoreType.DMA((1,))]
    first, second = call(functools.partial(unpack_own, factor), "unpack_own", [(sums, True)], outs, scratch, far=True)
    other, first, second = lax.optimization_barrier((other, first, second))
    first, second = call(
        functools.partial(unpack_other, factor), "unpack_other", [(other, True), (first, False), (second, False)], outs, scratch, far=True,
        aliases={1: 0, 2: 1})
    shape = (3, 3, 3, C, C)
    return out[None], first.reshape(shape), second.reshape(shape)


def solution(mesh):
    return jax.shard_map(
        shards,
        mesh=mesh,
        in_specs=(P("grp", "gx", "gy", None), P(), P(), P("grp", "gx", "gy", None)),
        out_specs=(P("grp", "gx", "gy", None), P(), P()),
        check_vma=False,
    )
```

```python
import functools
import math

import jax
import jax.numpy as jnp
from jax import lax
from jax.experimental import pallas as pl
from jax.experimental.pallas import tpu as pltpu
from jax.sharding import PartitionSpec as P

C = 64
NZ = 16
BF16 = jnp.bfloat16
F32 = jnp.float32
TAPS = [(dx, dy) for dy in range(3) for dx in range(3)]
BLOCKS = 14


def swap(array):
    return lax.ppermute(array, "gx", [(0, 1), (1, 0)])


def dot(a, b):
    return jnp.dot(a, b, preferred_element_type=F32)


def dot_nt(a, b):
    return lax.dot_general(a, b, (((1,), (1,)), ((), ())), preferred_element_type=F32)


def band(taps):
    zero = jnp.zeros((C, C), BF16)
    left = jnp.concatenate(list(taps) + [zero], axis=0)
    right = jnp.concatenate([zero] + list(taps), axis=0)
    return jnp.concatenate([left, right], axis=1)


def band_flipped(taps):
    zero = jnp.zeros((C, C), BF16)
    back = list(taps)[::-1]
    upper = jnp.concatenate(back + [zero], axis=1)
    lower = jnp.concatenate([zero] + back, axis=1)
    return jnp.concatenate([upper, lower], axis=0)


def packed(pieces):
    blocks = [piece[:, 0:2 * C] for piece in pieces]
    for pair in range(0, 9, 2):
        second = pieces[pair + 1][:, 2 * C:3 * C] if pair + 1 < 9 else jnp.zeros((C, C), F32)
        blocks.append(jnp.concatenate([pieces[pair][:, 2 * C:3 * C], second], axis=1))
    return blocks


def pack_edges(field_hbm, cot_hbm, w1_hbm, w2_hbm, field, cot, edge, given, w1, w2, rows, sems):
    copies = [
        pltpu.make_async_copy(source, target, sems.at[index])
        for index, (source, target) in enumerate(((field_hbm, field), (cot_hbm, cot), (w1_hbm, w1), (w2_hbm, w2)))
    ]
    for copy in copies:
        copy.start()
    for copy in copies[:2]:
        copy.wait()
    nx, ny, _ = field.shape
    gx = lax.axis_index("gx")
    for x in range(nx):
        fields = field[x].astype(F32)
        cots = cot[x].astype(F32)
        for index, row in enumerate((fields[0:1], fields[1:2], cots[0:1], fields[ny - 2:ny - 1], fields[ny - 1:ny], cots[ny - 1:ny])):
            rows[index, x:x + 1, :] = row
    head = rows[0:3].astype(BF16)
    tail = rows[3:6].astype(BF16)
    edge[...] = jnp.where(gx == 0, head, tail)
    given[...] = jnp.where(gx == 0, tail, head)
    for copy in copies[2:]:
        copy.wait()


def join_edges(edge, taken, whole):
    nx = edge.shape[1]
    gx = lax.axis_index("gx")

    @pl.when(gx == 0)
    def _():
        whole[:, 0:nx] = edge[...]
        whole[:, nx:2 * nx] = taken[...]

    @pl.when(gx != 0)
    def _():
        whole[:, 0:nx] = taken[...]
        whole[:, nx:2 * nx] = edge[...]


def put_rows(scratch, start, rows):
    lane = 2 * C
    for tile in range(scratch.shape[0]):
        scratch[tile, start:start + rows.shape[0], :] = rows[:, lane * tile:lane * (tile + 1)]


def take_rows(scratch, start, count, stride):
    return jnp.concatenate(
        [scratch[tile, pl.ds(start, count, stride=stride), :] for tile in range(scratch.shape[0])], axis=1).astype(BF16)


def pack_halves(field, cot, w1, w2, own, bulk, w1b, wfb, turned_f, turned_c):
    nx, ny, _ = field.shape
    half = ny // 2
    for source, target in ((field, turned_f), (cot, turned_c)):
        for x in range(nx):
            put_rows(target, x * ny, source[x].astype(F32))
    gx = lax.axis_index("gx")

    def place(target, first_f, first_c):
        for y in range(half + 2):
            target[y] = take_rows(turned_f, first_f + y, nx, ny)
        for y in range(half + 1):
            target[half + 2 + y] = take_rows(turned_c, first_c + y, nx, ny)

    @pl.when(gx == 0)
    def _():
        place(own, 0, 0)
        place(bulk, half - 2, half - 1)

    @pl.when(gx != 0)
    def _():
        place(own, half - 2, half - 1)
        place(bulk, 0, 0)

    make_bands(w1, w2, w1b, wfb)


def make_bands(w1, w2, w1b, wfb):
    for t, (dx, dy) in enumerate(TAPS):
        rows = slice(t * 4 * C, (t + 1) * 4 * C)
        first = 9 * dx + 3 * dy
        w1b[rows, :] = band([w1[first + z] for z in range(3)])
        wfb[:, rows] = band_flipped([w2[24 - first + z] for z in range(3)])


def blank_edges(copies):
    lane = 2 * C
    zero = jnp.zeros(copies.shape[:-1] + (lane,), BF16)
    copies[..., 0:lane] = zero
    copies[..., copies.shape[-1] - lane:] = zero


def blank_rows(scratch):
    zero = jnp.zeros((scratch.shape[0], 1, scratch.shape[2]), F32)
    scratch[:, 7:8, :] = zero
    scratch[:, scratch.shape[1] - 8:scratch.shape[1] - 7, :] = zero


def shift_rows(scratch, copies, start, first_lane, taps=(0, 1, 2)):
    count, rows, width = scratch.shape
    for dx in taps:
        copies[dx, pl.ds(start, count), :, first_lane:first_lane + width] = scratch[:, 7 + dx:rows - 9 + dx, :].astype(BF16)


def inside_lanes(p):
    lane_of = lax.broadcasted_iota(jnp.int32, (1, 2 * C), 1)
    if p == 0:
        return (lane_of >= C).astype(F32)
    if p == NZ // 2:
        return (lane_of < C).astype(F32)
    return 1.0


def windows(copies, first, count, p):
    lane = 2 * C
    rows = copies.shape[2]
    return jnp.concatenate(
        [
            copies[dx, pl.ds(first + dy, count), :, lane * p:lane * (p + 2)].reshape(count * rows, 2 * lane)
            for dx, dy in TAPS
        ],
        axis=1,
    )


def pre_gradient(grad, pre, p):
    sigma = jax.nn.sigmoid(pre)
    return grad * sigma * (1.0 + pre * (1.0 - sigma)) * inside_lanes(p)


def interior(own, got, w1b, wfb, fd, cd, hd, pg, hs, acc, fs, cs, pre):
    gx = lax.axis_index("gx")
    nx, width = own.shape[1:]
    across = 2 * nx
    count = pg.shape[0]
    cells = count * across
    lane = 2 * C
    pairs = NZ // 2

    def place(left, right):
        for scratch, copies, offset, start, size in ((fs, fd, 2 - 2 * gx, 0, count + 2), (cs, cd, 1 - gx, count + 2, count + 1)):
            for source, row in ((left, 0), (right, nx)):
                rows = source[start:start + size]
                scratch[:, 8 + row:8 + row + nx, :] = rows.astype(F32)
                copies[1, pl.ds(offset, size), row:row + nx, lane:lane + width] = rows

    @pl.when(gx == 0)
    def _():
        place(own, got)

    @pl.when(gx != 0)
    def _():
        place(got, own)

    for scratch in (fs, cs, hs):
        blank_rows(scratch)
    blank_edges(fd)
    blank_edges(cd)
    shift_rows(fs, fd, 2 - 2 * gx, lane, (0, 2))
    shift_rows(cs, cd, 1 - gx, lane, (0, 2))
    for group in range(0, pairs + 1, 3):
        value = dot(jnp.concatenate([windows(fd, 2 - 2 * gx, count, p) for p in range(group, group + 3)], axis=0), w1b[...])
        for p in range(group, group + 3):
            here = slice(lane * p, lane * (p + 1))
            part = value[cells * (p - group):cells * (p - group + 1)]
            pre[:, :, here] = part.reshape(count, across, lane)
            hidden = (part * jax.nn.sigmoid(part) * inside_lanes(p)).reshape(count, across, lane)
            hs[pl.ds(2 - 2 * gx, count), 8:8 + across, here] = hidden
            hd[1, pl.ds(2 - 2 * gx, count), :, here] = hidden.astype(BF16)
    cells = cells - across
    for group in range(0, pairs + 1, 3):
        value = dot_nt(jnp.concatenate([windows(cd, 1 - gx, count - 1, p) for p in range(group, group + 3)], axis=0), wfb[...])
        for p in range(group, group + 3):
            here = slice(lane * p, lane * (p + 1))
            part = value[cells * (p - group):cells * (p - group + 1)]
            grad = pre_gradient(part, pre[pl.ds(gx, count - 1), :, here].reshape(cells, lane), p)
            pg[pl.ds(1 - gx, count - 1), :, here] = grad.astype(BF16).reshape(count - 1, across, lane)
    pg[pl.ds((count - 1) * gx, 1)] = jnp.zeros((1,) + pg.shape[1:], BF16)

    @pl.when(gx == 0)
    def _():
        hd[:, 0:2] = jnp.zeros((3, 2) + hd.shape[2:], BF16)
        shift_rows(hs.at[2:2 + count], hd, 2, 0, (0, 2))
        for t, total in enumerate(second_products(hd, cd)):
            acc[t] = total

    @pl.when(gx != 0)
    def _():
        for t, total in enumerate(first_products(fd, pg)):
            acc[t] = total


def second_products(hd, cd):
    lane = 2 * C
    pairs = NZ // 2
    count, across = hd.shape[1] - 2, hd.shape[2]
    cells = count * across
    cot_t = jnp.concatenate(
        [cd[1, 1:1 + count, :, lane * (p + 1):lane * (p + 2)].reshape(cells, lane).T for p in range(pairs)], axis=1)
    return [
        dot(cot_t, jnp.concatenate(
            [hd[dx, dy:dy + count, :, lane * p:lane * (p + 2)].reshape(cells, 2 * lane) for p in range(pairs)], axis=0))
        for dx, dy in TAPS
    ]


def first_products(fd, pg):
    lane = 2 * C
    pairs = NZ // 2
    count, across, _ = pg.shape
    cells = count * across
    grad_t = jnp.concatenate(
        [pg[:, :, lane * p:lane * (p + 1)].reshape(cells, lane).T for p in range(pairs + 1)], axis=1)
    return [
        dot(grad_t, jnp.concatenate(
            [fd[dx, 1 + dy:1 + dy + count, :, lane * p:lane * (p + 2)].reshape(cells, 2 * lane) for p in range(pairs + 1)], axis=0))
        for dx, dy in TAPS
    ]


def folded(total):
    return total[0:C, 0:3 * C] + total[C:2 * C, C:4 * C]


def second_late(hd, cd):
    lane = 2 * C
    pairs = NZ // 2
    late = ((0, 1), (0,), ())
    products = []
    for dx, dy in TAPS:
        if late[dy]:
            cots = jnp.concatenate(
                [cd[1, 1 + y, :, lane * (p + 1):lane * (p + 2)] for y in late[dy] for p in range(pairs)], axis=0)
            rows = jnp.concatenate(
                [hd[dx, y + dy, :, lane * p:lane * (p + 2)] for y in late[dy] for p in range(pairs)], axis=0)
            products.append(dot(cots.T, rows))
        else:
            products.append(0.0)
    return products


def first_late(fd, pg):
    lane = 2 * C
    pairs = NZ // 2
    count, across, _ = pg.shape
    y = count - 1
    extra = 2 * lane - (pairs + 1) * across
    grad_t = jnp.concatenate(
        [pg[y, :, lane * p:lane * (p + 1)] for p in range(pairs + 1)] + [jnp.zeros((extra, lane), BF16)], axis=0).T
    pad = jnp.zeros((extra, 2 * lane), BF16)
    return [
        dot(grad_t, jnp.concatenate(
            [fd[dx, y + dy + 1, :, lane * p:lane * (p + 2)] for p in range(pairs + 1)] + [pad], axis=0))
        for dx, dy in TAPS
    ]


def sums_of(products):
    return packed([folded(product) for product in products])


def store_blocks(target, blocks):
    for index, block in enumerate(blocks):
        target[index * C:(index + 1) * C, :] = block.astype(target.dtype)
    if target.shape[0] > BLOCKS * C:
        target[BLOCKS * C:, :] = jnp.zeros((target.shape[0] - BLOCKS * C, 2 * C), target.dtype)


def hidden_of(value, p):
    return value * jax.nn.sigmoid(value) * inside_lanes(p)


def stacked(copies, first, count, pairs):
    return jnp.concatenate([windows(copies, first, count, p) for p in range(pairs + 1)], axis=0)


def late_rows(gy_count, fd_in, cd_in, hd_in, pg_in, hs_in, rows, acc, w1b, wfb, fd, cd, hd, pg, hs, send, pre_late, rs):
    gx = lax.axis_index("gx")
    gy = lax.axis_index("gy")
    count, across, _ = pg.shape
    lane = 2 * C
    pairs = NZ // 2
    rs[:, 8:8 + across, :] = rows[...].astype(F32)
    blank_rows(rs)

    @pl.when(gx == 0)
    def _():
        shift_rows(rs.at[0:2], fd, 0, lane)
        shift_rows(rs.at[2:3], cd, 0, lane)
        value = dot(stacked(fd, 0, 2, pairs), w1b[...])
        before = jnp.where(gy == 0, 0.0, 1.0)
        for p in range(pairs + 1):
            here = slice(lane * p, lane * (p + 1))
            early = value[2 * across * p:2 * across * p + across]
            later = value[2 * across * p + across:2 * across * (p + 1)]
            pre_late[:, here] = later
            both = jnp.stack([hidden_of(early, p) * before, hidden_of(later, p)])
            hs[0:2, 8:8 + across, here] = both
            hd[1, 0:2, :, here] = both.astype(BF16)
        shift_rows(hs.at[0:2], hd, 0, 0, (0, 2))
        store_blocks(send, sums_of([acc[t] + late for t, late in enumerate(second_late(hd, cd))]))

    @pl.when(gx != 0)
    def _():
        shift_rows(rs.at[0:2], fd, count + 2, lane)
        shift_rows(rs.at[2:3], cd, count + 1, lane)
        value = dot(stacked(fd, count, 1, pairs), w1b[...])
        grad = dot_nt(stacked(cd, count - 1, 1, pairs), wfb[...])
        for p in range(pairs + 1):
            here = slice(lane * p, lane * (p + 1))
            part = slice(across * p, across * (p + 1))
            pre_late[:, here] = value[part]
            pg[count - 1, :, here] = pre_gradient(grad[part], value[part], p).astype(BF16)
        store_blocks(send, sums_of([acc[t] + late for t, late in enumerate(first_late(fd, pg))]))


def keep_sums(gy_count, fd, cd, hd_in, pg_in, hs_in, pre_late, w1b, wfb, hd, pg, hs, keep):
    gx = lax.axis_index("gx")
    gy = lax.axis_index("gy")
    count, across, _ = pg.shape
    lane = 2 * C
    pairs = NZ // 2

    @pl.when(gx == 0)
    def _():
        grad = dot_nt(stacked(cd, 0, 1, pairs), wfb[...])
        for p in range(pairs + 1):
            here = slice(lane * p, lane * (p + 1))
            part = slice(across * p, across * (p + 1))
            pg[0, :, here] = pre_gradient(grad[part], pre_late[:, here], p).astype(BF16)
        store_blocks(keep, sums_of(first_products(fd, pg)))

    @pl.when(gx != 0)
    def _():
        value = dot(stacked(fd, count + 1, 1, pairs), w1b[...])
        beyond = jnp.where(gy == gy_count - 1, 0.0, 1.0)
        for p in range(pairs + 1):
            here = slice(lane * p, lane * (p + 1))
            part = slice(across * p, across * (p + 1))
            both = jnp.stack([hidden_of(pre_late[:, here], p), hidden_of(value[part], p) * beyond])
            hs[count:count + 2, 8:8 + across, here] = both
            hd[1, count:count + 2, :, here] = both.astype(BF16)
        shift_rows(hs, hd, 0, 0, (0, 2))
        store_blocks(keep, sums_of(second_products(hd, cd)))


def output_conv(hd, w2, mine, given, w2b):
    for t, (dx, dy) in enumerate(TAPS):
        w2b[t * 4 * C:(t + 1) * 4 * C, :] = band([w2[9 * dx + 3 * dy + z] for z in range(3)])
    gx = lax.axis_index("gx")
    count, half, _ = mine.shape
    lane = 2 * C
    for p in range(NZ // 2):
        here = slice(lane * p, lane * (p + 1))
        value = dot(windows(hd, 0, count, p), w2b[...]).reshape(count, 2 * half, lane)
        left, right = value[:, 0:half], value[:, half:]
        mine[:, :, here] = jnp.where(gx == 0, left, right).astype(BF16)
        given[:, :, here] = jnp.where(gx == 0, right, left).astype(BF16)


def finish_output(mine, other, out, turned, scratch, sems):
    count, nx, width = mine.shape
    gx = lax.axis_index("gx")
    for y in range(count):
        a = mine[y].astype(F32)
        b = other[y].astype(F32)
        put_rows(scratch, y * nx, jnp.where(gx == 0, a, b))
        put_rows(scratch, (count + y) * nx, jnp.where(gx == 0, b, a))
    copies = []
    for x in range(nx):
        turned[x] = take_rows(scratch, x, 2 * count, nx)
        if x % 2:
            copies.append(pltpu.make_async_copy(turned.at[x - 1:x + 1], out.at[x - 1:x + 1], sems.at[x // 2]))
            copies[-1].start()
    for copy in copies:
        copy.wait()


def add_pair(keep, other, out):
    out[...] = (keep[...] + other[...].astype(F32)).astype(BF16)


def add_and_repeat(terms, out):
    total = terms[0].astype(F32)
    for index in range(1, terms.shape[0]):
        total = total + terms[index].astype(F32)
    total = total.astype(BF16)
    for index in range(out.shape[0]):
        out[index] = total


def unpack(factor, is_first, rows, first, second, held, sems):
    def each(act):
        for chosen, target in ((is_first, first), (jnp.logical_not(is_first), second)):
            @pl.when(chosen)
            def _():
                act(target)

    def copy_of(dx, target):
        piece = slice(9 * dx, 9 * dx + 9)
        return pltpu.make_async_copy(held.at[piece], target.at[piece], sems.at[dx])

    for dx in range(3):
        for dy in range(3):
            t = 3 * dy + dx
            place = 9 * dx + 3 * dy
            turned = rows[t * C:(t + 1) * C, :].astype(F32).T * factor
            held[place] = turned[0:C]
            held[place + 1] = turned[C:2 * C]
            turned = rows[(9 + t // 2) * C:(10 + t // 2) * C, :].astype(F32).T * factor
            held[place + 2] = turned[t % 2 * C:(t % 2 + 1) * C]
        each(lambda target: copy_of(dx, target).start())
    each(lambda target: [copy_of(dx, target).wait() for dx in range(3)])


def unpack_own(factor, rows, first, second, held, sems):
    unpack(factor, lax.axis_index("gx") == 0, rows, first, second, held, sems)


def unpack_other(factor, rows, first_in, second_in, first, second, held, sems):
    unpack(factor, lax.axis_index("gx") != 0, rows, first, second, held, sems)


def near(shape, dtype):
    return pltpu.VMEM(shape, dtype)


def call(body, name, inputs, outs, scratch=(), limit=16, flops=0, far=False, aliases=None):
    placed = [pltpu.with_memory_space_constraint(x, pltpu.VMEM if held else pltpu.HBM) for x, held in inputs]
    size = sum(x.size * x.dtype.itemsize for x, _ in inputs)
    return pl.pallas_call(
        body,
        out_shape=list(outs),
        in_specs=[pl.BlockSpec(memory_space=pltpu.VMEM if held else pl.ANY) for _, held in inputs],
        out_specs=[pl.BlockSpec(memory_space=pl.ANY if far else pltpu.VMEM)] * len(outs),
        scratch_shapes=list(scratch),
        input_output_aliases=aliases or {},
        compiler_params=pltpu.CompilerParams(vmem_limit_bytes=limit * 1024 * 1024),
        cost_estimate=pl.CostEstimate(flops=flops, bytes_accessed=size, transcendentals=0),
        name=name,
    )(*placed)


def shards(field_in, first_weight, second_weight, cotangent):
    nx, ny, width = field_in.shape[1:]
    gx_count, gy_count, grp_count = (lax.axis_size(axis) for axis in ("gx", "gy", "grp"))
    total = field_in.shape[0] * nx * ny * NZ * gx_count * gy_count * grp_count
    factor = 1.0 / math.sqrt(total)
    ranks = gy_count * grp_count
    rows = -(-BLOCKS * C // (8 * ranks)) * 8 * ranks
    lane = 2 * C
    wide = width + 2 * lane
    count = ny // 2
    across = 2 * nx
    size = 2 * count + 3

    field, cot, edge, given, w1, w2 = call(
        pack_edges, "pack_edges",
        [(x, False) for x in (field_in[0], cotangent[0], first_weight.reshape(27, C, C), second_weight.reshape(27, C, C))],
        [
            near((nx, ny, width), BF16),
            near((nx, ny, width), BF16),
            near((3, nx, width), BF16),
            near((3, nx, width), BF16),
            near((27, C, C), BF16),
            near((27, C, C), BF16),
        ],
        [pltpu.VMEM((6, nx, width), F32), pltpu.SemaphoreType.DMA((4,))])
    taken = swap(given)
    own, bulk, w1b, wfb = call(
        pack_halves, "pack_halves", [(x, True) for x in (field, cot, w1, w2)],
        [
            near((size, nx, width), BF16),
            near((size, nx, width), BF16),
            near((9 * 4 * C, lane), BF16),
            near((lane, 9 * 4 * C), BF16),
        ],
        [pltpu.VMEM((width // lane, nx * ny, lane), F32)] * 2, flops=10 ** 9)
    bulk, taken, wfb = lax.optimization_barrier((bulk, taken, wfb))
    got = swap(bulk)
    whole, = call(join_edges, "join_edges", [(edge, True), (taken, True)], [near((3, across, width), BF16)])
    ends = [(gy_count + j, j + 1) for j in range(gy_count - 1)]
    late = lax.ppermute(whole, ("gx", "gy"), ends + [(b, a) for a, b in ends])
    held = [
        near((3, count + 4, across, wide), BF16),
        near((3, count + 2, across, wide), BF16),
        near((3, count + 2, across, width + lane), BF16),
        near((count, across, width + lane), BF16),
        near((count + 2, across + 16, width + lane), F32),
    ]
    fd, cd, hd, pg, hs, acc = call(
        interior, "interior",
        [(x, True) for x in (own, got, w1b, wfb)],
        held + [near((9, lane, 2 * lane), F32)],
        [
            pltpu.VMEM((count + 2, across + 16, width), F32),
            pltpu.VMEM((count + 1, across + 16, width), F32),
            pltpu.VMEM((count, across, width + lane), F32),
        ],
        limit=32, flops=4 * 10 ** 9)
    fd, cd, hd, pg, hs, send, pre_late = call(
        functools.partial(late_rows, gy_count), "late_rows",
        [(x, True) for x in (fd, cd, hd, pg, hs, late, acc, w1b, wfb)],
        held + [near((rows, lane), BF16), near((across, width + lane), F32)],
        [pltpu.VMEM((3, across + 16, width), F32)],
        limit=32, flops=10 ** 9, aliases={0: 0, 1: 1, 2: 2, 3: 3, 4: 4})

    other = swap(send)
    hd, _, _, keep = call(
        functools.partial(keep_sums, gy_count), "keep_sums",
        [(x, True) for x in (fd, cd, hd, pg, hs, pre_late, w1b, wfb)], held[2:] + [near((rows, lane), F32)],
        flops=2 * 10 ** 9, aliases={2: 0, 3: 1, 4: 2})
    other, keep = lax.optimization_barrier((other, keep))
    both, = call(add_pair, "add_pair", [(keep, True), (other, True)], [near((rows, lane), BF16)])
    terms = lax.all_to_all(both.reshape(ranks, rows // ranks, lane), ("gy", "grp"), 0, 0)
    spread, = call(add_and_repeat, "add_and_repeat", [(terms, True)], [near(terms.shape, BF16)])
    spread, hd, w2 = lax.optimization_barrier((spread, hd, w2))
    sums = lax.all_to_all(spread, ("gy", "grp"), 0, 0).reshape(rows, lane)
    mine, given = call(
        output_conv, "output_conv", [(hd, True), (w2, True)],
        [near((count, nx, width), BF16), near((count, nx, width), BF16)],
        [pltpu.VMEM((9 * 4 * C, lane), BF16)], flops=2 * 10 ** 9)
    given = swap(given)
    out, = call(
        finish_output, "finish_output", [(mine, True), (given, True)],
        [pltpu.HBM((nx, ny, width), BF16)],
        [pltpu.VMEM((nx, ny, width), BF16), pltpu.VMEM((width // lane, nx * ny, lane), F32), pltpu.SemaphoreType.DMA((nx // 2,))], far=True)
    sums, out = lax.optimization_barrier((sums, out))
    other = swap(sums)
    outs = [pltpu.HBM((27, C, C), F32)] * 2
    scratch = [pltpu.VMEM((27, C, C), F32), pltpu.SemaphoreType.DMA((3,))]
    first, second = call(functools.partial(unpack_own, factor), "unpack_own", [(sums, True)], outs, scratch, far=True)
    other, first, second = lax.optimization_barrier((other, first, second))
    first, second = call(
        functools.partial(unpack_other, factor), "unpack_other", [(other, True), (first, False), (second, False)], outs, scratch, far=True,
        aliases={1: 0, 2: 1})
    shape = (3, 3, 3, C, C)
    return out[None], first.reshape(shape), second.reshape(shape)


def solution(mesh):
    return jax.shard_map(
        shards,
        mesh=mesh,
        in_specs=(P("grp", "gx", "gy", None), P(), P(), P("grp", "gx", "gy", None)),
        out_specs=(P("grp", "gx", "gy", None), P(), P()),
        check_vma=False,
    )
```

```python
import functools
import math

import jax
import jax.numpy as jnp
from jax import lax
from jax.experimental import pallas as pl
from jax.experimental.pallas import tpu as pltpu
from jax.sharding import PartitionSpec as P

C = 64
NZ = 16
BF16 = jnp.bfloat16
F32 = jnp.float32
TAPS = [(dx, dy) for dy in range(3) for dx in range(3)]
BLOCKS = 14


def swap(array):
    return lax.ppermute(array, "gx", [(0, 1), (1, 0)])


def dot(a, b):
    return jnp.dot(a, b, preferred_element_type=F32)


def dot_nt(a, b):
    return lax.dot_general(a, b, (((1,), (1,)), ((), ())), preferred_element_type=F32)


def band(taps):
    zero = jnp.zeros((C, C), BF16)
    left = jnp.concatenate(list(taps) + [zero], axis=0)
    right = jnp.concatenate([zero] + list(taps), axis=0)
    return jnp.concatenate([left, right], axis=1)


def band_flipped(taps):
    zero = jnp.zeros((C, C), BF16)
    back = list(taps)[::-1]
    upper = jnp.concatenate(back + [zero], axis=1)
    lower = jnp.concatenate([zero] + back, axis=1)
    return jnp.concatenate([upper, lower], axis=0)


def packed(pieces):
    blocks = [piece[:, 0:2 * C] for piece in pieces]
    for pair in range(0, 9, 2):
        second = pieces[pair + 1][:, 2 * C:3 * C] if pair + 1 < 9 else jnp.zeros((C, C), F32)
        blocks.append(jnp.concatenate([pieces[pair][:, 2 * C:3 * C], second], axis=1))
    return blocks


def pack_edges(field_hbm, cot_hbm, w1_hbm, w2_hbm, field, cot, edge, given, w1, w2, rows, sems):
    copies = [
        pltpu.make_async_copy(source, target, sems.at[index])
        for index, (source, target) in enumerate(((field_hbm, field), (cot_hbm, cot), (w1_hbm, w1), (w2_hbm, w2)))
    ]
    for copy in copies:
        copy.start()
    for copy in copies[:2]:
        copy.wait()
    nx, ny, _ = field.shape
    gx = lax.axis_index("gx")
    for x in range(nx):
        fields = field[x].astype(F32)
        cots = cot[x].astype(F32)
        for index, row in enumerate((fields[0:1], fields[1:2], cots[0:1], fields[ny - 2:ny - 1], fields[ny - 1:ny], cots[ny - 1:ny])):
            rows[index, x:x + 1, :] = row
    head = rows[0:3].astype(BF16)
    tail = rows[3:6].astype(BF16)
    edge[...] = jnp.where(gx == 0, head, tail)
    given[...] = jnp.where(gx == 0, tail, head)
    for copy in copies[2:]:
        copy.wait()


def join_edges(edge, taken, whole):
    nx = edge.shape[1]
    gx = lax.axis_index("gx")

    @pl.when(gx == 0)
    def _():
        whole[:, 0:nx] = edge[...]
        whole[:, nx:2 * nx] = taken[...]

    @pl.when(gx != 0)
    def _():
        whole[:, 0:nx] = taken[...]
        whole[:, nx:2 * nx] = edge[...]


def put_rows(scratch, start, rows):
    lane = 2 * C
    for tile in range(scratch.shape[0]):
        scratch[tile, start:start + rows.shape[0], :] = rows[:, lane * tile:lane * (tile + 1)]


def take_rows(scratch, start, count, stride):
    return jnp.concatenate(
        [scratch[tile, pl.ds(start, count, stride=stride), :] for tile in range(scratch.shape[0])], axis=1).astype(BF16)


def pack_halves(field, cot, w1, w2, own, bulk, w1b, wfb, turned_f, turned_c):
    nx, ny, _ = field.shape
    half = ny // 2
    for source, target in ((field, turned_f), (cot, turned_c)):
        for x in range(nx):
            put_rows(target, x * ny, source[x].astype(F32))
    gx = lax.axis_index("gx")

    def place(target, first_f, first_c):
        for y in range(half + 2):
            target[y] = take_rows(turned_f, first_f + y, nx, ny)
        for y in range(half + 1):
            target[half + 2 + y] = take_rows(turned_c, first_c + y, nx, ny)

    @pl.when(gx == 0)
    def _():
        place(own, 0, 0)
        place(bulk, half - 2, half - 1)

    @pl.when(gx != 0)
    def _():
        place(own, half - 2, half - 1)
        place(bulk, 0, 0)

    make_bands(w1, w2, w1b, wfb)


def make_bands(w1, w2, w1b, wfb):
    for t, (dx, dy) in enumerate(TAPS):
        rows = slice(t * 4 * C, (t + 1) * 4 * C)
        first = 9 * dx + 3 * dy
        w1b[rows, :] = band([w1[first + z] for z in range(3)])
        wfb[:, rows] = band_flipped([w2[24 - first + z] for z in range(3)])


def blank_edges(copies):
    lane = 2 * C
    zero = jnp.zeros(copies.shape[:-1] + (lane,), BF16)
    copies[..., 0:lane] = zero
    copies[..., copies.shape[-1] - lane:] = zero


def blank_rows(scratch):
    zero = jnp.zeros((scratch.shape[0], 1, scratch.shape[2]), F32)
    scratch[:, 7:8, :] = zero
    scratch[:, scratch.shape[1] - 8:scratch.shape[1] - 7, :] = zero


def shift_rows(scratch, copies, start, first_lane, taps=(0, 1, 2)):
    count, rows, width = scratch.shape
    for dx in taps:
        copies[dx, pl.ds(start, count), :, first_lane:first_lane + width] = scratch[:, 7 + dx:rows - 9 + dx, :].astype(BF16)


def inside_lanes(p):
    lane_of = lax.broadcasted_iota(jnp.int32, (1, 2 * C), 1)
    if p == 0:
        return (lane_of >= C).astype(F32)
    if p == NZ // 2:
        return (lane_of < C).astype(F32)
    return 1.0


def windows(copies, first, count, p):
    lane = 2 * C
    rows = copies.shape[2]
    return jnp.concatenate(
        [
            copies[dx, pl.ds(first + dy, count), :, lane * p:lane * (p + 2)].reshape(count * rows, 2 * lane)
            for dx, dy in TAPS
        ],
        axis=1,
    )


def pre_gradient(grad, pre, p):
    sigma = jax.nn.sigmoid(pre)
    return grad * sigma * (1.0 + pre * (1.0 - sigma)) * inside_lanes(p)


def interior(own, got, w1b, wfb, fd, cd, hd, pg, hs, acc, fs, cs, pre):
    gx = lax.axis_index("gx")
    nx, width = own.shape[1:]
    across = 2 * nx
    count = pg.shape[0]
    cells = count * across
    lane = 2 * C
    pairs = NZ // 2

    def place(left, right):
        for scratch, copies, offset, start, size in ((fs, fd, 2 - 2 * gx, 0, count + 2), (cs, cd, 1 - gx, count + 2, count + 1)):
            for source, row in ((left, 0), (right, nx)):
                rows = source[start:start + size]
                scratch[:, 8 + row:8 + row + nx, :] = rows.astype(F32)
                copies[1, pl.ds(offset, size), row:row + nx, lane:lane + width] = rows

    @pl.when(gx == 0)
    def _():
        place(own, got)

    @pl.when(gx != 0)
    def _():
        place(got, own)

    for scratch in (fs, cs, hs):
        blank_rows(scratch)
    blank_edges(fd)
    blank_edges(cd)
    shift_rows(fs, fd, 2 - 2 * gx, lane, (0, 2))
    shift_rows(cs, cd, 1 - gx, lane, (0, 2))
    for group in range(0, pairs + 1, 3):
        value = dot(jnp.concatenate([windows(fd, 2 - 2 * gx, count, p) for p in range(group, group + 3)], axis=0), w1b[...])
        for p in range(group, group + 3):
            here = slice(lane * p, lane * (p + 1))
            part = value[cells * (p - group):cells * (p - group + 1)]
            pre[:, :, here] = part.reshape(count, across, lane)
            hidden = (part * jax.nn.sigmoid(part) * inside_lanes(p)).reshape(count, across, lane)
            hs[pl.ds(2 - 2 * gx, count), 8:8 + across, here] = hidden
            hd[1, pl.ds(2 - 2 * gx, count), :, here] = hidden.astype(BF16)
    cells = cells - across
    for group in range(0, pairs + 1, 3):
        value = dot_nt(jnp.concatenate([windows(cd, 1 - gx, count - 1, p) for p in range(group, group + 3)], axis=0), wfb[...])
        for p in range(group, group + 3):
            here = slice(lane * p, lane * (p + 1))
            part = value[cells * (p - group):cells * (p - group + 1)]
            grad = pre_gradient(part, pre[pl.ds(gx, count - 1), :, here].reshape(cells, lane), p)
            pg[pl.ds(1 - gx, count - 1), :, here] = grad.astype(BF16).reshape(count - 1, across, lane)
    pg[pl.ds((count - 1) * gx, 1)] = jnp.zeros((1,) + pg.shape[1:], BF16)

    @pl.when(gx == 0)
    def _():
        hd[:, 0:2] = jnp.zeros((3, 2) + hd.shape[2:], BF16)
        shift_rows(hs.at[2:2 + count], hd, 2, 0, (0, 2))
        for t, total in enumerate(second_products(hd, cd)):
            acc[t] = total

    @pl.when(gx != 0)
    def _():
        for t, total in enumerate(first_products(fd, pg)):
            acc[t] = total


def second_products(hd, cd):
    lane = 2 * C
    pairs = NZ // 2
    count, across = hd.shape[1] - 2, hd.shape[2]
    cells = count * across
    cot_t = jnp.concatenate(
        [cd[1, 1:1 + count, :, lane * (p + 1):lane * (p + 2)].reshape(cells, lane).T for p in range(pairs)], axis=1)
    return [
        dot(cot_t, jnp.concatenate(
            [hd[dx, dy:dy + count, :, lane * p:lane * (p + 2)].reshape(cells, 2 * lane) for p in range(pairs)], axis=0))
        for dx, dy in TAPS
    ]


def first_products(fd, pg):
    lane = 2 * C
    pairs = NZ // 2
    count, across, _ = pg.shape
    cells = count * across
    grad_t = jnp.concatenate(
        [pg[:, :, lane * p:lane * (p + 1)].reshape(cells, lane).T for p in range(pairs + 1)], axis=1)
    return [
        dot(grad_t, jnp.concatenate(
            [fd[dx, 1 + dy:1 + dy + count, :, lane * p:lane * (p + 2)].reshape(cells, 2 * lane) for p in range(pairs + 1)], axis=0))
        for dx, dy in TAPS
    ]


def folded(total):
    return total[0:C, 0:3 * C] + total[C:2 * C, C:4 * C]


def second_late(hd, cd):
    lane = 2 * C
    pairs = NZ // 2
    late = ((0, 1), (0,), ())
    products = []
    for dx, dy in TAPS:
        if late[dy]:
            cots = jnp.concatenate(
                [cd[1, 1 + y, :, lane * (p + 1):lane * (p + 2)] for y in late[dy] for p in range(pairs)], axis=0)
            rows = jnp.concatenate(
                [hd[dx, y + dy, :, lane * p:lane * (p + 2)] for y in late[dy] for p in range(pairs)], axis=0)
            products.append(dot(cots.T, rows))
        else:
            products.append(0.0)
    return products


def first_late(fd, pg):
    lane = 2 * C
    pairs = NZ // 2
    count, across, _ = pg.shape
    y = count - 1
    extra = 2 * lane - (pairs + 1) * across
    grad_t = jnp.concatenate(
        [pg[y, :, lane * p:lane * (p + 1)] for p in range(pairs + 1)] + [jnp.zeros((extra, lane), BF16)], axis=0).T
    pad = jnp.zeros((extra, 2 * lane), BF16)
    return [
        dot(grad_t, jnp.concatenate(
            [fd[dx, y + dy + 1, :, lane * p:lane * (p + 2)] for p in range(pairs + 1)] + [pad], axis=0))
        for dx, dy in TAPS
    ]


def sums_of(products):
    return packed([folded(product) for product in products])


def store_blocks(target, blocks):
    for index, block in enumerate(blocks):
        target[index * C:(index + 1) * C, :] = block.astype(target.dtype)
    if target.shape[0] > BLOCKS * C:
        target[BLOCKS * C:, :] = jnp.zeros((target.shape[0] - BLOCKS * C, 2 * C), target.dtype)


def hidden_of(value, p):
    return value * jax.nn.sigmoid(value) * inside_lanes(p)


def stacked(copies, first, count, pairs):
    return jnp.concatenate([windows(copies, first, count, p) for p in range(pairs + 1)], axis=0)


def late_rows(gy_count, fd_in, cd_in, hd_in, pg_in, hs_in, rows, acc, w1b, wfb, fd, cd, hd, pg, hs, send, pre_late, rs):
    gx = lax.axis_index("gx")
    gy = lax.axis_index("gy")
    count, across, _ = pg.shape
    lane = 2 * C
    pairs = NZ // 2
    rs[:, 8:8 + across, :] = rows[...].astype(F32)
    blank_rows(rs)

    @pl.when(gx == 0)
    def _():
        shift_rows(rs.at[0:2], fd, 0, lane)
        shift_rows(rs.at[2:3], cd, 0, lane)
        value = dot(stacked(fd, 0, 2, pairs), w1b[...])
        grad = dot_nt(stacked(cd, 0, 1, pairs), wfb[...])
        before = jnp.where(gy == 0, 0.0, 1.0)
        for p in range(pairs + 1):
            here = slice(lane * p, lane * (p + 1))
            early = value[2 * across * p:2 * across * p + across]
            later = value[2 * across * p + across:2 * across * (p + 1)]
            mine = pre_gradient(grad[across * p:across * (p + 1)], later, p)
            pg[0, :, here] = mine.astype(BF16)
            both = jnp.stack([hidden_of(early, p) * before, hidden_of(later, p)])
            hs[0:2, 8:8 + across, here] = both
            hd[1, 0:2, :, here] = both.astype(BF16)
        shift_rows(hs.at[0:2], hd, 0, 0, (0, 2))
        store_blocks(send, sums_of([acc[t] + late for t, late in enumerate(second_late(hd, cd))]))

    @pl.when(gx != 0)
    def _():
        shift_rows(rs.at[0:2], fd, count + 2, lane)
        shift_rows(rs.at[2:3], cd, count + 1, lane)
        value = dot(stacked(fd, count, 1, pairs), w1b[...])
        grad = dot_nt(stacked(cd, count - 1, 1, pairs), wfb[...])
        for p in range(pairs + 1):
            here = slice(lane * p, lane * (p + 1))
            part = slice(across * p, across * (p + 1))
            pre_late[:, here] = value[part]
            pg[count - 1, :, here] = pre_gradient(grad[part], value[part], p).astype(BF16)
        store_blocks(send, sums_of([acc[t] + late for t, late in enumerate(first_late(fd, pg))]))


def keep_sums(gy_count, fd, cd, hd_in, pg, hs_in, pre_late, w1b, hd, hs, keep):
    gx = lax.axis_index("gx")
    gy = lax.axis_index("gy")
    count, across, _ = pg.shape
    lane = 2 * C
    pairs = NZ // 2

    @pl.when(gx == 0)
    def _():
        store_blocks(keep, sums_of(first_products(fd, pg)))

    @pl.when(gx != 0)
    def _():
        value = dot(stacked(fd, count + 1, 1, pairs), w1b[...])
        beyond = jnp.where(gy == gy_count - 1, 0.0, 1.0)
        for p in range(pairs + 1):
            here = slice(lane * p, lane * (p + 1))
            part = slice(across * p, across * (p + 1))
            both = jnp.stack([hidden_of(pre_late[:, here], p), hidden_of(value[part], p) * beyond])
            hs[count:count + 2, 8:8 + across, here] = both
            hd[1, count:count + 2, :, here] = both.astype(BF16)
        shift_rows(hs, hd, 0, 0, (0, 2))
        store_blocks(keep, sums_of(second_products(hd, cd)))


def output_conv(hd, w2, mine, given, w2b):
    for t, (dx, dy) in enumerate(TAPS):
        w2b[t * 4 * C:(t + 1) * 4 * C, :] = band([w2[9 * dx + 3 * dy + z] for z in range(3)])
    gx = lax.axis_index("gx")
    count, half, _ = mine.shape
    lane = 2 * C
    for p in range(NZ // 2):
        here = slice(lane * p, lane * (p + 1))
        value = dot(windows(hd, 0, count, p), w2b[...]).reshape(count, 2 * half, lane)
        left, right = value[:, 0:half], value[:, half:]
        mine[:, :, here] = jnp.where(gx == 0, left, right).astype(BF16)
        given[:, :, here] = jnp.where(gx == 0, right, left).astype(BF16)


def finish_output(mine, other, out, turned, scratch, sems):
    count, nx, width = mine.shape
    gx = lax.axis_index("gx")
    for y in range(count):
        a = mine[y].astype(F32)
        b = other[y].astype(F32)
        put_rows(scratch, y * nx, jnp.where(gx == 0, a, b))
        put_rows(scratch, (count + y) * nx, jnp.where(gx == 0, b, a))
    copies = []
    for x in range(nx):
        turned[x] = take_rows(scratch, x, 2 * count, nx)
        if x % 2:
            copies.append(pltpu.make_async_copy(turned.at[x - 1:x + 1], out.at[x - 1:x + 1], sems.at[x // 2]))
            copies[-1].start()
    for copy in copies:
        copy.wait()


def add_pair(keep, other, out):
    out[...] = (keep[...] + other[...].astype(F32)).astype(BF16)


def add_and_repeat(terms, out):
    total = terms[0].astype(F32)
    for index in range(1, terms.shape[0]):
        total = total + terms[index].astype(F32)
    total = total.astype(BF16)
    for index in range(out.shape[0]):
        out[index] = total


def unpack(factor, is_first, rows, first, second, held, sems):
    def each(act):
        for chosen, target in ((is_first, first), (jnp.logical_not(is_first), second)):
            @pl.when(chosen)
            def _():
                act(target)

    def copy_of(dx, target):
        piece = slice(9 * dx, 9 * dx + 9)
        return pltpu.make_async_copy(held.at[piece], target.at[piece], sems.at[dx])

    for dx in range(3):
        for dy in range(3):
            t = 3 * dy + dx
            place = 9 * dx + 3 * dy
            turned = rows[t * C:(t + 1) * C, :].astype(F32).T * factor
            held[place] = turned[0:C]
            held[place + 1] = turned[C:2 * C]
            turned = rows[(9 + t // 2) * C:(10 + t // 2) * C, :].astype(F32).T * factor
            held[place + 2] = turned[t % 2 * C:(t % 2 + 1) * C]
        each(lambda target: copy_of(dx, target).start())
    each(lambda target: [copy_of(dx, target).wait() for dx in range(3)])


def unpack_own(factor, rows, first, second, held, sems):
    unpack(factor, lax.axis_index("gx") == 0, rows, first, second, held, sems)


def unpack_other(factor, rows, first_in, second_in, first, second, held, sems):
    unpack(factor, lax.axis_index("gx") != 0, rows, first, second, held, sems)


def near(shape, dtype):
    return pltpu.VMEM(shape, dtype)


def call(body, name, inputs, outs, scratch=(), limit=16, flops=0, far=False, aliases=None):
    placed = [pltpu.with_memory_space_constraint(x, pltpu.VMEM if held else pltpu.HBM) for x, held in inputs]
    size = sum(x.size * x.dtype.itemsize for x, _ in inputs)
    return pl.pallas_call(
        body,
        out_shape=list(outs),
        in_specs=[pl.BlockSpec(memory_space=pltpu.VMEM if held else pl.ANY) for _, held in inputs],
        out_specs=[pl.BlockSpec(memory_space=pl.ANY if far else pltpu.VMEM)] * len(outs),
        scratch_shapes=list(scratch),
        input_output_aliases=aliases or {},
        compiler_params=pltpu.CompilerParams(vmem_limit_bytes=limit * 1024 * 1024),
        cost_estimate=pl.CostEstimate(flops=flops, bytes_accessed=size, transcendentals=0),
        name=name,
    )(*placed)


def shards(field_in, first_weight, second_weight, cotangent):
    nx, ny, width = field_in.shape[1:]
    gx_count, gy_count, grp_count = (lax.axis_size(axis) for axis in ("gx", "gy", "grp"))
    total = field_in.shape[0] * nx * ny * NZ * gx_count * gy_count * grp_count
    factor = 1.0 / math.sqrt(total)
    ranks = gy_count * grp_count
    rows = -(-BLOCKS * C // (8 * ranks)) * 8 * ranks
    lane = 2 * C
    wide = width + 2 * lane
    count = ny // 2
    across = 2 * nx
    size = 2 * count + 3

    field, cot, edge, given, w1, w2 = call(
        pack_edges, "pack_edges",
        [(x, False) for x in (field_in[0], cotangent[0], first_weight.reshape(27, C, C), second_weight.reshape(27, C, C))],
        [
            near((nx, ny, width), BF16),
            near((nx, ny, width), BF16),
            near((3, nx, width), BF16),
            near((3, nx, width), BF16),
            near((27, C, C), BF16),
            near((27, C, C), BF16),
        ],
        [pltpu.VMEM((6, nx, width), F32), pltpu.SemaphoreType.DMA((4,))])
    taken = swap(given)
    own, bulk, w1b, wfb = call(
        pack_halves, "pack_halves", [(x, True) for x in (field, cot, w1, w2)],
        [
            near((size, nx, width), BF16),
            near((size, nx, width), BF16),
            near((9 * 4 * C, lane), BF16),
            near((lane, 9 * 4 * C), BF16),
        ],
        [pltpu.VMEM((width // lane, nx * ny, lane), F32)] * 2, flops=10 ** 9)
    bulk, taken, wfb = lax.optimization_barrier((bulk, taken, wfb))
    got = swap(bulk)
    whole, = call(join_edges, "join_edges", [(edge, True), (taken, True)], [near((3, across, width), BF16)])
    ends = [(gy_count + j, j + 1) for j in range(gy_count - 1)]
    late = lax.ppermute(whole, ("gx", "gy"), ends + [(b, a) for a, b in ends])
    held = [
        near((3, count + 4, across, wide), BF16),
        near((3, count + 2, across, wide), BF16),
        near((3, count + 2, across, width + lane), BF16),
        near((count, across, width + lane), BF16),
        near((count + 2, across + 16, width + lane), F32),
    ]
    fd, cd, hd, pg, hs, acc = call(
        interior, "interior",
        [(x, True) for x in (own, got, w1b, wfb)],
        held + [near((9, lane, 2 * lane), F32)],
        [
            pltpu.VMEM((count + 2, across + 16, width), F32),
            pltpu.VMEM((count + 1, across + 16, width), F32),
            pltpu.VMEM((count, across, width + lane), F32),
        ],
        limit=32, flops=4 * 10 ** 9)
    fd, cd, hd, pg, hs, send, pre_late = call(
        functools.partial(late_rows, gy_count), "late_rows",
        [(x, True) for x in (fd, cd, hd, pg, hs, late, acc, w1b, wfb)],
        held + [near((rows, lane), BF16), near((across, width + lane), F32)],
        [pltpu.VMEM((3, across + 16, width), F32)],
        limit=32, flops=10 ** 9, aliases={0: 0, 1: 1, 2: 2, 3: 3, 4: 4})

    other = swap(send)
    hd, _, keep = call(
        functools.partial(keep_sums, gy_count), "keep_sums",
        [(x, True) for x in (fd, cd, hd, pg, hs, pre_late, w1b)], [held[2], held[4], near((rows, lane), F32)],
        flops=2 * 10 ** 9, aliases={2: 0, 4: 1})
    other, keep = lax.optimization_barrier((other, keep))
    both, = call(add_pair, "add_pair", [(keep, True), (other, True)], [near((rows, lane), BF16)])
    terms = lax.all_to_all(both.reshape(ranks, rows // ranks, lane), ("grp", "gy"), 0, 0)
    spread, = call(add_and_repeat, "add_and_repeat", [(terms, True)], [near(terms.shape, BF16)])
    spread, hd, w2 = lax.optimization_barrier((spread, hd, w2))
    sums = lax.all_to_all(spread, ("grp", "gy"), 0, 0).reshape(rows, lane)
    mine, given = call(
        output_conv, "output_conv", [(hd, True), (w2, True)],
        [near((count, nx, width), BF16), near((count, nx, width), BF16)],
        [pltpu.VMEM((9 * 4 * C, lane), BF16)], flops=2 * 10 ** 9)
    given = swap(given)
    out, = call(
        finish_output, "finish_output", [(mine, True), (given, True)],
        [pltpu.HBM((nx, ny, width), BF16)],
        [pltpu.VMEM((nx, ny, width), BF16), pltpu.VMEM((width // lane, nx * ny, lane), F32), pltpu.SemaphoreType.DMA((nx // 2,))], far=True)
    sums, out = lax.optimization_barrier((sums, out))
    other = swap(sums)
    outs = [pltpu.HBM((27, C, C), F32)] * 2
    scratch = [pltpu.VMEM((27, C, C), F32), pltpu.SemaphoreType.DMA((3,))]
    first, second = call(functools.partial(unpack_own, factor), "unpack_own", [(sums, True)], outs, scratch, far=True)
    other, first, second = lax.optimization_barrier((other, first, second))
    first, second = call(
        functools.partial(unpack_other, factor), "unpack_other", [(other, True), (first, False), (second, False)], outs, scratch, far=True,
        aliases={1: 0, 2: 1})
    shape = (3, 3, 3, C, C)
    return out[None], first.reshape(shape), second.reshape(shape)


def solution(mesh):
    return jax.shard_map(
        shards,
        mesh=mesh,
        in_specs=(P("grp", "gx", "gy", None), P(), P(), P("grp", "gx", "gy", None)),
        out_specs=(P("grp", "gx", "gy", None), P(), P()),
        check_vma=False,
    )
```

```python
import functools
import math

import jax
import jax.numpy as jnp
from jax import lax
from jax.experimental import pallas as pl
from jax.experimental.pallas import tpu as pltpu
from jax.sharding import PartitionSpec as P

C = 64
NZ = 16
BF16 = jnp.bfloat16
F32 = jnp.float32
TAPS = [(dx, dy) for dy in range(3) for dx in range(3)]
BLOCKS = 14


def swap(array):
    return lax.ppermute(array, "gx", [(0, 1), (1, 0)])


def dot(a, b):
    return jnp.dot(a, b, preferred_element_type=F32)


def dot_nt(a, b):
    return lax.dot_general(a, b, (((1,), (1,)), ((), ())), preferred_element_type=F32)


def band(taps):
    zero = jnp.zeros((C, C), BF16)
    left = jnp.concatenate(list(taps) + [zero], axis=0)
    right = jnp.concatenate([zero] + list(taps), axis=0)
    return jnp.concatenate([left, right], axis=1)


def band_flipped(taps):
    zero = jnp.zeros((C, C), BF16)
    back = list(taps)[::-1]
    upper = jnp.concatenate(back + [zero], axis=1)
    lower = jnp.concatenate([zero] + back, axis=1)
    return jnp.concatenate([upper, lower], axis=0)


def packed(pieces):
    blocks = [piece[:, 0:2 * C] for piece in pieces]
    for pair in range(0, 9, 2):
        second = pieces[pair + 1][:, 2 * C:3 * C] if pair + 1 < 9 else jnp.zeros((C, C), F32)
        blocks.append(jnp.concatenate([pieces[pair][:, 2 * C:3 * C], second], axis=1))
    return blocks


def pack_edges(field_hbm, cot_hbm, w1_hbm, w2_hbm, field, cot, edge, given, w1, w2, rows, sems):
    copies = [
        pltpu.make_async_copy(source, target, sems.at[index])
        for index, (source, target) in enumerate(((field_hbm, field), (cot_hbm, cot), (w1_hbm, w1), (w2_hbm, w2)))
    ]
    for copy in copies:
        copy.start()
    for copy in copies[:2]:
        copy.wait()
    nx, ny, _ = field.shape
    gx = lax.axis_index("gx")
    for x in range(nx):
        fields = field[x].astype(F32)
        cots = cot[x].astype(F32)
        for index, row in enumerate((fields[0:1], fields[1:2], cots[0:1], fields[ny - 2:ny - 1], fields[ny - 1:ny], cots[ny - 1:ny])):
            rows[index, x:x + 1, :] = row
    head = rows[0:3].astype(BF16)
    tail = rows[3:6].astype(BF16)
    edge[...] = jnp.where(gx == 0, head, tail)
    given[...] = jnp.where(gx == 0, tail, head)
    for copy in copies[2:]:
        copy.wait()


def join_edges(edge, taken, whole):
    nx = edge.shape[1]
    gx = lax.axis_index("gx")

    @pl.when(gx == 0)
    def _():
        whole[:, 0:nx] = edge[...]
        whole[:, nx:2 * nx] = taken[...]

    @pl.when(gx != 0)
    def _():
        whole[:, 0:nx] = taken[...]
        whole[:, nx:2 * nx] = edge[...]


def put_rows(scratch, start, rows):
    lane = 2 * C
    for tile in range(scratch.shape[0]):
        scratch[tile, start:start + rows.shape[0], :] = rows[:, lane * tile:lane * (tile + 1)]


def take_rows(scratch, start, count, stride):
    return jnp.concatenate(
        [scratch[tile, pl.ds(start, count, stride=stride), :] for tile in range(scratch.shape[0])], axis=1).astype(BF16)


def pack_halves(field, cot, w1, w2, own, bulk, w1b, wfb, turned_f, turned_c):
    nx, ny, _ = field.shape
    half = ny // 2
    for source, target in ((field, turned_f), (cot, turned_c)):
        for x in range(nx):
            put_rows(target, x * ny, source[x].astype(F32))
    gx = lax.axis_index("gx")

    def place(target, first_f, first_c):
        for y in range(half + 2):
            target[y] = take_rows(turned_f, first_f + y, nx, ny)
        for y in range(half + 1):
            target[half + 2 + y] = take_rows(turned_c, first_c + y, nx, ny)

    @pl.when(gx == 0)
    def _():
        place(own, 0, 0)
        place(bulk, half - 2, half - 1)

    @pl.when(gx != 0)
    def _():
        place(own, half - 2, half - 1)
        place(bulk, 0, 0)

    make_bands(w1, w2, w1b, wfb)


def make_bands(w1, w2, w1b, wfb):
    for t, (dx, dy) in enumerate(TAPS):
        rows = slice(t * 4 * C, (t + 1) * 4 * C)
        first = 9 * dx + 3 * dy
        w1b[rows, :] = band([w1[first + z] for z in range(3)])
        wfb[:, rows] = band_flipped([w2[24 - first + z] for z in range(3)])


def blank_edges(copies):
    lane = 2 * C
    zero = jnp.zeros(copies.shape[:-1] + (lane,), BF16)
    copies[..., 0:lane] = zero
    copies[..., copies.shape[-1] - lane:] = zero


def blank_rows(scratch):
    zero = jnp.zeros((scratch.shape[0], 1, scratch.shape[2]), F32)
    scratch[:, 7:8, :] = zero
    scratch[:, scratch.shape[1] - 8:scratch.shape[1] - 7, :] = zero


def shift_rows(scratch, copies, start, first_lane, taps=(0, 1, 2)):
    count, rows, width = scratch.shape
    for dx in taps:
        copies[dx, pl.ds(start, count), :, first_lane:first_lane + width] = scratch[:, 7 + dx:rows - 9 + dx, :].astype(BF16)


def inside_lanes(p):
    lane_of = lax.broadcasted_iota(jnp.int32, (1, 2 * C), 1)
    if p == 0:
        return (lane_of >= C).astype(F32)
    if p == NZ // 2:
        return (lane_of < C).astype(F32)
    return 1.0


def windows(copies, first, count, p):
    lane = 2 * C
    rows = copies.shape[2]
    return jnp.concatenate(
        [
            copies[dx, pl.ds(first + dy, count), :, lane * p:lane * (p + 2)].reshape(count * rows, 2 * lane)
            for dx, dy in TAPS
        ],
        axis=1,
    )


def pre_gradient(grad, pre, p):
    sigma = jax.nn.sigmoid(pre)
    return grad * sigma * (1.0 + pre * (1.0 - sigma)) * inside_lanes(p)


def interior(own, got, w1b, wfb, fd, cd, hd, pg, hs, acc, fs, cs, pre):
    gx = lax.axis_index("gx")
    nx, width = own.shape[1:]
    across = 2 * nx
    count = pg.shape[0]
    cells = count * across
    lane = 2 * C
    pairs = NZ // 2

    def place(left, right):
        for scratch, copies, offset, start, size in ((fs, fd, 2 - 2 * gx, 0, count + 2), (cs, cd, 1 - gx, count + 2, count + 1)):
            for source, row in ((left, 0), (right, nx)):
                rows = source[start:start + size]
                scratch[:, 8 + row:8 + row + nx, :] = rows.astype(F32)
                copies[1, pl.ds(offset, size), row:row + nx, lane:lane + width] = rows

    @pl.when(gx == 0)
    def _():
        place(own, got)

    @pl.when(gx != 0)
    def _():
        place(got, own)

    for scratch in (fs, cs, hs):
        blank_rows(scratch)
    blank_edges(fd)
    blank_edges(cd)
    shift_rows(fs, fd, 2 - 2 * gx, lane, (0, 2))
    shift_rows(cs, cd, 1 - gx, lane, (0, 2))
    for group in range(0, pairs + 1, 3):
        value = dot(jnp.concatenate([windows(fd, 2 - 2 * gx, count, p) for p in range(group, group + 3)], axis=0), w1b[...])
        for p in range(group, group + 3):
            here = slice(lane * p, lane * (p + 1))
            part = value[cells * (p - group):cells * (p - group + 1)]
            pre[:, :, here] = part.reshape(count, across, lane)
            hidden = (part * jax.nn.sigmoid(part) * inside_lanes(p)).reshape(count, across, lane)
            hs[pl.ds(2 - 2 * gx, count), 8:8 + across, here] = hidden
            hd[1, pl.ds(2 - 2 * gx, count), :, here] = hidden.astype(BF16)
    cells = cells - across
    for group in range(0, pairs + 1, 3):
        value = dot_nt(jnp.concatenate([windows(cd, 1 - gx, count - 1, p) for p in range(group, group + 3)], axis=0), wfb[...])
        for p in range(group, group + 3):
            here = slice(lane * p, lane * (p + 1))
            part = value[cells * (p - group):cells * (p - group + 1)]
            grad = pre_gradient(part, pre[pl.ds(gx, count - 1), :, here].reshape(cells, lane), p)
            pg[pl.ds(1 - gx, count - 1), :, here] = grad.astype(BF16).reshape(count - 1, across, lane)
    pg[pl.ds((count - 1) * gx, 1)] = jnp.zeros((1,) + pg.shape[1:], BF16)

    @pl.when(gx == 0)
    def _():
        hd[:, 0:2] = jnp.zeros((3, 2) + hd.shape[2:], BF16)
        shift_rows(hs.at[2:2 + count], hd, 2, 0, (0, 2))
        for t, total in enumerate(second_products(hd, cd)):
            acc[t] = total

    @pl.when(gx != 0)
    def _():
        for t, total in enumerate(first_products(fd, pg)):
            acc[t] = total


def second_products(hd, cd):
    lane = 2 * C
    pairs = NZ // 2
    count, across = hd.shape[1] - 2, hd.shape[2]
    cells = count * across
    cot_t = jnp.concatenate(
        [cd[1, 1:1 + count, :, lane * (p + 1):lane * (p + 2)].reshape(cells, lane).T for p in range(pairs)], axis=1)
    return [
        dot(cot_t, jnp.concatenate(
            [hd[dx, dy:dy + count, :, lane * p:lane * (p + 2)].reshape(cells, 2 * lane) for p in range(pairs)], axis=0))
        for dx, dy in TAPS
    ]


def first_products(fd, pg):
    lane = 2 * C
    pairs = NZ // 2
    count, across, _ = pg.shape
    cells = count * across
    grad_t = jnp.concatenate(
        [pg[:, :, lane * p:lane * (p + 1)].reshape(cells, lane).T for p in range(pairs + 1)], axis=1)
    return [
        dot(grad_t, jnp.concatenate(
            [fd[dx, 1 + dy:1 + dy + count, :, lane * p:lane * (p + 2)].reshape(cells, 2 * lane) for p in range(pairs + 1)], axis=0))
        for dx, dy in TAPS
    ]


def folded(total):
    return total[0:C, 0:3 * C] + total[C:2 * C, C:4 * C]


def second_late(hd, cd):
    lane = 2 * C
    pairs = NZ // 2
    late = ((0, 1), (0,), ())
    products = []
    for dx, dy in TAPS:
        if late[dy]:
            cots = jnp.concatenate(
                [cd[1, 1 + y, :, lane * (p + 1):lane * (p + 2)] for y in late[dy] for p in range(pairs)], axis=0)
            rows = jnp.concatenate(
                [hd[dx, y + dy, :, lane * p:lane * (p + 2)] for y in late[dy] for p in range(pairs)], axis=0)
            products.append(dot(cots.T, rows))
        else:
            products.append(0.0)
    return products


def first_late(fd, pg):
    lane = 2 * C
    pairs = NZ // 2
    count, across, _ = pg.shape
    y = count - 1
    extra = 2 * lane - (pairs + 1) * across
    grad_t = jnp.concatenate(
        [pg[y, :, lane * p:lane * (p + 1)] for p in range(pairs + 1)] + [jnp.zeros((extra, lane), BF16)], axis=0).T
    pad = jnp.zeros((extra, 2 * lane), BF16)
    return [
        dot(grad_t, jnp.concatenate(
            [fd[dx, y + dy + 1, :, lane * p:lane * (p + 2)] for p in range(pairs + 1)] + [pad], axis=0))
        for dx, dy in TAPS
    ]


def sums_of(products):
    return packed([folded(product) for product in products])


def store_blocks(target, blocks):
    for index, block in enumerate(blocks):
        target[index * C:(index + 1) * C, :] = block.astype(target.dtype)
    if target.shape[0] > BLOCKS * C:
        target[BLOCKS * C:, :] = jnp.zeros((target.shape[0] - BLOCKS * C, 2 * C), target.dtype)


def hidden_of(value, p):
    return value * jax.nn.sigmoid(value) * inside_lanes(p)


def stacked(copies, first, count, pairs):
    return jnp.concatenate([windows(copies, first, count, p) for p in range(pairs + 1)], axis=0)


def late_rows(gy_count, fd_in, cd_in, hd_in, pg_in, hs_in, rows, acc, w1b, wfb, fd, cd, hd, pg, hs, send, pre_late, rs):
    gx = lax.axis_index("gx")
    gy = lax.axis_index("gy")
    count, across, _ = pg.shape
    lane = 2 * C
    pairs = NZ // 2
    rs[:, 8:8 + across, :] = rows[...].astype(F32)
    blank_rows(rs)

    @pl.when(gx == 0)
    def _():
        shift_rows(rs.at[0:2], fd, 0, lane)
        shift_rows(rs.at[2:3], cd, 0, lane)
        value = dot(stacked(fd, 0, 2, pairs), w1b[...])
        grad = dot_nt(stacked(cd, 0, 1, pairs), wfb[...])
        before = jnp.where(gy == 0, 0.0, 1.0)
        for p in range(pairs + 1):
            here = slice(lane * p, lane * (p + 1))
            early = value[2 * across * p:2 * across * p + across]
            later = value[2 * across * p + across:2 * across * (p + 1)]
            mine = pre_gradient(grad[across * p:across * (p + 1)], later, p)
            pg[0, :, here] = mine.astype(BF16)
            both = jnp.stack([hidden_of(early, p) * before, hidden_of(later, p)])
            hs[0:2, 8:8 + across, here] = both
            hd[1, 0:2, :, here] = both.astype(BF16)
        shift_rows(hs.at[0:2], hd, 0, 0, (0, 2))
        store_blocks(send, sums_of([acc[t] + late for t, late in enumerate(second_late(hd, cd))]))

    @pl.when(gx != 0)
    def _():
        shift_rows(rs.at[0:2], fd, count + 2, lane)
        shift_rows(rs.at[2:3], cd, count + 1, lane)
        value = dot(stacked(fd, count, 1, pairs), w1b[...])
        grad = dot_nt(stacked(cd, count - 1, 1, pairs), wfb[...])
        for p in range(pairs + 1):
            here = slice(lane * p, lane * (p + 1))
            part = slice(across * p, across * (p + 1))
            pre_late[:, here] = value[part]
            pg[count - 1, :, here] = pre_gradient(grad[part], value[part], p).astype(BF16)
        store_blocks(send, sums_of([acc[t] + late for t, late in enumerate(first_late(fd, pg))]))


def keep_sums(gy_count, fd, cd, hd_in, pg, hs_in, pre_late, w1b, hd, hs, keep):
    gx = lax.axis_index("gx")
    gy = lax.axis_index("gy")
    count, across, _ = pg.shape
    lane = 2 * C
    pairs = NZ // 2

    @pl.when(gx == 0)
    def _():
        store_blocks(keep, sums_of(first_products(fd, pg)))

    @pl.when(gx != 0)
    def _():
        value = dot(stacked(fd, count + 1, 1, pairs), w1b[...])
        beyond = jnp.where(gy == gy_count - 1, 0.0, 1.0)
        for p in range(pairs + 1):
            here = slice(lane * p, lane * (p + 1))
            part = slice(across * p, across * (p + 1))
            both = jnp.stack([hidden_of(pre_late[:, here], p), hidden_of(value[part], p) * beyond])
            hs[count:count + 2, 8:8 + across, here] = both
            hd[1, count:count + 2, :, here] = both.astype(BF16)
        shift_rows(hs, hd, 0, 0, (0, 2))
        store_blocks(keep, sums_of(second_products(hd, cd)))


def output_conv(hd, w2, mine, given, w2b):
    for t, (dx, dy) in enumerate(TAPS):
        w2b[t * 4 * C:(t + 1) * 4 * C, :] = band([w2[9 * dx + 3 * dy + z] for z in range(3)])
    gx = lax.axis_index("gx")
    count, half, _ = mine.shape
    lane = 2 * C
    for p in range(NZ // 2):
        here = slice(lane * p, lane * (p + 1))
        value = dot(windows(hd, 0, count, p), w2b[...]).reshape(count, 2 * half, lane)
        left, right = value[:, 0:half], value[:, half:]
        mine[:, :, here] = jnp.where(gx == 0, left, right).astype(BF16)
        given[:, :, here] = jnp.where(gx == 0, right, left).astype(BF16)


def finish_output(mine, other, out, turned, scratch, sems):
    count, nx, width = mine.shape
    gx = lax.axis_index("gx")
    for y in range(count):
        a = mine[y].astype(F32)
        b = other[y].astype(F32)
        put_rows(scratch, y * nx, jnp.where(gx == 0, a, b))
        put_rows(scratch, (count + y) * nx, jnp.where(gx == 0, b, a))
    copies = []
    for x in range(nx):
        turned[x] = take_rows(scratch, x, 2 * count, nx)
        if x % 2:
            copies.append(pltpu.make_async_copy(turned.at[x - 1:x + 1], out.at[x - 1:x + 1], sems.at[x // 2]))
            copies[-1].start()
    for copy in copies:
        copy.wait()


def add_pair(keep, other, out):
    out[...] = (keep[...] + other[...].astype(F32)).astype(BF16)


def add_terms(terms, out):
    total = terms[0].astype(F32)
    for index in range(1, terms.shape[0]):
        total = total + terms[index].astype(F32)
    out[...] = total.astype(BF16)


def unpack(factor, is_first, rows, first, second, held, sems):
    def each(act):
        for chosen, target in ((is_first, first), (jnp.logical_not(is_first), second)):
            @pl.when(chosen)
            def _():
                act(target)

    def copy_of(dx, target):
        piece = slice(9 * dx, 9 * dx + 9)
        return pltpu.make_async_copy(held.at[piece], target.at[piece], sems.at[dx])

    for dx in range(3):
        for dy in range(3):
            t = 3 * dy + dx
            place = 9 * dx + 3 * dy
            turned = rows[t * C:(t + 1) * C, :].T.astype(F32) * factor
            held[place] = turned[0:C]
            held[place + 1] = turned[C:2 * C]
            turned = rows[(9 + t // 2) * C:(10 + t // 2) * C, :].T.astype(F32) * factor
            held[place + 2] = turned[t % 2 * C:(t % 2 + 1) * C]
        each(lambda target: copy_of(dx, target).start())
    each(lambda target: [copy_of(dx, target).wait() for dx in range(3)])


def unpack_own(factor, rows, first, second, held, sems):
    unpack(factor, lax.axis_index("gx") == 0, rows, first, second, held, sems)


def unpack_other(factor, rows, first_in, second_in, first, second, held, sems):
    unpack(factor, lax.axis_index("gx") != 0, rows, first, second, held, sems)


def near(shape, dtype):
    return pltpu.VMEM(shape, dtype)


def call(body, name, inputs, outs, scratch=(), limit=16, flops=0, far=False, aliases=None):
    placed = [pltpu.with_memory_space_constraint(x, pltpu.VMEM if held else pltpu.HBM) for x, held in inputs]
    size = sum(x.size * x.dtype.itemsize for x, _ in inputs)
    return pl.pallas_call(
        body,
        out_shape=list(outs),
        in_specs=[pl.BlockSpec(memory_space=pltpu.VMEM if held else pl.ANY) for _, held in inputs],
        out_specs=[pl.BlockSpec(memory_space=pl.ANY if far else pltpu.VMEM)] * len(outs),
        scratch_shapes=list(scratch),
        input_output_aliases=aliases or {},
        compiler_params=pltpu.CompilerParams(vmem_limit_bytes=limit * 1024 * 1024),
        cost_estimate=pl.CostEstimate(flops=flops, bytes_accessed=size, transcendentals=0),
        name=name,
    )(*placed)


def shards(field_in, first_weight, second_weight, cotangent):
    nx, ny, width = field_in.shape[1:]
    gx_count, gy_count, grp_count = (lax.axis_size(axis) for axis in ("gx", "gy", "grp"))
    total = field_in.shape[0] * nx * ny * NZ * gx_count * gy_count * grp_count
    factor = 1.0 / math.sqrt(total)
    ranks = gy_count * grp_count
    rows = -(-BLOCKS * C // (8 * ranks)) * 8 * ranks
    lane = 2 * C
    wide = width + 2 * lane
    count = ny // 2
    across = 2 * nx
    size = 2 * count + 3

    field, cot, edge, given, w1, w2 = call(
        pack_edges, "pack_edges",
        [(x, False) for x in (field_in[0], cotangent[0], first_weight.reshape(27, C, C), second_weight.reshape(27, C, C))],
        [
            near((nx, ny, width), BF16),
            near((nx, ny, width), BF16),
            near((3, nx, width), BF16),
            near((3, nx, width), BF16),
            near((27, C, C), BF16),
            near((27, C, C), BF16),
        ],
        [pltpu.VMEM((6, nx, width), F32), pltpu.SemaphoreType.DMA((4,))])
    taken = swap(given)
    own, bulk, w1b, wfb = call(
        pack_halves, "pack_halves", [(x, True) for x in (field, cot, w1, w2)],
        [
            near((size, nx, width), BF16),
            near((size, nx, width), BF16),
            near((9 * 4 * C, lane), BF16),
            near((lane, 9 * 4 * C), BF16),
        ],
        [pltpu.VMEM((width // lane, nx * ny, lane), F32)] * 2, flops=10 ** 9)
    bulk, taken, wfb = lax.optimization_barrier((bulk, taken, wfb))
    got = swap(bulk)
    whole, = call(join_edges, "join_edges", [(edge, True), (taken, True)], [near((3, across, width), BF16)])
    ends = [(gy_count + j, j + 1) for j in range(gy_count - 1)]
    late = lax.ppermute(whole, ("gx", "gy"), ends + [(b, a) for a, b in ends])
    held = [
        near((3, count + 4, across, wide), BF16),
        near((3, count + 2, across, wide), BF16),
        near((3, count + 2, across, width + lane), BF16),
        near((count, across, width + lane), BF16),
        near((count + 2, across + 16, width + lane), F32),
    ]
    fd, cd, hd, pg, hs, acc = call(
        interior, "interior",
        [(x, True) for x in (own, got, w1b, wfb)],
        held + [near((9, lane, 2 * lane), F32)],
        [
            pltpu.VMEM((count + 2, across + 16, width), F32),
            pltpu.VMEM((count + 1, across + 16, width), F32),
            pltpu.VMEM((count, across, width + lane), F32),
        ],
        limit=32, flops=4 * 10 ** 9)
    fd, cd, hd, pg, hs, send, pre_late = call(
        functools.partial(late_rows, gy_count), "late_rows",
        [(x, True) for x in (fd, cd, hd, pg, hs, late, acc, w1b, wfb)],
        held + [near((rows, lane), BF16), near((across, width + lane), F32)],
        [pltpu.VMEM((3, across + 16, width), F32)],
        limit=32, flops=10 ** 9, aliases={0: 0, 1: 1, 2: 2, 3: 3, 4: 4})

    other = swap(send)
    hd, _, keep = call(
        functools.partial(keep_sums, gy_count), "keep_sums",
        [(x, True) for x in (fd, cd, hd, pg, hs, pre_late, w1b)], [held[2], held[4], near((rows, lane), F32)],
        flops=2 * 10 ** 9, aliases={2: 0, 4: 1})
    other, keep = lax.optimization_barrier((other, keep))
    both, = call(add_pair, "add_pair", [(keep, True), (other, True)], [near((rows, lane), BF16)])
    terms = lax.all_to_all(both.reshape(ranks, rows // ranks, lane), ("grp", "gy"), 0, 0)
    part, = call(add_terms, "add_terms", [(terms, True)], [near(terms.shape[1:], BF16)])
    part, hd, w2 = lax.optimization_barrier((part, hd, w2))
    spread = jnp.broadcast_to(part[None], terms.shape)
    sums = lax.all_to_all(spread, ("grp", "gy"), 0, 0).reshape(rows, lane)
    mine, given = call(
        output_conv, "output_conv", [(hd, True), (w2, True)],
        [near((count, nx, width), BF16), near((count, nx, width), BF16)],
        [pltpu.VMEM((9 * 4 * C, lane), BF16)], flops=2 * 10 ** 9)
    given = swap(given)
    out, = call(
        finish_output, "finish_output", [(mine, True), (given, True)],
        [pltpu.HBM((nx, ny, width), BF16)],
        [pltpu.VMEM((nx, ny, width), BF16), pltpu.VMEM((width // lane, nx * ny, lane), F32), pltpu.SemaphoreType.DMA((nx // 2,))], far=True)
    sums, out = lax.optimization_barrier((sums, out))
    other = swap(sums)
    outs = [pltpu.HBM((27, C, C), F32)] * 2
    scratch = [pltpu.VMEM((27, C, C), F32), pltpu.SemaphoreType.DMA((3,))]
    first, second = call(functools.partial(unpack_own, factor), "unpack_own", [(sums, True)], outs, scratch, far=True)
    other, first, second = lax.optimization_barrier((other, first, second))
    first, second = call(
        functools.partial(unpack_other, factor), "unpack_other", [(other, True), (first, False), (second, False)], outs, scratch, far=True,
        aliases={1: 0, 2: 1})
    shape = (3, 3, 3, C, C)
    return out[None], first.reshape(shape), second.reshape(shape)


def solution(mesh):
    return jax.shard_map(
        shards,
        mesh=mesh,
        in_specs=(P("grp", "gx", "gy", None), P(), P(), P("grp", "gx", "gy", None)),
        out_specs=(P("grp", "gx", "gy", None), P(), P()),
        check_vma=False,
    )
```

```python
import functools
import math

import jax
import jax.numpy as jnp
from jax import lax
from jax.experimental import pallas as pl
from jax.experimental.pallas import tpu as pltpu
from jax.sharding import PartitionSpec as P

C = 64
NZ = 16
BF16 = jnp.bfloat16
F32 = jnp.float32
TAPS = [(dx, dy) for dy in range(3) for dx in range(3)]
BLOCKS = 14


def swap(array):
    return lax.ppermute(array, "gx", [(0, 1), (1, 0)])


def dot(a, b):
    return jnp.dot(a, b, preferred_element_type=F32)


def dot_nt(a, b):
    return lax.dot_general(a, b, (((1,), (1,)), ((), ())), preferred_element_type=F32)


def band(taps):
    zero = jnp.zeros((C, C), BF16)
    left = jnp.concatenate(list(taps) + [zero], axis=0)
    right = jnp.concatenate([zero] + list(taps), axis=0)
    return jnp.concatenate([left, right], axis=1)


def band_flipped(taps):
    zero = jnp.zeros((C, C), BF16)
    back = list(taps)[::-1]
    upper = jnp.concatenate(back + [zero], axis=1)
    lower = jnp.concatenate([zero] + back, axis=1)
    return jnp.concatenate([upper, lower], axis=0)


def packed(pieces):
    blocks = [piece[:, 0:2 * C] for piece in pieces]
    for pair in range(0, 9, 2):
        second = pieces[pair + 1][:, 2 * C:3 * C] if pair + 1 < 9 else jnp.zeros((C, C), F32)
        blocks.append(jnp.concatenate([pieces[pair][:, 2 * C:3 * C], second], axis=1))
    return blocks


def pack_edges(field_hbm, cot_hbm, w1_hbm, w2_hbm, field, cot, edge, given, w1, w2, rows, sems):
    copies = [
        pltpu.make_async_copy(source, target, sems.at[index])
        for index, (source, target) in enumerate(((field_hbm, field), (cot_hbm, cot), (w1_hbm, w1), (w2_hbm, w2)))
    ]
    for copy in copies:
        copy.start()
    for copy in copies[:2]:
        copy.wait()
    nx, ny, _ = field.shape
    gx = lax.axis_index("gx")
    for x in range(nx):
        fields = field[x].astype(F32)
        cots = cot[x].astype(F32)
        for index, row in enumerate((fields[0:1], fields[1:2], cots[0:1], fields[ny - 2:ny - 1], fields[ny - 1:ny], cots[ny - 1:ny])):
            rows[index, x:x + 1, :] = row
    head = rows[0:3].astype(BF16)
    tail = rows[3:6].astype(BF16)
    edge[...] = jnp.where(gx == 0, head, tail)
    given[...] = jnp.where(gx == 0, tail, head)
    for copy in copies[2:]:
        copy.wait()


def join_edges(edge, taken, whole):
    nx = edge.shape[1]
    gx = lax.axis_index("gx")

    @pl.when(gx == 0)
    def _():
        whole[:, 0:nx] = edge[...]
        whole[:, nx:2 * nx] = taken[...]

    @pl.when(gx != 0)
    def _():
        whole[:, 0:nx] = taken[...]
        whole[:, nx:2 * nx] = edge[...]


def put_rows(scratch, start, rows):
    lane = 2 * C
    for tile in range(scratch.shape[0]):
        scratch[tile, start:start + rows.shape[0], :] = rows[:, lane * tile:lane * (tile + 1)]


def take_rows(scratch, start, count, stride):
    return jnp.concatenate(
        [scratch[tile, pl.ds(start, count, stride=stride), :] for tile in range(scratch.shape[0])], axis=1).astype(BF16)


def pack_halves(field, cot, w1, w2, own, bulk, w1b, wfb, turned_f, turned_c):
    nx, ny, _ = field.shape
    half = ny // 2
    for source, target in ((field, turned_f), (cot, turned_c)):
        for x in range(nx):
            put_rows(target, x * ny, source[x].astype(F32))
    gx = lax.axis_index("gx")

    def place(target, first_f, first_c):
        for y in range(half + 2):
            target[y] = take_rows(turned_f, first_f + y, nx, ny)
        for y in range(half + 1):
            target[half + 2 + y] = take_rows(turned_c, first_c + y, nx, ny)

    @pl.when(gx == 0)
    def _():
        place(own, 0, 0)
        place(bulk, half - 2, half - 1)

    @pl.when(gx != 0)
    def _():
        place(own, half - 2, half - 1)
        place(bulk, 0, 0)

    make_bands(w1, w2, w1b, wfb)


def make_bands(w1, w2, w1b, wfb):
    for t, (dx, dy) in enumerate(TAPS):
        rows = slice(t * 4 * C, (t + 1) * 4 * C)
        first = 9 * dx + 3 * dy
        w1b[rows, :] = band([w1[first + z] for z in range(3)])
        wfb[:, rows] = band_flipped([w2[24 - first + z] for z in range(3)])


def blank_edges(copies):
    lane = 2 * C
    zero = jnp.zeros(copies.shape[:-1] + (lane,), BF16)
    copies[..., 0:lane] = zero
    copies[..., copies.shape[-1] - lane:] = zero


def blank_rows(scratch):
    zero = jnp.zeros((scratch.shape[0], 1, scratch.shape[2]), F32)
    scratch[:, 7:8, :] = zero
    scratch[:, scratch.shape[1] - 8:scratch.shape[1] - 7, :] = zero


def shift_rows(scratch, copies, start, first_lane, taps=(0, 1, 2)):
    count, rows, width = scratch.shape
    for dx in taps:
        copies[dx, pl.ds(start, count), :, first_lane:first_lane + width] = scratch[:, 7 + dx:rows - 9 + dx, :].astype(BF16)


def inside_lanes(p):
    lane_of = lax.broadcasted_iota(jnp.int32, (1, 2 * C), 1)
    if p == 0:
        return (lane_of >= C).astype(F32)
    if p == NZ // 2:
        return (lane_of < C).astype(F32)
    return 1.0


def windows(copies, first, count, p):
    lane = 2 * C
    rows = copies.shape[2]
    return jnp.concatenate(
        [
            copies[dx, pl.ds(first + dy, count), :, lane * p:lane * (p + 2)].reshape(count * rows, 2 * lane)
            for dx, dy in TAPS
        ],
        axis=1,
    )


def pre_gradient(grad, pre, p):
    sigma = jax.nn.sigmoid(pre)
    return grad * sigma * (1.0 + pre * (1.0 - sigma)) * inside_lanes(p)


def interior(own, got, w1b, wfb, fd, cd, hd, pg, hs, acc, fs, cs, pre):
    gx = lax.axis_index("gx")
    nx, width = own.shape[1:]
    across = 2 * nx
    count = pg.shape[0]
    cells = count * across
    lane = 2 * C
    pairs = NZ // 2

    def place(left, right):
        for scratch, copies, offset, start, size in ((fs, fd, 2 - 2 * gx, 0, count + 2), (cs, cd, 1 - gx, count + 2, count + 1)):
            for source, row in ((left, 0), (right, nx)):
                rows = source[start:start + size]
                scratch[:, 8 + row:8 + row + nx, :] = rows.astype(F32)
                copies[1, pl.ds(offset, size), row:row + nx, lane:lane + width] = rows

    @pl.when(gx == 0)
    def _():
        place(own, got)

    @pl.when(gx != 0)
    def _():
        place(got, own)

    for scratch in (fs, cs, hs):
        blank_rows(scratch)
    blank_edges(fd)
    blank_edges(cd)
    shift_rows(fs, fd, 2 - 2 * gx, lane, (0, 2))
    shift_rows(cs, cd, 1 - gx, lane, (0, 2))
    for group in range(0, pairs + 1, 3):
        value = dot(jnp.concatenate([windows(fd, 2 - 2 * gx, count, p) for p in range(group, group + 3)], axis=0), w1b[...])
        for p in range(group, group + 3):
            here = slice(lane * p, lane * (p + 1))
            part = value[cells * (p - group):cells * (p - group + 1)]
            pre[:, :, here] = part.reshape(count, across, lane)
            hidden = (part * jax.nn.sigmoid(part) * inside_lanes(p)).reshape(count, across, lane)
            hs[pl.ds(2 - 2 * gx, count), 8:8 + across, here] = hidden
            hd[1, pl.ds(2 - 2 * gx, count), :, here] = hidden.astype(BF16)
    cells = cells - across
    for group in range(0, pairs + 1, 3):
        value = dot_nt(jnp.concatenate([windows(cd, 1 - gx, count - 1, p) for p in range(group, group + 3)], axis=0), wfb[...])
        for p in range(group, group + 3):
            here = slice(lane * p, lane * (p + 1))
            part = value[cells * (p - group):cells * (p - group + 1)]
            grad = pre_gradient(part, pre[pl.ds(gx, count - 1), :, here].reshape(cells, lane), p)
            pg[pl.ds(1 - gx, count - 1), :, here] = grad.astype(BF16).reshape(count - 1, across, lane)
    pg[pl.ds((count - 1) * gx, 1)] = jnp.zeros((1,) + pg.shape[1:], BF16)

    @pl.when(gx == 0)
    def _():
        hd[:, 0:2] = jnp.zeros((3, 2) + hd.shape[2:], BF16)
        shift_rows(hs.at[2:2 + count], hd, 2, 0, (0, 2))
        for t, total in enumerate(second_products(hd, cd)):
            acc[t] = total

    @pl.when(gx != 0)
    def _():
        fd[:, count + 2:count + 4] = jnp.zeros((3, 2) + fd.shape[2:], BF16)
        for t, total in enumerate(first_products(fd, pg)):
            acc[t] = total


def second_products(hd, cd):
    lane = 2 * C
    pairs = NZ // 2
    count, across = hd.shape[1] - 2, hd.shape[2]
    cells = count * across
    cot_t = jnp.concatenate(
        [cd[1, 1:1 + count, :, lane * (p + 1):lane * (p + 2)].reshape(cells, lane).T for p in range(pairs)], axis=1)
    return [
        dot(cot_t, jnp.concatenate(
            [hd[dx, dy:dy + count, :, lane * p:lane * (p + 2)].reshape(cells, 2 * lane) for p in range(pairs)], axis=0))
        for dx, dy in TAPS
    ]


def first_products(fd, pg):
    lane = 2 * C
    pairs = NZ // 2
    count, across, _ = pg.shape
    cells = count * across
    grad_t = jnp.concatenate(
        [pg[:, :, lane * p:lane * (p + 1)].reshape(cells, lane).T for p in range(pairs + 1)], axis=1)
    return [
        dot(grad_t, jnp.concatenate(
            [fd[dx, 1 + dy:1 + dy + count, :, lane * p:lane * (p + 2)].reshape(cells, 2 * lane) for p in range(pairs + 1)], axis=0))
        for dx, dy in TAPS
    ]


def folded(total):
    return total[0:C, 0:3 * C] + total[C:2 * C, C:4 * C]


def second_late(hd, cd):
    lane = 2 * C
    pairs = NZ // 2
    late = ((0, 1), (0,), ())
    products = []
    for dx, dy in TAPS:
        if late[dy]:
            cots = jnp.concatenate(
                [cd[1, 1 + y, :, lane * (p + 1):lane * (p + 2)] for y in late[dy] for p in range(pairs)], axis=0)
            rows = jnp.concatenate(
                [hd[dx, y + dy, :, lane * p:lane * (p + 2)] for y in late[dy] for p in range(pairs)], axis=0)
            products.append(dot(cots.T, rows))
        else:
            products.append(0.0)
    return products


def first_late(fd, pg):
    lane = 2 * C
    pairs = NZ // 2
    count, across, _ = pg.shape
    y = count - 1
    extra = 2 * lane - (pairs + 1) * across
    grad_t = jnp.concatenate(
        [pg[y, :, lane * p:lane * (p + 1)] for p in range(pairs + 1)] + [jnp.zeros((extra, lane), BF16)], axis=0).T
    pad = jnp.zeros((extra, 2 * lane), BF16)
    return [
        dot(grad_t, jnp.concatenate(
            [fd[dx, y + dy + 1, :, lane * p:lane * (p + 2)] for p in range(pairs + 1)] + [pad], axis=0))
        for dx, dy in TAPS
    ]


def sums_of(products):
    return packed([folded(product) for product in products])


def store_blocks(target, blocks):
    for index, block in enumerate(blocks):
        target[index * C:(index + 1) * C, :] = block.astype(target.dtype)
    if target.shape[0] > BLOCKS * C:
        target[BLOCKS * C:, :] = jnp.zeros((target.shape[0] - BLOCKS * C, 2 * C), target.dtype)


def hidden_of(value, p):
    return value * jax.nn.sigmoid(value) * inside_lanes(p)


def stacked(copies, first, count, pairs):
    return jnp.concatenate([windows(copies, first, count, p) for p in range(pairs + 1)], axis=0)


def late_rows(gy_count, fd_in, cd_in, hd_in, pg_in, hs_in, rows, acc, w1b, wfb, fd, cd, hd, pg, hs, send, pre_late, rs):
    gx = lax.axis_index("gx")
    gy = lax.axis_index("gy")
    count, across, _ = pg.shape
    lane = 2 * C
    pairs = NZ // 2
    rs[:, 8:8 + across, :] = rows[...].astype(F32)
    blank_rows(rs)

    @pl.when(gx == 0)
    def _():
        shift_rows(rs.at[0:2], fd, 0, lane)
        shift_rows(rs.at[2:3], cd, 0, lane)
        value = dot(stacked(fd, 0, 2, pairs), w1b[...])
        grad = dot_nt(stacked(cd, 0, 1, pairs), wfb[...])
        before = jnp.where(gy == 0, 0.0, 1.0)
        for p in range(pairs + 1):
            here = slice(lane * p, lane * (p + 1))
            early = value[2 * across * p:2 * across * p + across]
            later = value[2 * across * p + across:2 * across * (p + 1)]
            mine = pre_gradient(grad[across * p:across * (p + 1)], later, p)
            pg[0, :, here] = mine.astype(BF16)
            both = jnp.stack([hidden_of(early, p) * before, hidden_of(later, p)])
            hs[0:2, 8:8 + across, here] = both
            hd[1, 0:2, :, here] = both.astype(BF16)
        shift_rows(hs.at[0:2], hd, 0, 0, (0, 2))
        store_blocks(send, sums_of([acc[t] + late for t, late in enumerate(second_late(hd, cd))]))

    @pl.when(gx != 0)
    def _():
        shift_rows(rs.at[0:2], fd, count + 2, lane)
        shift_rows(rs.at[2:3], cd, count + 1, lane)
        value = dot(stacked(fd, count, 1, pairs), w1b[...])
        grad = dot_nt(stacked(cd, count - 1, 1, pairs), wfb[...])
        for p in range(pairs + 1):
            here = slice(lane * p, lane * (p + 1))
            part = slice(across * p, across * (p + 1))
            pre_late[:, here] = value[part]
            pg[count - 1, :, here] = pre_gradient(grad[part], value[part], p).astype(BF16)
        store_blocks(send, sums_of([acc[t] + late for t, late in enumerate(first_late(fd, pg))]))


def keep_sums(gy_count, fd, cd, hd_in, pg, hs_in, pre_late, w1b, hd, hs, keep):
    gx = lax.axis_index("gx")
    gy = lax.axis_index("gy")
    count, across, _ = pg.shape
    lane = 2 * C
    pairs = NZ // 2

    @pl.when(gx == 0)
    def _():
        store_blocks(keep, sums_of(first_products(fd, pg)))

    @pl.when(gx != 0)
    def _():
        value = dot(stacked(fd, count + 1, 1, pairs), w1b[...])
        beyond = jnp.where(gy == gy_count - 1, 0.0, 1.0)
        for p in range(pairs + 1):
            here = slice(lane * p, lane * (p + 1))
            part = slice(across * p, across * (p + 1))
            both = jnp.stack([hidden_of(pre_late[:, here], p), hidden_of(value[part], p) * beyond])
            hs[count:count + 2, 8:8 + across, here] = both
            hd[1, count:count + 2, :, here] = both.astype(BF16)
        shift_rows(hs, hd, 0, 0, (0, 2))
        store_blocks(keep, sums_of(second_products(hd, cd)))


def output_conv(hd, w2, mine, given, w2b):
    for t, (dx, dy) in enumerate(TAPS):
        w2b[t * 4 * C:(t + 1) * 4 * C, :] = band([w2[9 * dx + 3 * dy + z] for z in range(3)])
    gx = lax.axis_index("gx")
    count, half, _ = mine.shape
    lane = 2 * C
    for p in range(NZ // 2):
        here = slice(lane * p, lane * (p + 1))
        value = dot(windows(hd, 0, count, p), w2b[...]).reshape(count, 2 * half, lane)
        left, right = value[:, 0:half], value[:, half:]
        mine[:, :, here] = jnp.where(gx == 0, left, right).astype(BF16)
        given[:, :, here] = jnp.where(gx == 0, right, left).astype(BF16)


def finish_output(mine, other, out, turned, scratch, sems):
    count, nx, width = mine.shape
    gx = lax.axis_index("gx")
    for y in range(count):
        a = mine[y].astype(F32)
        b = other[y].astype(F32)
        put_rows(scratch, y * nx, jnp.where(gx == 0, a, b))
        put_rows(scratch, (count + y) * nx, jnp.where(gx == 0, b, a))
    copies = []
    for x in range(nx):
        turned[x] = take_rows(scratch, x, 2 * count, nx)
        if x % 2:
            copies.append(pltpu.make_async_copy(turned.at[x - 1:x + 1], out.at[x - 1:x + 1], sems.at[x // 2]))
            copies[-1].start()
    for copy in copies:
        copy.wait()


def add_pair(keep, other, out):
    out[...] = (keep[...] + other[...].astype(F32)).astype(BF16)


def add_terms(terms, out):
    total = terms[0].astype(F32)
    for index in range(1, terms.shape[0]):
        total = total + terms[index].astype(F32)
    out[...] = total.astype(BF16)


def unpack(factor, is_first, rows, first, second, held, sems):
    def each(act):
        for chosen, target in ((is_first, first), (jnp.logical_not(is_first), second)):
            @pl.when(chosen)
            def _():
                act(target)

    def copy_of(dx, target):
        piece = slice(9 * dx, 9 * dx + 9)
        return pltpu.make_async_copy(held.at[piece], target.at[piece], sems.at[dx])

    for dx in range(3):
        for dy in range(3):
            t = 3 * dy + dx
            place = 9 * dx + 3 * dy
            turned = rows[t * C:(t + 1) * C, :].T.astype(F32) * factor
            held[place] = turned[0:C]
            held[place + 1] = turned[C:2 * C]
            turned = rows[(9 + t // 2) * C:(10 + t // 2) * C, :].T.astype(F32) * factor
            held[place + 2] = turned[t % 2 * C:(t % 2 + 1) * C]
        each(lambda target: copy_of(dx, target).start())
    each(lambda target: [copy_of(dx, target).wait() for dx in range(3)])


def unpack_own(factor, rows, first, second, held, sems):
    unpack(factor, lax.axis_index("gx") == 0, rows, first, second, held, sems)


def unpack_other(factor, rows, first_in, second_in, first, second, held, sems):
    unpack(factor, lax.axis_index("gx") != 0, rows, first, second, held, sems)


def near(shape, dtype):
    return pltpu.VMEM(shape, dtype)


def call(body, name, inputs, outs, scratch=(), limit=16, flops=0, far=False, aliases=None):
    placed = [pltpu.with_memory_space_constraint(x, pltpu.VMEM if held else pltpu.HBM) for x, held in inputs]
    size = sum(x.size * x.dtype.itemsize for x, _ in inputs)
    return pl.pallas_call(
        body,
        out_shape=list(outs),
        in_specs=[pl.BlockSpec(memory_space=pltpu.VMEM if held else pl.ANY) for _, held in inputs],
        out_specs=[pl.BlockSpec(memory_space=pl.ANY if far else pltpu.VMEM)] * len(outs),
        scratch_shapes=list(scratch),
        input_output_aliases=aliases or {},
        compiler_params=pltpu.CompilerParams(vmem_limit_bytes=limit * 1024 * 1024),
        cost_estimate=pl.CostEstimate(flops=flops, bytes_accessed=size, transcendentals=0),
        name=name,
    )(*placed)


def shards(field_in, first_weight, second_weight, cotangent):
    nx, ny, width = field_in.shape[1:]
    gx_count, gy_count, grp_count = (lax.axis_size(axis) for axis in ("gx", "gy", "grp"))
    total = field_in.shape[0] * nx * ny * NZ * gx_count * gy_count * grp_count
    factor = 1.0 / math.sqrt(total)
    ranks = gy_count * grp_count
    rows = -(-BLOCKS * C // (8 * ranks)) * 8 * ranks
    lane = 2 * C
    wide = width + 2 * lane
    count = ny // 2
    across = 2 * nx
    size = 2 * count + 3

    field, cot, edge, given, w1, w2 = call(
        pack_edges, "pack_edges",
        [(x, False) for x in (field_in[0], cotangent[0], first_weight.reshape(27, C, C), second_weight.reshape(27, C, C))],
        [
            near((nx, ny, width), BF16),
            near((nx, ny, width), BF16),
            near((3, nx, width), BF16),
            near((3, nx, width), BF16),
            near((27, C, C), BF16),
            near((27, C, C), BF16),
        ],
        [pltpu.VMEM((6, nx, width), F32), pltpu.SemaphoreType.DMA((4,))])
    taken = swap(given)
    own, bulk, w1b, wfb = call(
        pack_halves, "pack_halves", [(x, True) for x in (field, cot, w1, w2)],
        [
            near((size, nx, width), BF16),
            near((size, nx, width), BF16),
            near((9 * 4 * C, lane), BF16),
            near((lane, 9 * 4 * C), BF16),
        ],
        [pltpu.VMEM((width // lane, nx * ny, lane), F32)] * 2, flops=10 ** 9)
    bulk, taken, wfb = lax.optimization_barrier((bulk, taken, wfb))
    got = swap(bulk)
    whole, = call(join_edges, "join_edges", [(edge, True), (taken, True)], [near((3, across, width), BF16)])
    ends = [(gy_count + j, j + 1) for j in range(gy_count - 1)]
    late = lax.ppermute(whole, ("gx", "gy"), ends + [(b, a) for a, b in ends])
    held = [
        near((3, count + 4, across, wide), BF16),
        near((3, count + 2, across, wide), BF16),
        near((3, count + 2, across, width + lane), BF16),
        near((count, across, width + lane), BF16),
        near((count + 2, across + 16, width + lane), F32),
    ]
    fd, cd, hd, pg, hs, acc = call(
        interior, "interior",
        [(x, True) for x in (own, got, w1b, wfb)],
        held + [near((9, lane, 2 * lane), F32)],
        [
            pltpu.VMEM((count + 2, across + 16, width), F32),
            pltpu.VMEM((count + 1, across + 16, width), F32),
            pltpu.VMEM((count, across, width + lane), F32),
        ],
        limit=32, flops=4 * 10 ** 9)
    fd, cd, hd, pg, hs, send, pre_late = call(
        functools.partial(late_rows, gy_count), "late_rows",
        [(x, True) for x in (fd, cd, hd, pg, hs, late, acc, w1b, wfb)],
        held + [near((rows, lane), BF16), near((across, width + lane), F32)],
        [pltpu.VMEM((3, across + 16, width), F32)],
        limit=32, flops=10 ** 9, aliases={0: 0, 1: 1, 2: 2, 3: 3, 4: 4})

    other = swap(send)
    hd, _, keep = call(
        functools.partial(keep_sums, gy_count), "keep_sums",
        [(x, True) for x in (fd, cd, hd, pg, hs, pre_late, w1b)], [held[2], held[4], near((rows, lane), F32)],
        flops=2 * 10 ** 9, aliases={2: 0, 4: 1})
    other, keep = lax.optimization_barrier((other, keep))
    both, = call(add_pair, "add_pair", [(keep, True), (other, True)], [near((rows, lane), BF16)])
    terms = lax.all_to_all(both.reshape(ranks, rows // ranks, lane), ("gy", "grp"), 0, 0)
    part, = call(add_terms, "add_terms", [(terms, True)], [near(terms.shape[1:], BF16)])
    part, hd, w2 = lax.optimization_barrier((part, hd, w2))
    spread = jnp.broadcast_to(part[None], terms.shape)
    sums = lax.all_to_all(spread, ("gy", "grp"), 0, 0).reshape(rows, lane)
    mine, given = call(
        output_conv, "output_conv", [(hd, True), (w2, True)],
        [near((count, nx, width), BF16), near((count, nx, width), BF16)],
        [pltpu.VMEM((9 * 4 * C, lane), BF16)], flops=2 * 10 ** 9)
    given = swap(given)
    out, = call(
        finish_output, "finish_output", [(mine, True), (given, True)],
        [pltpu.HBM((nx, ny, width), BF16)],
        [pltpu.VMEM((nx, ny, width), BF16), pltpu.VMEM((width // lane, nx * ny, lane), F32), pltpu.SemaphoreType.DMA((nx // 2,))], far=True)
    sums, out = lax.optimization_barrier((sums, out))
    other = swap(sums)
    outs = [pltpu.HBM((27, C, C), F32)] * 2
    scratch = [pltpu.VMEM((27, C, C), F32), pltpu.SemaphoreType.DMA((3,))]
    first, second = call(functools.partial(unpack_own, factor), "unpack_own", [(sums, True)], outs, scratch, far=True)
    other, first, second = lax.optimization_barrier((other, first, second))
    first, second = call(
        functools.partial(unpack_other, factor), "unpack_other", [(other, True), (first, False), (second, False)], outs, scratch, far=True,
        aliases={1: 0, 2: 1})
    shape = (3, 3, 3, C, C)
    return out[None], first.reshape(shape), second.reshape(shape)


def solution(mesh):
    return jax.shard_map(
        shards,
        mesh=mesh,
        in_specs=(P("grp", "gx", "gy", None), P(), P(), P("grp", "gx", "gy", None)),
        out_specs=(P("grp", "gx", "gy", None), P(), P()),
        check_vma=False,
    )
```

```python
import functools
import math

import jax
import jax.numpy as jnp
from jax import lax
from jax.experimental import pallas as pl
from jax.experimental.pallas import tpu as pltpu
from jax.sharding import PartitionSpec as P

C = 64
NZ = 16
BF16 = jnp.bfloat16
F32 = jnp.float32
TAPS = [(dx, dy) for dy in range(3) for dx in range(3)]
BLOCKS = 14


def swap(array):
    return lax.ppermute(array, "gx", [(0, 1), (1, 0)])


def dot(a, b):
    return jnp.dot(a, b, preferred_element_type=F32)


def dot_nt(a, b):
    return lax.dot_general(a, b, (((1,), (1,)), ((), ())), preferred_element_type=F32)


def band(taps):
    zero = jnp.zeros((C, C), BF16)
    left = jnp.concatenate(list(taps) + [zero], axis=0)
    right = jnp.concatenate([zero] + list(taps), axis=0)
    return jnp.concatenate([left, right], axis=1)


def band_flipped(taps):
    zero = jnp.zeros((C, C), BF16)
    back = list(taps)[::-1]
    upper = jnp.concatenate(back + [zero], axis=1)
    lower = jnp.concatenate([zero] + back, axis=1)
    return jnp.concatenate([upper, lower], axis=0)


def packed(pieces):
    blocks = [piece[:, 0:2 * C] for piece in pieces]
    for pair in range(0, 9, 2):
        second = pieces[pair + 1][:, 2 * C:3 * C] if pair + 1 < 9 else jnp.zeros((C, C), F32)
        blocks.append(jnp.concatenate([pieces[pair][:, 2 * C:3 * C], second], axis=1))
    return blocks


def pack_edges(field_hbm, cot_hbm, w1_hbm, w2_hbm, field, cot, edge, given, w1, w2, rows, sems):
    copies = [
        pltpu.make_async_copy(source, target, sems.at[index])
        for index, (source, target) in enumerate(((field_hbm, field), (cot_hbm, cot), (w1_hbm, w1), (w2_hbm, w2)))
    ]
    for copy in copies:
        copy.start()
    for copy in copies[:2]:
        copy.wait()
    nx, ny, _ = field.shape
    gx = lax.axis_index("gx")
    for x in range(nx):
        fields = field[x].astype(F32)
        cots = cot[x].astype(F32)
        for index, row in enumerate((fields[0:1], fields[1:2], cots[0:1], fields[ny - 2:ny - 1], fields[ny - 1:ny], cots[ny - 1:ny])):
            rows[index, x:x + 1, :] = row
    head = rows[0:3].astype(BF16)
    tail = rows[3:6].astype(BF16)
    edge[...] = jnp.where(gx == 0, head, tail)
    given[...] = jnp.where(gx == 0, tail, head)
    for copy in copies[2:]:
        copy.wait()


def join_edges(edge, taken, whole):
    nx = edge.shape[1]
    gx = lax.axis_index("gx")

    @pl.when(gx == 0)
    def _():
        whole[:, 0:nx] = edge[...]
        whole[:, nx:2 * nx] = taken[...]

    @pl.when(gx != 0)
    def _():
        whole[:, 0:nx] = taken[...]
        whole[:, nx:2 * nx] = edge[...]


def put_rows(scratch, start, rows):
    lane = 2 * C
    for tile in range(scratch.shape[0]):
        scratch[tile, start:start + rows.shape[0], :] = rows[:, lane * tile:lane * (tile + 1)]


def take_rows(scratch, start, count, stride):
    return jnp.concatenate(
        [scratch[tile, pl.ds(start, count, stride=stride), :] for tile in range(scratch.shape[0])], axis=1).astype(BF16)


def pack_halves(field, cot, w1, w2, own, bulk, w1b, wfb, turned_f, turned_c):
    nx, ny, _ = field.shape
    half = ny // 2
    for source, target in ((field, turned_f), (cot, turned_c)):
        for x in range(nx):
            put_rows(target, x * ny, source[x].astype(F32))
    gx = lax.axis_index("gx")

    def place(target, first_f, first_c):
        for y in range(half + 2):
            target[y] = take_rows(turned_f, first_f + y, nx, ny)
        for y in range(half + 1):
            target[half + 2 + y] = take_rows(turned_c, first_c + y, nx, ny)

    @pl.when(gx == 0)
    def _():
        place(own, 0, 0)
        place(bulk, half - 2, half - 1)

    @pl.when(gx != 0)
    def _():
        place(own, half - 2, half - 1)
        place(bulk, 0, 0)

    make_bands(w1, w2, w1b, wfb)


def make_bands(w1, w2, w1b, wfb):
    for t, (dx, dy) in enumerate(TAPS):
        rows = slice(t * 4 * C, (t + 1) * 4 * C)
        first = 9 * dx + 3 * dy
        w1b[rows, :] = band([w1[first + z] for z in range(3)])
        wfb[:, rows] = band_flipped([w2[24 - first + z] for z in range(3)])


def blank_edges(copies):
    lane = 2 * C
    zero = jnp.zeros(copies.shape[:-1] + (lane,), BF16)
    copies[..., 0:lane] = zero
    copies[..., copies.shape[-1] - lane:] = zero


def blank_rows(scratch):
    zero = jnp.zeros((scratch.shape[0], 1, scratch.shape[2]), F32)
    scratch[:, 7:8, :] = zero
    scratch[:, scratch.shape[1] - 8:scratch.shape[1] - 7, :] = zero


def shift_rows(scratch, copies, start, first_lane, taps=(0, 1, 2)):
    count, rows, width = scratch.shape
    for dx in taps:
        copies[dx, pl.ds(start, count), :, first_lane:first_lane + width] = scratch[:, 7 + dx:rows - 9 + dx, :].astype(BF16)


def inside_lanes(p):
    lane_of = lax.broadcasted_iota(jnp.int32, (1, 2 * C), 1)
    if p == 0:
        return (lane_of >= C).astype(F32)
    if p == NZ // 2:
        return (lane_of < C).astype(F32)
    return 1.0


def windows(copies, first, count, p):
    lane = 2 * C
    rows = copies.shape[2]
    return jnp.concatenate(
        [
            copies[dx, pl.ds(first + dy, count), :, lane * p:lane * (p + 2)].reshape(count * rows, 2 * lane)
            for dx, dy in TAPS
        ],
        axis=1,
    )


def pre_gradient(grad, pre, p):
    sigma = jax.nn.sigmoid(pre)
    return grad * sigma * (1.0 + pre * (1.0 - sigma)) * inside_lanes(p)


def interior(own, got, w1b, wfb, fd, cd, hd, pg, hs, acc, fs, cs, pre):
    gx = lax.axis_index("gx")
    nx, width = own.shape[1:]
    across = 2 * nx
    count = pg.shape[0]
    cells = count * across
    lane = 2 * C
    pairs = NZ // 2

    def place(left, right):
        for scratch, copies, offset, start, size in ((fs, fd, 2 - 2 * gx, 0, count + 2), (cs, cd, 1 - gx, count + 2, count + 1)):
            for source, row in ((left, 0), (right, nx)):
                rows = source[start:start + size]
                scratch[:, 8 + row:8 + row + nx, :] = rows.astype(F32)
                copies[1, pl.ds(offset, size), row:row + nx, lane:lane + width] = rows

    @pl.when(gx == 0)
    def _():
        place(own, got)

    @pl.when(gx != 0)
    def _():
        place(got, own)

    for scratch in (fs, cs, hs):
        blank_rows(scratch)
    blank_edges(fd)
    blank_edges(cd)
    shift_rows(fs, fd, 2 - 2 * gx, lane, (0, 2))
    shift_rows(cs, cd, 1 - gx, lane, (0, 2))
    for group in range(0, pairs + 1, 3):
        value = dot(jnp.concatenate([windows(fd, 2 - 2 * gx, count, p) for p in range(group, group + 3)], axis=0), w1b[...])
        for p in range(group, group + 3):
            here = slice(lane * p, lane * (p + 1))
            part = value[cells * (p - group):cells * (p - group + 1)]
            pre[:, :, here] = part.reshape(count, across, lane)
            hidden = (part * jax.nn.sigmoid(part) * inside_lanes(p)).reshape(count, across, lane)
            hs[pl.ds(2 - 2 * gx, count), 8:8 + across, here] = hidden
            hd[1, pl.ds(2 - 2 * gx, count), :, here] = hidden.astype(BF16)
    cells = cells - across
    for group in range(0, pairs + 1, 3):
        value = dot_nt(jnp.concatenate([windows(cd, 1 - gx, count - 1, p) for p in range(group, group + 3)], axis=0), wfb[...])
        for p in range(group, group + 3):
            here = slice(lane * p, lane * (p + 1))
            part = value[cells * (p - group):cells * (p - group + 1)]
            grad = pre_gradient(part, pre[pl.ds(gx, count - 1), :, here].reshape(cells, lane), p)
            pg[pl.ds(1 - gx, count - 1), :, here] = grad.astype(BF16).reshape(count - 1, across, lane)
    pg[pl.ds((count - 1) * gx, 1)] = jnp.zeros((1,) + pg.shape[1:], BF16)

    @pl.when(gx == 0)
    def _():
        hd[:, 0:2] = jnp.zeros((3, 2) + hd.shape[2:], BF16)
        shift_rows(hs.at[2:2 + count], hd, 2, 0, (0, 2))
        for t, total in enumerate(second_products(hd, cd)):
            acc[t] = total

    @pl.when(gx != 0)
    def _():
        fd[:, count + 2:count + 4] = jnp.zeros((3, 2) + fd.shape[2:], BF16)
        for t, total in enumerate(first_products(fd, pg)):
            acc[t] = total


def second_products(hd, cd):
    lane = 2 * C
    pairs = NZ // 2
    count, across = hd.shape[1] - 2, hd.shape[2]
    cells = count * across
    cot_t = jnp.concatenate(
        [cd[1, 1:1 + count, :, lane * (p + 1):lane * (p + 2)].reshape(cells, lane).T for p in range(pairs)], axis=1)
    return [
        dot(cot_t, jnp.concatenate(
            [hd[dx, dy:dy + count, :, lane * p:lane * (p + 2)].reshape(cells, 2 * lane) for p in range(pairs)], axis=0))
        for dx, dy in TAPS
    ]


def first_products(fd, pg):
    lane = 2 * C
    pairs = NZ // 2
    count, across, _ = pg.shape
    cells = count * across
    grad_t = jnp.concatenate(
        [pg[:, :, lane * p:lane * (p + 1)].reshape(cells, lane).T for p in range(pairs + 1)], axis=1)
    return [
        dot(grad_t, jnp.concatenate(
            [fd[dx, 1 + dy:1 + dy + count, :, lane * p:lane * (p + 2)].reshape(cells, 2 * lane) for p in range(pairs + 1)], axis=0))
        for dx, dy in TAPS
    ]


def folded(total):
    return total[0:C, 0:3 * C] + total[C:2 * C, C:4 * C]


def second_late(hd, cd):
    lane = 2 * C
    pairs = NZ // 2
    late = ((0, 1), (0,), ())
    products = []
    for dx, dy in TAPS:
        if late[dy]:
            cots = jnp.concatenate(
                [cd[1, 1 + y, :, lane * (p + 1):lane * (p + 2)] for y in late[dy] for p in range(pairs)], axis=0)
            rows = jnp.concatenate(
                [hd[dx, y + dy, :, lane * p:lane * (p + 2)] for y in late[dy] for p in range(pairs)], axis=0)
            products.append(dot(cots.T, rows))
        else:
            products.append(0.0)
    return products


def first_late(fd, pg):
    lane = 2 * C
    pairs = NZ // 2
    count, across, _ = pg.shape
    y = count - 1
    extra = 2 * lane - (pairs + 1) * across
    grad_t = jnp.concatenate(
        [pg[y, :, lane * p:lane * (p + 1)] for p in range(pairs + 1)] + [jnp.zeros((extra, lane), BF16)], axis=0).T
    pad = jnp.zeros((extra, 2 * lane), BF16)
    return [
        dot(grad_t, jnp.concatenate(
            [fd[dx, y + dy + 1, :, lane * p:lane * (p + 2)] for p in range(pairs + 1)] + [pad], axis=0))
        for dx, dy in TAPS
    ]


def sums_of(products):
    return packed([folded(product) for product in products])


def store_blocks(target, blocks):
    for index, block in enumerate(blocks):
        target[index * C:(index + 1) * C, :] = block.astype(target.dtype)
    if target.shape[0] > BLOCKS * C:
        target[BLOCKS * C:, :] = jnp.zeros((target.shape[0] - BLOCKS * C, 2 * C), target.dtype)


def hidden_of(value, p):
    return value * jax.nn.sigmoid(value) * inside_lanes(p)


def stacked(copies, first, count, pairs):
    return jnp.concatenate([windows(copies, first, count, p) for p in range(pairs + 1)], axis=0)


def late_rows(gy_count, fd_in, cd_in, hd_in, pg_in, hs_in, rows, acc, w1b, wfb, fd, cd, hd, pg, hs, send, pre_late, rs):
    gx = lax.axis_index("gx")
    gy = lax.axis_index("gy")
    count, across, _ = pg.shape
    lane = 2 * C
    pairs = NZ // 2
    rs[:, 8:8 + across, :] = rows[...].astype(F32)
    blank_rows(rs)

    @pl.when(gx == 0)
    def _():
        shift_rows(rs.at[0:2], fd, 0, lane)
        shift_rows(rs.at[2:3], cd, 0, lane)
        value = dot(stacked(fd, 0, 2, pairs), w1b[...])
        grad = dot_nt(stacked(cd, 0, 1, pairs), wfb[...])
        before = jnp.where(gy == 0, 0.0, 1.0)
        for p in range(pairs + 1):
            here = slice(lane * p, lane * (p + 1))
            early = value[2 * across * p:2 * across * p + across]
            later = value[2 * across * p + across:2 * across * (p + 1)]
            mine = pre_gradient(grad[across * p:across * (p + 1)], later, p)
            pg[0, :, here] = mine.astype(BF16)
            both = jnp.stack([hidden_of(early, p) * before, hidden_of(later, p)])
            hs[0:2, 8:8 + across, here] = both
            hd[1, 0:2, :, here] = both.astype(BF16)
        shift_rows(hs.at[0:2], hd, 0, 0, (0, 2))
        store_blocks(send, sums_of([acc[t] + late for t, late in enumerate(second_late(hd, cd))]))

    @pl.when(gx != 0)
    def _():
        shift_rows(rs.at[0:2], fd, count + 2, lane)
        shift_rows(rs.at[2:3], cd, count + 1, lane)
        value = dot(stacked(fd, count, 1, pairs), w1b[...])
        grad = dot_nt(stacked(cd, count - 1, 1, pairs), wfb[...])
        for p in range(pairs + 1):
            here = slice(lane * p, lane * (p + 1))
            part = slice(across * p, across * (p + 1))
            pre_late[:, here] = value[part]
            pg[count - 1, :, here] = pre_gradient(grad[part], value[part], p).astype(BF16)
        store_blocks(send, sums_of([acc[t] + late for t, late in enumerate(first_late(fd, pg))]))


def keep_sums(gy_count, fd, cd, hd_in, pg, hs_in, pre_late, w1b, hd, hs, keep):
    gx = lax.axis_index("gx")
    gy = lax.axis_index("gy")
    count, across, _ = pg.shape
    lane = 2 * C
    pairs = NZ // 2

    @pl.when(gx == 0)
    def _():
        store_blocks(keep, sums_of(first_products(fd, pg)))

    @pl.when(gx != 0)
    def _():
        value = dot(stacked(fd, count + 1, 1, pairs), w1b[...])
        beyond = jnp.where(gy == gy_count - 1, 0.0, 1.0)
        for p in range(pairs + 1):
            here = slice(lane * p, lane * (p + 1))
            part = slice(across * p, across * (p + 1))
            both = jnp.stack([hidden_of(pre_late[:, here], p), hidden_of(value[part], p) * beyond])
            hs[count:count + 2, 8:8 + across, here] = both
            hd[1, count:count + 2, :, here] = both.astype(BF16)
        shift_rows(hs, hd, 0, 0, (0, 2))
        store_blocks(keep, sums_of(second_products(hd, cd)))


def output_conv(hd, w2, mine, given, w2b):
    for t, (dx, dy) in enumerate(TAPS):
        w2b[t * 4 * C:(t + 1) * 4 * C, :] = band([w2[9 * dx + 3 * dy + z] for z in range(3)])
    gx = lax.axis_index("gx")
    count, half, _ = mine.shape
    lane = 2 * C
    for p in range(NZ // 2):
        here = slice(lane * p, lane * (p + 1))
        value = dot(windows(hd, 0, count, p), w2b[...]).reshape(count, 2 * half, lane)
        left, right = value[:, 0:half], value[:, half:]
        mine[:, :, here] = jnp.where(gx == 0, left, right).astype(BF16)
        given[:, :, here] = jnp.where(gx == 0, right, left).astype(BF16)


def finish_output(mine, other, out, turned, scratch, sems):
    count, nx, width = mine.shape
    gx = lax.axis_index("gx")
    for y in range(count):
        a = mine[y].astype(F32)
        b = other[y].astype(F32)
        put_rows(scratch, y * nx, jnp.where(gx == 0, a, b))
        put_rows(scratch, (count + y) * nx, jnp.where(gx == 0, b, a))
    copies = []
    for x in range(nx):
        turned[x] = take_rows(scratch, x, 2 * count, nx)
        if x % 2:
            copies.append(pltpu.make_async_copy(turned.at[x - 1:x + 1], out.at[x - 1:x + 1], sems.at[x // 2]))
            copies[-1].start()
    for copy in copies:
        copy.wait()


def add_pair(keep, other, out):
    out[...] = (keep[...] + other[...].astype(F32)).astype(BF16)


def add_terms(terms, out):
    total = terms[0].astype(F32)
    for index in range(1, terms.shape[0]):
        total = total + terms[index].astype(F32)
    out[...] = total.astype(BF16)


def unpack(factor, is_first, rows, first, second, held, sems):
    def each(act):
        for chosen, target in ((is_first, first), (jnp.logical_not(is_first), second)):
            @pl.when(chosen)
            def _():
                act(target)

    def copy_of(dx, target):
        piece = slice(9 * dx, 9 * dx + 9)
        return pltpu.make_async_copy(held.at[piece], target.at[piece], sems.at[dx])

    for dx in range(3):
        for dy in range(3):
            t = 3 * dy + dx
            place = 9 * dx + 3 * dy
            turned = rows[t * C:(t + 1) * C, :].T.astype(F32) * factor
            held[place] = turned[0:C]
            held[place + 1] = turned[C:2 * C]
            turned = rows[(9 + t // 2) * C:(10 + t // 2) * C, :].T.astype(F32) * factor
            held[place + 2] = turned[t % 2 * C:(t % 2 + 1) * C]
        each(lambda target: copy_of(dx, target).start())
    each(lambda target: [copy_of(dx, target).wait() for dx in range(3)])


def unpack_own(factor, rows, first, second, held, sems):
    unpack(factor, lax.axis_index("gx") == 0, rows, first, second, held, sems)


def unpack_other(factor, rows, first_in, second_in, first, second, held, sems):
    unpack(factor, lax.axis_index("gx") != 0, rows, first, second, held, sems)


def near(shape, dtype):
    return pltpu.VMEM(shape, dtype)


def call(body, name, inputs, outs, scratch=(), limit=16, flops=0, far=False, aliases=None):
    placed = [pltpu.with_memory_space_constraint(x, pltpu.VMEM if held else pltpu.HBM) for x, held in inputs]
    size = sum(x.size * x.dtype.itemsize for x, _ in inputs)
    return pl.pallas_call(
        body,
        out_shape=list(outs),
        in_specs=[pl.BlockSpec(memory_space=pltpu.VMEM if held else pl.ANY) for _, held in inputs],
        out_specs=[pl.BlockSpec(memory_space=pl.ANY if far else pltpu.VMEM)] * len(outs),
        scratch_shapes=list(scratch),
        input_output_aliases=aliases or {},
        compiler_params=pltpu.CompilerParams(vmem_limit_bytes=limit * 1024 * 1024),
        cost_estimate=pl.CostEstimate(flops=flops, bytes_accessed=size, transcendentals=0),
        name=name,
    )(*placed)


def shards(field_in, first_weight, second_weight, cotangent):
    nx, ny, width = field_in.shape[1:]
    gx_count, gy_count, grp_count = (lax.axis_size(axis) for axis in ("gx", "gy", "grp"))
    total = field_in.shape[0] * nx * ny * NZ * gx_count * gy_count * grp_count
    factor = 1.0 / math.sqrt(total)
    ranks = gy_count * grp_count
    rows = -(-BLOCKS * C // (8 * ranks)) * 8 * ranks
    lane = 2 * C
    wide = width + 2 * lane
    count = ny // 2
    across = 2 * nx
    size = 2 * count + 3

    field, cot, edge, given, w1, w2 = call(
        pack_edges, "pack_edges",
        [(x, False) for x in (field_in[0], cotangent[0], first_weight.reshape(27, C, C), second_weight.reshape(27, C, C))],
        [
            near((nx, ny, width), BF16),
            near((nx, ny, width), BF16),
            near((3, nx, width), BF16),
            near((3, nx, width), BF16),
            near((27, C, C), BF16),
            near((27, C, C), BF16),
        ],
        [pltpu.VMEM((6, nx, width), F32), pltpu.SemaphoreType.DMA((4,))])
    taken = swap(given)
    own, bulk, w1b, wfb = call(
        pack_halves, "pack_halves", [(x, True) for x in (field, cot, w1, w2)],
        [
            near((size, nx, width), BF16),
            near((size, nx, width), BF16),
            near((9 * 4 * C, lane), BF16),
            near((lane, 9 * 4 * C), BF16),
        ],
        [pltpu.VMEM((width // lane, nx * ny, lane), F32)] * 2, flops=10 ** 9)
    bulk, taken, wfb = lax.optimization_barrier((bulk, taken, wfb))
    got = swap(bulk)
    whole, = call(join_edges, "join_edges", [(edge, True), (taken, True)], [near((3, across, width), BF16)])
    ends = [(gy_count + j, j + 1) for j in range(gy_count - 1)]
    late = lax.ppermute(whole, ("gx", "gy"), ends + [(b, a) for a, b in ends])
    held = [
        near((3, count + 4, across, wide), BF16),
        near((3, count + 2, across, wide), BF16),
        near((3, count + 2, across, width + lane), BF16),
        near((count, across, width + lane), BF16),
        near((count + 2, across + 16, width + lane), F32),
    ]
    fd, cd, hd, pg, hs, acc = call(
        interior, "interior",
        [(x, True) for x in (own, got, w1b, wfb)],
        held + [near((9, lane, 2 * lane), F32)],
        [
            pltpu.VMEM((count + 2, across + 16, width), F32),
            pltpu.VMEM((count + 1, across + 16, width), F32),
            pltpu.VMEM((count, across, width + lane), F32),
        ],
        limit=32, flops=4 * 10 ** 9)
    fd, cd, hd, pg, hs, send, pre_late = call(
        functools.partial(late_rows, gy_count), "late_rows",
        [(x, True) for x in (fd, cd, hd, pg, hs, late, acc, w1b, wfb)],
        held + [near((rows, lane), BF16), near((across, width + lane), F32)],
        [pltpu.VMEM((3, across + 16, width), F32)],
        limit=32, flops=10 ** 9, aliases={0: 0, 1: 1, 2: 2, 3: 3, 4: 4})

    other = swap(send)
    hd, _, keep = call(
        functools.partial(keep_sums, gy_count), "keep_sums",
        [(x, True) for x in (fd, cd, hd, pg, hs, pre_late, w1b)], [held[2], held[4], near((rows, lane), F32)],
        flops=2 * 10 ** 9, aliases={2: 0, 4: 1})
    other, keep = lax.optimization_barrier((other, keep))
    both, = call(add_pair, "add_pair", [(keep, True), (other, True)], [near((rows, lane), BF16)])
    terms = lax.all_to_all(both.reshape(ranks, rows // ranks, lane), ("grp", "gy"), 0, 0)
    part, = call(add_terms, "add_terms", [(terms, True)], [near(terms.shape[1:], BF16)])
    part, hd, w2 = lax.optimization_barrier((part, hd, w2))
    spread = jnp.broadcast_to(part[None], terms.shape)
    sums = lax.all_to_all(spread, ("grp", "gy"), 0, 0).reshape(rows, lane)
    mine, given = call(
        output_conv, "output_conv", [(hd, True), (w2, True)],
        [near((count, nx, width), BF16), near((count, nx, width), BF16)],
        [pltpu.VMEM((9 * 4 * C, lane), BF16)], flops=2 * 10 ** 9)
    given = swap(given)
    out, = call(
        finish_output, "finish_output", [(mine, True), (given, True)],
        [pltpu.HBM((nx, ny, width), BF16)],
        [pltpu.VMEM((nx, ny, width), BF16), pltpu.VMEM((width // lane, nx * ny, lane), F32), pltpu.SemaphoreType.DMA((nx // 2,))], far=True)
    sums, out = lax.optimization_barrier((sums, out))
    other = swap(sums)
    outs = [pltpu.HBM((27, C, C), F32)] * 2
    scratch = [pltpu.VMEM((27, C, C), F32), pltpu.SemaphoreType.DMA((3,))]
    first, second = call(functools.partial(unpack_own, factor), "unpack_own", [(sums, True)], outs, scratch, far=True)
    other, first, second = lax.optimization_barrier((other, first, second))
    first, second = call(
        functools.partial(unpack_other, factor), "unpack_other", [(other, True), (first, False), (second, False)], outs, scratch, far=True,
        aliases={1: 0, 2: 1})
    shape = (3, 3, 3, C, C)
    return out[None], first.reshape(shape), second.reshape(shape)


def solution(mesh):
    return jax.shard_map(
        shards,
        mesh=mesh,
        in_specs=(P("grp", "gx", "gy", None), P(), P(), P("grp", "gx", "gy", None)),
        out_specs=(P("grp", "gx", "gy", None), P(), P()),
        check_vma=False,
    )
```

```python
import functools
import math

import jax
import jax.numpy as jnp
from jax import lax
from jax.experimental import pallas as pl
from jax.experimental.pallas import tpu as pltpu
from jax.sharding import PartitionSpec as P

C = 64
NZ = 16
BF16 = jnp.bfloat16
F32 = jnp.float32
TAPS = [(dx, dy) for dy in range(3) for dx in range(3)]
BLOCKS = 14


def swap(array):
    return lax.ppermute(array, "gx", [(0, 1), (1, 0)])


def dot(a, b):
    return jnp.dot(a, b, preferred_element_type=F32)


def dot_nt(a, b):
    return lax.dot_general(a, b, (((1,), (1,)), ((), ())), preferred_element_type=F32)


def band(taps):
    zero = jnp.zeros((C, C), BF16)
    left = jnp.concatenate(list(taps) + [zero], axis=0)
    right = jnp.concatenate([zero] + list(taps), axis=0)
    return jnp.concatenate([left, right], axis=1)


def band_flipped(taps):
    zero = jnp.zeros((C, C), BF16)
    back = list(taps)[::-1]
    upper = jnp.concatenate(back + [zero], axis=1)
    lower = jnp.concatenate([zero] + back, axis=1)
    return jnp.concatenate([upper, lower], axis=0)


def packed(pieces):
    blocks = [piece[:, 0:2 * C] for piece in pieces]
    for pair in range(0, 9, 2):
        second = pieces[pair + 1][:, 2 * C:3 * C] if pair + 1 < 9 else jnp.zeros((C, C), F32)
        blocks.append(jnp.concatenate([pieces[pair][:, 2 * C:3 * C], second], axis=1))
    return blocks


def pack_edges(field_hbm, cot_hbm, w1_hbm, w2_hbm, field, cot, edge, given, w1, w2, rows, sems):
    copies = [
        pltpu.make_async_copy(source, target, sems.at[index])
        for index, (source, target) in enumerate(((field_hbm, field), (cot_hbm, cot), (w1_hbm, w1), (w2_hbm, w2)))
    ]
    for copy in copies:
        copy.start()
    for copy in copies[:2]:
        copy.wait()
    nx, ny, _ = field.shape
    gx = lax.axis_index("gx")
    for x in range(nx):
        fields = field[x].astype(F32)
        cots = cot[x].astype(F32)
        for index, row in enumerate((fields[0:1], fields[1:2], cots[0:1], fields[ny - 2:ny - 1], fields[ny - 1:ny], cots[ny - 1:ny])):
            rows[index, x:x + 1, :] = row
    head = rows[0:3].astype(BF16)
    tail = rows[3:6].astype(BF16)
    edge[...] = jnp.where(gx == 0, head, tail)
    given[...] = jnp.where(gx == 0, tail, head)
    for copy in copies[2:]:
        copy.wait()


def join_edges(edge, taken, whole):
    nx = edge.shape[1]
    gx = lax.axis_index("gx")

    @pl.when(gx == 0)
    def _():
        whole[:, 0:nx] = edge[...]
        whole[:, nx:2 * nx] = taken[...]

    @pl.when(gx != 0)
    def _():
        whole[:, 0:nx] = taken[...]
        whole[:, nx:2 * nx] = edge[...]


def put_rows(scratch, start, rows):
    lane = 2 * C
    for tile in range(scratch.shape[0]):
        scratch[tile, start:start + rows.shape[0], :] = rows[:, lane * tile:lane * (tile + 1)]


def take_rows(scratch, start, count, stride):
    return jnp.concatenate(
        [scratch[tile, pl.ds(start, count, stride=stride), :] for tile in range(scratch.shape[0])], axis=1).astype(BF16)


def pack_halves(field, cot, w1, w2, own, bulk, w1b, wfb, turned_f, turned_c):
    nx, ny, _ = field.shape
    half = ny // 2
    for source, target in ((field, turned_f), (cot, turned_c)):
        for x in range(nx):
            put_rows(target, x * ny, source[x].astype(F32))
    gx = lax.axis_index("gx")

    def place(target, first_f, first_c):
        for y in range(half + 2):
            target[y] = take_rows(turned_f, first_f + y, nx, ny)
        for y in range(half + 1):
            target[half + 2 + y] = take_rows(turned_c, first_c + y, nx, ny)

    @pl.when(gx == 0)
    def _():
        place(own, 0, 0)
        place(bulk, half - 2, half - 1)

    @pl.when(gx != 0)
    def _():
        place(own, half - 2, half - 1)
        place(bulk, 0, 0)

    make_bands(w1, w2, w1b, wfb)


def make_bands(w1, w2, w1b, wfb):
    for t, (dx, dy) in enumerate(TAPS):
        rows = slice(t * 4 * C, (t + 1) * 4 * C)
        first = 9 * dx + 3 * dy
        w1b[rows, :] = band([w1[first + z] for z in range(3)])
        wfb[:, rows] = band_flipped([w2[24 - first + z] for z in range(3)])


def blank_edges(copies):
    lane = 2 * C
    zero = jnp.zeros(copies.shape[:-1] + (lane,), BF16)
    copies[..., 0:lane] = zero
    copies[..., copies.shape[-1] - lane:] = zero


def blank_rows(scratch):
    zero = jnp.zeros((scratch.shape[0], 1, scratch.shape[2]), F32)
    scratch[:, 7:8, :] = zero
    scratch[:, scratch.shape[1] - 8:scratch.shape[1] - 7, :] = zero


def shift_rows(scratch, copies, start, first_lane, taps=(0, 1, 2)):
    count, rows, width = scratch.shape
    for dx in taps:
        copies[dx, pl.ds(start, count), :, first_lane:first_lane + width] = scratch[:, 7 + dx:rows - 9 + dx, :].astype(BF16)


def inside_lanes(p):
    lane_of = lax.broadcasted_iota(jnp.int32, (1, 2 * C), 1)
    if p == 0:
        return (lane_of >= C).astype(F32)
    if p == NZ // 2:
        return (lane_of < C).astype(F32)
    return 1.0


def windows(copies, first, count, p):
    lane = 2 * C
    rows = copies.shape[2]
    return jnp.concatenate(
        [
            copies[dx, pl.ds(first + dy, count), :, lane * p:lane * (p + 2)].reshape(count * rows, 2 * lane)
            for dx, dy in TAPS
        ],
        axis=1,
    )


def pre_gradient(grad, pre, p):
    sigma = jax.nn.sigmoid(pre)
    return grad * sigma * (1.0 + pre * (1.0 - sigma)) * inside_lanes(p)


def interior(own, got, w1b, wfb, fd, cd, hd, pg, hs, acc, fs, cs, pre):
    gx = lax.axis_index("gx")
    nx, width = own.shape[1:]
    across = 2 * nx
    count = pg.shape[0]
    cells = count * across
    lane = 2 * C
    pairs = NZ // 2

    def place(left, right):
        for scratch, copies, offset, start, size in ((fs, fd, 2 - 2 * gx, 0, count + 2), (cs, cd, 1 - gx, count + 2, count + 1)):
            for source, row in ((left, 0), (right, nx)):
                rows = source[start:start + size]
                scratch[:, 8 + row:8 + row + nx, :] = rows.astype(F32)
                copies[1, pl.ds(offset, size), row:row + nx, lane:lane + width] = rows

    @pl.when(gx == 0)
    def _():
        place(own, got)

    @pl.when(gx != 0)
    def _():
        place(got, own)

    for scratch in (fs, cs, hs):
        blank_rows(scratch)
    blank_edges(fd)
    shift_rows(fs, fd, 2 - 2 * gx, lane, (0, 2))
    for group in range(0, pairs + 1, 3):
        value = dot(jnp.concatenate([windows(fd, 2 - 2 * gx, count, p) for p in range(group, group + 3)], axis=0), w1b[...])
        for p in range(group, group + 3):
            here = slice(lane * p, lane * (p + 1))
            part = value[cells * (p - group):cells * (p - group + 1)]
            pre[:, :, here] = part.reshape(count, across, lane)
            hidden = (part * jax.nn.sigmoid(part) * inside_lanes(p)).reshape(count, across, lane)
            hs[pl.ds(2 - 2 * gx, count), 8:8 + across, here] = hidden
            hd[1, pl.ds(2 - 2 * gx, count), :, here] = hidden.astype(BF16)
    blank_edges(cd)
    shift_rows(cs, cd, 1 - gx, lane, (0, 2))
    cells = cells - across
    for group in range(0, pairs + 1, 3):
        value = dot_nt(jnp.concatenate([windows(cd, 1 - gx, count - 1, p) for p in range(group, group + 3)], axis=0), wfb[...])
        for p in range(group, group + 3):
            here = slice(lane * p, lane * (p + 1))
            part = value[cells * (p - group):cells * (p - group + 1)]
            grad = pre_gradient(part, pre[pl.ds(gx, count - 1), :, here].reshape(cells, lane), p)
            pg[pl.ds(1 - gx, count - 1), :, here] = grad.astype(BF16).reshape(count - 1, across, lane)
    pg[pl.ds((count - 1) * gx, 1)] = jnp.zeros((1,) + pg.shape[1:], BF16)

    @pl.when(gx == 0)
    def _():
        hd[:, 0:2] = jnp.zeros((3, 2) + hd.shape[2:], BF16)
        shift_rows(hs.at[2:2 + count], hd, 2, 0, (0, 2))
        for t, total in enumerate(second_products(hd, cd)):
            acc[t] = total

    @pl.when(gx != 0)
    def _():
        fd[:, count + 2:count + 4] = jnp.zeros((3, 2) + fd.shape[2:], BF16)
        for t, total in enumerate(first_products(fd, pg)):
            acc[t] = total


def second_products(hd, cd):
    lane = 2 * C
    pairs = NZ // 2
    count, across = hd.shape[1] - 2, hd.shape[2]
    cells = count * across
    cot_t = jnp.concatenate(
        [cd[1, 1:1 + count, :, lane * (p + 1):lane * (p + 2)].reshape(cells, lane).T for p in range(pairs)], axis=1)
    return [
        dot(cot_t, jnp.concatenate(
            [hd[dx, dy:dy + count, :, lane * p:lane * (p + 2)].reshape(cells, 2 * lane) for p in range(pairs)], axis=0))
        for dx, dy in TAPS
    ]


def first_products(fd, pg):
    lane = 2 * C
    pairs = NZ // 2
    count, across, _ = pg.shape
    cells = count * across
    grad_t = jnp.concatenate(
        [pg[:, :, lane * p:lane * (p + 1)].reshape(cells, lane).T for p in range(pairs + 1)], axis=1)
    return [
        dot(grad_t, jnp.concatenate(
            [fd[dx, 1 + dy:1 + dy + count, :, lane * p:lane * (p + 2)].reshape(cells, 2 * lane) for p in range(pairs + 1)], axis=0))
        for dx, dy in TAPS
    ]


def folded(total):
    return total[0:C, 0:3 * C] + total[C:2 * C, C:4 * C]


def second_late(hd, cd):
    lane = 2 * C
    pairs = NZ // 2
    late = ((0, 1), (0,), ())
    products = []
    for dx, dy in TAPS:
        if late[dy]:
            cots = jnp.concatenate(
                [cd[1, 1 + y, :, lane * (p + 1):lane * (p + 2)] for y in late[dy] for p in range(pairs)], axis=0)
            rows = jnp.concatenate(
                [hd[dx, y + dy, :, lane * p:lane * (p + 2)] for y in late[dy] for p in range(pairs)], axis=0)
            products.append(dot(cots.T, rows))
        else:
            products.append(0.0)
    return products


def first_late(fd, pg):
    lane = 2 * C
    pairs = NZ // 2
    count, across, _ = pg.shape
    y = count - 1
    extra = 2 * lane - (pairs + 1) * across
    grad_t = jnp.concatenate(
        [pg[y, :, lane * p:lane * (p + 1)] for p in range(pairs + 1)] + [jnp.zeros((extra, lane), BF16)], axis=0).T
    pad = jnp.zeros((extra, 2 * lane), BF16)
    return [
        dot(grad_t, jnp.concatenate(
            [fd[dx, y + dy + 1, :, lane * p:lane * (p + 2)] for p in range(pairs + 1)] + [pad], axis=0))
        for dx, dy in TAPS
    ]


def sums_of(products):
    return packed([folded(product) for product in products])


def store_blocks(target, blocks):
    for index, block in enumerate(blocks):
        target[index * C:(index + 1) * C, :] = block.astype(target.dtype)
    if target.shape[0] > BLOCKS * C:
        target[BLOCKS * C:, :] = jnp.zeros((target.shape[0] - BLOCKS * C, 2 * C), target.dtype)


def hidden_of(value, p):
    return value * jax.nn.sigmoid(value) * inside_lanes(p)


def stacked(copies, first, count, pairs):
    return jnp.concatenate([windows(copies, first, count, p) for p in range(pairs + 1)], axis=0)


def late_rows(gy_count, fd_in, cd_in, hd_in, pg_in, hs_in, rows, acc, w1b, wfb, fd, cd, hd, pg, hs, send, pre_late, rs):
    gx = lax.axis_index("gx")
    gy = lax.axis_index("gy")
    count, across, _ = pg.shape
    lane = 2 * C
    pairs = NZ // 2
    rs[:, 8:8 + across, :] = rows[...].astype(F32)
    blank_rows(rs)

    @pl.when(gx == 0)
    def _():
        shift_rows(rs.at[0:2], fd, 0, lane)
        shift_rows(rs.at[2:3], cd, 0, lane)
        value = dot(stacked(fd, 0, 2, pairs), w1b[...])
        grad = dot_nt(stacked(cd, 0, 1, pairs), wfb[...])
        before = jnp.where(gy == 0, 0.0, 1.0)
        for p in range(pairs + 1):
            here = slice(lane * p, lane * (p + 1))
            early = value[2 * across * p:2 * across * p + across]
            later = value[2 * across * p + across:2 * across * (p + 1)]
            mine = pre_gradient(grad[across * p:across * (p + 1)], later, p)
            pg[0, :, here] = mine.astype(BF16)
            both = jnp.stack([hidden_of(early, p) * before, hidden_of(later, p)])
            hs[0:2, 8:8 + across, here] = both
            hd[1, 0:2, :, here] = both.astype(BF16)
        shift_rows(hs.at[0:2], hd, 0, 0, (0, 2))
        store_blocks(send, sums_of([acc[t] + late for t, late in enumerate(second_late(hd, cd))]))

    @pl.when(gx != 0)
    def _():
        shift_rows(rs.at[0:2], fd, count + 2, lane)
        shift_rows(rs.at[2:3], cd, count + 1, lane)
        value = dot(stacked(fd, count, 1, pairs), w1b[...])
        grad = dot_nt(stacked(cd, count - 1, 1, pairs), wfb[...])
        for p in range(pairs + 1):
            here = slice(lane * p, lane * (p + 1))
            part = slice(across * p, across * (p + 1))
            pre_late[:, here] = value[part]
            pg[count - 1, :, here] = pre_gradient(grad[part], value[part], p).astype(BF16)
        store_blocks(send, sums_of([acc[t] + late for t, late in enumerate(first_late(fd, pg))]))


def keep_sums(gy_count, fd, cd, hd_in, pg, hs_in, pre_late, w1b, hd, hs, keep):
    gx = lax.axis_index("gx")
    gy = lax.axis_index("gy")
    count, across, _ = pg.shape
    lane = 2 * C
    pairs = NZ // 2

    @pl.when(gx == 0)
    def _():
        store_blocks(keep, sums_of(first_products(fd, pg)))

    @pl.when(gx != 0)
    def _():
        value = dot(stacked(fd, count + 1, 1, pairs), w1b[...])
        beyond = jnp.where(gy == gy_count - 1, 0.0, 1.0)
        for p in range(pairs + 1):
            here = slice(lane * p, lane * (p + 1))
            part = slice(across * p, across * (p + 1))
            both = jnp.stack([hidden_of(pre_late[:, here], p), hidden_of(value[part], p) * beyond])
            hs[count:count + 2, 8:8 + across, here] = both
            hd[1, count:count + 2, :, here] = both.astype(BF16)
        shift_rows(hs, hd, 0, 0, (0, 2))
        store_blocks(keep, sums_of(second_products(hd, cd)))


def output_conv(hd, w2, mine, given, w2b):
    for t, (dx, dy) in enumerate(TAPS):
        w2b[t * 4 * C:(t + 1) * 4 * C, :] = band([w2[9 * dx + 3 * dy + z] for z in range(3)])
    gx = lax.axis_index("gx")
    count, half, _ = mine.shape
    lane = 2 * C
    for p in range(NZ // 2):
        here = slice(lane * p, lane * (p + 1))
        value = dot(windows(hd, 0, count, p), w2b[...]).reshape(count, 2 * half, lane)
        left, right = value[:, 0:half], value[:, half:]
        mine[:, :, here] = jnp.where(gx == 0, left, right).astype(BF16)
        given[:, :, here] = jnp.where(gx == 0, right, left).astype(BF16)


def finish_output(mine, other, out, turned, scratch, sems):
    count, nx, width = mine.shape
    gx = lax.axis_index("gx")
    for y in range(count):
        a = mine[y].astype(F32)
        b = other[y].astype(F32)
        put_rows(scratch, y * nx, jnp.where(gx == 0, a, b))
        put_rows(scratch, (count + y) * nx, jnp.where(gx == 0, b, a))
    copies = []
    for x in range(nx):
        turned[x] = take_rows(scratch, x, 2 * count, nx)
        if x % 2:
            copies.append(pltpu.make_async_copy(turned.at[x - 1:x + 1], out.at[x - 1:x + 1], sems.at[x // 2]))
            copies[-1].start()
    for copy in copies:
        copy.wait()


def add_pair(keep, other, out):
    out[...] = (keep[...] + other[...].astype(F32)).astype(BF16)


def add_terms(terms, out):
    total = terms[0].astype(F32)
    for index in range(1, terms.shape[0]):
        total = total + terms[index].astype(F32)
    out[...] = total.astype(BF16)


def unpack(factor, is_first, rows, first, second, held, sems):
    def each(act):
        for chosen, target in ((is_first, first), (jnp.logical_not(is_first), second)):
            @pl.when(chosen)
            def _():
                act(target)

    def copy_of(dx, target):
        piece = slice(9 * dx, 9 * dx + 9)
        return pltpu.make_async_copy(held.at[piece], target.at[piece], sems.at[dx])

    for dx in range(3):
        for dy in range(3):
            t = 3 * dy + dx
            place = 9 * dx + 3 * dy
            turned = rows[t * C:(t + 1) * C, :].T.astype(F32) * factor
            held[place] = turned[0:C]
            held[place + 1] = turned[C:2 * C]
            turned = rows[(9 + t // 2) * C:(10 + t // 2) * C, :].T.astype(F32) * factor
            held[place + 2] = turned[t % 2 * C:(t % 2 + 1) * C]
        each(lambda target: copy_of(dx, target).start())
    each(lambda target: [copy_of(dx, target).wait() for dx in range(3)])


def unpack_own(factor, rows, first, second, held, sems):
    unpack(factor, lax.axis_index("gx") == 0, rows, first, second, held, sems)


def unpack_other(factor, rows, first_in, second_in, first, second, held, sems):
    unpack(factor, lax.axis_index("gx") != 0, rows, first, second, held, sems)


def near(shape, dtype):
    return pltpu.VMEM(shape, dtype)


def call(body, name, inputs, outs, scratch=(), limit=16, flops=0, far=False, aliases=None):
    placed = [pltpu.with_memory_space_constraint(x, pltpu.VMEM if held else pltpu.HBM) for x, held in inputs]
    size = sum(x.size * x.dtype.itemsize for x, _ in inputs)
    return pl.pallas_call(
        body,
        out_shape=list(outs),
        in_specs=[pl.BlockSpec(memory_space=pltpu.VMEM if held else pl.ANY) for _, held in inputs],
        out_specs=[pl.BlockSpec(memory_space=pl.ANY if far else pltpu.VMEM)] * len(outs),
        scratch_shapes=list(scratch),
        input_output_aliases=aliases or {},
        compiler_params=pltpu.CompilerParams(vmem_limit_bytes=limit * 1024 * 1024),
        cost_estimate=pl.CostEstimate(flops=flops, bytes_accessed=size, transcendentals=0),
        name=name,
    )(*placed)


def shards(field_in, first_weight, second_weight, cotangent):
    nx, ny, width = field_in.shape[1:]
    gx_count, gy_count, grp_count = (lax.axis_size(axis) for axis in ("gx", "gy", "grp"))
    total = field_in.shape[0] * nx * ny * NZ * gx_count * gy_count * grp_count
    factor = 1.0 / math.sqrt(total)
    ranks = gy_count * grp_count
    rows = -(-BLOCKS * C // (8 * ranks)) * 8 * ranks
    lane = 2 * C
    wide = width + 2 * lane
    count = ny // 2
    across = 2 * nx
    size = 2 * count + 3

    field, cot, edge, given, w1, w2 = call(
        pack_edges, "pack_edges",
        [(x, False) for x in (field_in[0], cotangent[0], first_weight.reshape(27, C, C), second_weight.reshape(27, C, C))],
        [
            near((nx, ny, width), BF16),
            near((nx, ny, width), BF16),
            near((3, nx, width), BF16),
            near((3, nx, width), BF16),
            near((27, C, C), BF16),
            near((27, C, C), BF16),
        ],
        [pltpu.VMEM((6, nx, width), F32), pltpu.SemaphoreType.DMA((4,))])
    taken = swap(given)
    own, bulk, w1b, wfb = call(
        pack_halves, "pack_halves", [(x, True) for x in (field, cot, w1, w2)],
        [
            near((size, nx, width), BF16),
            near((size, nx, width), BF16),
            near((9 * 4 * C, lane), BF16),
            near((lane, 9 * 4 * C), BF16),
        ],
        [pltpu.VMEM((width // lane, nx * ny, lane), F32)] * 2, flops=10 ** 9)
    bulk, taken, wfb = lax.optimization_barrier((bulk, taken, wfb))
    got = swap(bulk)
    whole, = call(join_edges, "join_edges", [(edge, True), (taken, True)], [near((3, across, width), BF16)])
    ends = [(gy_count + j, j + 1) for j in range(gy_count - 1)]
    late = lax.ppermute(whole, ("gx", "gy"), ends + [(b, a) for a, b in ends])
    held = [
        near((3, count + 4, across, wide), BF16),
        near((3, count + 2, across, wide), BF16),
        near((3, count + 2, across, width + lane), BF16),
        near((count, across, width + lane), BF16),
        near((count + 2, across + 16, width + lane), F32),
    ]
    fd, cd, hd, pg, hs, acc = call(
        interior, "interior",
        [(x, True) for x in (own, got, w1b, wfb)],
        held + [near((9, lane, 2 * lane), F32)],
        [
            pltpu.VMEM((count + 2, across + 16, width), F32),
            pltpu.VMEM((count + 1, across + 16, width), F32),
            pltpu.VMEM((count, across, width + lane), F32),
        ],
        limit=32, flops=4 * 10 ** 9)
    fd, cd, hd, pg, hs, send, pre_late = call(
        functools.partial(late_rows, gy_count), "late_rows",
        [(x, True) for x in (fd, cd, hd, pg, hs, late, acc, w1b, wfb)],
        held + [near((rows, lane), BF16), near((across, width + lane), F32)],
        [pltpu.VMEM((3, across + 16, width), F32)],
        limit=32, flops=10 ** 9, aliases={0: 0, 1: 1, 2: 2, 3: 3, 4: 4})

    other = swap(send)
    hd, _, keep = call(
        functools.partial(keep_sums, gy_count), "keep_sums",
        [(x, True) for x in (fd, cd, hd, pg, hs, pre_late, w1b)], [held[2], held[4], near((rows, lane), F32)],
        flops=2 * 10 ** 9, aliases={2: 0, 4: 1})
    other, keep = lax.optimization_barrier((other, keep))
    both, = call(add_pair, "add_pair", [(keep, True), (other, True)], [near((rows, lane), BF16)])
    terms = lax.all_to_all(both.reshape(ranks, rows // ranks, lane), ("grp", "gy"), 0, 0)
    part, = call(add_terms, "add_terms", [(terms, True)], [near(terms.shape[1:], BF16)])
    part, hd, w2 = lax.optimization_barrier((part, hd, w2))
    spread = jnp.broadcast_to(part[None], terms.shape)
    sums = lax.all_to_all(spread, ("grp", "gy"), 0, 0).reshape(rows, lane)
    mine, given = call(
        output_conv, "output_conv", [(hd, True), (w2, True)],
        [near((count, nx, width), BF16), near((count, nx, width), BF16)],
        [pltpu.VMEM((9 * 4 * C, lane), BF16)], flops=2 * 10 ** 9)
    given = swap(given)
    out, = call(
        finish_output, "finish_output", [(mine, True), (given, True)],
        [pltpu.HBM((nx, ny, width), BF16)],
        [pltpu.VMEM((nx, ny, width), BF16), pltpu.VMEM((width // lane, nx * ny, lane), F32), pltpu.SemaphoreType.DMA((nx // 2,))], far=True)
    sums, out = lax.optimization_barrier((sums, out))
    other = swap(sums)
    outs = [pltpu.HBM((27, C, C), F32)] * 2
    scratch = [pltpu.VMEM((27, C, C), F32), pltpu.SemaphoreType.DMA((3,))]
    first, second = call(functools.partial(unpack_own, factor), "unpack_own", [(sums, True)], outs, scratch, far=True)
    other, first, second = lax.optimization_barrier((other, first, second))
    first, second = call(
        functools.partial(unpack_other, factor), "unpack_other", [(other, True), (first, False), (second, False)], outs, scratch, far=True,
        aliases={1: 0, 2: 1})
    shape = (3, 3, 3, C, C)
    return out[None], first.reshape(shape), second.reshape(shape)


def solution(mesh):
    return jax.shard_map(
        shards,
        mesh=mesh,
        in_specs=(P("grp", "gx", "gy", None), P(), P(), P("grp", "gx", "gy", None)),
        out_specs=(P("grp", "gx", "gy", None), P(), P()),
        check_vma=False,
    )
```

```python
import functools
import math

import jax
import jax.numpy as jnp
from jax import lax
from jax.experimental import pallas as pl
from jax.experimental.pallas import tpu as pltpu
from jax.sharding import PartitionSpec as P

C = 64
NZ = 16
BF16 = jnp.bfloat16
F32 = jnp.float32
TAPS = [(dx, dy) for dy in range(3) for dx in range(3)]
BLOCKS = 14


def swap(array):
    return lax.ppermute(array, "gx", [(0, 1), (1, 0)])


def dot(a, b):
    return jnp.dot(a, b, preferred_element_type=F32)


def dot_nt(a, b):
    return lax.dot_general(a, b, (((1,), (1,)), ((), ())), preferred_element_type=F32)


def band(taps):
    zero = jnp.zeros((C, C), BF16)
    left = jnp.concatenate(list(taps) + [zero], axis=0)
    right = jnp.concatenate([zero] + list(taps), axis=0)
    return jnp.concatenate([left, right], axis=1)


def band_flipped(taps):
    zero = jnp.zeros((C, C), BF16)
    back = list(taps)[::-1]
    upper = jnp.concatenate(back + [zero], axis=1)
    lower = jnp.concatenate([zero] + back, axis=1)
    return jnp.concatenate([upper, lower], axis=0)


def packed(pieces):
    blocks = [piece[:, 0:2 * C] for piece in pieces]
    for pair in range(0, 9, 2):
        second = pieces[pair + 1][:, 2 * C:3 * C] if pair + 1 < 9 else jnp.zeros((C, C), F32)
        blocks.append(jnp.concatenate([pieces[pair][:, 2 * C:3 * C], second], axis=1))
    return blocks


def pack_edges(field_hbm, cot_hbm, w1_hbm, w2_hbm, field, cot, edge, given, w1, w2, rows, sems):
    copies = [
        pltpu.make_async_copy(source, target, sems.at[index])
        for index, (source, target) in enumerate(((field_hbm, field), (cot_hbm, cot), (w1_hbm, w1), (w2_hbm, w2)))
    ]
    for copy in copies:
        copy.start()
    for copy in copies[:2]:
        copy.wait()
    nx, ny, _ = field.shape
    gx = lax.axis_index("gx")
    for x in range(nx):
        fields = field[x].astype(F32)
        cots = cot[x].astype(F32)
        for index, row in enumerate((fields[0:1], fields[1:2], cots[0:1], fields[ny - 2:ny - 1], fields[ny - 1:ny], cots[ny - 1:ny])):
            rows[index, x:x + 1, :] = row
    head = rows[0:3].astype(BF16)
    tail = rows[3:6].astype(BF16)
    edge[...] = jnp.where(gx == 0, head, tail)
    given[...] = jnp.where(gx == 0, tail, head)
    for copy in copies[2:]:
        copy.wait()


def join_edges(edge, taken, whole):
    nx = edge.shape[1]
    gx = lax.axis_index("gx")

    @pl.when(gx == 0)
    def _():
        whole[:, 0:nx] = edge[...]
        whole[:, nx:2 * nx] = taken[...]

    @pl.when(gx != 0)
    def _():
        whole[:, 0:nx] = taken[...]
        whole[:, nx:2 * nx] = edge[...]


def put_rows(scratch, start, rows):
    lane = 2 * C
    for tile in range(scratch.shape[0]):
        scratch[tile, start:start + rows.shape[0], :] = rows[:, lane * tile:lane * (tile + 1)]


def take_rows(scratch, start, count, stride):
    return jnp.concatenate(
        [scratch[tile, pl.ds(start, count, stride=stride), :] for tile in range(scratch.shape[0])], axis=1).astype(BF16)


def pack_halves(field, cot, w1, w2, own, bulk, w1b, wfb, turned_f, turned_c):
    nx, ny, _ = field.shape
    half = ny // 2
    for source, target in ((field, turned_f), (cot, turned_c)):
        for x in range(nx):
            put_rows(target, x * ny, source[x].astype(F32))
    gx = lax.axis_index("gx")

    def place(target, first_f, first_c):
        for y in range(half + 2):
            target[y] = take_rows(turned_f, first_f + y, nx, ny)
        for y in range(half + 1):
            target[half + 2 + y] = take_rows(turned_c, first_c + y, nx, ny)

    @pl.when(gx == 0)
    def _():
        place(own, 0, 0)
        place(bulk, half - 2, half - 1)

    @pl.when(gx != 0)
    def _():
        place(own, half - 2, half - 1)
        place(bulk, 0, 0)

    make_bands(w1, w2, w1b, wfb)


def make_bands(w1, w2, w1b, wfb):
    for t, (dx, dy) in enumerate(TAPS):
        rows = slice(t * 4 * C, (t + 1) * 4 * C)
        first = 9 * dx + 3 * dy
        w1b[rows, :] = band([w1[first + z] for z in range(3)])
        wfb[:, rows] = band_flipped([w2[24 - first + z] for z in range(3)])


def blank_edges(copies):
    lane = 2 * C
    zero = jnp.zeros(copies.shape[:-1] + (lane,), BF16)
    copies[..., 0:lane] = zero
    copies[..., copies.shape[-1] - lane:] = zero


def blank_rows(scratch):
    zero = jnp.zeros((scratch.shape[0], 1, scratch.shape[2]), F32)
    scratch[:, 7:8, :] = zero
    scratch[:, scratch.shape[1] - 8:scratch.shape[1] - 7, :] = zero


def shift_rows(scratch, copies, start, first_lane, taps=(0, 1, 2)):
    count, rows, width = scratch.shape
    for dx in taps:
        copies[dx, pl.ds(start, count), :, first_lane:first_lane + width] = scratch[:, 7 + dx:rows - 9 + dx, :].astype(BF16)


def inside_lanes(p):
    lane_of = lax.broadcasted_iota(jnp.int32, (1, 2 * C), 1)
    if p == 0:
        return (lane_of >= C).astype(F32)
    if p == NZ // 2:
        return (lane_of < C).astype(F32)
    return 1.0


def windows(copies, first, count, p):
    lane = 2 * C
    rows = copies.shape[2]
    return jnp.concatenate(
        [
            copies[dx, pl.ds(first + dy, count), :, lane * p:lane * (p + 2)].reshape(count * rows, 2 * lane)
            for dx, dy in TAPS
        ],
        axis=1,
    )


def pre_gradient(grad, pre, p):
    sigma = jax.nn.sigmoid(pre)
    return grad * sigma * (1.0 + pre * (1.0 - sigma)) * inside_lanes(p)


def interior(own, got, w1b, wfb, fd, cd, hd, pg, hs, acc, fs, cs, pre):
    gx = lax.axis_index("gx")
    nx, width = own.shape[1:]
    across = 2 * nx
    count = pg.shape[0]
    cells = count * across
    lane = 2 * C
    pairs = NZ // 2

    def place(left, right):
        for scratch, copies, offset, start, size in ((fs, fd, 2 - 2 * gx, 0, count + 2), (cs, cd, 1 - gx, count + 2, count + 1)):
            for source, row in ((left, 0), (right, nx)):
                rows = source[start:start + size]
                scratch[:, 8 + row:8 + row + nx, :] = rows.astype(F32)
                copies[1, pl.ds(offset, size), row:row + nx, lane:lane + width] = rows

    @pl.when(gx == 0)
    def _():
        place(own, got)

    @pl.when(gx != 0)
    def _():
        place(got, own)

    for scratch in (fs, cs, hs):
        blank_rows(scratch)
    blank_edges(fd)
    blank_edges(cd)
    shift_rows(fs, fd, 2 - 2 * gx, lane, (0, 2))
    shift_rows(cs, cd, 1 - gx, lane, (0, 2))
    for group in range(0, pairs + 1, 3):
        value = dot(jnp.concatenate([windows(fd, 2 - 2 * gx, count, p) for p in range(group, group + 3)], axis=0), w1b[...])
        for p in range(group, group + 3):
            here = slice(lane * p, lane * (p + 1))
            part = value[cells * (p - group):cells * (p - group + 1)]
            pre[:, :, here] = part.reshape(count, across, lane)
            hidden = (part * jax.nn.sigmoid(part) * inside_lanes(p)).reshape(count, across, lane)
            hs[pl.ds(2 - 2 * gx, count), 8:8 + across, here] = hidden
            hd[1, pl.ds(2 - 2 * gx, count), :, here] = hidden.astype(BF16)
    cells = cells - across
    for group in range(0, pairs + 1, 3):
        value = dot_nt(jnp.concatenate([windows(cd, 1 - gx, count - 1, p) for p in range(group, group + 3)], axis=0), wfb[...])
        for p in range(group, group + 3):
            here = slice(lane * p, lane * (p + 1))
            part = value[cells * (p - group):cells * (p - group + 1)]
            grad = pre_gradient(part, pre[pl.ds(gx, count - 1), :, here].reshape(cells, lane), p)
            pg[pl.ds(1 - gx, count - 1), :, here] = grad.astype(BF16).reshape(count - 1, across, lane)
    pg[pl.ds((count - 1) * gx, 1)] = jnp.zeros((1,) + pg.shape[1:], BF16)

    @pl.when(gx == 0)
    def _():
        hd[:, 0:2] = jnp.zeros((3, 2) + hd.shape[2:], BF16)
        shift_rows(hs.at[2:2 + count], hd, 2, 0, (0, 2))
        for t, total in enumerate(second_products(hd, cd)):
            acc[t] = total

    @pl.when(gx != 0)
    def _():
        fd[:, count + 2:count + 4] = jnp.zeros((3, 2) + fd.shape[2:], BF16)
        for t, total in enumerate(first_products(fd, pg)):
            acc[t] = total


def second_products(hd, cd):
    lane = 2 * C
    pairs = NZ // 2
    count, across = hd.shape[1] - 2, hd.shape[2]
    cells = count * across
    cot_t = jnp.concatenate(
        [cd[1, 1:1 + count, :, lane * (p + 1):lane * (p + 2)].reshape(cells, lane).T for p in range(pairs)], axis=1)
    return [
        dot(cot_t, jnp.concatenate(
            [hd[dx, dy:dy + count, :, lane * p:lane * (p + 2)].reshape(cells, 2 * lane) for p in range(pairs)], axis=0))
        for dx, dy in TAPS
    ]


def first_products(fd, pg):
    lane = 2 * C
    pairs = NZ // 2
    count, across, _ = pg.shape
    cells = count * across
    grad_t = jnp.concatenate(
        [pg[:, :, lane * p:lane * (p + 1)].reshape(cells, lane).T for p in range(pairs + 1)], axis=1)
    return [
        dot(grad_t, jnp.concatenate(
            [fd[dx, 1 + dy:1 + dy + count, :, lane * p:lane * (p + 2)].reshape(cells, 2 * lane) for p in range(pairs + 1)], axis=0))
        for dx, dy in TAPS
    ]


def folded(total):
    return total[0:C, 0:3 * C] + total[C:2 * C, C:4 * C]


def second_late(hd, cd):
    lane = 2 * C
    pairs = NZ // 2
    late = ((0, 1), (0,), ())
    products = []
    for dx, dy in TAPS:
        if late[dy]:
            cots = jnp.concatenate(
                [cd[1, 1 + y, :, lane * (p + 1):lane * (p + 2)] for y in late[dy] for p in range(pairs)], axis=0)
            rows = jnp.concatenate(
                [hd[dx, y + dy, :, lane * p:lane * (p + 2)] for y in late[dy] for p in range(pairs)], axis=0)
            products.append(dot(cots.T, rows))
        else:
            products.append(0.0)
    return products


def first_late(fd, pg):
    lane = 2 * C
    pairs = NZ // 2
    count, across, _ = pg.shape
    y = count - 1
    extra = 2 * lane - (pairs + 1) * across
    grad_t = jnp.concatenate(
        [pg[y, :, lane * p:lane * (p + 1)] for p in range(pairs + 1)] + [jnp.zeros((extra, lane), BF16)], axis=0).T
    pad = jnp.zeros((extra, 2 * lane), BF16)
    return [
        dot(grad_t, jnp.concatenate(
            [fd[dx, y + dy + 1, :, lane * p:lane * (p + 2)] for p in range(pairs + 1)] + [pad], axis=0))
        for dx, dy in TAPS
    ]


def sums_of(products):
    return packed([folded(product) for product in products])


def store_blocks(target, blocks):
    for index, block in enumerate(blocks):
        target[index * C:(index + 1) * C, :] = block.astype(target.dtype)
    if target.shape[0] > BLOCKS * C:
        target[BLOCKS * C:, :] = jnp.zeros((target.shape[0] - BLOCKS * C, 2 * C), target.dtype)


def hidden_of(value, p):
    return value * jax.nn.sigmoid(value) * inside_lanes(p)


def stacked(copies, first, count, pairs):
    return jnp.concatenate([windows(copies, first, count, p) for p in range(pairs + 1)], axis=0)


def late_rows(gy_count, fd_in, cd_in, hd_in, pg_in, hs_in, rows, acc, w1b, wfb, fd, cd, hd, pg, hs, send, pre_late, rs):
    gx = lax.axis_index("gx")
    gy = lax.axis_index("gy")
    count, across, _ = pg.shape
    lane = 2 * C
    pairs = NZ // 2
    rs[:, 8:8 + across, :] = rows[...].astype(F32)
    blank_rows(rs)

    @pl.when(gx == 0)
    def _():
        shift_rows(rs.at[0:2], fd, 0, lane)
        shift_rows(rs.at[2:3], cd, 0, lane)
        value = dot(stacked(fd, 0, 2, pairs), w1b[...])
        grad = dot_nt(stacked(cd, 0, 1, pairs), wfb[...])
        before = jnp.where(gy == 0, 0.0, 1.0)
        for p in range(pairs + 1):
            here = slice(lane * p, lane * (p + 1))
            early = value[2 * across * p:2 * across * p + across]
            later = value[2 * across * p + across:2 * across * (p + 1)]
            mine = pre_gradient(grad[across * p:across * (p + 1)], later, p)
            pg[0, :, here] = mine.astype(BF16)
            both = jnp.stack([hidden_of(early, p) * before, hidden_of(later, p)])
            hs[0:2, 8:8 + across, here] = both
            hd[1, 0:2, :, here] = both.astype(BF16)
        shift_rows(hs.at[0:2], hd, 0, 0, (0, 2))
        store_blocks(send, sums_of([acc[t] + late for t, late in enumerate(second_late(hd, cd))]))

    @pl.when(gx != 0)
    def _():
        shift_rows(rs.at[0:2], fd, count + 2, lane)
        shift_rows(rs.at[2:3], cd, count + 1, lane)
        value = dot(stacked(fd, count, 1, pairs), w1b[...])
        grad = dot_nt(stacked(cd, count - 1, 1, pairs), wfb[...])
        for p in range(pairs + 1):
            here = slice(lane * p, lane * (p + 1))
            part = slice(across * p, across * (p + 1))
            pre_late[:, here] = value[part]
            pg[count - 1, :, here] = pre_gradient(grad[part], value[part], p).astype(BF16)
        store_blocks(send, sums_of([acc[t] + late for t, late in enumerate(first_late(fd, pg))]))


def keep_sums(gy_count, fd, cd, hd_in, pg, hs_in, pre_late, w1b, hd, hs, keep):
    gx = lax.axis_index("gx")
    gy = lax.axis_index("gy")
    count, across, _ = pg.shape
    lane = 2 * C
    pairs = NZ // 2

    @pl.when(gx == 0)
    def _():
        store_blocks(keep, sums_of(first_products(fd, pg)))

    @pl.when(gx != 0)
    def _():
        value = dot(stacked(fd, count + 1, 1, pairs), w1b[...])
        beyond = jnp.where(gy == gy_count - 1, 0.0, 1.0)
        for p in range(pairs + 1):
            here = slice(lane * p, lane * (p + 1))
            part = slice(across * p, across * (p + 1))
            both = jnp.stack([hidden_of(pre_late[:, here], p), hidden_of(value[part], p) * beyond])
            hs[count:count + 2, 8:8 + across, here] = both
            hd[1, count:count + 2, :, here] = both.astype(BF16)
        shift_rows(hs, hd, 0, 0, (0, 2))
        store_blocks(keep, sums_of(second_products(hd, cd)))


def output_conv(hd, w2, mine, given, w2b):
    for t, (dx, dy) in enumerate(TAPS):
        w2b[t * 4 * C:(t + 1) * 4 * C, :] = band([w2[9 * dx + 3 * dy + z] for z in range(3)])
    gx = lax.axis_index("gx")
    count, half, _ = mine.shape
    lane = 2 * C
    for p in range(NZ // 2):
        here = slice(lane * p, lane * (p + 1))
        value = dot(windows(hd, 0, count, p), w2b[...]).reshape(count, 2 * half, lane)
        left, right = value[:, 0:half], value[:, half:]
        mine[:, :, here] = jnp.where(gx == 0, left, right).astype(BF16)
        given[:, :, here] = jnp.where(gx == 0, right, left).astype(BF16)


def finish_output(mine, other, out, turned, scratch, sems):
    count, nx, width = mine.shape
    gx = lax.axis_index("gx")
    for y in range(count):
        a = mine[y].astype(F32)
        b = other[y].astype(F32)
        put_rows(scratch, y * nx, jnp.where(gx == 0, a, b))
        put_rows(scratch, (count + y) * nx, jnp.where(gx == 0, b, a))
    copies = []
    for x in range(nx):
        turned[x] = take_rows(scratch, x, 2 * count, nx)
        if x % 2:
            copies.append(pltpu.make_async_copy(turned.at[x - 1:x + 1], out.at[x - 1:x + 1], sems.at[x // 2]))
            copies[-1].start()
    for copy in copies:
        copy.wait()


def add_pair(keep, other, out):
    out[...] = (keep[...] + other[...].astype(F32)).astype(BF16)


def add_terms(terms, out):
    total = terms[0].astype(F32)
    for index in range(1, terms.shape[0]):
        total = total + terms[index].astype(F32)
    out[...] = total.astype(BF16)


def unpack(factor, is_first, rows, first, second, held, sems):
    def each(act):
        for chosen, target in ((is_first, first), (jnp.logical_not(is_first), second)):
            @pl.when(chosen)
            def _():
                act(target)

    def copy_of(dx, target):
        piece = slice(9 * dx, 9 * dx + 9)
        return pltpu.make_async_copy(held.at[piece], target.at[piece], sems.at[dx])

    for dx in range(3):
        for dy in range(3):
            t = 3 * dy + dx
            place = 9 * dx + 3 * dy
            turned = rows[t * C:(t + 1) * C, :].T.astype(F32) * factor
            held[place] = turned[0:C]
            held[place + 1] = turned[C:2 * C]
            turned = rows[(9 + t // 2) * C:(10 + t // 2) * C, :].T.astype(F32) * factor
            held[place + 2] = turned[t % 2 * C:(t % 2 + 1) * C]
        each(lambda target: copy_of(dx, target).start())
    each(lambda target: [copy_of(dx, target).wait() for dx in range(3)])


def unpack_own(factor, rows, first, second, held, sems):
    unpack(factor, lax.axis_index("gx") == 0, rows, first, second, held, sems)


def unpack_other(factor, rows, first_in, second_in, first, second, held, sems):
    unpack(factor, lax.axis_index("gx") != 0, rows, first, second, held, sems)


def near(shape, dtype):
    return pltpu.VMEM(shape, dtype)


def call(body, name, inputs, outs, scratch=(), limit=16, flops=0, far=False, aliases=None):
    placed = [pltpu.with_memory_space_constraint(x, pltpu.VMEM if held else pltpu.HBM) for x, held in inputs]
    size = sum(x.size * x.dtype.itemsize for x, _ in inputs)
    return pl.pallas_call(
        body,
        out_shape=list(outs),
        in_specs=[pl.BlockSpec(memory_space=pltpu.VMEM if held else pl.ANY) for _, held in inputs],
        out_specs=[pl.BlockSpec(memory_space=pl.ANY if far else pltpu.VMEM)] * len(outs),
        scratch_shapes=list(scratch),
        input_output_aliases=aliases or {},
        compiler_params=pltpu.CompilerParams(vmem_limit_bytes=limit * 1024 * 1024),
        cost_estimate=pl.CostEstimate(flops=flops, bytes_accessed=size, transcendentals=0),
        name=name,
    )(*placed)


def shards(field_in, first_weight, second_weight, cotangent):
    nx, ny, width = field_in.shape[1:]
    gx_count, gy_count, grp_count = (lax.axis_size(axis) for axis in ("gx", "gy", "grp"))
    total = field_in.shape[0] * nx * ny * NZ * gx_count * gy_count * grp_count
    factor = 1.0 / math.sqrt(total)
    ranks = gy_count * grp_count
    rows = -(-BLOCKS * C // (8 * ranks)) * 8 * ranks
    lane = 2 * C
    wide = width + 2 * lane
    count = ny // 2
    across = 2 * nx
    size = 2 * count + 3

    field, cot, edge, given, w1, w2 = call(
        pack_edges, "pack_edges",
        [(x, False) for x in (field_in[0], cotangent[0], first_weight.reshape(27, C, C), second_weight.reshape(27, C, C))],
        [
            near((nx, ny, width), BF16),
            near((nx, ny, width), BF16),
            near((3, nx, width), BF16),
            near((3, nx, width), BF16),
            near((27, C, C), BF16),
            near((27, C, C), BF16),
        ],
        [pltpu.VMEM((6, nx, width), F32), pltpu.SemaphoreType.DMA((4,))])
    taken = swap(given)
    own, bulk, w1b, wfb = call(
        pack_halves, "pack_halves", [(x, True) for x in (field, cot, w1, w2)],
        [
            near((size, nx, width), BF16),
            near((size, nx, width), BF16),
            near((9 * 4 * C, lane), BF16),
            near((lane, 9 * 4 * C), BF16),
        ],
        [pltpu.VMEM((width // lane, nx * ny, lane), F32)] * 2, flops=10 ** 9)
    bulk, taken, wfb = lax.optimization_barrier((bulk, taken, wfb))
    got = swap(bulk)
    whole, = call(join_edges, "join_edges", [(edge, True), (taken, True)], [near((3, across, width), BF16)])
    ends = [(gy_count + j, j + 1) for j in range(gy_count - 1)]
    late = lax.ppermute(whole, ("gx", "gy"), ends + [(b, a) for a, b in ends])
    held = [
        near((3, count + 4, across, wide), BF16),
        near((3, count + 2, across, wide), BF16),
        near((3, count + 2, across, width + lane), BF16),
        near((count, across, width + lane), BF16),
        near((count + 2, across + 16, width + lane), F32),
    ]
    fd, cd, hd, pg, hs, acc = call(
        interior, "interior",
        [(x, True) for x in (own, got, w1b, wfb)],
        held + [near((9, lane, 2 * lane), F32)],
        [
            pltpu.VMEM((count + 2, across + 16, width), F32),
            pltpu.VMEM((count + 1, across + 16, width), F32),
            pltpu.VMEM((count, across, width + lane), F32),
        ],
        limit=32, flops=4 * 10 ** 9)
    fd, cd, hd, pg, hs, send, pre_late = call(
        functools.partial(late_rows, gy_count), "late_rows",
        [(x, True) for x in (fd, cd, hd, pg, hs, late, acc, w1b, wfb)],
        held + [near((rows, lane), BF16), near((across, width + lane), F32)],
        [pltpu.VMEM((3, across + 16, width), F32)],
        limit=32, flops=10 ** 9, aliases={0: 0, 1: 1, 2: 2, 3: 3, 4: 4})

    other = swap(send)
    hd, _, keep = call(
        functools.partial(keep_sums, gy_count), "keep_sums",
        [(x, True) for x in (fd, cd, hd, pg, hs, pre_late, w1b)], [held[2], held[4], near((rows, lane), F32)],
        flops=2 * 10 ** 9, aliases={2: 0, 4: 1})
    other, keep = lax.optimization_barrier((other, keep))
    both, = call(add_pair, "add_pair", [(keep, True), (other, True)], [near((rows, lane), BF16)])
    both, hd, w2 = lax.optimization_barrier((both, hd, w2))
    terms = lax.all_to_all(both.reshape(ranks, rows // ranks, lane), ("grp", "gy"), 0, 0)
    mine, given = call(
        output_conv, "output_conv", [(hd, True), (w2, True)],
        [near((count, nx, width), BF16), near((count, nx, width), BF16)],
        [pltpu.VMEM((9 * 4 * C, lane), BF16)], flops=2 * 10 ** 9)
    given = swap(given)
    out, = call(
        finish_output, "finish_output", [(mine, True), (given, True)],
        [pltpu.HBM((nx, ny, width), BF16)],
        [pltpu.VMEM((nx, ny, width), BF16), pltpu.VMEM((width // lane, nx * ny, lane), F32), pltpu.SemaphoreType.DMA((nx // 2,))], far=True)
    terms, out = lax.optimization_barrier((terms, out))
    part, = call(add_terms, "add_terms", [(terms, True)], [near(terms.shape[1:], BF16)])
    spread = jnp.broadcast_to(part[None], terms.shape)
    sums = lax.all_to_all(spread, ("grp", "gy"), 0, 0).reshape(rows, lane)
    other = swap(sums)
    outs = [pltpu.HBM((27, C, C), F32)] * 2
    scratch = [pltpu.VMEM((27, C, C), F32), pltpu.SemaphoreType.DMA((3,))]
    first, second = call(functools.partial(unpack_own, factor), "unpack_own", [(sums, True)], outs, scratch, far=True)
    other, first, second = lax.optimization_barrier((other, first, second))
    first, second = call(
        functools.partial(unpack_other, factor), "unpack_other", [(other, True), (first, False), (second, False)], outs, scratch, far=True,
        aliases={1: 0, 2: 1})
    shape = (3, 3, 3, C, C)
    return out[None], first.reshape(shape), second.reshape(shape)


def solution(mesh):
    return jax.shard_map(
        shards,
        mesh=mesh,
        in_specs=(P("grp", "gx", "gy", None), P(), P(), P("grp", "gx", "gy", None)),
        out_specs=(P("grp", "gx", "gy", None), P(), P()),
        check_vma=False,
    )
```

```python
import functools
import math

import jax
import jax.numpy as jnp
from jax import lax
from jax.experimental import pallas as pl
from jax.experimental.pallas import tpu as pltpu
from jax.sharding import PartitionSpec as P

C = 64
NZ = 16
BF16 = jnp.bfloat16
F32 = jnp.float32
TAPS = [(dx, dy) for dy in range(3) for dx in range(3)]
BLOCKS = 14


def swap(array):
    return lax.ppermute(array, "gx", [(0, 1), (1, 0)])


def dot(a, b):
    return jnp.dot(a, b, preferred_element_type=F32)


def dot_nt(a, b):
    return lax.dot_general(a, b, (((1,), (1,)), ((), ())), preferred_element_type=F32)


def band(taps):
    zero = jnp.zeros((C, C), BF16)
    left = jnp.concatenate(list(taps) + [zero], axis=0)
    right = jnp.concatenate([zero] + list(taps), axis=0)
    return jnp.concatenate([left, right], axis=1)


def band_flipped(taps):
    zero = jnp.zeros((C, C), BF16)
    back = list(taps)[::-1]
    upper = jnp.concatenate(back + [zero], axis=1)
    lower = jnp.concatenate([zero] + back, axis=1)
    return jnp.concatenate([upper, lower], axis=0)


def packed(pieces):
    blocks = [piece[:, 0:2 * C] for piece in pieces]
    for pair in range(0, 9, 2):
        second = pieces[pair + 1][:, 2 * C:3 * C] if pair + 1 < 9 else jnp.zeros((C, C), F32)
        blocks.append(jnp.concatenate([pieces[pair][:, 2 * C:3 * C], second], axis=1))
    return blocks


def pack_edges(field_hbm, cot_hbm, w1_hbm, w2_hbm, field, cot, edge, given, w1, w2, rows, sems):
    copies = [
        pltpu.make_async_copy(source, target, sems.at[index])
        for index, (source, target) in enumerate(((field_hbm, field), (cot_hbm, cot), (w1_hbm, w1), (w2_hbm, w2)))
    ]
    for copy in copies:
        copy.start()
    for copy in copies[:2]:
        copy.wait()
    nx, ny, _ = field.shape
    gx = lax.axis_index("gx")
    for x in range(nx):
        fields = field[x].astype(F32)
        cots = cot[x].astype(F32)
        for index, row in enumerate((fields[0:1], fields[1:2], cots[0:1], fields[ny - 2:ny - 1], fields[ny - 1:ny], cots[ny - 1:ny])):
            rows[index, x:x + 1, :] = row
    head = rows[0:3].astype(BF16)
    tail = rows[3:6].astype(BF16)
    edge[...] = jnp.where(gx == 0, head, tail)
    given[...] = jnp.where(gx == 0, tail, head)
    for copy in copies[2:]:
        copy.wait()


def join_edges(edge, taken, whole):
    nx = edge.shape[1]
    gx = lax.axis_index("gx")

    @pl.when(gx == 0)
    def _():
        whole[:, 0:nx] = edge[...]
        whole[:, nx:2 * nx] = taken[...]

    @pl.when(gx != 0)
    def _():
        whole[:, 0:nx] = taken[...]
        whole[:, nx:2 * nx] = edge[...]


def put_rows(scratch, start, rows):
    lane = 2 * C
    for tile in range(scratch.shape[0]):
        scratch[tile, start:start + rows.shape[0], :] = rows[:, lane * tile:lane * (tile + 1)]


def take_rows(scratch, start, count, stride):
    return jnp.concatenate(
        [scratch[tile, pl.ds(start, count, stride=stride), :] for tile in range(scratch.shape[0])], axis=1).astype(BF16)


def pack_halves(field, cot, w1, w2, own, bulk, w1b, wfb, turned_f, turned_c):
    nx, ny, _ = field.shape
    half = ny // 2
    for source, target in ((field, turned_f), (cot, turned_c)):
        for x in range(nx):
            put_rows(target, x * ny, source[x].astype(F32))
    gx = lax.axis_index("gx")

    def place(target, first_f, first_c):
        for y in range(half + 2):
            target[y] = take_rows(turned_f, first_f + y, nx, ny)
        for y in range(half + 1):
            target[half + 2 + y] = take_rows(turned_c, first_c + y, nx, ny)

    @pl.when(gx == 0)
    def _():
        place(own, 0, 0)
        place(bulk, half - 2, half - 1)

    @pl.when(gx != 0)
    def _():
        place(own, half - 2, half - 1)
        place(bulk, 0, 0)

    make_bands(w1, w2, w1b, wfb)


def make_bands(w1, w2, w1b, wfb):
    for t, (dx, dy) in enumerate(TAPS):
        rows = slice(t * 4 * C, (t + 1) * 4 * C)
        first = 9 * dx + 3 * dy
        w1b[rows, :] = band([w1[first + z] for z in range(3)])
        wfb[:, rows] = band_flipped([w2[24 - first + z] for z in range(3)])


def blank_edges(copies):
    lane = 2 * C
    zero = jnp.zeros(copies.shape[:-1] + (lane,), BF16)
    copies[..., 0:lane] = zero
    copies[..., copies.shape[-1] - lane:] = zero


def blank_rows(scratch):
    zero = jnp.zeros((scratch.shape[0], 1, scratch.shape[2]), F32)
    scratch[:, 7:8, :] = zero
    scratch[:, scratch.shape[1] - 8:scratch.shape[1] - 7, :] = zero


def shift_rows(scratch, copies, start, first_lane, taps=(0, 1, 2)):
    count, rows, width = scratch.shape
    for dx in taps:
        copies[dx, pl.ds(start, count), :, first_lane:first_lane + width] = scratch[:, 7 + dx:rows - 9 + dx, :].astype(BF16)


def inside_lanes(p):
    lane_of = lax.broadcasted_iota(jnp.int32, (1, 2 * C), 1)
    if p == 0:
        return (lane_of >= C).astype(F32)
    if p == NZ // 2:
        return (lane_of < C).astype(F32)
    return 1.0


def windows(copies, first, count, p):
    lane = 2 * C
    rows = copies.shape[2]
    return jnp.concatenate(
        [
            copies[dx, pl.ds(first + dy, count), :, lane * p:lane * (p + 2)].reshape(count * rows, 2 * lane)
            for dx, dy in TAPS
        ],
        axis=1,
    )


def pre_gradient(grad, pre, p):
    sigma = jax.nn.sigmoid(pre)
    return grad * sigma * (1.0 + pre * (1.0 - sigma)) * inside_lanes(p)


def interior(own, got, w1b, wfb, fd, cd, hd, pg, hs, acc, fs, cs, pre):
    gx = lax.axis_index("gx")
    nx, width = own.shape[1:]
    across = 2 * nx
    count = pg.shape[0]
    cells = count * across
    lane = 2 * C
    pairs = NZ // 2

    def place(left, right):
        for scratch, copies, offset, start, size in ((fs, fd, 2 - 2 * gx, 0, count + 2), (cs, cd, 1 - gx, count + 2, count + 1)):
            for source, row in ((left, 0), (right, nx)):
                rows = source[start:start + size]
                scratch[:, 8 + row:8 + row + nx, :] = rows.astype(F32)
                copies[1, pl.ds(offset, size), row:row + nx, lane:lane + width] = rows

    @pl.when(gx == 0)
    def _():
        place(own, got)

    @pl.when(gx != 0)
    def _():
        place(got, own)

    for scratch in (fs, cs, hs):
        blank_rows(scratch)
    blank_edges(fd)
    blank_edges(cd)
    shift_rows(fs, fd, 2 - 2 * gx, lane, (0, 2))
    shift_rows(cs, cd, 1 - gx, lane, (0, 2))
    for group in range(0, pairs + 1, pairs + 1):
        value = dot(jnp.concatenate([windows(fd, 2 - 2 * gx, count, p) for p in range(group, group + pairs + 1)], axis=0), w1b[...])
        for p in range(group, group + pairs + 1):
            here = slice(lane * p, lane * (p + 1))
            part = value[cells * (p - group):cells * (p - group + 1)]
            pre[:, :, here] = part.reshape(count, across, lane)
            hidden = (part * jax.nn.sigmoid(part) * inside_lanes(p)).reshape(count, across, lane)
            hs[pl.ds(2 - 2 * gx, count), 8:8 + across, here] = hidden
            hd[1, pl.ds(2 - 2 * gx, count), :, here] = hidden.astype(BF16)
    cells = cells - across
    for group in range(0, pairs + 1, pairs + 1):
        value = dot_nt(jnp.concatenate([windows(cd, 1 - gx, count - 1, p) for p in range(group, group + pairs + 1)], axis=0), wfb[...])
        for p in range(group, group + pairs + 1):
            here = slice(lane * p, lane * (p + 1))
            part = value[cells * (p - group):cells * (p - group + 1)]
            grad = pre_gradient(part, pre[pl.ds(gx, count - 1), :, here].reshape(cells, lane), p)
            pg[pl.ds(1 - gx, count - 1), :, here] = grad.astype(BF16).reshape(count - 1, across, lane)
    pg[pl.ds((count - 1) * gx, 1)] = jnp.zeros((1,) + pg.shape[1:], BF16)

    @pl.when(gx == 0)
    def _():
        hd[:, 0:2] = jnp.zeros((3, 2) + hd.shape[2:], BF16)
        shift_rows(hs.at[2:2 + count], hd, 2, 0, (0, 2))
        for t, total in enumerate(second_products(hd, cd)):
            acc[t] = total

    @pl.when(gx != 0)
    def _():
        fd[:, count + 2:count + 4] = jnp.zeros((3, 2) + fd.shape[2:], BF16)
        for t, total in enumerate(first_products(fd, pg)):
            acc[t] = total


def second_products(hd, cd):
    lane = 2 * C
    pairs = NZ // 2
    count, across = hd.shape[1] - 2, hd.shape[2]
    cells = count * across
    cot_t = jnp.concatenate(
        [cd[1, 1:1 + count, :, lane * (p + 1):lane * (p + 2)].reshape(cells, lane).T for p in range(pairs)], axis=1)
    return [
        dot(cot_t, jnp.concatenate(
            [hd[dx, dy:dy + count, :, lane * p:lane * (p + 2)].reshape(cells, 2 * lane) for p in range(pairs)], axis=0))
        for dx, dy in TAPS
    ]


def first_products(fd, pg):
    lane = 2 * C
    pairs = NZ // 2
    count, across, _ = pg.shape
    cells = count * across
    grad_t = jnp.concatenate(
        [pg[:, :, lane * p:lane * (p + 1)].reshape(cells, lane).T for p in range(pairs + 1)], axis=1)
    return [
        dot(grad_t, jnp.concatenate(
            [fd[dx, 1 + dy:1 + dy + count, :, lane * p:lane * (p + 2)].reshape(cells, 2 * lane) for p in range(pairs + 1)], axis=0))
        for dx, dy in TAPS
    ]


def folded(total):
    return total[0:C, 0:3 * C] + total[C:2 * C, C:4 * C]


def second_late(hd, cd):
    lane = 2 * C
    pairs = NZ // 2
    late = ((0, 1), (0,), ())
    products = []
    for dx, dy in TAPS:
        if late[dy]:
            cots = jnp.concatenate(
                [cd[1, 1 + y, :, lane * (p + 1):lane * (p + 2)] for y in late[dy] for p in range(pairs)], axis=0)
            rows = jnp.concatenate(
                [hd[dx, y + dy, :, lane * p:lane * (p + 2)] for y in late[dy] for p in range(pairs)], axis=0)
            products.append(dot(cots.T, rows))
        else:
            products.append(0.0)
    return products


def first_late(fd, pg):
    lane = 2 * C
    pairs = NZ // 2
    count, across, _ = pg.shape
    y = count - 1
    extra = 2 * lane - (pairs + 1) * across
    grad_t = jnp.concatenate(
        [pg[y, :, lane * p:lane * (p + 1)] for p in range(pairs + 1)] + [jnp.zeros((extra, lane), BF16)], axis=0).T
    pad = jnp.zeros((extra, 2 * lane), BF16)
    return [
        dot(grad_t, jnp.concatenate(
            [fd[dx, y + dy + 1, :, lane * p:lane * (p + 2)] for p in range(pairs + 1)] + [pad], axis=0))
        for dx, dy in TAPS
    ]


def sums_of(products):
    return packed([folded(product) for product in products])


def store_blocks(target, blocks):
    for index, block in enumerate(blocks):
        target[index * C:(index + 1) * C, :] = block.astype(target.dtype)
    if target.shape[0] > BLOCKS * C:
        target[BLOCKS * C:, :] = jnp.zeros((target.shape[0] - BLOCKS * C, 2 * C), target.dtype)


def hidden_of(value, p):
    return value * jax.nn.sigmoid(value) * inside_lanes(p)


def stacked(copies, first, count, pairs):
    return jnp.concatenate([windows(copies, first, count, p) for p in range(pairs + 1)], axis=0)


def late_rows(gy_count, fd_in, cd_in, hd_in, pg_in, hs_in, rows, acc, w1b, wfb, fd, cd, hd, pg, hs, send, pre_late, rs):
    gx = lax.axis_index("gx")
    gy = lax.axis_index("gy")
    count, across, _ = pg.shape
    lane = 2 * C
    pairs = NZ // 2
    rs[:, 8:8 + across, :] = rows[...].astype(F32)
    blank_rows(rs)

    @pl.when(gx == 0)
    def _():
        shift_rows(rs.at[0:2], fd, 0, lane)
        shift_rows(rs.at[2:3], cd, 0, lane)
        value = dot(stacked(fd, 0, 2, pairs), w1b[...])
        grad = dot_nt(stacked(cd, 0, 1, pairs), wfb[...])
        before = jnp.where(gy == 0, 0.0, 1.0)
        for p in range(pairs + 1):
            here = slice(lane * p, lane * (p + 1))
            early = value[2 * across * p:2 * across * p + across]
            later = value[2 * across * p + across:2 * across * (p + 1)]
            mine = pre_gradient(grad[across * p:across * (p + 1)], later, p)
            pg[0, :, here] = mine.astype(BF16)
            both = jnp.stack([hidden_of(early, p) * before, hidden_of(later, p)])
            hs[0:2, 8:8 + across, here] = both
            hd[1, 0:2, :, here] = both.astype(BF16)
        shift_rows(hs.at[0:2], hd, 0, 0, (0, 2))
        store_blocks(send, sums_of([acc[t] + late for t, late in enumerate(second_late(hd, cd))]))

    @pl.when(gx != 0)
    def _():
        shift_rows(rs.at[0:2], fd, count + 2, lane)
        shift_rows(rs.at[2:3], cd, count + 1, lane)
        value = dot(stacked(fd, count, 1, pairs), w1b[...])
        grad = dot_nt(stacked(cd, count - 1, 1, pairs), wfb[...])
        for p in range(pairs + 1):
            here = slice(lane * p, lane * (p + 1))
            part = slice(across * p, across * (p + 1))
            pre_late[:, here] = value[part]
            pg[count - 1, :, here] = pre_gradient(grad[part], value[part], p).astype(BF16)
        store_blocks(send, sums_of([acc[t] + late for t, late in enumerate(first_late(fd, pg))]))


def keep_sums(gy_count, fd, cd, hd_in, pg, hs_in, pre_late, w1b, hd, hs, keep):
    gx = lax.axis_index("gx")
    gy = lax.axis_index("gy")
    count, across, _ = pg.shape
    lane = 2 * C
    pairs = NZ // 2

    @pl.when(gx == 0)
    def _():
        store_blocks(keep, sums_of(first_products(fd, pg)))

    @pl.when(gx != 0)
    def _():
        value = dot(stacked(fd, count + 1, 1, pairs), w1b[...])
        beyond = jnp.where(gy == gy_count - 1, 0.0, 1.0)
        for p in range(pairs + 1):
            here = slice(lane * p, lane * (p + 1))
            part = slice(across * p, across * (p + 1))
            both = jnp.stack([hidden_of(pre_late[:, here], p), hidden_of(value[part], p) * beyond])
            hs[count:count + 2, 8:8 + across, here] = both
            hd[1, count:count + 2, :, here] = both.astype(BF16)
        shift_rows(hs, hd, 0, 0, (0, 2))
        store_blocks(keep, sums_of(second_products(hd, cd)))


def output_conv(hd, w2, mine, given, w2b):
    for t, (dx, dy) in enumerate(TAPS):
        w2b[t * 4 * C:(t + 1) * 4 * C, :] = band([w2[9 * dx + 3 * dy + z] for z in range(3)])
    gx = lax.axis_index("gx")
    count, half, _ = mine.shape
    lane = 2 * C
    for p in range(NZ // 2):
        here = slice(lane * p, lane * (p + 1))
        value = dot(windows(hd, 0, count, p), w2b[...]).reshape(count, 2 * half, lane)
        left, right = value[:, 0:half], value[:, half:]
        mine[:, :, here] = jnp.where(gx == 0, left, right).astype(BF16)
        given[:, :, here] = jnp.where(gx == 0, right, left).astype(BF16)


def finish_output(mine, other, out, turned, scratch, sems):
    count, nx, width = mine.shape
    gx = lax.axis_index("gx")
    for y in range(count):
        a = mine[y].astype(F32)
        b = other[y].astype(F32)
        put_rows(scratch, y * nx, jnp.where(gx == 0, a, b))
        put_rows(scratch, (count + y) * nx, jnp.where(gx == 0, b, a))
    copies = []
    for x in range(nx):
        turned[x] = take_rows(scratch, x, 2 * count, nx)
        if x % 2:
            copies.append(pltpu.make_async_copy(turned.at[x - 1:x + 1], out.at[x - 1:x + 1], sems.at[x // 2]))
            copies[-1].start()
    for copy in copies:
        copy.wait()


def add_pair(keep, other, out):
    out[...] = (keep[...] + other[...].astype(F32)).astype(BF16)


def add_terms(terms, out):
    total = terms[0].astype(F32)
    for index in range(1, terms.shape[0]):
        total = total + terms[index].astype(F32)
    out[...] = total.astype(BF16)


def unpack(factor, is_first, rows, first, second, held, sems):
    def each(act):
        for chosen, target in ((is_first, first), (jnp.logical_not(is_first), second)):
            @pl.when(chosen)
            def _():
                act(target)

    def copy_of(dx, target):
        piece = slice(9 * dx, 9 * dx + 9)
        return pltpu.make_async_copy(held.at[piece], target.at[piece], sems.at[dx])

    for dx in range(3):
        for dy in range(3):
            t = 3 * dy + dx
            place = 9 * dx + 3 * dy
            turned = rows[t * C:(t + 1) * C, :].T.astype(F32) * factor
            held[place] = turned[0:C]
            held[place + 1] = turned[C:2 * C]
            turned = rows[(9 + t // 2) * C:(10 + t // 2) * C, :].T.astype(F32) * factor
            held[place + 2] = turned[t % 2 * C:(t % 2 + 1) * C]
        each(lambda target: copy_of(dx, target).start())
    each(lambda target: [copy_of(dx, target).wait() for dx in range(3)])


def unpack_own(factor, rows, first, second, held, sems):
    unpack(factor, lax.axis_index("gx") == 0, rows, first, second, held, sems)


def unpack_other(factor, rows, first_in, second_in, first, second, held, sems):
    unpack(factor, lax.axis_index("gx") != 0, rows, first, second, held, sems)


def near(shape, dtype):
    return pltpu.VMEM(shape, dtype)


def call(body, name, inputs, outs, scratch=(), limit=16, flops=0, far=False, aliases=None):
    placed = [pltpu.with_memory_space_constraint(x, pltpu.VMEM if held else pltpu.HBM) for x, held in inputs]
    size = sum(x.size * x.dtype.itemsize for x, _ in inputs)
    return pl.pallas_call(
        body,
        out_shape=list(outs),
        in_specs=[pl.BlockSpec(memory_space=pltpu.VMEM if held else pl.ANY) for _, held in inputs],
        out_specs=[pl.BlockSpec(memory_space=pl.ANY if far else pltpu.VMEM)] * len(outs),
        scratch_shapes=list(scratch),
        input_output_aliases=aliases or {},
        compiler_params=pltpu.CompilerParams(vmem_limit_bytes=limit * 1024 * 1024),
        cost_estimate=pl.CostEstimate(flops=flops, bytes_accessed=size, transcendentals=0),
        name=name,
    )(*placed)


def shards(field_in, first_weight, second_weight, cotangent):
    nx, ny, width = field_in.shape[1:]
    gx_count, gy_count, grp_count = (lax.axis_size(axis) for axis in ("gx", "gy", "grp"))
    total = field_in.shape[0] * nx * ny * NZ * gx_count * gy_count * grp_count
    factor = 1.0 / math.sqrt(total)
    ranks = gy_count * grp_count
    rows = -(-BLOCKS * C // (8 * ranks)) * 8 * ranks
    lane = 2 * C
    wide = width + 2 * lane
    count = ny // 2
    across = 2 * nx
    size = 2 * count + 3

    field, cot, edge, given, w1, w2 = call(
        pack_edges, "pack_edges",
        [(x, False) for x in (field_in[0], cotangent[0], first_weight.reshape(27, C, C), second_weight.reshape(27, C, C))],
        [
            near((nx, ny, width), BF16),
            near((nx, ny, width), BF16),
            near((3, nx, width), BF16),
            near((3, nx, width), BF16),
            near((27, C, C), BF16),
            near((27, C, C), BF16),
        ],
        [pltpu.VMEM((6, nx, width), F32), pltpu.SemaphoreType.DMA((4,))])
    taken = swap(given)
    own, bulk, w1b, wfb = call(
        pack_halves, "pack_halves", [(x, True) for x in (field, cot, w1, w2)],
        [
            near((size, nx, width), BF16),
            near((size, nx, width), BF16),
            near((9 * 4 * C, lane), BF16),
            near((lane, 9 * 4 * C), BF16),
        ],
        [pltpu.VMEM((width // lane, nx * ny, lane), F32)] * 2, flops=10 ** 9)
    bulk, taken, wfb = lax.optimization_barrier((bulk, taken, wfb))
    got = swap(bulk)
    whole, = call(join_edges, "join_edges", [(edge, True), (taken, True)], [near((3, across, width), BF16)])
    ends = [(gy_count + j, j + 1) for j in range(gy_count - 1)]
    late = lax.ppermute(whole, ("gx", "gy"), ends + [(b, a) for a, b in ends])
    held = [
        near((3, count + 4, across, wide), BF16),
        near((3, count + 2, across, wide), BF16),
        near((3, count + 2, across, width + lane), BF16),
        near((count, across, width + lane), BF16),
        near((count + 2, across + 16, width + lane), F32),
    ]
    fd, cd, hd, pg, hs, acc = call(
        interior, "interior",
        [(x, True) for x in (own, got, w1b, wfb)],
        held + [near((9, lane, 2 * lane), F32)],
        [
            pltpu.VMEM((count + 2, across + 16, width), F32),
            pltpu.VMEM((count + 1, across + 16, width), F32),
            pltpu.VMEM((count, across, width + lane), F32),
        ],
        limit=32, flops=4 * 10 ** 9)
    fd, cd, hd, pg, hs, send, pre_late = call(
        functools.partial(late_rows, gy_count), "late_rows",
        [(x, True) for x in (fd, cd, hd, pg, hs, late, acc, w1b, wfb)],
        held + [near((rows, lane), BF16), near((across, width + lane), F32)],
        [pltpu.VMEM((3, across + 16, width), F32)],
        limit=32, flops=10 ** 9, aliases={0: 0, 1: 1, 2: 2, 3: 3, 4: 4})

    other = swap(send)
    hd, _, keep = call(
        functools.partial(keep_sums, gy_count), "keep_sums",
        [(x, True) for x in (fd, cd, hd, pg, hs, pre_late, w1b)], [held[2], held[4], near((rows, lane), F32)],
        flops=2 * 10 ** 9, aliases={2: 0, 4: 1})
    other, keep = lax.optimization_barrier((other, keep))
    both, = call(add_pair, "add_pair", [(keep, True), (other, True)], [near((rows, lane), BF16)])
    both, hd, w2 = lax.optimization_barrier((both, hd, w2))
    terms = lax.all_to_all(both.reshape(ranks, rows // ranks, lane), ("grp", "gy"), 0, 0)
    mine, given = call(
        output_conv, "output_conv", [(hd, True), (w2, True)],
        [near((count, nx, width), BF16), near((count, nx, width), BF16)],
        [pltpu.VMEM((9 * 4 * C, lane), BF16)], flops=2 * 10 ** 9)
    given = swap(given)
    out, = call(
        finish_output, "finish_output", [(mine, True), (given, True)],
        [pltpu.HBM((nx, ny, width), BF16)],
        [pltpu.VMEM((nx, ny, width), BF16), pltpu.VMEM((width // lane, nx * ny, lane), F32), pltpu.SemaphoreType.DMA((nx // 2,))], far=True)
    terms, out = lax.optimization_barrier((terms, out))
    part, = call(add_terms, "add_terms", [(terms, True)], [near(terms.shape[1:], BF16)])
    spread = jnp.broadcast_to(part[None], terms.shape)
    sums = lax.all_to_all(spread, ("grp", "gy"), 0, 0).reshape(rows, lane)
    other = swap(sums)
    outs = [pltpu.HBM((27, C, C), F32)] * 2
    scratch = [pltpu.VMEM((27, C, C), F32), pltpu.SemaphoreType.DMA((3,))]
    first, second = call(functools.partial(unpack_own, factor), "unpack_own", [(sums, True)], outs, scratch, far=True)
    other, first, second = lax.optimization_barrier((other, first, second))
    first, second = call(
        functools.partial(unpack_other, factor), "unpack_other", [(other, True), (first, False), (second, False)], outs, scratch, far=True,
        aliases={1: 0, 2: 1})
    shape = (3, 3, 3, C, C)
    return out[None], first.reshape(shape), second.reshape(shape)


def solution(mesh):
    return jax.shard_map(
        shards,
        mesh=mesh,
        in_specs=(P("grp", "gx", "gy", None), P(), P(), P("grp", "gx", "gy", None)),
        out_specs=(P("grp", "gx", "gy", None), P(), P()),
        check_vma=False,
    )
```

```python
import functools
import math

import jax
import jax.numpy as jnp
from jax import lax
from jax.experimental import pallas as pl
from jax.experimental.pallas import tpu as pltpu
from jax.sharding import PartitionSpec as P

C = 64
NZ = 16
BF16 = jnp.bfloat16
F32 = jnp.float32
TAPS = [(dx, dy) for dy in range(3) for dx in range(3)]
BLOCKS = 14


def swap(array):
    return lax.ppermute(array, "gx", [(0, 1), (1, 0)])


def dot(a, b):
    return jnp.dot(a, b, preferred_element_type=F32)


def dot_nt(a, b):
    return lax.dot_general(a, b, (((1,), (1,)), ((), ())), preferred_element_type=F32)


def band(taps):
    zero = jnp.zeros((C, C), BF16)
    left = jnp.concatenate(list(taps) + [zero], axis=0)
    right = jnp.concatenate([zero] + list(taps), axis=0)
    return jnp.concatenate([left, right], axis=1)


def band_flipped(taps):
    zero = jnp.zeros((C, C), BF16)
    back = list(taps)[::-1]
    upper = jnp.concatenate(back + [zero], axis=1)
    lower = jnp.concatenate([zero] + back, axis=1)
    return jnp.concatenate([upper, lower], axis=0)


def packed(pieces):
    blocks = [piece[:, 0:2 * C] for piece in pieces]
    for pair in range(0, 9, 2):
        second = pieces[pair + 1][:, 2 * C:3 * C] if pair + 1 < 9 else jnp.zeros((C, C), F32)
        blocks.append(jnp.concatenate([pieces[pair][:, 2 * C:3 * C], second], axis=1))
    return blocks


def pack_edges(field_hbm, cot_hbm, w1_hbm, w2_hbm, field, cot, edge, given, w1, w2, rows, sems):
    copies = [
        pltpu.make_async_copy(source, target, sems.at[index])
        for index, (source, target) in enumerate(((field_hbm, field), (cot_hbm, cot), (w1_hbm, w1), (w2_hbm, w2)))
    ]
    for copy in copies:
        copy.start()
    for copy in copies[:2]:
        copy.wait()
    nx, ny, _ = field.shape
    gx = lax.axis_index("gx")
    for x in range(nx):
        fields = field[x].astype(F32)
        cots = cot[x].astype(F32)
        for index, row in enumerate((fields[0:1], fields[1:2], cots[0:1], fields[ny - 2:ny - 1], fields[ny - 1:ny], cots[ny - 1:ny])):
            rows[index, x:x + 1, :] = row
    head = rows[0:3].astype(BF16)
    tail = rows[3:6].astype(BF16)
    edge[...] = jnp.where(gx == 0, head, tail)
    given[...] = jnp.where(gx == 0, tail, head)
    for copy in copies[2:]:
        copy.wait()


def join_edges(edge, taken, whole):
    nx = edge.shape[1]
    gx = lax.axis_index("gx")

    @pl.when(gx == 0)
    def _():
        whole[:, 0:nx] = edge[...]
        whole[:, nx:2 * nx] = taken[...]

    @pl.when(gx != 0)
    def _():
        whole[:, 0:nx] = taken[...]
        whole[:, nx:2 * nx] = edge[...]


def put_rows(scratch, start, rows):
    lane = 2 * C
    for tile in range(scratch.shape[0]):
        scratch[tile, start:start + rows.shape[0], :] = rows[:, lane * tile:lane * (tile + 1)]


def take_rows(scratch, start, count, stride):
    return jnp.concatenate(
        [scratch[tile, pl.ds(start, count, stride=stride), :] for tile in range(scratch.shape[0])], axis=1).astype(BF16)


def pack_halves(field, cot, w1, w2, own, bulk, w1b, wfb, turned_f, turned_c):
    nx, ny, _ = field.shape
    half = ny // 2
    for source, target in ((field, turned_f), (cot, turned_c)):
        for x in range(nx):
            put_rows(target, x * ny, source[x].astype(F32))
    gx = lax.axis_index("gx")

    def place(target, first_f, first_c):
        for y in range(half + 2):
            target[y] = take_rows(turned_f, first_f + y, nx, ny)
        for y in range(half + 1):
            target[half + 2 + y] = take_rows(turned_c, first_c + y, nx, ny)

    @pl.when(gx == 0)
    def _():
        place(own, 0, 0)
        place(bulk, half - 2, half - 1)

    @pl.when(gx != 0)
    def _():
        place(own, half - 2, half - 1)
        place(bulk, 0, 0)

    make_bands(w1, w2, w1b, wfb)


def make_bands(w1, w2, w1b, wfb):
    for t, (dx, dy) in enumerate(TAPS):
        rows = slice(t * 4 * C, (t + 1) * 4 * C)
        first = 9 * dx + 3 * dy
        w1b[rows, :] = band([w1[first + z] for z in range(3)])
        wfb[:, rows] = band_flipped([w2[24 - first + z] for z in range(3)])


def blank_edges(copies):
    lane = 2 * C
    zero = jnp.zeros(copies.shape[:-1] + (lane,), BF16)
    copies[..., 0:lane] = zero
    copies[..., copies.shape[-1] - lane:] = zero


def blank_rows(scratch):
    zero = jnp.zeros((scratch.shape[0], 1, scratch.shape[2]), F32)
    scratch[:, 7:8, :] = zero
    scratch[:, scratch.shape[1] - 8:scratch.shape[1] - 7, :] = zero


def shift_rows(scratch, copies, start, first_lane, taps=(0, 1, 2)):
    count, rows, width = scratch.shape
    for dx in taps:
        copies[dx, pl.ds(start, count), :, first_lane:first_lane + width] = scratch[:, 7 + dx:rows - 9 + dx, :].astype(BF16)


def inside_lanes(p):
    lane_of = lax.broadcasted_iota(jnp.int32, (1, 2 * C), 1)
    if p == 0:
        return (lane_of >= C).astype(F32)
    if p == NZ // 2:
        return (lane_of < C).astype(F32)
    return 1.0


def windows(copies, first, count, p):
    lane = 2 * C
    rows = copies.shape[2]
    return jnp.concatenate(
        [
            copies[dx, pl.ds(first + dy, count), :, lane * p:lane * (p + 2)].reshape(count * rows, 2 * lane)
            for dx, dy in TAPS
        ],
        axis=1,
    )


def pre_gradient(grad, pre, p):
    sigma = jax.nn.sigmoid(pre)
    return grad * sigma * (1.0 + pre * (1.0 - sigma)) * inside_lanes(p)


def interior(own, got, w1b, wfb, fd, cd, hd, pg, hs, acc, fs, cs, slope):
    gx = lax.axis_index("gx")
    nx, width = own.shape[1:]
    across = 2 * nx
    count = pg.shape[0]
    cells = count * across
    lane = 2 * C
    pairs = NZ // 2

    def place(left, right):
        for scratch, copies, offset, start, size in ((fs, fd, 2 - 2 * gx, 0, count + 2), (cs, cd, 1 - gx, count + 2, count + 1)):
            for source, row in ((left, 0), (right, nx)):
                rows = source[start:start + size]
                scratch[:, 8 + row:8 + row + nx, :] = rows.astype(F32)
                copies[1, pl.ds(offset, size), row:row + nx, lane:lane + width] = rows

    @pl.when(gx == 0)
    def _():
        place(own, got)

    @pl.when(gx != 0)
    def _():
        place(got, own)

    for scratch in (fs, cs, hs):
        blank_rows(scratch)
    blank_edges(fd)
    blank_edges(cd)
    shift_rows(fs, fd, 2 - 2 * gx, lane, (0, 2))
    shift_rows(cs, cd, 1 - gx, lane, (0, 2))
    for group in range(0, pairs + 1, 3):
        value = dot(jnp.concatenate([windows(fd, 2 - 2 * gx, count, p) for p in range(group, group + 3)], axis=0), w1b[...])
        for p in range(group, group + 3):
            here = slice(lane * p, lane * (p + 1))
            part = value[cells * (p - group):cells * (p - group + 1)]
            sigma = jax.nn.sigmoid(part)
            slope[:, :, here] = (sigma * (1.0 + part * (1.0 - sigma)) * inside_lanes(p)).reshape(count, across, lane)
            hidden = (part * sigma * inside_lanes(p)).reshape(count, across, lane)
            hs[pl.ds(2 - 2 * gx, count), 8:8 + across, here] = hidden
            hd[1, pl.ds(2 - 2 * gx, count), :, here] = hidden.astype(BF16)
    cells = cells - across
    for group in range(0, pairs + 1, 3):
        value = dot_nt(jnp.concatenate([windows(cd, 1 - gx, count - 1, p) for p in range(group, group + 3)], axis=0), wfb[...])
        for p in range(group, group + 3):
            here = slice(lane * p, lane * (p + 1))
            part = value[cells * (p - group):cells * (p - group + 1)]
            grad = part * slope[pl.ds(gx, count - 1), :, here].reshape(cells, lane)
            pg[pl.ds(1 - gx, count - 1), :, here] = grad.astype(BF16).reshape(count - 1, across, lane)
    pg[pl.ds((count - 1) * gx, 1)] = jnp.zeros((1,) + pg.shape[1:], BF16)

    @pl.when(gx == 0)
    def _():
        hd[:, 0:2] = jnp.zeros((3, 2) + hd.shape[2:], BF16)
        shift_rows(hs.at[2:2 + count], hd, 2, 0, (0, 2))
        for t, total in enumerate(second_products(hd, cd)):
            acc[t] = total

    @pl.when(gx != 0)
    def _():
        fd[:, count + 2:count + 4] = jnp.zeros((3, 2) + fd.shape[2:], BF16)
        for t, total in enumerate(first_products(fd, pg)):
            acc[t] = total


def second_products(hd, cd):
    lane = 2 * C
    pairs = NZ // 2
    count, across = hd.shape[1] - 2, hd.shape[2]
    cells = count * across
    cot_t = jnp.concatenate(
        [cd[1, 1:1 + count, :, lane * (p + 1):lane * (p + 2)].reshape(cells, lane).T for p in range(pairs)], axis=1)
    return [
        dot(cot_t, jnp.concatenate(
            [hd[dx, dy:dy + count, :, lane * p:lane * (p + 2)].reshape(cells, 2 * lane) for p in range(pairs)], axis=0))
        for dx, dy in TAPS
    ]


def first_products(fd, pg):
    lane = 2 * C
    pairs = NZ // 2
    count, across, _ = pg.shape
    cells = count * across
    grad_t = jnp.concatenate(
        [pg[:, :, lane * p:lane * (p + 1)].reshape(cells, lane).T for p in range(pairs + 1)], axis=1)
    return [
        dot(grad_t, jnp.concatenate(
            [fd[dx, 1 + dy:1 + dy + count, :, lane * p:lane * (p + 2)].reshape(cells, 2 * lane) for p in range(pairs + 1)], axis=0))
        for dx, dy in TAPS
    ]


def folded(total):
    return total[0:C, 0:3 * C] + total[C:2 * C, C:4 * C]


def second_late(hd, cd):
    lane = 2 * C
    pairs = NZ // 2
    late = ((0, 1), (0,), ())
    products = []
    for dx, dy in TAPS:
        if late[dy]:
            cots = jnp.concatenate(
                [cd[1, 1 + y, :, lane * (p + 1):lane * (p + 2)] for y in late[dy] for p in range(pairs)], axis=0)
            rows = jnp.concatenate(
                [hd[dx, y + dy, :, lane * p:lane * (p + 2)] for y in late[dy] for p in range(pairs)], axis=0)
            products.append(dot(cots.T, rows))
        else:
            products.append(0.0)
    return products


def first_late(fd, pg):
    lane = 2 * C
    pairs = NZ // 2
    count, across, _ = pg.shape
    y = count - 1
    extra = 2 * lane - (pairs + 1) * across
    grad_t = jnp.concatenate(
        [pg[y, :, lane * p:lane * (p + 1)] for p in range(pairs + 1)] + [jnp.zeros((extra, lane), BF16)], axis=0).T
    pad = jnp.zeros((extra, 2 * lane), BF16)
    return [
        dot(grad_t, jnp.concatenate(
            [fd[dx, y + dy + 1, :, lane * p:lane * (p + 2)] for p in range(pairs + 1)] + [pad], axis=0))
        for dx, dy in TAPS
    ]


def sums_of(products):
    return packed([folded(product) for product in products])


def store_blocks(target, blocks):
    for index, block in enumerate(blocks):
        target[index * C:(index + 1) * C, :] = block.astype(target.dtype)
    if target.shape[0] > BLOCKS * C:
        target[BLOCKS * C:, :] = jnp.zeros((target.shape[0] - BLOCKS * C, 2 * C), target.dtype)


def hidden_of(value, p):
    return value * jax.nn.sigmoid(value) * inside_lanes(p)


def stacked(copies, first, count, pairs):
    return jnp.concatenate([windows(copies, first, count, p) for p in range(pairs + 1)], axis=0)


def late_rows(gy_count, fd_in, cd_in, hd_in, pg_in, hs_in, rows, acc, w1b, wfb, fd, cd, hd, pg, hs, send, pre_late, rs):
    gx = lax.axis_index("gx")
    gy = lax.axis_index("gy")
    count, across, _ = pg.shape
    lane = 2 * C
    pairs = NZ // 2
    rs[:, 8:8 + across, :] = rows[...].astype(F32)
    blank_rows(rs)

    @pl.when(gx == 0)
    def _():
        shift_rows(rs.at[0:2], fd, 0, lane)
        shift_rows(rs.at[2:3], cd, 0, lane)
        value = dot(stacked(fd, 0, 2, pairs), w1b[...])
        grad = dot_nt(stacked(cd, 0, 1, pairs), wfb[...])
        before = jnp.where(gy == 0, 0.0, 1.0)
        for p in range(pairs + 1):
            here = slice(lane * p, lane * (p + 1))
            early = value[2 * across * p:2 * across * p + across]
            later = value[2 * across * p + across:2 * across * (p + 1)]
            mine = pre_gradient(grad[across * p:across * (p + 1)], later, p)
            pg[0, :, here] = mine.astype(BF16)
            both = jnp.stack([hidden_of(early, p) * before, hidden_of(later, p)])
            hs[0:2, 8:8 + across, here] = both
            hd[1, 0:2, :, here] = both.astype(BF16)
        shift_rows(hs.at[0:2], hd, 0, 0, (0, 2))
        store_blocks(send, sums_of([acc[t] + late for t, late in enumerate(second_late(hd, cd))]))

    @pl.when(gx != 0)
    def _():
        shift_rows(rs.at[0:2], fd, count + 2, lane)
        shift_rows(rs.at[2:3], cd, count + 1, lane)
        value = dot(stacked(fd, count, 1, pairs), w1b[...])
        grad = dot_nt(stacked(cd, count - 1, 1, pairs), wfb[...])
        for p in range(pairs + 1):
            here = slice(lane * p, lane * (p + 1))
            part = slice(across * p, across * (p + 1))
            pre_late[:, here] = value[part]
            pg[count - 1, :, here] = pre_gradient(grad[part], value[part], p).astype(BF16)
        store_blocks(send, sums_of([acc[t] + late for t, late in enumerate(first_late(fd, pg))]))


def keep_sums(gy_count, fd, cd, hd_in, pg, hs_in, pre_late, w1b, hd, hs, keep):
    gx = lax.axis_index("gx")
    gy = lax.axis_index("gy")
    count, across, _ = pg.shape
    lane = 2 * C
    pairs = NZ // 2

    @pl.when(gx == 0)
    def _():
        store_blocks(keep, sums_of(first_products(fd, pg)))

    @pl.when(gx != 0)
    def _():
        value = dot(stacked(fd, count + 1, 1, pairs), w1b[...])
        beyond = jnp.where(gy == gy_count - 1, 0.0, 1.0)
        for p in range(pairs + 1):
            here = slice(lane * p, lane * (p + 1))
            part = slice(across * p, across * (p + 1))
            both = jnp.stack([hidden_of(pre_late[:, here], p), hidden_of(value[part], p) * beyond])
            hs[count:count + 2, 8:8 + across, here] = both
            hd[1, count:count + 2, :, here] = both.astype(BF16)
        shift_rows(hs, hd, 0, 0, (0, 2))
        store_blocks(keep, sums_of(second_products(hd, cd)))


def output_conv(hd, w2, mine, given, w2b):
    for t, (dx, dy) in enumerate(TAPS):
        w2b[t * 4 * C:(t + 1) * 4 * C, :] = band([w2[9 * dx + 3 * dy + z] for z in range(3)])
    gx = lax.axis_index("gx")
    count, half, _ = mine.shape
    lane = 2 * C
    for p in range(NZ // 2):
        here = slice(lane * p, lane * (p + 1))
        value = dot(windows(hd, 0, count, p), w2b[...]).reshape(count, 2 * half, lane)
        left, right = value[:, 0:half], value[:, half:]
        mine[:, :, here] = jnp.where(gx == 0, left, right).astype(BF16)
        given[:, :, here] = jnp.where(gx == 0, right, left).astype(BF16)


def finish_output(mine, other, out, turned, scratch, sems):
    count, nx, width = mine.shape
    gx = lax.axis_index("gx")
    for y in range(count):
        a = mine[y].astype(F32)
        b = other[y].astype(F32)
        put_rows(scratch, y * nx, jnp.where(gx == 0, a, b))
        put_rows(scratch, (count + y) * nx, jnp.where(gx == 0, b, a))
    copies = []
    for x in range(nx):
        turned[x] = take_rows(scratch, x, 2 * count, nx)
        if x % 2:
            copies.append(pltpu.make_async_copy(turned.at[x - 1:x + 1], out.at[x - 1:x + 1], sems.at[x // 2]))
            copies[-1].start()
    for copy in copies:
        copy.wait()


def add_pair(keep, other, out):
    out[...] = (keep[...] + other[...].astype(F32)).astype(BF16)


def add_terms(terms, out):
    total = terms[0].astype(F32)
    for index in range(1, terms.shape[0]):
        total = total + terms[index].astype(F32)
    out[...] = total.astype(BF16)


def unpack(factor, is_first, rows, first, second, held, sems):
    def each(act):
        for chosen, target in ((is_first, first), (jnp.logical_not(is_first), second)):
            @pl.when(chosen)
            def _():
                act(target)

    def copy_of(dx, target):
        piece = slice(9 * dx, 9 * dx + 9)
        return pltpu.make_async_copy(held.at[piece], target.at[piece], sems.at[dx])

    for dx in range(3):
        for dy in range(3):
            t = 3 * dy + dx
            place = 9 * dx + 3 * dy
            turned = rows[t * C:(t + 1) * C, :].T.astype(F32) * factor
            held[place] = turned[0:C]
            held[place + 1] = turned[C:2 * C]
            turned = rows[(9 + t // 2) * C:(10 + t // 2) * C, :].T.astype(F32) * factor
            held[place + 2] = turned[t % 2 * C:(t % 2 + 1) * C]
        each(lambda target: copy_of(dx, target).start())
    each(lambda target: [copy_of(dx, target).wait() for dx in range(3)])


def unpack_own(factor, rows, first, second, held, sems):
    unpack(factor, lax.axis_index("gx") == 0, rows, first, second, held, sems)


def unpack_other(factor, rows, first_in, second_in, first, second, held, sems):
    unpack(factor, lax.axis_index("gx") != 0, rows, first, second, held, sems)


def near(shape, dtype):
    return pltpu.VMEM(shape, dtype)


def call(body, name, inputs, outs, scratch=(), limit=16, flops=0, far=False, aliases=None):
    placed = [pltpu.with_memory_space_constraint(x, pltpu.VMEM if held else pltpu.HBM) for x, held in inputs]
    size = sum(x.size * x.dtype.itemsize for x, _ in inputs)
    return pl.pallas_call(
        body,
        out_shape=list(outs),
        in_specs=[pl.BlockSpec(memory_space=pltpu.VMEM if held else pl.ANY) for _, held in inputs],
        out_specs=[pl.BlockSpec(memory_space=pl.ANY if far else pltpu.VMEM)] * len(outs),
        scratch_shapes=list(scratch),
        input_output_aliases=aliases or {},
        compiler_params=pltpu.CompilerParams(vmem_limit_bytes=limit * 1024 * 1024),
        cost_estimate=pl.CostEstimate(flops=flops, bytes_accessed=size, transcendentals=0),
        name=name,
    )(*placed)


def shards(field_in, first_weight, second_weight, cotangent):
    nx, ny, width = field_in.shape[1:]
    gx_count, gy_count, grp_count = (lax.axis_size(axis) for axis in ("gx", "gy", "grp"))
    total = field_in.shape[0] * nx * ny * NZ * gx_count * gy_count * grp_count
    factor = 1.0 / math.sqrt(total)
    ranks = gy_count * grp_count
    rows = -(-BLOCKS * C // (8 * ranks)) * 8 * ranks
    lane = 2 * C
    wide = width + 2 * lane
    count = ny // 2
    across = 2 * nx
    size = 2 * count + 3

    field, cot, edge, given, w1, w2 = call(
        pack_edges, "pack_edges",
        [(x, False) for x in (field_in[0], cotangent[0], first_weight.reshape(27, C, C), second_weight.reshape(27, C, C))],
        [
            near((nx, ny, width), BF16),
            near((nx, ny, width), BF16),
            near((3, nx, width), BF16),
            near((3, nx, width), BF16),
            near((27, C, C), BF16),
            near((27, C, C), BF16),
        ],
        [pltpu.VMEM((6, nx, width), F32), pltpu.SemaphoreType.DMA((4,))])
    taken = swap(given)
    own, bulk, w1b, wfb = call(
        pack_halves, "pack_halves", [(x, True) for x in (field, cot, w1, w2)],
        [
            near((size, nx, width), BF16),
            near((size, nx, width), BF16),
            near((9 * 4 * C, lane), BF16),
            near((lane, 9 * 4 * C), BF16),
        ],
        [pltpu.VMEM((width // lane, nx * ny, lane), F32)] * 2, flops=10 ** 9)
    bulk, taken, wfb = lax.optimization_barrier((bulk, taken, wfb))
    got = swap(bulk)
    whole, = call(join_edges, "join_edges", [(edge, True), (taken, True)], [near((3, across, width), BF16)])
    ends = [(gy_count + j, j + 1) for j in range(gy_count - 1)]
    late = lax.ppermute(whole, ("gx", "gy"), ends + [(b, a) for a, b in ends])
    held = [
        near((3, count + 4, across, wide), BF16),
        near((3, count + 2, across, wide), BF16),
        near((3, count + 2, across, width + lane), BF16),
        near((count, across, width + lane), BF16),
        near((count + 2, across + 16, width + lane), F32),
    ]
    fd, cd, hd, pg, hs, acc = call(
        interior, "interior",
        [(x, True) for x in (own, got, w1b, wfb)],
        held + [near((9, lane, 2 * lane), F32)],
        [
            pltpu.VMEM((count + 2, across + 16, width), F32),
            pltpu.VMEM((count + 1, across + 16, width), F32),
            pltpu.VMEM((count, across, width + lane), F32),
        ],
        limit=32, flops=4 * 10 ** 9)
    fd, cd, hd, pg, hs, send, pre_late = call(
        functools.partial(late_rows, gy_count), "late_rows",
        [(x, True) for x in (fd, cd, hd, pg, hs, late, acc, w1b, wfb)],
        held + [near((rows, lane), BF16), near((across, width + lane), F32)],
        [pltpu.VMEM((3, across + 16, width), F32)],
        limit=32, flops=10 ** 9, aliases={0: 0, 1: 1, 2: 2, 3: 3, 4: 4})

    other = swap(send)
    hd, _, keep = call(
        functools.partial(keep_sums, gy_count), "keep_sums",
        [(x, True) for x in (fd, cd, hd, pg, hs, pre_late, w1b)], [held[2], held[4], near((rows, lane), F32)],
        flops=2 * 10 ** 9, aliases={2: 0, 4: 1})
    other, keep = lax.optimization_barrier((other, keep))
    both, = call(add_pair, "add_pair", [(keep, True), (other, True)], [near((rows, lane), BF16)])
    both, hd, w2 = lax.optimization_barrier((both, hd, w2))
    terms = lax.all_to_all(both.reshape(ranks, rows // ranks, lane), ("grp", "gy"), 0, 0)
    mine, given = call(
        output_conv, "output_conv", [(hd, True), (w2, True)],
        [near((count, nx, width), BF16), near((count, nx, width), BF16)],
        [pltpu.VMEM((9 * 4 * C, lane), BF16)], flops=2 * 10 ** 9)
    given = swap(given)
    out, = call(
        finish_output, "finish_output", [(mine, True), (given, True)],
        [pltpu.HBM((nx, ny, width), BF16)],
        [pltpu.VMEM((nx, ny, width), BF16), pltpu.VMEM((width // lane, nx * ny, lane), F32), pltpu.SemaphoreType.DMA((nx // 2,))], far=True)
    terms, out = lax.optimization_barrier((terms, out))
    part, = call(add_terms, "add_terms", [(terms, True)], [near(terms.shape[1:], BF16)])
    spread = jnp.broadcast_to(part[None], terms.shape)
    sums = lax.all_to_all(spread, ("grp", "gy"), 0, 0).reshape(rows, lane)
    other = swap(sums)
    outs = [pltpu.HBM((27, C, C), F32)] * 2
    scratch = [pltpu.VMEM((27, C, C), F32), pltpu.SemaphoreType.DMA((3,))]
    first, second = call(functools.partial(unpack_own, factor), "unpack_own", [(sums, True)], outs, scratch, far=True)
    other, first, second = lax.optimization_barrier((other, first, second))
    first, second = call(
        functools.partial(unpack_other, factor), "unpack_other", [(other, True), (first, False), (second, False)], outs, scratch, far=True,
        aliases={1: 0, 2: 1})
    shape = (3, 3, 3, C, C)
    return out[None], first.reshape(shape), second.reshape(shape)


def solution(mesh):
    return jax.shard_map(
        shards,
        mesh=mesh,
        in_specs=(P("grp", "gx", "gy", None), P(), P(), P("grp", "gx", "gy", None)),
        out_specs=(P("grp", "gx", "gy", None), P(), P()),
        check_vma=False,
    )
```
